32 devices in a mesh: stn: 16 (over z, y, core), chan: 2 (over x).
Axes of the slice: x: 2, y: 2, z: 4, core: 2. Of those that a mesh axis runs over, the one named last changes fastest.
Arguments:
- volts: bfloat16 [48, 2, 16, 32768], P('chan', None, None, 'stn'), may hold values from -6 to 6
- antenna_tile_weights: bfloat16 [48, 2, 32768], P('chan', None, 'stn'), may hold values from -1 to 1
- station_weights: bfloat16 [48, 2, 2048], P('chan', None, 'stn'), may hold values from -1 to 1
- tile_station: int32 [2048], P('stn'), may hold values from 0 to 127, as said below
- station_group: int32 [128], replicated, may hold values from 0 to 3
- station_pos: float32 [128, 2], replicated, may hold values from -3 to 3
- beam_dir: float32 [64, 2], replicated, may hold values from -1 to 1
- beam_order: int32 [64], replicated, may hold values from 0 to 63, each once
Outputs:
- tied_beams: bfloat16 [64, 48, 32], P(('stn', 'chan'))
The draws below stay inside these ranges and needn't reach their ends.
Inputs may be any that keep to these rules, and one draw needn't show every extreme that they name: `tile_station`: the tiles of aligned block j of 128 tiles belong to stations j * 8 to j * 8 + 7, each of them exactly 16 tiles.
All inputs are finite; a program needn't handle non-finite values.
Results may differ from the reference program's by a relative error of at most 0.011.
Values may be sent and summed in bfloat16 or wider, within the bound.
No kernel may reach another device: no remote copies, remote signals or barrier semaphores. Data moves between devices by JAX's collectives and lax.ppermute only.
A program may use at most 128 MiB of HBM per device.

```python
import math
import jax
import jax.numpy as jnp
from jax import lax

TILE_ANTENNAS = 16
TPS = 16
STN_DEV = 8
TIME_SAMPLES = 16
GROUPS = 4
STATIONS = 128
TILE_COUNT = 2048
ANTENNA_COUNT = 32768
CHANNEL_COUNT = 48
BEAMS = 64


def draw_tile_station(key, part):
    key = jax.random.fold_in(key, 11)
    blocks = STATIONS // STN_DEV
    pattern = jnp.repeat(jnp.arange(STN_DEV, dtype=jnp.int32), TPS)
    block_keys = jax.random.split(key, blocks)

    def shuffle(block_key):
        return jax.random.permutation(block_key, pattern)
    shuffled = jax.vmap(shuffle)(block_keys)
    offsets = (jnp.arange(blocks, dtype=jnp.int32) * STN_DEV)[:, None]
    return (shuffled + offsets).reshape(-1)


def plant(entries, stream_key, smallest, high):
    longest = entries.shape.index(max(entries.shape))
    spots = []
    for shift in (0, 1):
        where = [jax.random.randint(jax.random.fold_in(stream_key, axis), (), 0, length) for axis, length in enumerate(entries.shape)]
        where[longest] = (where[longest] + shift) % entries.shape[longest]
        spots.append(tuple(where))
    return entries.at[spots[0]].set(smallest).at[spots[1]].set(high)


def levels(own_key, dims, cuts, smallest, top_value):
    level, own = 1.0, jax.random.fold_in(own_key, 6)
    for dim, parts in cuts:
        steps = jnp.exp(jax.random.uniform(jax.random.fold_in(own, dim), (parts,), jnp.float32, smallest / len(cuts), top_value / len(cuts)))
        level = level * jnp.repeat(steps, dims[dim] // parts).reshape([-1 if axis == dim else 1 for axis in range(len(dims))])
    return level


def bell_draw(stream_key, extent, scale, bound, pieces=(), kind=jnp.bfloat16):
    drawn = scale * jax.random.normal(stream_key, extent, jnp.float32)
    if pieces:
        drawn = drawn * levels(stream_key, extent, pieces, -0.22, 0.18)
    return jnp.clip(drawn, -bound, bound).astype(kind)


def setup_inputs(seed: int = 0) -> dict:
    key_list = jax.random.split(jax.random.key(seed), 9)
    return {
        "volts": bell_draw(key_list[0], (CHANNEL_COUNT, 2, TIME_SAMPLES, ANTENNA_COUNT), 1.0, 6.0, ((0, 2), (3, 16))),
        "antenna_tile_weights": bell_draw(key_list[1], (CHANNEL_COUNT, 2, ANTENNA_COUNT), (2 * TILE_ANTENNAS) ** -0.5, 1.0, ((0, 2), (2, 16))),
        "station_weights": bell_draw(key_list[2], (CHANNEL_COUNT, 2, TILE_COUNT), (2 * TPS) ** -0.5, 1.0, ((0, 2), (2, 16))),
        "tile_station": draw_tile_station(jax.random.fold_in(key_list[8], 71), 0),
        "station_group": plant(jax.random.randint(key_list[4], (STATIONS,), 0, GROUPS), jax.random.fold_in(key_list[4], 1), 0, GROUPS - 1).astype(jnp.int32),
        "station_pos": jnp.clip(jax.random.uniform(key_list[5], (STATIONS, 2), jnp.float32, -3.0, 3.0), -3.0, 3.0),
        "beam_dir": jnp.clip(jax.random.uniform(key_list[6], (BEAMS, 2), jnp.float32, -1.0, 1.0), -1.0, 1.0),
        "beam_order": jax.random.permutation(key_list[7], BEAMS).astype(jnp.int32),
    }


def tied_weights(directions, positions, groups, beam_ids, freq, scale):
    delay = directions[:, 0:1] * positions[None, :, 0] + directions[:, 1:2] * positions[None, :, 1]
    phase = (2.0 * math.pi * freq)[None, None, :] * delay[:, :, None]
    member = (groups[None, :] == beam_ids[:, None] % GROUPS).astype(jnp.float32)
    return (jnp.stack([jnp.cos(phase), jnp.sin(phase)], axis=-1) * (member * scale)[:, :, None, None]).astype(jnp.bfloat16)

def reference(volts, antenna_tile_weights, station_weights, tile_station, station_group, station_pos, beam_dir, beam_order):

    def one_channel(inputs):
        volt, tile_w, station_w = inputs
        volt_re = volt[0].astype(jnp.float32)
        volt_im = volt[1].astype(jnp.float32)
        weight_re = tile_w[0].astype(jnp.float32)[None, :]
        weight_im = tile_w[1].astype(jnp.float32)[None, :]
        product_real = weight_re * volt_re - weight_im * volt_im
        product_imaginary = weight_re * volt_im + weight_im * volt_re
        tile_beam_real = product_real.reshape(TIME_SAMPLES, TILE_COUNT, TILE_ANTENNAS).sum(-1).astype(jnp.bfloat16).astype(jnp.float32)
        tile_beam_imaginary = product_imaginary.reshape(TIME_SAMPLES, TILE_COUNT, TILE_ANTENNAS).sum(-1).astype(jnp.bfloat16).astype(jnp.float32)
        swt_re = station_w[0].astype(jnp.float32)[None, :]
        swt_im = station_w[1].astype(jnp.float32)[None, :]
        term_re = swt_re * tile_beam_real - swt_im * tile_beam_imaginary
        term_im = swt_re * tile_beam_imaginary + swt_im * tile_beam_real
        stn_re = jax.ops.segment_sum(term_re.T, tile_station, num_segments=STATIONS).astype(jnp.bfloat16)
        stn_im = jax.ops.segment_sum(term_im.T, tile_station, num_segments=STATIONS).astype(jnp.bfloat16)
        first = jnp.concatenate([stn_re, stn_im], axis=1)
        second = jnp.concatenate([stn_im, -stn_re], axis=1)
        return jnp.stack([first, second], axis=1)
    stacked = lax.map(one_channel, (volts, antenna_tile_weights, station_weights))
    stacked = jnp.transpose(stacked, (1, 0, 2, 3))
    freq = 1.0 + jnp.arange(CHANNEL_COUNT, dtype=jnp.float32) / CHANNEL_COUNT
    directions = beam_dir[beam_order]
    weights = tied_weights(directions, station_pos, station_group, beam_order, freq, 1.0 / math.sqrt(STATIONS))
    tied = jnp.einsum('bscp,scpx->bcx', weights.astype(jnp.float32), stacked.astype(jnp.float32), precision=lax.Precision.HIGHEST)
    return tied.astype(jnp.bfloat16)
```

```python
import functools
import math

import jax
import jax.numpy as jnp
from jax import lax
from jax.experimental import pallas as pl
from jax.experimental.pallas import tpu as pltpu
from jax.sharding import PartitionSpec as P

TILE_ANTENNAS = 16
TPS = 16
GROUPS = 4
CB = 8
CHUNK = 256
NT = (((1,), (1,)), ((), ()))
SIN = [(-1) ** i * (2 * math.pi) ** (2 * i + 1) / math.factorial(2 * i + 1) for i in range(7)]


def dot_nt(a, b):
    return lax.dot_general(a, b, NT, preferred_element_type=jnp.float32)


def iota(shape, dim):
    return lax.broadcasted_iota(jnp.int32, shape, dim)


def beam_columns(order_ref, dir_ref, start, rows):
    beams = order_ref.shape[1]
    order = order_ref[...].astype(jnp.float32)
    lane = iota((rows, beams), 1)
    own = lane == iota((rows, beams), 0) + start
    ids = jnp.sum(jnp.where(own, order, 0.0), axis=1, keepdims=True)
    pick = lane.astype(jnp.float32) == ids
    east = jnp.sum(jnp.where(pick, dir_ref[0:1, :], 0.0), axis=1, keepdims=True)
    north = jnp.sum(jnp.where(pick, dir_ref[1:2, :], 0.0), axis=1, keepdims=True)
    group = ids - GROUPS * jnp.floor(ids * (1.0 / GROUPS))
    return east, north, group


def station_rows(pos_ref, group_ref, stations, lanes):
    total = group_ref.shape[1]
    first = lax.axis_index("stn") * stations
    own = iota((stations, total), 1) == iota((stations, total), 0) + first
    spread = iota((stations, lanes), 0) == iota((stations, lanes), 1) % stations

    def turn(row):
        column = jnp.sum(jnp.where(own, row, 0.0), axis=1, keepdims=True)
        return jnp.sum(jnp.where(spread, column, 0.0), axis=0, keepdims=True)

    return turn(pos_ref[0:1, :]), turn(pos_ref[1:2, :]), turn(group_ref[...].astype(jnp.float32))


def cos_turns(t):
    y = t - jnp.floor(t + 0.5)
    z = 0.25 - jnp.abs(y)
    z2 = z * z
    value = jnp.full_like(z, SIN[-1])
    for coefficient in SIN[-2::-1]:
        value = value * z2 + coefficient
    return value * z


def kernel(
    volt_hbm, aw_ref, sw_ref, ts_ref, group_ref, pos_ref, dir_ref, order_ref, out_ref, volts, sems
):
    channels, _, samples, antennas = volt_hbm.shape
    tiles = sw_ref.shape[2]
    stations = tiles // TPS
    chunks = antennas // CHUNK
    per_chunk = CHUNK // TILE_ANTENNAS
    groups = channels // CB
    rows_c = 2 * samples
    beams = order_ref.shape[1]
    lanes = CB * 2 * stations
    scale = 1.0 / math.sqrt(group_ref.shape[1])

    copies = []
    for g in range(groups):
        part = pl.ds(g * CB, CB)
        copy = pltpu.make_async_copy(volt_hbm.at[part], volts.at[part], sems.at[g])
        copy.start()
        copies.append(copy)

    east_s, north_s, group_s = station_rows(pos_ref, group_ref, stations, lanes)
    lane = iota((1, lanes), 1)
    channel_lane = lane // (2 * stations)
    quarter = 0.25 * ((lane // stations) % 2).astype(jnp.float32)
    first_chan = lax.axis_index("chan") * channels
    total_chans = channels * lax.axis_size("chan")
    block = min(64, beams)

    mask16 = (iota((per_chunk, CHUNK), 1) // TILE_ANTENNAS == iota((per_chunk, CHUNK), 0)).astype(
        jnp.float32
    )
    member_table = (iota((stations, tiles), 0) == ts_ref[...] % stations).astype(jnp.float32)
    own_channel = iota((CB * rows_c, lanes), 0) // rows_c == iota((CB * rows_c, lanes), 1) // (
        2 * stations
    )
    lane_chunk = iota((rows_c, 2 * tiles), 1) // per_chunk % chunks

    for g in range(groups):
        channel0 = g * CB
        weights = aw_ref[channel0 : channel0 + CB].astype(jnp.float32)
        copies[g].wait()
        found = [None] * CB
        for step in range(chunks):
            left = jnp.concatenate(
                [
                    volts[
                        channel0 + c,
                        :,
                        :,
                        (c + step) % chunks * CHUNK : ((c + step) % chunks + 1) * CHUNK,
                    ].reshape(rows_c, CHUNK)
                    for c in range(CB)
                ],
                axis=0,
            )
            right = jnp.concatenate(
                [
                    (
                        weights[(q - step) % CB, part : part + 1, q * CHUNK : (q + 1) * CHUNK]
                        * mask16
                    ).astype(jnp.bfloat16)
                    for part in range(2)
                    for q in range(chunks)
                ],
                axis=0,
            )
            product = dot_nt(left, right)
            for c in range(CB):
                mine = product[c * rows_c : (c + 1) * rows_c]
                if step == 0:
                    found[c] = mine
                else:
                    found[c] = jnp.where(lane_chunk == (c + step) % chunks, mine, found[c])
        left = []
        for c in range(CB):
            real, imag = found[c][:samples], found[c][samples:]
            tile_re = (real[:, :tiles] - imag[:, tiles:]).astype(jnp.bfloat16)
            tile_im = (imag[:, :tiles] + real[:, tiles:]).astype(jnp.bfloat16)
            left.append(jnp.concatenate([tile_re, tile_im], axis=1))
            left.append(jnp.concatenate([tile_im, -tile_re], axis=1))
        right = []
        swt = sw_ref[channel0 : channel0 + CB].astype(jnp.float32)
        for c in range(CB):
            re = swt[c, 0:1] * member_table
            im = swt[c, 1:2] * member_table
            right.append(jnp.concatenate([re, -im], axis=1))
            right.append(jnp.concatenate([im, re], axis=1))
        station = dot_nt(
            jnp.concatenate(left, axis=0), jnp.concatenate(right, axis=0).astype(jnp.bfloat16)
        )
        station = jnp.where(own_channel, station, 0.0).astype(jnp.bfloat16)

        freq = 1.0 + (first_chan + channel0 + channel_lane).astype(jnp.float32) / total_chans

        def tied_rows(start):
            east, north, group = beam_columns(order_ref, dir_ref, start, block)
            delay = east * east_s + north * north_s
            wave = cos_turns(delay * freq - quarter)
            tied_weight = wave * jnp.where(group == group_s, scale, 0.0)
            return dot_nt(tied_weight.astype(jnp.bfloat16), station).astype(jnp.bfloat16)

        columns = slice(channel0 * rows_c, (channel0 + CB) * rows_c)
        if beams == block:
            out_ref[:, columns] = tied_rows(0)
        else:

            def body(i, carry):
                start = pl.multiple_of(i * block, block)
                out_ref[pl.ds(start, block), columns] = tied_rows(start)
                return carry

            lax.fori_loop(0, beams // block, body, 0)


def shards(
    volts,
    antenna_tile_weights,
    station_weights,
    tile_station,
    station_group,
    station_pos,
    beam_dir,
    beam_order,
):
    channels, _, samples, _ = volts.shape
    beams = beam_order.shape[0]
    n_stn, n_chan = lax.axis_size("stn"), lax.axis_size("chan")
    rows = beams // (n_stn * n_chan)
    width = channels * 2 * samples
    vmem = pl.BlockSpec(memory_space=pltpu.VMEM)
    partial = pl.pallas_call(
        kernel,
        out_shape=jax.ShapeDtypeStruct((beams, width), jnp.bfloat16),
        in_specs=[pl.BlockSpec(memory_space=pl.ANY)] + [vmem] * 7,
        out_specs=vmem,
        scratch_shapes=[
            pltpu.VMEM(volts.shape, volts.dtype),
            pltpu.SemaphoreType.DMA((channels // CB,)),
        ],
        compiler_params=pltpu.CompilerParams(vmem_limit_bytes=32 * 2**20),
        name="partial_tied",
    )(
        volts,
        antenna_tile_weights,
        station_weights,
        tile_station[None, :],
        station_group[None, :],
        station_pos.T,
        beam_dir.T,
        beam_order[None, :],
    )
    partial = partial.reshape(n_stn * n_chan, rows, width)
    parts = lax.all_to_all(partial, ("stn", "chan"), split_axis=0, concat_axis=0, tiled=True)
    parts = parts.reshape(n_stn, n_chan, rows, channels, 2 * samples)
    tied = jnp.sum(parts.astype(jnp.float32), axis=0).astype(jnp.bfloat16)
    return tied.transpose(1, 0, 2, 3).reshape(rows, n_chan * channels, 2 * samples)


def solution(mesh):
    in_specs = (
        P("chan", None, None, "stn"),
        P("chan", None, "stn"),
        P("chan", None, "stn"),
        P("stn"),
        P(),
        P(),
        P(),
        P(),
    )
    out_specs = P(("stn", "chan"), None, None)
    return jax.shard_map(shards, mesh=mesh, in_specs=in_specs, out_specs=out_specs, check_vma=False)
```

```python
import functools
import math

import jax
import jax.numpy as jnp
from jax import lax
from jax.experimental import pallas as pl
from jax.experimental.pallas import tpu as pltpu
from jax.sharding import PartitionSpec as P

TILE_ANTENNAS = 16
TPS = 16
GROUPS = 4
CB = 8
CHUNK = 256
NT = (((1,), (1,)), ((), ()))
SIN = [(-1) ** i * (2 * math.pi) ** (2 * i + 1) / math.factorial(2 * i + 1) for i in range(7)]


def dot_nt(a, b):
    return lax.dot_general(a, b, NT, preferred_element_type=jnp.float32)


def iota(shape, dim):
    return lax.broadcasted_iota(jnp.int32, shape, dim)


def beam_columns(order_ref, dir_ref, start, rows):
    beams = order_ref.shape[1]
    order = order_ref[...].astype(jnp.float32)
    lane = iota((rows, beams), 1)
    own = lane == iota((rows, beams), 0) + start
    ids = jnp.sum(jnp.where(own, order, 0.0), axis=1, keepdims=True)
    pick = lane.astype(jnp.float32) == ids
    east = jnp.sum(jnp.where(pick, dir_ref[0:1, :], 0.0), axis=1, keepdims=True)
    north = jnp.sum(jnp.where(pick, dir_ref[1:2, :], 0.0), axis=1, keepdims=True)
    group = ids - GROUPS * jnp.floor(ids * (1.0 / GROUPS))
    return east, north, group


def station_rows(pos_ref, group_ref, stations, lanes):
    total = group_ref.shape[1]
    first = lax.axis_index("stn") * stations
    own = iota((stations, total), 1) == iota((stations, total), 0) + first
    spread = iota((stations, lanes), 0) == iota((stations, lanes), 1) % stations

    def turn(row):
        column = jnp.sum(jnp.where(own, row, 0.0), axis=1, keepdims=True)
        return jnp.sum(jnp.where(spread, column, 0.0), axis=0, keepdims=True)

    return turn(pos_ref[0:1, :]), turn(pos_ref[1:2, :]), turn(group_ref[...].astype(jnp.float32))


def cos_turns(t):
    y = t - jnp.floor(t + 0.5)
    z = 0.25 - jnp.abs(y)
    z2 = z * z
    value = jnp.full_like(z, SIN[-1])
    for coefficient in SIN[-2::-1]:
        value = value * z2 + coefficient
    return value * z


def kernel(
    volt_hbm,
    aw_hbm,
    sw_hbm,
    ts_hbm,
    group_hbm,
    pos_hbm,
    dir_hbm,
    order_hbm,
    out_ref,
    volts,
    aw_ref,
    sw_ref,
    ts_ref,
    group_ref,
    pos_ref,
    dir_ref,
    order_ref,
    tied_ref,
    sems,
):
    channels, _, samples, antennas = volt_hbm.shape
    tiles = sw_ref.shape[2]
    stations = tiles // TPS
    chunks = antennas // CHUNK
    per_chunk = CHUNK // TILE_ANTENNAS
    groups = channels // CB
    rows_c = 2 * samples
    beams = order_ref.shape[1]
    lanes = CB * 2 * stations
    scale = 1.0 / math.sqrt(group_ref.shape[1])

    def start(source, target, k):
        copy = pltpu.make_async_copy(source, target, sems.at[k])
        copy.start()
        return copy

    small = [
        start(source, target, k)
        for k, (source, target) in enumerate(
            [
                (order_hbm, order_ref),
                (dir_hbm, dir_ref),
                (pos_hbm, pos_ref),
                (group_hbm, group_ref),
                (ts_hbm, ts_ref),
                (sw_hbm, sw_ref),
                (aw_hbm, aw_ref),
            ]
        )
    ]
    large = []
    for k in range(2 * groups):
        part = pl.ds(k * CB // 2, CB // 2)
        large.append(start(volt_hbm.at[part], volts.at[part], len(small) + k))
    for copy in small[:4]:
        copy.wait()

    east_s, north_s, group_s = station_rows(pos_ref, group_ref, stations, lanes)
    lane = iota((1, lanes), 1)
    channel_lane = lane // (2 * stations)
    quarter = 0.25 * ((lane // stations) % 2).astype(jnp.float32)
    first_chan = lax.axis_index("chan") * channels
    total_chans = channels * lax.axis_size("chan")
    block = min(64, beams)

    def tied_rows(first):
        east, north, group = beam_columns(order_ref, dir_ref, first, block)
        delay = east * east_s + north * north_s
        member = jnp.where(group == group_s, scale, 0.0)
        for g in range(groups):
            freq = 1.0 + (first_chan + g * CB + channel_lane).astype(jnp.float32) / total_chans
            wave = cos_turns(delay * freq - quarter)
            tied_ref[pl.ds(first, block), g * lanes : (g + 1) * lanes] = (wave * member).astype(
                jnp.bfloat16
            )

    if beams == block:
        tied_rows(0)
    else:

        def body(i, carry):
            tied_rows(pl.multiple_of(i * block, block))
            return carry

        lax.fori_loop(0, beams // block, body, 0)

    for copy in small[4:]:
        copy.wait()
    mask16 = (iota((per_chunk, CHUNK), 1) // TILE_ANTENNAS == iota((per_chunk, CHUNK), 0)).astype(
        jnp.float32
    )
    member_table = (iota((stations, tiles), 0) == ts_ref[...] % stations).astype(jnp.float32)
    own_channel = iota((CB * rows_c, lanes), 0) // rows_c == iota((CB * rows_c, lanes), 1) // (
        2 * stations
    )
    lane_chunk = iota((rows_c, 2 * tiles), 1) // per_chunk % chunks

    for g in range(groups):
        channel0 = g * CB
        weights = aw_ref[channel0 : channel0 + CB].astype(jnp.float32)
        large[2 * g].wait()
        large[2 * g + 1].wait()
        found = [None] * CB
        for step in range(chunks):
            left = jnp.concatenate(
                [
                    volts[
                        channel0 + c,
                        :,
                        :,
                        (c + step) % chunks * CHUNK : ((c + step) % chunks + 1) * CHUNK,
                    ].reshape(rows_c, CHUNK)
                    for c in range(CB)
                ],
                axis=0,
            )
            right = jnp.concatenate(
                [
                    (
                        weights[(q - step) % CB, part : part + 1, q * CHUNK : (q + 1) * CHUNK]
                        * mask16
                    ).astype(jnp.bfloat16)
                    for part in range(2)
                    for q in range(chunks)
                ],
                axis=0,
            )
            product = dot_nt(left, right)
            for c in range(CB):
                mine = product[c * rows_c : (c + 1) * rows_c]
                if step == 0:
                    found[c] = mine
                else:
                    found[c] = jnp.where(lane_chunk == (c + step) % chunks, mine, found[c])
        left = []
        for c in range(CB):
            real, imag = found[c][:samples], found[c][samples:]
            tile_re = (real[:, :tiles] - imag[:, tiles:]).astype(jnp.bfloat16)
            tile_im = (imag[:, :tiles] + real[:, tiles:]).astype(jnp.bfloat16)
            left.append(jnp.concatenate([tile_re, tile_im], axis=1))
            left.append(jnp.concatenate([tile_im, -tile_re], axis=1))
        right = []
        swt = sw_ref[channel0 : channel0 + CB].astype(jnp.float32)
        for c in range(CB):
            re = swt[c, 0:1] * member_table
            im = swt[c, 1:2] * member_table
            right.append(jnp.concatenate([re, -im], axis=1))
            right.append(jnp.concatenate([im, re], axis=1))
        station = dot_nt(
            jnp.concatenate(left, axis=0), jnp.concatenate(right, axis=0).astype(jnp.bfloat16)
        )
        station = jnp.where(own_channel, station, 0.0).astype(jnp.bfloat16)
        tied = dot_nt(tied_ref[:, g * lanes : (g + 1) * lanes], station)
        devices, rows, _ = out_ref.shape
        out_ref[:, :, channel0 * rows_c : (channel0 + CB) * rows_c] = tied.astype(
            jnp.bfloat16
        ).reshape(devices, rows, CB * rows_c)


def shards(
    volts,
    antenna_tile_weights,
    station_weights,
    tile_station,
    station_group,
    station_pos,
    beam_dir,
    beam_order,
):
    channels, _, samples, _ = volts.shape
    beams = beam_order.shape[0]
    n_stn, n_chan = lax.axis_size("stn"), lax.axis_size("chan")
    rows = beams // (n_stn * n_chan)
    width = channels * 2 * samples
    operands = (
        volts,
        antenna_tile_weights,
        station_weights,
        tile_station[None, :],
        station_group[None, :],
        station_pos.T,
        beam_dir.T,
        beam_order[None, :],
    )
    groups = channels // CB
    partial = pl.pallas_call(
        kernel,
        out_shape=jax.ShapeDtypeStruct((n_stn * n_chan, rows, width), jnp.bfloat16),
        in_specs=[pl.BlockSpec(memory_space=pltpu.HBM)] * len(operands),
        out_specs=pl.BlockSpec(memory_space=pltpu.VMEM),
        scratch_shapes=[pltpu.VMEM(x.shape, x.dtype) for x in operands]
        + [
            pltpu.VMEM((beams, channels * 2 * (station_weights.shape[2] // TPS)), jnp.bfloat16),
            pltpu.SemaphoreType.DMA((len(operands) - 1 + 2 * groups,)),
        ],
        compiler_params=pltpu.CompilerParams(vmem_limit_bytes=60 * 2**20),
        name="partial_tied",
    )(*operands)
    parts = lax.all_to_all(partial, ("stn", "chan"), split_axis=0, concat_axis=0, tiled=True)
    parts = parts.reshape(n_stn, n_chan, rows, channels, 2 * samples)
    tied = jnp.sum(parts.astype(jnp.float32), axis=0).astype(jnp.bfloat16)
    return tied.transpose(1, 0, 2, 3).reshape(rows, n_chan * channels, 2 * samples)


def solution(mesh):
    in_specs = (
        P("chan", None, None, "stn"),
        P("chan", None, "stn"),
        P("chan", None, "stn"),
        P("stn"),
        P(),
        P(),
        P(),
        P(),
    )
    out_specs = P(("stn", "chan"), None, None)
    return jax.shard_map(shards, mesh=mesh, in_specs=in_specs, out_specs=out_specs, check_vma=False)
```

```python
import functools
import math

import jax
import jax.numpy as jnp
from jax import lax
from jax.experimental import pallas as pl
from jax.experimental.pallas import tpu as pltpu
from jax.sharding import PartitionSpec as P

TILE_ANTENNAS = 16
TPS = 16
GROUPS = 4
CB = 8
CHUNK = 256
NT = (((1,), (1,)), ((), ()))
SIN = [(-1) ** i * (2 * math.pi) ** (2 * i + 1) / math.factorial(2 * i + 1) for i in range(7)]


def dot_nt(a, b):
    return lax.dot_general(a, b, NT, preferred_element_type=jnp.float32)


def iota(shape, dim):
    return lax.broadcasted_iota(jnp.int32, shape, dim)


def cos_turns(t):
    y = t - jnp.floor(t + 0.5)
    z = 0.25 - jnp.abs(y)
    z2 = z * z
    value = jnp.full_like(z, SIN[-1])
    for coefficient in SIN[-2::-1]:
        value = value * z2 + coefficient
    return value * z


def kernel(
    volt_hbm,
    aw_hbm,
    sw_hbm,
    ts_hbm,
    group_hbm,
    pos_hbm,
    dir_hbm,
    order_hbm,
    out_ref,
    tied_ref,
    volts,
    aw_ref,
    sw_ref,
    ts_ref,
    group_ref,
    pos_ref,
    dir_ref,
    order_ref,
    sems,
):
    channels, _, samples, antennas = volt_hbm.shape
    tiles = sw_ref.shape[2]
    stations = tiles // TPS
    chunks = antennas // CHUNK
    per_chunk = CHUNK // TILE_ANTENNAS
    groups = channels // CB
    rows_c = 2 * samples
    beams = order_ref.shape[1]
    n_chan = lax.axis_size("chan")
    total_chans = channels * n_chan
    scale = 1.0 / math.sqrt(group_ref.shape[1])

    def start(source, target, k):
        copy = pltpu.make_async_copy(source, target, sems.at[k])
        copy.start()
        return copy

    small = [
        start(source, target, k)
        for k, (source, target) in enumerate(
            [
                (order_hbm, order_ref),
                (dir_hbm, dir_ref),
                (pos_hbm, pos_ref),
                (group_hbm, group_ref),
                (ts_hbm, ts_ref),
                (sw_hbm, sw_ref),
                (aw_hbm, aw_ref),
            ]
        )
    ]
    large = []
    for k in range(2 * groups):
        part = pl.ds(k * CB // 2, CB // 2)
        large.append(start(volt_hbm.at[part], volts.at[part], len(small) + k))
    for copy in small[:4]:
        copy.wait()

    own_beams = tied_ref.shape[0] // (2 * total_chans)
    order = order_ref[...].astype(jnp.float32)
    first_beam = (lax.axis_index("stn") * n_chan + lax.axis_index("chan")) * own_beams
    lane_beam = iota((1, beams), 1)
    freq_of = iota((CB, 1), 0)
    waves = [[] for _ in range(total_chans // CB)]
    for b in range(own_beams):
        own_id = jnp.sum(jnp.where(lane_beam == first_beam + b, order, 0.0), axis=1, keepdims=True)
        pick = lane_beam.astype(jnp.float32) == own_id
        east = jnp.sum(jnp.where(pick, dir_ref[0:1, :], 0.0), axis=1, keepdims=True)
        north = jnp.sum(jnp.where(pick, dir_ref[1:2, :], 0.0), axis=1, keepdims=True)
        own_group = own_id - GROUPS * jnp.floor(own_id * (1.0 / GROUPS))
        delay = east * pos_ref[0:1, :] + north * pos_ref[1:2, :]
        member = jnp.where(group_ref[...].astype(jnp.float32) == own_group, scale, 0.0)
        for g, wave in enumerate(waves):
            turns = (1.0 + (freq_of + g * CB).astype(jnp.float32) / total_chans) * delay
            wave.append((cos_turns(turns) * member, cos_turns(turns - 0.25) * member))
    for g, wave in enumerate(waves):
        rows = [wave[b][part] for part in range(2) for b in range(own_beams)]
        size = len(rows) * CB
        tied_ref[g * size : (g + 1) * size, :] = jnp.concatenate(rows, axis=0).astype(jnp.bfloat16)

    for copy in small[4:]:
        copy.wait()
    mask16 = (iota((per_chunk, CHUNK), 1) // TILE_ANTENNAS == iota((per_chunk, CHUNK), 0)).astype(
        jnp.float32
    )
    member_table = (iota((stations, tiles), 0) == ts_ref[...] % stations).astype(jnp.float32)
    own_channel = iota((CB * stations, CB * rows_c), 0) // stations == iota(
        (CB * stations, CB * rows_c), 1
    ) // rows_c
    lane_chunk = iota((rows_c, 2 * tiles), 1) // per_chunk % chunks

    for g in range(groups):
        channel0 = g * CB
        weights = aw_ref[channel0 : channel0 + CB].astype(jnp.float32)
        large[2 * g].wait()
        large[2 * g + 1].wait()
        found = [None] * CB
        for step in range(chunks):
            left = jnp.concatenate(
                [
                    volts[
                        channel0 + c,
                        :,
                        :,
                        (c + step) % chunks * CHUNK : ((c + step) % chunks + 1) * CHUNK,
                    ].reshape(rows_c, CHUNK)
                    for c in range(CB)
                ],
                axis=0,
            )
            right = jnp.concatenate(
                [
                    (
                        weights[(q - step) % CB, part : part + 1, q * CHUNK : (q + 1) * CHUNK]
                        * mask16
                    ).astype(jnp.bfloat16)
                    for part in range(2)
                    for q in range(chunks)
                ],
                axis=0,
            )
            product = dot_nt(left, right)
            for c in range(CB):
                mine = product[c * rows_c : (c + 1) * rows_c]
                if step == 0:
                    found[c] = mine
                else:
                    found[c] = jnp.where(lane_chunk == (c + step) % chunks, mine, found[c])
        left = []
        for c in range(CB):
            real, imag = found[c][:samples], found[c][samples:]
            tile_re = (real[:, :tiles] - imag[:, tiles:]).astype(jnp.bfloat16)
            tile_im = (imag[:, :tiles] + real[:, tiles:]).astype(jnp.bfloat16)
            left.append(jnp.concatenate([tile_re, tile_im], axis=1))
            left.append(jnp.concatenate([tile_im, -tile_re], axis=1))
        right = []
        swt = sw_ref[channel0 : channel0 + CB].astype(jnp.float32)
        for c in range(CB):
            re = swt[c, 0:1] * member_table
            im = swt[c, 1:2] * member_table
            right.append(jnp.concatenate([re, -im], axis=1))
        station = dot_nt(
            jnp.concatenate(right, axis=0).astype(jnp.bfloat16), jnp.concatenate(left, axis=0)
        )
        station = jnp.where(own_channel, station, 0.0).reshape(CB, stations, CB * rows_c)
        out_ref[:, channel0 * rows_c : (channel0 + CB) * rows_c] = jnp.sum(station, axis=0).astype(
            jnp.bfloat16
        )


def tied_kernel(gathered_ref, tied_ref, out_ref):
    n_stn, n_chan = lax.axis_size("stn"), lax.axis_size("chan")
    own_beams, rows_c, total_chans = out_ref.shape
    samples = rows_c // 2
    stations = gathered_ref.shape[0] // (n_stn * n_chan)
    per_chan = total_chans // n_chan // CB
    width = CB * rows_c
    gathered = gathered_ref[...].reshape(n_stn, n_chan, stations, per_chan * width)
    diagonal = iota((CB, width), 0) == iota((CB, width), 1) // rows_c
    real_lane = iota((CB, width), 1) % rows_c < samples
    beams = [[] for _ in range(own_beams)]
    size = 2 * own_beams * CB
    for g in range(total_chans // CB):
        chan, column = g // per_chan, g % per_chan * width
        station = gathered[:, chan, :, column : column + width].reshape(n_stn * stations, width)
        sums = jnp.dot(
            tied_ref[g * size : (g + 1) * size, :], station, preferred_element_type=jnp.float32
        )
        for b in range(own_beams):
            by_cos = sums[b * CB : (b + 1) * CB]
            by_sin = sums[(own_beams + b) * CB : (own_beams + b + 1) * CB]
            turned = jnp.where(
                real_lane,
                pltpu.roll(by_sin, width - samples, 1),
                -pltpu.roll(by_sin, samples, 1),
            )
            beams[b].append(jnp.where(diagonal, by_cos + turned, 0.0))
    spread = (iota((rows_c, width), 0) == iota((rows_c, width), 1) % rows_c).astype(jnp.bfloat16)
    for b in range(own_beams):
        rows = jnp.concatenate(beams[b], axis=0).astype(jnp.bfloat16)
        out_ref[b] = dot_nt(spread, rows).astype(jnp.bfloat16)


def shards(
    volts,
    antenna_tile_weights,
    station_weights,
    tile_station,
    station_group,
    station_pos,
    beam_dir,
    beam_order,
):
    channels, _, samples, _ = volts.shape
    beams = beam_order.shape[0]
    n_stn, n_chan = lax.axis_size("stn"), lax.axis_size("chan")
    rows = beams // (n_stn * n_chan)
    width = channels * 2 * samples
    operands = (
        volts,
        antenna_tile_weights,
        station_weights,
        tile_station[None, :],
        station_group[None, :],
        station_pos.T,
        beam_dir.T,
        beam_order[None, :],
    )
    groups = channels // CB
    vmem = pl.BlockSpec(memory_space=pltpu.VMEM)
    tied_shape = (2 * rows * n_chan * channels, station_group.shape[0])
    stations, tied_weight = pl.pallas_call(
        kernel,
        out_shape=(
            jax.ShapeDtypeStruct((station_weights.shape[2] // TPS, width), jnp.bfloat16),
            jax.ShapeDtypeStruct(tied_shape, jnp.bfloat16),
        ),
        in_specs=[pl.BlockSpec(memory_space=pltpu.HBM)] * len(operands),
        out_specs=(vmem, vmem),
        scratch_shapes=[pltpu.VMEM(x.shape, x.dtype) for x in operands]
        + [pltpu.SemaphoreType.DMA((len(operands) - 1 + 2 * groups,))],
        compiler_params=pltpu.CompilerParams(vmem_limit_bytes=60 * 2**20),
        name="station_beams",
    )(*operands)
    gathered = lax.all_gather(stations, ("stn", "chan"), axis=0, tiled=True)
    tied = pl.pallas_call(
        tied_kernel,
        out_shape=jax.ShapeDtypeStruct((rows, 2 * samples, n_chan * channels), jnp.bfloat16),
        in_specs=[vmem, vmem],
        out_specs=vmem,
        compiler_params=pltpu.CompilerParams(vmem_limit_bytes=32 * 2**20),
        name="tied_beams",
    )(gathered, tied_weight)
    return tied.transpose(0, 2, 1)


def solution(mesh):
    in_specs = (
        P("chan", None, None, "stn"),
        P("chan", None, "stn"),
        P("chan", None, "stn"),
        P("stn"),
        P(),
        P(),
        P(),
        P(),
    )
    out_specs = P(("stn", "chan"), None, None)
    return jax.shard_map(shards, mesh=mesh, in_specs=in_specs, out_specs=out_specs, check_vma=False)
```

```python
import functools
import math

import jax
import jax.numpy as jnp
from jax import lax
from jax.experimental import pallas as pl
from jax.experimental.pallas import tpu as pltpu
from jax.sharding import PartitionSpec as P

TILE_ANTENNAS = 16
TPS = 16
GROUPS = 4
CB = 8
CHUNK = 256
NT = (((1,), (1,)), ((), ()))
SIN = [(-1) ** i * (2 * math.pi) ** (2 * i + 1) / math.factorial(2 * i + 1) for i in range(7)]


def dot_nt(a, b):
    return lax.dot_general(a, b, NT, preferred_element_type=jnp.float32)


def iota(shape, dim):
    return lax.broadcasted_iota(jnp.int32, shape, dim)


def split_devices():
    devices = lax.axis_size("stn") * lax.axis_size("chan")
    near = lax.axis_size("chan") * min(4, lax.axis_size("stn"))
    return devices // near, near


def beam_columns(order_ref, dir_ref, start, rows):
    beams = order_ref.shape[1]
    order = order_ref[...].astype(jnp.float32)
    lane = iota((rows, beams), 1)
    far, near = split_devices()
    each = beams // (far * near)
    device = lax.axis_index("stn") * lax.axis_size("chan") + lax.axis_index("chan")
    slot = iota((rows, beams), 0) + start
    slot_near = (slot // (far * each)) ^ (device % near)
    slot_far = (slot // each % far) ^ (device // near)
    own = lane == (slot_far * near + slot_near) * each + slot % each
    ids = jnp.sum(jnp.where(own, order, 0.0), axis=1, keepdims=True)
    pick = lane.astype(jnp.float32) == ids
    east = jnp.sum(jnp.where(pick, dir_ref[0:1, :], 0.0), axis=1, keepdims=True)
    north = jnp.sum(jnp.where(pick, dir_ref[1:2, :], 0.0), axis=1, keepdims=True)
    group = ids - GROUPS * jnp.floor(ids * (1.0 / GROUPS))
    return east, north, group


def station_rows(pos_ref, group_ref, stations, lanes):
    total = group_ref.shape[1]
    first = lax.axis_index("stn") * stations
    own = iota((stations, total), 1) == iota((stations, total), 0) + first
    spread = iota((stations, lanes), 0) == iota((stations, lanes), 1) % stations

    def turn(row):
        column = jnp.sum(jnp.where(own, row, 0.0), axis=1, keepdims=True)
        return jnp.sum(jnp.where(spread, column, 0.0), axis=0, keepdims=True)

    return turn(pos_ref[0:1, :]), turn(pos_ref[1:2, :]), turn(group_ref[...].astype(jnp.float32))


def cos_turns(t):
    y = t - jnp.floor(t + 0.5)
    z = 0.25 - jnp.abs(y)
    z2 = z * z
    value = jnp.full_like(z, SIN[-1])
    for coefficient in SIN[-2::-1]:
        value = value * z2 + coefficient
    return value * z


def kernel(
    volt_hbm,
    aw_hbm,
    sw_hbm,
    ts_hbm,
    group_hbm,
    pos_hbm,
    dir_hbm,
    order_hbm,
    *refs,
):
    out_refs = refs[: split_devices()[1]]
    (
        volts,
        aw_ref,
        sw_ref,
        ts_ref,
        group_ref,
        pos_ref,
        dir_ref,
        order_ref,
        tied_ref,
        sems,
    ) = refs[split_devices()[1] :]
    channels, _, samples, antennas = volt_hbm.shape
    tiles = sw_ref.shape[2]
    stations = tiles // TPS
    chunks = antennas // CHUNK
    per_chunk = CHUNK // TILE_ANTENNAS
    groups = channels // CB
    rows_c = 2 * samples
    beams = order_ref.shape[1]
    lanes = CB * 2 * stations
    scale = 1.0 / math.sqrt(group_ref.shape[1])

    def start(source, target, k):
        copy = pltpu.make_async_copy(source, target, sems.at[k])
        copy.start()
        return copy

    small = [
        start(source, target, k)
        for k, (source, target) in enumerate(
            [
                (order_hbm, order_ref),
                (dir_hbm, dir_ref),
                (pos_hbm, pos_ref),
                (group_hbm, group_ref),
                (ts_hbm, ts_ref),
                (sw_hbm, sw_ref),
                (aw_hbm, aw_ref),
            ]
        )
    ]
    large = []
    for k in range(2 * groups):
        part = pl.ds(k * CB // 2, CB // 2)
        large.append(start(volt_hbm.at[part], volts.at[part], len(small) + k))
    for copy in small[:4]:
        copy.wait()

    east_s, north_s, group_s = station_rows(pos_ref, group_ref, stations, lanes)
    lane = iota((1, lanes), 1)
    channel_lane = lane // (2 * stations)
    quarter = 0.25 * ((lane // stations) % 2).astype(jnp.float32)
    first_chan = lax.axis_index("chan") * channels
    total_chans = channels * lax.axis_size("chan")
    block = min(64, beams)

    def tied_rows(first):
        east, north, group = beam_columns(order_ref, dir_ref, first, block)
        delay = east * east_s + north * north_s
        member = jnp.where(group == group_s, scale, 0.0)
        for g in range(groups):
            freq = 1.0 + (first_chan + g * CB + channel_lane).astype(jnp.float32) / total_chans
            wave = cos_turns(delay * freq - quarter)
            tied_ref[pl.ds(first, block), g * lanes : (g + 1) * lanes] = (wave * member).astype(
                jnp.bfloat16
            )

    if beams == block:
        tied_rows(0)
    else:

        def body(i, carry):
            tied_rows(pl.multiple_of(i * block, block))
            return carry

        lax.fori_loop(0, beams // block, body, 0)

    for copy in small[4:]:
        copy.wait()
    mask16 = (iota((per_chunk, CHUNK), 1) // TILE_ANTENNAS == iota((per_chunk, CHUNK), 0)).astype(
        jnp.float32
    )
    member_table = (iota((stations, tiles), 0) == ts_ref[...] % stations).astype(jnp.float32)
    own_channel = iota((CB * rows_c, lanes), 0) // rows_c == iota((CB * rows_c, lanes), 1) // (
        2 * stations
    )
    lane_chunk = iota((rows_c, 2 * tiles), 1) // per_chunk % chunks

    for g in range(groups):
        channel0 = g * CB
        weights = aw_ref[channel0 : channel0 + CB].astype(jnp.float32)
        large[2 * g].wait()
        large[2 * g + 1].wait()
        found = [None] * CB
        for step in range(chunks):
            left = jnp.concatenate(
                [
                    volts[
                        channel0 + c,
                        :,
                        :,
                        (c + step) % chunks * CHUNK : ((c + step) % chunks + 1) * CHUNK,
                    ].reshape(rows_c, CHUNK)
                    for c in range(CB)
                ],
                axis=0,
            )
            right = jnp.concatenate(
                [
                    (
                        weights[(q - step) % CB, part : part + 1, q * CHUNK : (q + 1) * CHUNK]
                        * mask16
                    ).astype(jnp.bfloat16)
                    for part in range(2)
                    for q in range(chunks)
                ],
                axis=0,
            )
            product = dot_nt(left, right)
            for c in range(CB):
                mine = product[c * rows_c : (c + 1) * rows_c]
                if step == 0:
                    found[c] = mine
                else:
                    found[c] = jnp.where(lane_chunk == (c + step) % chunks, mine, found[c])
        left = []
        for c in range(CB):
            real, imag = found[c][:samples], found[c][samples:]
            tile_re = (real[:, :tiles] - imag[:, tiles:]).astype(jnp.bfloat16)
            tile_im = (imag[:, :tiles] + real[:, tiles:]).astype(jnp.bfloat16)
            left.append(jnp.concatenate([tile_re, tile_im], axis=1))
            left.append(jnp.concatenate([tile_im, -tile_re], axis=1))
        right = []
        swt = sw_ref[channel0 : channel0 + CB].astype(jnp.float32)
        for c in range(CB):
            re = swt[c, 0:1] * member_table
            im = swt[c, 1:2] * member_table
            right.append(jnp.concatenate([re, -im], axis=1))
            right.append(jnp.concatenate([im, re], axis=1))
        station = dot_nt(
            jnp.concatenate(left, axis=0), jnp.concatenate(right, axis=0).astype(jnp.bfloat16)
        )
        station = jnp.where(own_channel, station, 0.0).astype(jnp.bfloat16)
        tied = dot_nt(tied_ref[:, g * lanes : (g + 1) * lanes], station)
        tied = tied.astype(jnp.bfloat16)
        rows = beams // len(out_refs)
        for k, out_ref in enumerate(out_refs):
            out_ref[:, channel0 * rows_c : (channel0 + CB) * rows_c] = tied[
                k * rows : (k + 1) * rows
            ]


def last_kernel(*refs):
    parts, out_ref = refs[:-1], refs[-1]
    n_chan = lax.axis_size("chan")
    own_beams, rows_c, total_chans = out_ref.shape
    channels = total_chans // n_chan
    width = channels * rows_c
    diagonal = iota((channels, width), 0) == iota((channels, width), 1) // rows_c
    spread = (iota((rows_c, width), 0) == iota((rows_c, width), 1) % rows_c).astype(jnp.bfloat16)
    for b in range(own_beams):
        blocks = []
        for chan in range(n_chan):
            offset = lax.axis_index("chan") ^ chan
            row = sum(part[offset, b : b + 1, :].astype(jnp.float32) for part in parts)
            blocks.append(jnp.where(diagonal, row, 0.0))
        rows = jnp.concatenate(blocks, axis=0).astype(jnp.bfloat16)
        out_ref[b] = dot_nt(spread, rows).astype(jnp.bfloat16)


def shards(
    volts,
    antenna_tile_weights,
    station_weights,
    tile_station,
    station_group,
    station_pos,
    beam_dir,
    beam_order,
):
    channels, _, samples, _ = volts.shape
    beams = beam_order.shape[0]
    n_stn, n_chan = lax.axis_size("stn"), lax.axis_size("chan")
    rows = beams // (n_stn * n_chan)
    width = channels * 2 * samples
    operands = (
        volts,
        antenna_tile_weights,
        station_weights,
        tile_station[None, :],
        station_group[None, :],
        station_pos.T,
        beam_dir.T,
        beam_order[None, :],
    )
    groups = channels // CB
    far, near = split_devices()
    axes = ("stn", "chan")
    vmem = pl.BlockSpec(memory_space=pltpu.VMEM)
    partial = list(pl.pallas_call(
        kernel,
        out_shape=[jax.ShapeDtypeStruct((far * rows, width), jnp.bfloat16)] * near,
        in_specs=[pl.BlockSpec(memory_space=pltpu.HBM)] * len(operands),
        out_specs=[vmem] * near,
        scratch_shapes=[pltpu.VMEM(x.shape, x.dtype) for x in operands]
        + [
            pltpu.VMEM((beams, channels * 2 * (station_weights.shape[2] // TPS)), jnp.bfloat16),
            pltpu.SemaphoreType.DMA((len(operands) - 1 + 2 * groups,)),
        ],
        compiler_params=pltpu.CompilerParams(vmem_limit_bytes=60 * 2**20),
        name="partial_tied",
    )(*operands))
    for k in range(1, near):
        perm = [(d, d ^ k) for d in range(far * near)]
        partial[k] = lax.ppermute(partial[k], axes, perm)
    sums = [
        sum(block.astype(jnp.float32) for block in partial[chan::n_chan])
        .astype(jnp.bfloat16)
        .reshape(far, rows, width)
        for chan in range(n_chan)
    ]
    parts = [jnp.stack([block[m] for block in sums]) for m in range(far)]
    for m in range(1, far):
        perm = [(d, d ^ (m * near)) for d in range(far * near)]
        parts[m] = lax.ppermute(parts[m], axes, perm)
    tied = pl.pallas_call(
        last_kernel,
        out_shape=jax.ShapeDtypeStruct((rows, 2 * samples, n_chan * channels), jnp.bfloat16),
        in_specs=[vmem] * far,
        out_specs=vmem,
        compiler_params=pltpu.CompilerParams(vmem_limit_bytes=16 * 2**20),
        name="tied_beams",
    )(*parts)
    return tied.transpose(0, 2, 1)


def solution(mesh):
    in_specs = (
        P("chan", None, None, "stn"),
        P("chan", None, "stn"),
        P("chan", None, "stn"),
        P("stn"),
        P(),
        P(),
        P(),
        P(),
    )
    out_specs = P(("stn", "chan"), None, None)
    return jax.shard_map(shards, mesh=mesh, in_specs=in_specs, out_specs=out_specs, check_vma=False)
```

```python
import functools
import math

import jax
import jax.numpy as jnp
from jax import lax
from jax.experimental import pallas as pl
from jax.experimental.pallas import tpu as pltpu
from jax.sharding import PartitionSpec as P

TILE_ANTENNAS = 16
TPS = 16
GROUPS = 4
CB = 8
NT = (((1,), (1,)), ((), ()))
SIN = [(-1) ** i * (2 * math.pi) ** (2 * i + 1) / math.factorial(2 * i + 1) for i in range(7)]


def dot_nt(a, b):
    return lax.dot_general(a, b, NT, preferred_element_type=jnp.float32)


def iota(shape, dim):
    return lax.broadcasted_iota(jnp.int32, shape, dim)


def beam_columns(order_ref, dir_ref, start, rows):
    beams = order_ref.shape[1]
    order = order_ref[...].astype(jnp.float32)
    lane = iota((rows, beams), 1)
    own = lane == iota((rows, beams), 0) + start
    ids = jnp.sum(jnp.where(own, order, 0.0), axis=1, keepdims=True)
    pick = lane.astype(jnp.float32) == ids
    east = jnp.sum(jnp.where(pick, dir_ref[0:1, :], 0.0), axis=1, keepdims=True)
    north = jnp.sum(jnp.where(pick, dir_ref[1:2, :], 0.0), axis=1, keepdims=True)
    group = ids - GROUPS * jnp.floor(ids * (1.0 / GROUPS))
    return east, north, group


def station_rows(pos_ref, group_ref, stations, lanes):
    total = group_ref.shape[1]
    first = lax.axis_index("stn") * stations
    own = iota((stations, total), 1) == iota((stations, total), 0) + first
    spread = iota((stations, lanes), 0) == iota((stations, lanes), 1) % stations

    def turn(row):
        column = jnp.sum(jnp.where(own, row, 0.0), axis=1, keepdims=True)
        return jnp.sum(jnp.where(spread, column, 0.0), axis=0, keepdims=True)

    return turn(pos_ref[0:1, :]), turn(pos_ref[1:2, :]), turn(group_ref[...].astype(jnp.float32))


def cos_turns(t):
    y = t - jnp.floor(t + 0.5)
    z = 0.25 - jnp.abs(y)
    z2 = z * z
    value = jnp.full_like(z, SIN[-1])
    for coefficient in SIN[-2::-1]:
        value = value * z2 + coefficient
    return value * z


def kernel(
    volt_hbm,
    aw_hbm,
    sw_hbm,
    ts_hbm,
    group_hbm,
    pos_hbm,
    dir_hbm,
    order_hbm,
    out_ref,
    volts,
    aw_ref,
    sw_ref,
    ts_ref,
    group_ref,
    pos_ref,
    dir_ref,
    order_ref,
    tied_ref,
    sum_ref,
    sems,
):
    channels, _, samples, antennas = volt_hbm.shape
    tiles = sw_ref.shape[2]
    stations = tiles // TPS
    groups = channels // CB
    rows_c = 2 * samples
    beams = order_ref.shape[1]
    lanes = CB * 2 * stations
    scale = 1.0 / math.sqrt(group_ref.shape[1])

    def start(source, target, k):
        copy = pltpu.make_async_copy(source, target, sems.at[k])
        copy.start()
        return copy

    small = [
        start(source, target, k)
        for k, (source, target) in enumerate(
            [
                (order_hbm, order_ref),
                (dir_hbm, dir_ref),
                (pos_hbm, pos_ref),
                (group_hbm, group_ref),
                (ts_hbm, ts_ref),
                (sw_hbm, sw_ref),
                (aw_hbm, aw_ref),
            ]
        )
    ]
    large = []
    for k in range(2 * groups):
        part = pl.ds(k * CB // 2, CB // 2)
        large.append(start(volt_hbm.at[part], volts.at[part], len(small) + k))
    for copy in small[:4]:
        copy.wait()

    east_s, north_s, group_s = station_rows(pos_ref, group_ref, stations, lanes)
    lane = iota((1, lanes), 1)
    channel_lane = lane // (2 * stations)
    quarter = 0.25 * ((lane // stations) % 2).astype(jnp.float32)
    first_chan = lax.axis_index("chan") * channels
    total_chans = channels * lax.axis_size("chan")
    block = min(64, beams)

    def tied_rows(first):
        east, north, group = beam_columns(order_ref, dir_ref, first, block)
        delay = east * east_s + north * north_s
        member = jnp.where(group == group_s, scale, 0.0)
        for g in range(groups):
            freq = 1.0 + (first_chan + g * CB + channel_lane).astype(jnp.float32) / total_chans
            wave = cos_turns(delay * freq - quarter)
            tied_ref[pl.ds(first, block), g * lanes : (g + 1) * lanes] = (wave * member).astype(
                jnp.bfloat16
            )

    if beams == block:
        tied_rows(0)
    else:

        def body(i, carry):
            tied_rows(pl.multiple_of(i * block, block))
            return carry

        lax.fori_loop(0, beams // block, body, 0)

    antenna_tile = iota((antennas, tiles), 0) // TILE_ANTENNAS == iota((antennas, tiles), 1)
    sum_ref[...] = antenna_tile.astype(jnp.bfloat16)
    for copy in small[4:]:
        copy.wait()
    member_table = (iota((stations, tiles), 0) == ts_ref[...] % stations).astype(jnp.float32)
    own_channel = iota((lanes, CB * rows_c), 0) // (2 * stations) == iota(
        (lanes, CB * rows_c), 1
    ) // rows_c

    for g in range(groups):
        channel0 = g * CB
        weights = aw_ref[channel0 : channel0 + CB].astype(jnp.float32)
        large[2 * g].wait()
        large[2 * g + 1].wait()
        products = []
        for c in range(CB):
            w_re = jnp.broadcast_to(weights[c, 0:1], (samples, antennas)).astype(jnp.bfloat16)
            w_im = jnp.broadcast_to(weights[c, 1:2], (samples, antennas)).astype(jnp.bfloat16)
            v_re, v_im = volts[channel0 + c, 0], volts[channel0 + c, 1]
            products.append(w_re * v_re - w_im * v_im)
            products.append(w_re * v_im + w_im * v_re)
        beams_tile = jnp.dot(
            jnp.concatenate(products, axis=0), sum_ref[...], preferred_element_type=jnp.float32
        ).astype(jnp.bfloat16)
        left = []
        for c in range(CB):
            tile_re = beams_tile[c * rows_c : c * rows_c + samples]
            tile_im = beams_tile[c * rows_c + samples : (c + 1) * rows_c]
            left.append(jnp.concatenate([tile_re, tile_im], axis=1))
            left.append(jnp.concatenate([tile_im, -tile_re], axis=1))
        right = []
        swt = sw_ref[channel0 : channel0 + CB].astype(jnp.float32)
        for c in range(CB):
            re = swt[c, 0:1] * member_table
            im = swt[c, 1:2] * member_table
            right.append(jnp.concatenate([re, -im], axis=1))
            right.append(jnp.concatenate([im, re], axis=1))
        station = dot_nt(
            jnp.concatenate(right, axis=0).astype(jnp.bfloat16), jnp.concatenate(left, axis=0)
        )
        station = jnp.where(own_channel, station, 0.0).astype(jnp.bfloat16)
        tied = jnp.dot(
            tied_ref[:, g * lanes : (g + 1) * lanes], station, preferred_element_type=jnp.float32
        )
        devices, rows, _ = out_ref.shape
        out_ref[:, :, channel0 * rows_c : (channel0 + CB) * rows_c] = tied.astype(
            jnp.bfloat16
        ).reshape(devices, rows, CB * rows_c)


def last_kernel(parts_ref, out_ref):
    n_stn, n_chan = lax.axis_size("stn"), lax.axis_size("chan")
    own_beams, rows_c, total_chans = out_ref.shape
    channels = total_chans // n_chan
    width = channels * rows_c
    parts = parts_ref[...].astype(jnp.float32).reshape(n_stn, n_chan, own_beams, width)
    tied = jnp.sum(parts, axis=0)
    diagonal = iota((channels, width), 0) == iota((channels, width), 1) // rows_c
    spread = (iota((rows_c, width), 0) == iota((rows_c, width), 1) % rows_c).astype(jnp.bfloat16)
    for b in range(own_beams):
        rows = [jnp.where(diagonal, tied[chan, b : b + 1], 0.0) for chan in range(n_chan)]
        rows = jnp.concatenate(rows, axis=0).astype(jnp.bfloat16)
        out_ref[b] = dot_nt(spread, rows).astype(jnp.bfloat16)


def shards(
    volts,
    antenna_tile_weights,
    station_weights,
    tile_station,
    station_group,
    station_pos,
    beam_dir,
    beam_order,
):
    channels, _, samples, _ = volts.shape
    beams = beam_order.shape[0]
    n_stn, n_chan = lax.axis_size("stn"), lax.axis_size("chan")
    rows = beams // (n_stn * n_chan)
    width = channels * 2 * samples
    operands = (
        volts,
        antenna_tile_weights,
        station_weights,
        tile_station[None, :],
        station_group[None, :],
        station_pos.T,
        beam_dir.T,
        beam_order[None, :],
    )
    groups = channels // CB
    partial = pl.pallas_call(
        kernel,
        out_shape=jax.ShapeDtypeStruct((n_stn * n_chan, rows, width), jnp.bfloat16),
        in_specs=[pl.BlockSpec(memory_space=pltpu.HBM)] * len(operands),
        out_specs=pl.BlockSpec(memory_space=pltpu.VMEM),
        scratch_shapes=[pltpu.VMEM(x.shape, x.dtype) for x in operands]
        + [
            pltpu.VMEM((beams, channels * 2 * (station_weights.shape[2] // TPS)), jnp.bfloat16),
            pltpu.VMEM((volts.shape[3], station_weights.shape[2]), jnp.bfloat16),
            pltpu.SemaphoreType.DMA((len(operands) - 1 + 2 * groups,)),
        ],
        compiler_params=pltpu.CompilerParams(vmem_limit_bytes=60 * 2**20),
        name="partial_tied",
    )(*operands)
    parts = lax.all_to_all(partial, ("stn", "chan"), split_axis=0, concat_axis=0, tiled=True)
    vmem = pl.BlockSpec(memory_space=pltpu.VMEM)
    tied = pl.pallas_call(
        last_kernel,
        out_shape=jax.ShapeDtypeStruct((rows, 2 * samples, n_chan * channels), jnp.bfloat16),
        in_specs=[vmem],
        out_specs=vmem,
        compiler_params=pltpu.CompilerParams(vmem_limit_bytes=16 * 2**20),
        name="tied_beams",
    )(parts)
    return tied.transpose(0, 2, 1)


def solution(mesh):
    in_specs = (
        P("chan", None, None, "stn"),
        P("chan", None, "stn"),
        P("chan", None, "stn"),
        P("stn"),
        P(),
        P(),
        P(),
        P(),
    )
    out_specs = P(("stn", "chan"), None, None)
    return jax.shard_map(shards, mesh=mesh, in_specs=in_specs, out_specs=out_specs, check_vma=False)
```

```python
import functools
import math

import jax
import jax.numpy as jnp
from jax import lax
from jax.experimental import pallas as pl
from jax.experimental.pallas import tpu as pltpu
from jax.sharding import PartitionSpec as P

TILE_ANTENNAS = 16
TPS = 16
GROUPS = 4
CB = 8
NT = (((1,), (1,)), ((), ()))
SIN = [(-1) ** i * (2 * math.pi) ** (2 * i + 1) / math.factorial(2 * i + 1) for i in range(7)]


def dot_nt(a, b):
    return lax.dot_general(a, b, NT, preferred_element_type=jnp.float32)


def iota(shape, dim):
    return lax.broadcasted_iota(jnp.int32, shape, dim)


def beam_columns(order_ref, dir_ref, start, rows):
    beams = order_ref.shape[1]
    order = order_ref[...].astype(jnp.float32)
    lane = iota((rows, beams), 1)
    own = lane == iota((rows, beams), 0) + start
    ids = jnp.sum(jnp.where(own, order, 0.0), axis=1, keepdims=True)
    pick = lane.astype(jnp.float32) == ids
    east = jnp.sum(jnp.where(pick, dir_ref[0:1, :], 0.0), axis=1, keepdims=True)
    north = jnp.sum(jnp.where(pick, dir_ref[1:2, :], 0.0), axis=1, keepdims=True)
    group = ids - GROUPS * jnp.floor(ids * (1.0 / GROUPS))
    return east, north, group


def station_rows(pos_ref, group_ref, stations, lanes):
    total = group_ref.shape[1]
    first = lax.axis_index("stn") * stations
    own = iota((stations, total), 1) == iota((stations, total), 0) + first
    spread = iota((stations, lanes), 0) == iota((stations, lanes), 1) % stations

    def turn(row):
        column = jnp.sum(jnp.where(own, row, 0.0), axis=1, keepdims=True)
        return jnp.sum(jnp.where(spread, column, 0.0), axis=0, keepdims=True)

    return turn(pos_ref[0:1, :]), turn(pos_ref[1:2, :]), turn(group_ref[...].astype(jnp.float32))


def cos_turns(t):
    y = t - jnp.floor(t + 0.5)
    z = 0.25 - jnp.abs(y)
    z2 = z * z
    value = jnp.full_like(z, SIN[-1])
    for coefficient in SIN[-2::-1]:
        value = value * z2 + coefficient
    return value * z


def kernel(
    volt_hbm,
    aw_hbm,
    sw_hbm,
    ts_hbm,
    group_hbm,
    pos_hbm,
    dir_hbm,
    order_hbm,
    out_ref,
    volts,
    aw_ref,
    sw_ref,
    ts_ref,
    group_ref,
    pos_ref,
    dir_ref,
    order_ref,
    tied_ref,
    sum_ref,
    sems,
):
    channels, _, samples, antennas = volt_hbm.shape
    tiles = sw_ref.shape[2]
    stations = tiles // TPS
    groups = channels // CB
    rows_c = 2 * samples
    beams = order_ref.shape[1]
    lanes = CB * 2 * stations
    scale = 1.0 / math.sqrt(group_ref.shape[1])

    def start(source, target, k):
        copy = pltpu.make_async_copy(source, target, sems.at[k])
        copy.start()
        return copy

    small = [
        start(source, target, k)
        for k, (source, target) in enumerate(
            [
                (order_hbm, order_ref),
                (dir_hbm, dir_ref),
                (pos_hbm, pos_ref),
                (group_hbm, group_ref),
                (ts_hbm, ts_ref),
                (sw_hbm, sw_ref),
                (aw_hbm, aw_ref),
            ]
        )
    ]
    large = []
    for k in range(2 * groups):
        part = pl.ds(k * CB // 2, CB // 2)
        large.append(start(volt_hbm.at[part], volts.at[part], len(small) + k))
    for copy in small[:4]:
        copy.wait()

    east_s, north_s, group_s = station_rows(pos_ref, group_ref, stations, lanes)
    lane = iota((1, lanes), 1)
    channel_lane = lane // (2 * stations)
    quarter = 0.25 * ((lane // stations) % 2).astype(jnp.float32)
    first_chan = lax.axis_index("chan") * channels
    total_chans = channels * lax.axis_size("chan")
    block = min(64, beams)

    def tied_rows(first):
        east, north, group = beam_columns(order_ref, dir_ref, first, block)
        delay = east * east_s + north * north_s
        member = jnp.where(group == group_s, scale, 0.0)
        for g in range(groups):
            freq = 1.0 + (first_chan + g * CB + channel_lane).astype(jnp.float32) / total_chans
            wave = cos_turns(delay * freq - quarter)
            tied_ref[pl.ds(first, block), g * lanes : (g + 1) * lanes] = (wave * member).astype(
                jnp.bfloat16
            )

    if beams == block:
        tied_rows(0)
    else:

        def body(i, carry):
            tied_rows(pl.multiple_of(i * block, block))
            return carry

        lax.fori_loop(0, beams // block, body, 0)

    antenna_tile = iota((antennas, tiles), 0) // TILE_ANTENNAS == iota((antennas, tiles), 1)
    sum_ref[...] = antenna_tile.astype(jnp.bfloat16)
    for copy in small[4:]:
        copy.wait()
    member_table = (iota((stations, tiles), 0) == ts_ref[...] % stations).astype(jnp.float32)
    own_channel = iota((lanes, CB * rows_c), 0) // (2 * stations) == iota(
        (lanes, CB * rows_c), 1
    ) // rows_c

    for g in range(groups):
        channel0 = g * CB
        weights = aw_ref[channel0 : channel0 + CB].astype(jnp.float32)
        large[2 * g].wait()
        large[2 * g + 1].wait()
        products = []
        for c in range(CB):
            w_re = jnp.broadcast_to(weights[c, 0:1], (samples, antennas)).astype(jnp.bfloat16)
            w_im = jnp.broadcast_to(weights[c, 1:2], (samples, antennas)).astype(jnp.bfloat16)
            v_re, v_im = volts[channel0 + c, 0], volts[channel0 + c, 1]
            products.append(w_re * v_re - w_im * v_im)
            products.append(w_re * v_im + w_im * v_re)
        beams_tile = jnp.dot(
            jnp.concatenate(products, axis=0), sum_ref[...], preferred_element_type=jnp.float32
        ).astype(jnp.bfloat16)
        left = []
        for c in range(CB):
            tile_re = beams_tile[c * rows_c : c * rows_c + samples]
            tile_im = beams_tile[c * rows_c + samples : (c + 1) * rows_c]
            left.append(jnp.concatenate([tile_re, tile_im], axis=1))
            left.append(jnp.concatenate([tile_im, -tile_re], axis=1))
        right = []
        swt = sw_ref[channel0 : channel0 + CB].astype(jnp.float32)
        for c in range(CB):
            re = swt[c, 0:1] * member_table
            im = swt[c, 1:2] * member_table
            right.append(jnp.concatenate([re, -im], axis=1))
            right.append(jnp.concatenate([im, re], axis=1))
        station = dot_nt(
            jnp.concatenate(right, axis=0).astype(jnp.bfloat16), jnp.concatenate(left, axis=0)
        )
        station = jnp.where(own_channel, station, 0.0).astype(jnp.bfloat16)
        tied = jnp.dot(
            tied_ref[:, g * lanes : (g + 1) * lanes], station, preferred_element_type=jnp.float32
        )
        devices, rows, _ = out_ref.shape
        out_ref[:, :, channel0 * rows_c : (channel0 + CB) * rows_c] = tied.astype(
            jnp.bfloat16
        ).reshape(devices, rows, CB * rows_c)


def last_kernel(parts_ref, out_ref):
    n_stn, n_chan = lax.axis_size("stn"), lax.axis_size("chan")
    own_beams, rows_c, total_chans = out_ref.shape
    channels = total_chans // n_chan
    width = channels * rows_c
    parts = parts_ref[...].astype(jnp.float32).reshape(n_stn, n_chan, own_beams, width)
    tied = jnp.sum(parts, axis=0)
    diagonal = iota((channels, width), 0) == iota((channels, width), 1) // rows_c
    spread = (iota((rows_c, width), 0) == iota((rows_c, width), 1) % rows_c).astype(jnp.bfloat16)
    for b in range(own_beams):
        rows = [jnp.where(diagonal, tied[chan, b : b + 1], 0.0) for chan in range(n_chan)]
        rows = jnp.concatenate(rows, axis=0).astype(jnp.bfloat16)
        out_ref[b] = dot_nt(spread, rows).astype(jnp.bfloat16)


def shards(
    volts,
    antenna_tile_weights,
    station_weights,
    tile_station,
    station_group,
    station_pos,
    beam_dir,
    beam_order,
):
    channels, _, samples, _ = volts.shape
    beams = beam_order.shape[0]
    n_stn, n_chan = lax.axis_size("stn"), lax.axis_size("chan")
    rows = beams // (n_stn * n_chan)
    width = channels * 2 * samples
    operands = (
        volts,
        antenna_tile_weights,
        station_weights,
        tile_station[None, :],
        station_group[None, :],
        station_pos.T,
        beam_dir.T,
        beam_order[None, :],
    )
    operands = [pltpu.with_memory_space_constraint(x, pltpu.HBM) for x in operands]
    groups = channels // CB
    partial = pl.pallas_call(
        kernel,
        out_shape=pltpu.VMEM((n_stn * n_chan, rows, width), jnp.bfloat16),
        in_specs=[pl.BlockSpec(memory_space=pltpu.HBM)] * len(operands),
        out_specs=pl.BlockSpec(memory_space=pltpu.VMEM),
        scratch_shapes=[pltpu.VMEM(x.shape, x.dtype) for x in operands]
        + [
            pltpu.VMEM((beams, channels * 2 * (station_weights.shape[2] // TPS)), jnp.bfloat16),
            pltpu.VMEM((volts.shape[3], station_weights.shape[2]), jnp.bfloat16),
            pltpu.SemaphoreType.DMA((len(operands) - 1 + 2 * groups,)),
        ],
        compiler_params=pltpu.CompilerParams(vmem_limit_bytes=24 * 2**20),
        name="partial_tied",
    )(*operands)
    parts = lax.all_to_all(partial, ("stn", "chan"), split_axis=0, concat_axis=0, tiled=True)
    vmem = pl.BlockSpec(memory_space=pltpu.VMEM)
    tied = pl.pallas_call(
        last_kernel,
        out_shape=jax.ShapeDtypeStruct((rows, 2 * samples, n_chan * channels), jnp.bfloat16),
        in_specs=[vmem],
        out_specs=vmem,
        compiler_params=pltpu.CompilerParams(vmem_limit_bytes=16 * 2**20),
        name="tied_beams",
    )(parts)
    return tied.transpose(0, 2, 1)


def solution(mesh):
    in_specs = (
        P("chan", None, None, "stn"),
        P("chan", None, "stn"),
        P("chan", None, "stn"),
        P("stn"),
        P(),
        P(),
        P(),
        P(),
    )
    out_specs = P(("stn", "chan"), None, None)
    return jax.shard_map(shards, mesh=mesh, in_specs=in_specs, out_specs=out_specs, check_vma=False)
```

```python
import functools
import math

import jax
import jax.numpy as jnp
from jax import lax
from jax.experimental import pallas as pl
from jax.experimental.pallas import tpu as pltpu
from jax.sharding import PartitionSpec as P

TILE_ANTENNAS = 16
TPS = 16
GROUPS = 4
CB = 8
NT = (((1,), (1,)), ((), ()))
SIN = [(-1) ** i * (2 * math.pi) ** (2 * i + 1) / math.factorial(2 * i + 1) for i in range(7)]


def dot_nt(a, b):
    return lax.dot_general(a, b, NT, preferred_element_type=jnp.float32)


def iota(shape, dim):
    return lax.broadcasted_iota(jnp.int32, shape, dim)


def beam_columns(order_ref, dir_ref, start, rows):
    beams = order_ref.shape[1]
    order = order_ref[...].astype(jnp.float32)
    lane = iota((rows, beams), 1)
    n_chan = lax.axis_size("chan")
    each = beams // (n_chan * lax.axis_size("stn"))
    slot = iota((rows, beams), 0) + start
    low = (slot // (beams // 2)) ^ (lax.axis_index("stn") % 2)
    pair, rest = slot % (beams // 2) // (n_chan * each), slot % (n_chan * each)
    own = lane == (pair * 2 + low) * (n_chan * each) + rest
    ids = jnp.sum(jnp.where(own, order, 0.0), axis=1, keepdims=True)
    pick = lane.astype(jnp.float32) == ids
    east = jnp.sum(jnp.where(pick, dir_ref[0:1, :], 0.0), axis=1, keepdims=True)
    north = jnp.sum(jnp.where(pick, dir_ref[1:2, :], 0.0), axis=1, keepdims=True)
    group = ids - GROUPS * jnp.floor(ids * (1.0 / GROUPS))
    return east, north, group


def station_rows(pos_ref, group_ref, stations, lanes):
    total = group_ref.shape[1]
    first = lax.axis_index("stn") * stations
    own = iota((stations, total), 1) == iota((stations, total), 0) + first
    spread = iota((stations, lanes), 0) == iota((stations, lanes), 1) % stations

    def turn(row):
        column = jnp.sum(jnp.where(own, row, 0.0), axis=1, keepdims=True)
        return jnp.sum(jnp.where(spread, column, 0.0), axis=0, keepdims=True)

    return turn(pos_ref[0:1, :]), turn(pos_ref[1:2, :]), turn(group_ref[...].astype(jnp.float32))


def cos_turns(t):
    y = t - jnp.floor(t + 0.5)
    z = 0.25 - jnp.abs(y)
    z2 = z * z
    value = jnp.full_like(z, SIN[-1])
    for coefficient in SIN[-2::-1]:
        value = value * z2 + coefficient
    return value * z


def kernel(
    volt_hbm,
    aw_hbm,
    sw_hbm,
    ts_hbm,
    group_hbm,
    pos_hbm,
    dir_hbm,
    order_hbm,
    keep_ref,
    send_ref,
    volts,
    aw_ref,
    sw_ref,
    ts_ref,
    group_ref,
    pos_ref,
    dir_ref,
    order_ref,
    tied_ref,
    sum_ref,
    sems,
):
    channels, _, samples, antennas = volt_hbm.shape
    tiles = sw_ref.shape[2]
    stations = tiles // TPS
    groups = channels // CB
    rows_c = 2 * samples
    beams = order_ref.shape[1]
    lanes = CB * 2 * stations
    scale = 1.0 / math.sqrt(group_ref.shape[1])

    def start(source, target, k):
        copy = pltpu.make_async_copy(source, target, sems.at[k])
        copy.start()
        return copy

    small = [
        start(source, target, k)
        for k, (source, target) in enumerate(
            [
                (order_hbm, order_ref),
                (dir_hbm, dir_ref),
                (pos_hbm, pos_ref),
                (group_hbm, group_ref),
                (ts_hbm, ts_ref),
                (sw_hbm, sw_ref),
                (aw_hbm, aw_ref),
            ]
        )
    ]
    large = []
    for k in range(2 * groups):
        part = pl.ds(k * CB // 2, CB // 2)
        large.append(start(volt_hbm.at[part], volts.at[part], len(small) + k))
    for copy in small[:4]:
        copy.wait()

    east_s, north_s, group_s = station_rows(pos_ref, group_ref, stations, lanes)
    lane = iota((1, lanes), 1)
    channel_lane = lane // (2 * stations)
    quarter = 0.25 * ((lane // stations) % 2).astype(jnp.float32)
    first_chan = lax.axis_index("chan") * channels
    total_chans = channels * lax.axis_size("chan")
    block = min(64, beams)

    def tied_rows(first):
        east, north, group = beam_columns(order_ref, dir_ref, first, block)
        delay = east * east_s + north * north_s
        member = jnp.where(group == group_s, scale, 0.0)
        for g in range(groups):
            freq = 1.0 + (first_chan + g * CB + channel_lane).astype(jnp.float32) / total_chans
            wave = cos_turns(delay * freq - quarter)
            tied_ref[pl.ds(first, block), g * lanes : (g + 1) * lanes] = (wave * member).astype(
                jnp.bfloat16
            )

    if beams == block:
        tied_rows(0)
    else:

        def body(i, carry):
            tied_rows(pl.multiple_of(i * block, block))
            return carry

        lax.fori_loop(0, beams // block, body, 0)

    antenna_tile = iota((antennas, tiles), 0) // TILE_ANTENNAS == iota((antennas, tiles), 1)
    sum_ref[...] = antenna_tile.astype(jnp.bfloat16)
    for copy in small[4:]:
        copy.wait()
    member_table = (iota((stations, tiles), 0) == ts_ref[...] % stations).astype(jnp.float32)
    own_channel = iota((lanes, CB * rows_c), 0) // (2 * stations) == iota(
        (lanes, CB * rows_c), 1
    ) // rows_c

    for g in range(groups):
        channel0 = g * CB
        weights = aw_ref[channel0 : channel0 + CB].astype(jnp.float32)
        large[2 * g].wait()
        large[2 * g + 1].wait()
        products = []
        for c in range(CB):
            w_re = jnp.broadcast_to(weights[c, 0:1], (samples, antennas)).astype(jnp.bfloat16)
            w_im = jnp.broadcast_to(weights[c, 1:2], (samples, antennas)).astype(jnp.bfloat16)
            v_re, v_im = volts[channel0 + c, 0], volts[channel0 + c, 1]
            products.append(w_re * v_re - w_im * v_im)
            products.append(w_re * v_im + w_im * v_re)
        beams_tile = jnp.dot(
            jnp.concatenate(products, axis=0), sum_ref[...], preferred_element_type=jnp.float32
        ).astype(jnp.bfloat16)
        left = []
        for c in range(CB):
            tile_re = beams_tile[c * rows_c : c * rows_c + samples]
            tile_im = beams_tile[c * rows_c + samples : (c + 1) * rows_c]
            left.append(jnp.concatenate([tile_re, tile_im], axis=1))
            left.append(jnp.concatenate([tile_im, -tile_re], axis=1))
        right = []
        swt = sw_ref[channel0 : channel0 + CB].astype(jnp.float32)
        for c in range(CB):
            re = swt[c, 0:1] * member_table
            im = swt[c, 1:2] * member_table
            right.append(jnp.concatenate([re, -im], axis=1))
            right.append(jnp.concatenate([im, re], axis=1))
        station = dot_nt(
            jnp.concatenate(right, axis=0).astype(jnp.bfloat16), jnp.concatenate(left, axis=0)
        )
        station = jnp.where(own_channel, station, 0.0).astype(jnp.bfloat16)
        tied = jnp.dot(
            tied_ref[:, g * lanes : (g + 1) * lanes], station, preferred_element_type=jnp.float32
        )
        tied = tied.astype(jnp.bfloat16)
        columns = slice(channel0 * rows_c, (channel0 + CB) * rows_c)
        for half, out_ref in enumerate((keep_ref, send_ref)):
            devices, rows, _ = out_ref.shape
            part = tied[half * devices * rows : (half + 1) * devices * rows]
            out_ref[:, :, columns] = part.reshape(devices, rows, CB * rows_c)


def last_kernel(parts_ref, out_ref):
    n_chan = lax.axis_size("chan")
    pairs = lax.axis_size("stn") // 2
    own_beams, rows_c, total_chans = out_ref.shape
    channels = total_chans // n_chan
    width = channels * rows_c
    parts = parts_ref[...].astype(jnp.float32).reshape(pairs, n_chan, own_beams, width)
    tied = jnp.sum(parts, axis=0)
    diagonal = iota((channels, width), 0) == iota((channels, width), 1) // rows_c
    spread = (iota((rows_c, width), 0) == iota((rows_c, width), 1) % rows_c).astype(jnp.bfloat16)
    for b in range(own_beams):
        rows = [jnp.where(diagonal, tied[chan, b : b + 1], 0.0) for chan in range(n_chan)]
        rows = jnp.concatenate(rows, axis=0).astype(jnp.bfloat16)
        out_ref[b] = dot_nt(spread, rows).astype(jnp.bfloat16)


def shards(
    volts,
    antenna_tile_weights,
    station_weights,
    tile_station,
    station_group,
    station_pos,
    beam_dir,
    beam_order,
):
    channels, _, samples, _ = volts.shape
    beams = beam_order.shape[0]
    n_stn, n_chan = lax.axis_size("stn"), lax.axis_size("chan")
    rows = beams // (n_stn * n_chan)
    width = channels * 2 * samples
    operands = (
        volts,
        antenna_tile_weights,
        station_weights,
        tile_station[None, :],
        station_group[None, :],
        station_pos.T,
        beam_dir.T,
        beam_order[None, :],
    )
    operands = [pltpu.with_memory_space_constraint(x, pltpu.HBM) for x in operands]
    groups = channels // CB
    keep, send = pl.pallas_call(
        kernel,
        out_shape=[pltpu.VMEM((n_stn // 2 * n_chan, rows, width), jnp.bfloat16)] * 2,
        in_specs=[pl.BlockSpec(memory_space=pltpu.HBM)] * len(operands),
        out_specs=[pl.BlockSpec(memory_space=pltpu.VMEM)] * 2,
        scratch_shapes=[pltpu.VMEM(x.shape, x.dtype) for x in operands]
        + [
            pltpu.VMEM((beams, channels * 2 * (station_weights.shape[2] // TPS)), jnp.bfloat16),
            pltpu.VMEM((volts.shape[3], station_weights.shape[2]), jnp.bfloat16),
            pltpu.SemaphoreType.DMA((len(operands) - 1 + 2 * groups,)),
        ],
        compiler_params=pltpu.CompilerParams(vmem_limit_bytes=24 * 2**20),
        name="partial_tied",
    )(*operands)
    axes = ("stn", "chan")
    flat = range(n_stn * n_chan)
    received = lax.ppermute(send, axes, [(d, d ^ n_chan) for d in flat])
    pair_sum = (keep.astype(jnp.float32) + received.astype(jnp.float32)).astype(jnp.bfloat16)
    groups = [[d for d in flat if d // n_chan % 2 == low] for low in range(2)]
    parts = lax.all_to_all(
        pair_sum, axes, split_axis=0, concat_axis=0, axis_index_groups=groups, tiled=True
    )
    vmem = pl.BlockSpec(memory_space=pltpu.VMEM)
    tied = pl.pallas_call(
        last_kernel,
        out_shape=jax.ShapeDtypeStruct((rows, 2 * samples, n_chan * channels), jnp.bfloat16),
        in_specs=[vmem],
        out_specs=vmem,
        compiler_params=pltpu.CompilerParams(vmem_limit_bytes=16 * 2**20),
        name="tied_beams",
    )(parts)
    return tied.transpose(0, 2, 1)


def solution(mesh):
    in_specs = (
        P("chan", None, None, "stn"),
        P("chan", None, "stn"),
        P("chan", None, "stn"),
        P("stn"),
        P(),
        P(),
        P(),
        P(),
    )
    out_specs = P(("stn", "chan"), None, None)
    return jax.shard_map(shards, mesh=mesh, in_specs=in_specs, out_specs=out_specs, check_vma=False)
```

```python
import functools
import math

import jax
import jax.numpy as jnp
from jax import lax
from jax.experimental import pallas as pl
from jax.experimental.pallas import tpu as pltpu
from jax.sharding import PartitionSpec as P

TILE_ANTENNAS = 16
TPS = 16
GROUPS = 4
CB = 8
NT = (((1,), (1,)), ((), ()))
SIN = [(-1) ** i * (2 * math.pi) ** (2 * i + 1) / math.factorial(2 * i + 1) for i in range(7)]


def dot_nt(a, b):
    return lax.dot_general(a, b, NT, preferred_element_type=jnp.float32)


def iota(shape, dim):
    return lax.broadcasted_iota(jnp.int32, shape, dim)


def beam_columns(order_ref, dir_ref, start, rows):
    beams = order_ref.shape[1]
    order = order_ref[...].astype(jnp.float32)
    lane = iota((rows, beams), 1)
    n_stn, n_chan = lax.axis_size("stn"), lax.axis_size("chan")
    each = beams // (n_stn * n_chan)
    slot = iota((rows, beams), 0) + start
    device = slot // each
    bits = n_stn.bit_length() - 1
    stn = lax.axis_index("stn")
    for bit in range(bits):
        stn = stn ^ (((device // n_chan) >> (bits - 1 - bit)) % 2 << bit)
    chan = device % n_chan ^ lax.axis_index("chan")
    own = lane == (stn * n_chan + chan) * each + slot % each
    ids = jnp.sum(jnp.where(own, order, 0.0), axis=1, keepdims=True)
    pick = lane.astype(jnp.float32) == ids
    east = jnp.sum(jnp.where(pick, dir_ref[0:1, :], 0.0), axis=1, keepdims=True)
    north = jnp.sum(jnp.where(pick, dir_ref[1:2, :], 0.0), axis=1, keepdims=True)
    group = ids - GROUPS * jnp.floor(ids * (1.0 / GROUPS))
    return east, north, group


def station_rows(pos_ref, group_ref, stations, lanes):
    total = group_ref.shape[1]
    first = lax.axis_index("stn") * stations
    own = iota((stations, total), 1) == iota((stations, total), 0) + first
    spread = iota((stations, lanes), 0) == iota((stations, lanes), 1) % stations

    def turn(row):
        column = jnp.sum(jnp.where(own, row, 0.0), axis=1, keepdims=True)
        return jnp.sum(jnp.where(spread, column, 0.0), axis=0, keepdims=True)

    return turn(pos_ref[0:1, :]), turn(pos_ref[1:2, :]), turn(group_ref[...].astype(jnp.float32))


def cos_turns(t):
    y = t - jnp.floor(t + 0.5)
    z = 0.25 - jnp.abs(y)
    z2 = z * z
    value = jnp.full_like(z, SIN[-1])
    for coefficient in SIN[-2::-1]:
        value = value * z2 + coefficient
    return value * z


def kernel(
    volt_hbm,
    aw_hbm,
    sw_hbm,
    ts_hbm,
    group_hbm,
    pos_hbm,
    dir_hbm,
    order_hbm,
    keep_ref,
    send_ref,
    volts,
    aw_ref,
    sw_ref,
    ts_ref,
    group_ref,
    pos_ref,
    dir_ref,
    order_ref,
    tied_ref,
    sum_ref,
    sems,
):
    channels, _, samples, antennas = volt_hbm.shape
    tiles = sw_ref.shape[2]
    stations = tiles // TPS
    groups = channels // CB
    rows_c = 2 * samples
    beams = order_ref.shape[1]
    lanes = CB * 2 * stations
    scale = 1.0 / math.sqrt(group_ref.shape[1])

    def start(source, target, k):
        copy = pltpu.make_async_copy(source, target, sems.at[k])
        copy.start()
        return copy

    small = [
        start(source, target, k)
        for k, (source, target) in enumerate(
            [
                (order_hbm, order_ref),
                (dir_hbm, dir_ref),
                (pos_hbm, pos_ref),
                (group_hbm, group_ref),
                (ts_hbm, ts_ref),
                (sw_hbm, sw_ref),
                (aw_hbm, aw_ref),
            ]
        )
    ]
    large = []
    for k in range(2 * groups):
        part = pl.ds(k * CB // 2, CB // 2)
        large.append(start(volt_hbm.at[part], volts.at[part], len(small) + k))
    for copy in small[:4]:
        copy.wait()

    east_s, north_s, group_s = station_rows(pos_ref, group_ref, stations, lanes)
    lane = iota((1, lanes), 1)
    channel_lane = lane // (2 * stations)
    quarter = 0.25 * ((lane // stations) % 2).astype(jnp.float32)
    first_chan = lax.axis_index("chan") * channels
    total_chans = channels * lax.axis_size("chan")
    block = min(64, beams)

    def tied_rows(first):
        east, north, group = beam_columns(order_ref, dir_ref, first, block)
        delay = east * east_s + north * north_s
        member = jnp.where(group == group_s, scale, 0.0)
        for g in range(groups):
            freq = 1.0 + (first_chan + g * CB + channel_lane).astype(jnp.float32) / total_chans
            wave = cos_turns(delay * freq - quarter)
            tied_ref[pl.ds(first, block), g * lanes : (g + 1) * lanes] = (wave * member).astype(
                jnp.bfloat16
            )

    if beams == block:
        tied_rows(0)
    else:

        def body(i, carry):
            tied_rows(pl.multiple_of(i * block, block))
            return carry

        lax.fori_loop(0, beams // block, body, 0)

    antenna_tile = iota((antennas, tiles), 0) // TILE_ANTENNAS == iota((antennas, tiles), 1)
    sum_ref[...] = antenna_tile.astype(jnp.bfloat16)
    for copy in small[4:]:
        copy.wait()
    member_table = (iota((stations, tiles), 0) == ts_ref[...] % stations).astype(jnp.float32)
    own_channel = iota((lanes, CB * rows_c), 0) // (2 * stations) == iota(
        (lanes, CB * rows_c), 1
    ) // rows_c

    for g in range(groups):
        channel0 = g * CB
        weights = aw_ref[channel0 : channel0 + CB].astype(jnp.float32)
        large[2 * g].wait()
        large[2 * g + 1].wait()
        products = []
        for c in range(CB):
            w_re = jnp.broadcast_to(weights[c, 0:1], (samples, antennas)).astype(jnp.bfloat16)
            w_im = jnp.broadcast_to(weights[c, 1:2], (samples, antennas)).astype(jnp.bfloat16)
            v_re, v_im = volts[channel0 + c, 0], volts[channel0 + c, 1]
            products.append(w_re * v_re - w_im * v_im)
            products.append(w_re * v_im + w_im * v_re)
        beams_tile = jnp.dot(
            jnp.concatenate(products, axis=0), sum_ref[...], preferred_element_type=jnp.float32
        ).astype(jnp.bfloat16)
        left = []
        for c in range(CB):
            tile_re = beams_tile[c * rows_c : c * rows_c + samples]
            tile_im = beams_tile[c * rows_c + samples : (c + 1) * rows_c]
            left.append(jnp.concatenate([tile_re, tile_im], axis=1))
            left.append(jnp.concatenate([tile_im, -tile_re], axis=1))
        right = []
        swt = sw_ref[channel0 : channel0 + CB].astype(jnp.float32)
        for c in range(CB):
            re = swt[c, 0:1] * member_table
            im = swt[c, 1:2] * member_table
            right.append(jnp.concatenate([re, -im], axis=1))
            right.append(jnp.concatenate([im, re], axis=1))
        station = dot_nt(
            jnp.concatenate(right, axis=0).astype(jnp.bfloat16), jnp.concatenate(left, axis=0)
        )
        station = jnp.where(own_channel, station, 0.0).astype(jnp.bfloat16)
        tied = jnp.dot(
            tied_ref[:, g * lanes : (g + 1) * lanes], station, preferred_element_type=jnp.float32
        )
        tied = tied.astype(jnp.bfloat16)
        columns = slice(channel0 * rows_c, (channel0 + CB) * rows_c)
        for half, out_ref in enumerate((keep_ref, send_ref)):
            devices, rows, _ = out_ref.shape
            part = tied[half * devices * rows : (half + 1) * devices * rows]
            out_ref[:, :, columns] = part.reshape(devices, rows, CB * rows_c)


def last_kernel(*refs):
    parts, out_ref = refs[:-1], refs[-1]
    n_chan = len(parts)
    own_beams, rows_c, total_chans = out_ref.shape
    channels = total_chans // n_chan
    width = channels * rows_c
    diagonal = iota((channels, width), 0) == iota((channels, width), 1) // rows_c
    spread = (iota((rows_c, width), 0) == iota((rows_c, width), 1) % rows_c).astype(jnp.bfloat16)
    values = [part[...].astype(jnp.float32).reshape(own_beams, width) for part in parts]
    own_chan = lax.axis_index("chan")
    for b in range(own_beams):
        rows = []
        for chan in range(n_chan):
            row = values[0][b : b + 1]
            for offset in range(1, n_chan):
                row = jnp.where(own_chan ^ offset == chan, values[offset][b : b + 1], row)
            rows.append(jnp.where(diagonal, row, 0.0))
        rows = jnp.concatenate(rows, axis=0).astype(jnp.bfloat16)
        out_ref[b] = dot_nt(spread, rows).astype(jnp.bfloat16)


def shards(
    volts,
    antenna_tile_weights,
    station_weights,
    tile_station,
    station_group,
    station_pos,
    beam_dir,
    beam_order,
):
    channels, _, samples, _ = volts.shape
    beams = beam_order.shape[0]
    n_stn, n_chan = lax.axis_size("stn"), lax.axis_size("chan")
    rows = beams // (n_stn * n_chan)
    width = channels * 2 * samples
    operands = (
        volts,
        antenna_tile_weights,
        station_weights,
        tile_station[None, :],
        station_group[None, :],
        station_pos.T,
        beam_dir.T,
        beam_order[None, :],
    )
    operands = [pltpu.with_memory_space_constraint(x, pltpu.HBM) for x in operands]
    groups = channels // CB
    keep, send = pl.pallas_call(
        kernel,
        out_shape=[pltpu.VMEM((n_stn // 2 * n_chan, rows, width), jnp.bfloat16)] * 2,
        in_specs=[pl.BlockSpec(memory_space=pltpu.HBM)] * len(operands),
        out_specs=[pl.BlockSpec(memory_space=pltpu.VMEM)] * 2,
        scratch_shapes=[pltpu.VMEM(x.shape, x.dtype) for x in operands]
        + [
            pltpu.VMEM((beams, channels * 2 * (station_weights.shape[2] // TPS)), jnp.bfloat16),
            pltpu.VMEM((volts.shape[3], station_weights.shape[2]), jnp.bfloat16),
            pltpu.SemaphoreType.DMA((len(operands) - 1 + 2 * groups,)),
        ],
        compiler_params=pltpu.CompilerParams(vmem_limit_bytes=24 * 2**20),
        name="partial_tied",
    )(*operands)
    axes = ("stn", "chan")
    flat = range(n_stn * n_chan)
    bit = n_chan
    while True:
        received = lax.ppermute(send, axes, [(d, d ^ bit) for d in flat])
        keep = (keep.astype(jnp.float32) + received.astype(jnp.float32)).astype(jnp.bfloat16)
        bit *= 2
        if bit == n_stn * n_chan:
            break
        half = keep.shape[0] // 2
        keep, send = keep[:half], keep[half:]
    parts = [keep[:1]]
    for offset in range(1, n_chan):
        perm = [(d, d ^ offset) for d in flat]
        parts.append(lax.ppermute(keep[offset : offset + 1], axes, perm))
    vmem = pl.BlockSpec(memory_space=pltpu.VMEM)
    tied = pl.pallas_call(
        last_kernel,
        out_shape=jax.ShapeDtypeStruct((rows, 2 * samples, n_chan * channels), jnp.bfloat16),
        in_specs=[vmem] * n_chan,
        out_specs=vmem,
        compiler_params=pltpu.CompilerParams(vmem_limit_bytes=16 * 2**20),
        name="tied_beams",
    )(*parts)
    return tied.transpose(0, 2, 1)


def solution(mesh):
    in_specs = (
        P("chan", None, None, "stn"),
        P("chan", None, "stn"),
        P("chan", None, "stn"),
        P("stn"),
        P(),
        P(),
        P(),
        P(),
    )
    out_specs = P(("stn", "chan"), None, None)
    return jax.shard_map(shards, mesh=mesh, in_specs=in_specs, out_specs=out_specs, check_vma=False)
```

```python
import functools
import math

import jax
import jax.numpy as jnp
from jax import lax
from jax.experimental import pallas as pl
from jax.experimental.pallas import tpu as pltpu
from jax.sharding import PartitionSpec as P

TILE_ANTENNAS = 16
TPS = 16
GROUPS = 4
LANES = 128
CB = 8
NT = (((1,), (1,)), ((), ()))
SIN = [(-1) ** i * (2 * math.pi) ** (2 * i + 1) / math.factorial(2 * i + 1) for i in range(7)]


def dot_nt(a, b):
    return lax.dot_general(a, b, NT, preferred_element_type=jnp.float32)


def iota(shape, dim):
    return lax.broadcasted_iota(jnp.int32, shape, dim)


def beam_columns(order_ref, dir_ref, start, rows):
    beams = order_ref.shape[1]
    order = order_ref[...].astype(jnp.float32)
    lane = iota((rows, beams), 1)
    own = lane == iota((rows, beams), 0) + start
    ids = jnp.sum(jnp.where(own, order, 0.0), axis=1, keepdims=True)
    pick = lane.astype(jnp.float32) == ids
    east = jnp.sum(jnp.where(pick, dir_ref[0:1, :], 0.0), axis=1, keepdims=True)
    north = jnp.sum(jnp.where(pick, dir_ref[1:2, :], 0.0), axis=1, keepdims=True)
    group = ids - GROUPS * jnp.floor(ids * (1.0 / GROUPS))
    return east, north, group


def station_rows(pos_ref, group_ref, stations, lanes):
    total = group_ref.shape[1]
    first = lax.axis_index("stn") * stations
    own = iota((stations, total), 1) == iota((stations, total), 0) + first
    spread = iota((stations, lanes), 0) == iota((stations, lanes), 1) % stations

    def turn(row):
        column = jnp.sum(jnp.where(own, row, 0.0), axis=1, keepdims=True)
        return jnp.sum(jnp.where(spread, column, 0.0), axis=0, keepdims=True)

    return turn(pos_ref[0:1, :]), turn(pos_ref[1:2, :]), turn(group_ref[...].astype(jnp.float32))


def cos_turns(t):
    y = t - jnp.floor(t + 0.5)
    z = 0.25 - jnp.abs(y)
    z2 = z * z
    value = jnp.full_like(z, SIN[-1])
    for coefficient in SIN[-2::-1]:
        value = value * z2 + coefficient
    return value * z


def fold(x):
    half = x.shape[1] // 2
    low = iota((x.shape[0], LANES), 1) % TILE_ANTENNAS < TILE_ANTENNAS // 2
    out = []
    for start in range(0, half, LANES):
        a, b = x[:, start : start + LANES], x[:, half + start : half + start + LANES]
        a = a + pltpu.roll(a, LANES - TILE_ANTENNAS // 2, 1)
        b = b + pltpu.roll(b, TILE_ANTENNAS // 2, 1)
        out.append(jnp.where(low, a, b))
    return jnp.concatenate(out, axis=1)


def kernel(
    volt_hbm,
    aw_hbm,
    sw_hbm,
    ts_hbm,
    group_hbm,
    pos_hbm,
    dir_hbm,
    order_hbm,
    out_ref,
    volts,
    aw_ref,
    sw_ref,
    ts_ref,
    group_ref,
    pos_ref,
    dir_ref,
    order_ref,
    tied_ref,
    sum_ref,
    sems,
):
    channels, _, samples, antennas = volt_hbm.shape
    tiles = sw_ref.shape[2]
    stations = tiles // TPS
    groups = channels // CB
    rows_c = 2 * samples
    beams = order_ref.shape[1]
    lanes = CB * 2 * stations
    scale = 1.0 / math.sqrt(group_ref.shape[1])

    def start(source, target, k):
        copy = pltpu.make_async_copy(source, target, sems.at[k])
        copy.start()
        return copy

    small = [
        start(source, target, k)
        for k, (source, target) in enumerate(
            [
                (order_hbm, order_ref),
                (dir_hbm, dir_ref),
                (pos_hbm, pos_ref),
                (group_hbm, group_ref),
                (ts_hbm, ts_ref),
                (sw_hbm, sw_ref),
                (aw_hbm, aw_ref),
            ]
        )
    ]
    large = []
    for k in range(2 * groups):
        part = pl.ds(k * CB // 2, CB // 2)
        large.append(start(volt_hbm.at[part], volts.at[part], len(small) + k))
    for copy in small[:4]:
        copy.wait()

    east_s, north_s, group_s = station_rows(pos_ref, group_ref, stations, lanes)
    lane = iota((1, lanes), 1)
    channel_lane = lane // (2 * stations)
    quarter = 0.25 * ((lane // stations) % 2).astype(jnp.float32)
    first_chan = lax.axis_index("chan") * channels
    total_chans = channels * lax.axis_size("chan")
    block = min(64, beams)

    def tied_rows(first):
        east, north, group = beam_columns(order_ref, dir_ref, first, block)
        delay = east * east_s + north * north_s
        member = jnp.where(group == group_s, scale, 0.0)
        for g in range(groups):
            freq = 1.0 + (first_chan + g * CB + channel_lane).astype(jnp.float32) / total_chans
            wave = cos_turns(delay * freq - quarter)
            tied_ref[pl.ds(first, block), g * lanes : (g + 1) * lanes] = (wave * member).astype(
                jnp.bfloat16
            )

    if beams == block:
        tied_rows(0)
    else:

        def body(i, carry):
            tied_rows(pl.multiple_of(i * block, block))
            return carry

        lax.fori_loop(0, beams // block, body, 0)

    row, tile = iota(sum_ref.shape, 0), iota(sum_ref.shape, 1)
    right_half = row // (TILE_ANTENNAS // 2) % 2 * (tiles // 2)
    sum_ref[...] = (row // TILE_ANTENNAS + right_half == tile).astype(jnp.bfloat16)
    for copy in small[4:]:
        copy.wait()
    member_table = (iota((stations, tiles), 0) == ts_ref[...] % stations).astype(jnp.float32)
    own_channel = iota((lanes, CB * rows_c), 0) // (2 * stations) == iota(
        (lanes, CB * rows_c), 1
    ) // rows_c

    for g in range(groups):
        channel0 = g * CB
        weights = aw_ref[channel0 : channel0 + CB].astype(jnp.float32)
        large[2 * g].wait()
        large[2 * g + 1].wait()
        products = []
        for c in range(CB):
            w_re = jnp.broadcast_to(weights[c, 0:1], (samples, antennas)).astype(jnp.bfloat16)
            w_im = jnp.broadcast_to(weights[c, 1:2], (samples, antennas)).astype(jnp.bfloat16)
            v_re, v_im = volts[channel0 + c, 0], volts[channel0 + c, 1]
            products.append(w_re * v_re - w_im * v_im)
            products.append(w_re * v_im + w_im * v_re)
        products = [fold(x) for x in products]
        beams_tile = jnp.dot(
            jnp.concatenate(products, axis=0), sum_ref[...], preferred_element_type=jnp.float32
        ).astype(jnp.bfloat16)
        left = []
        for c in range(CB):
            tile_re = beams_tile[c * rows_c : c * rows_c + samples]
            tile_im = beams_tile[c * rows_c + samples : (c + 1) * rows_c]
            left.append(jnp.concatenate([tile_re, tile_im], axis=1))
            left.append(jnp.concatenate([tile_im, -tile_re], axis=1))
        right = []
        swt = sw_ref[channel0 : channel0 + CB].astype(jnp.float32)
        for c in range(CB):
            re = swt[c, 0:1] * member_table
            im = swt[c, 1:2] * member_table
            right.append(jnp.concatenate([re, -im], axis=1))
            right.append(jnp.concatenate([im, re], axis=1))
        station = dot_nt(
            jnp.concatenate(right, axis=0).astype(jnp.bfloat16), jnp.concatenate(left, axis=0)
        )
        station = jnp.where(own_channel, station, 0.0).astype(jnp.bfloat16)
        tied = jnp.dot(
            tied_ref[:, g * lanes : (g + 1) * lanes], station, preferred_element_type=jnp.float32
        )
        devices, rows, _ = out_ref.shape
        out_ref[:, :, channel0 * rows_c : (channel0 + CB) * rows_c] = tied.astype(
            jnp.bfloat16
        ).reshape(devices, rows, CB * rows_c)


def last_kernel(parts_ref, out_ref):
    n_stn, n_chan = lax.axis_size("stn"), lax.axis_size("chan")
    own_beams, rows_c, total_chans = out_ref.shape
    channels = total_chans // n_chan
    width = channels * rows_c
    parts = parts_ref[...].astype(jnp.float32).reshape(n_stn, n_chan, own_beams, width)
    tied = jnp.sum(parts, axis=0)
    diagonal = iota((channels, width), 0) == iota((channels, width), 1) // rows_c
    spread = (iota((rows_c, width), 0) == iota((rows_c, width), 1) % rows_c).astype(jnp.bfloat16)
    for b in range(own_beams):
        rows = [jnp.where(diagonal, tied[chan, b : b + 1], 0.0) for chan in range(n_chan)]
        rows = jnp.concatenate(rows, axis=0).astype(jnp.bfloat16)
        out_ref[b] = dot_nt(spread, rows).astype(jnp.bfloat16)


def shards(
    volts,
    antenna_tile_weights,
    station_weights,
    tile_station,
    station_group,
    station_pos,
    beam_dir,
    beam_order,
):
    channels, _, samples, _ = volts.shape
    beams = beam_order.shape[0]
    n_stn, n_chan = lax.axis_size("stn"), lax.axis_size("chan")
    rows = beams // (n_stn * n_chan)
    width = channels * 2 * samples
    operands = (
        volts,
        antenna_tile_weights,
        station_weights,
        tile_station[None, :],
        station_group[None, :],
        station_pos.T,
        beam_dir.T,
        beam_order[None, :],
    )
    operands = [pltpu.with_memory_space_constraint(x, pltpu.HBM) for x in operands]
    groups = channels // CB
    partial = pl.pallas_call(
        kernel,
        out_shape=pltpu.VMEM((n_stn * n_chan, rows, width), jnp.bfloat16),
        in_specs=[pl.BlockSpec(memory_space=pltpu.HBM)] * len(operands),
        out_specs=pl.BlockSpec(memory_space=pltpu.VMEM),
        scratch_shapes=[pltpu.VMEM(x.shape, x.dtype) for x in operands]
        + [
            pltpu.VMEM((beams, channels * 2 * (station_weights.shape[2] // TPS)), jnp.bfloat16),
            pltpu.VMEM((volts.shape[3] // 2, station_weights.shape[2]), jnp.bfloat16),
            pltpu.SemaphoreType.DMA((len(operands) - 1 + 2 * groups,)),
        ],
        compiler_params=pltpu.CompilerParams(vmem_limit_bytes=24 * 2**20),
        name="partial_tied",
    )(*operands)
    parts = lax.all_to_all(partial, ("stn", "chan"), split_axis=0, concat_axis=0, tiled=True)
    vmem = pl.BlockSpec(memory_space=pltpu.VMEM)
    tied = pl.pallas_call(
        last_kernel,
        out_shape=jax.ShapeDtypeStruct((rows, 2 * samples, n_chan * channels), jnp.bfloat16),
        in_specs=[vmem],
        out_specs=vmem,
        compiler_params=pltpu.CompilerParams(vmem_limit_bytes=16 * 2**20),
        name="tied_beams",
    )(parts)
    return tied.transpose(0, 2, 1)


def solution(mesh):
    in_specs = (
        P("chan", None, None, "stn"),
        P("chan", None, "stn"),
        P("chan", None, "stn"),
        P("stn"),
        P(),
        P(),
        P(),
        P(),
    )
    out_specs = P(("stn", "chan"), None, None)
    return jax.shard_map(shards, mesh=mesh, in_specs=in_specs, out_specs=out_specs, check_vma=False)
```

```python
import functools
import math

import jax
import jax.numpy as jnp
from jax import lax
from jax.experimental import pallas as pl
from jax.experimental.pallas import tpu as pltpu
from jax.sharding import PartitionSpec as P

TILE_ANTENNAS = 16
TPS = 16
GROUPS = 4
CB = 8
NT = (((1,), (1,)), ((), ()))
SIN = [(-1) ** i * (2 * math.pi) ** (2 * i + 1) / math.factorial(2 * i + 1) for i in range(7)]


def dot_nt(a, b):
    return lax.dot_general(a, b, NT, preferred_element_type=jnp.float32)


def iota(shape, dim):
    return lax.broadcasted_iota(jnp.int32, shape, dim)


def beam_columns(order_ref, dir_ref, start, rows):
    beams = order_ref.shape[1]
    order = order_ref[...].astype(jnp.float32)
    lane = iota((rows, beams), 1)
    own = lane == iota((rows, beams), 0) + start
    ids = jnp.sum(jnp.where(own, order, 0.0), axis=1, keepdims=True)
    pick = lane.astype(jnp.float32) == ids
    east = jnp.sum(jnp.where(pick, dir_ref[0:1, :], 0.0), axis=1, keepdims=True)
    north = jnp.sum(jnp.where(pick, dir_ref[1:2, :], 0.0), axis=1, keepdims=True)
    group = ids - GROUPS * jnp.floor(ids * (1.0 / GROUPS))
    return east, north, group


def station_rows(pos_ref, group_ref, stations, lanes):
    total = group_ref.shape[1]
    first = lax.axis_index("stn") * stations
    own = iota((stations, total), 1) == iota((stations, total), 0) + first
    spread = iota((stations, lanes), 0) == iota((stations, lanes), 1) % stations

    def turn(row):
        column = jnp.sum(jnp.where(own, row, 0.0), axis=1, keepdims=True)
        return jnp.sum(jnp.where(spread, column, 0.0), axis=0, keepdims=True)

    return turn(pos_ref[0:1, :]), turn(pos_ref[1:2, :]), turn(group_ref[...].astype(jnp.float32))


def cos_turns(t):
    y = t - jnp.floor(t + 0.5)
    z = 0.25 - jnp.abs(y)
    z2 = z * z
    value = jnp.full_like(z, SIN[-1])
    for coefficient in SIN[-2::-1]:
        value = value * z2 + coefficient
    return value * z


def kernel(
    volt_hbm,
    aw_hbm,
    sw_hbm,
    ts_hbm,
    group_hbm,
    pos_hbm,
    dir_hbm,
    order_hbm,
    out_ref,
    volts,
    aw_ref,
    sw_ref,
    ts_ref,
    group_ref,
    pos_ref,
    dir_ref,
    order_ref,
    tied_ref,
    sum_ref,
    sems,
):
    channels, _, samples, antennas = volt_hbm.shape
    tiles = sw_ref.shape[2]
    stations = tiles // TPS
    groups = channels // CB
    rows_c = 2 * samples
    beams = order_ref.shape[1]
    lanes = CB * 2 * stations
    scale = 1.0 / math.sqrt(group_ref.shape[1])

    def start(source, target, k):
        copy = pltpu.make_async_copy(source, target, sems.at[k])
        copy.start()
        return copy

    small = [
        start(source, target, k)
        for k, (source, target) in enumerate(
            [
                (order_hbm, order_ref),
                (dir_hbm, dir_ref),
                (pos_hbm, pos_ref),
                (group_hbm, group_ref),
                (ts_hbm, ts_ref),
                (sw_hbm, sw_ref),
                (aw_hbm, aw_ref),
            ]
        )
    ]
    large = []
    for k in range(2 * groups):
        part = pl.ds(k * CB // 2, CB // 2)
        large.append(start(volt_hbm.at[part], volts.at[part], len(small) + k))
    antenna_tile = iota((antennas, tiles), 0) // TILE_ANTENNAS == iota((antennas, tiles), 1)
    sum_ref[...] = antenna_tile.astype(jnp.bfloat16)
    for copy in small[:4]:
        copy.wait()

    east_s, north_s, group_s = station_rows(pos_ref, group_ref, stations, lanes)
    lane = iota((1, lanes), 1)
    channel_lane = lane // (2 * stations)
    quarter = 0.25 * ((lane // stations) % 2).astype(jnp.float32)
    first_chan = lax.axis_index("chan") * channels
    total_chans = channels * lax.axis_size("chan")
    block = min(64, beams)

    def tied_rows(first):
        east, north, group = beam_columns(order_ref, dir_ref, first, block)
        delay = east * east_s + north * north_s
        member = jnp.where(group == group_s, scale, 0.0)
        for g in range(groups):
            freq = 1.0 + (first_chan + g * CB + channel_lane).astype(jnp.float32) / total_chans
            wave = cos_turns(delay * freq - quarter)
            tied_ref[pl.ds(first, block), g * lanes : (g + 1) * lanes] = (wave * member).astype(
                jnp.bfloat16
            )

    if beams == block:
        tied_rows(0)
    else:

        def body(i, carry):
            tied_rows(pl.multiple_of(i * block, block))
            return carry

        lax.fori_loop(0, beams // block, body, 0)

    for copy in small[4:]:
        copy.wait()
    member_table = (iota((stations, tiles), 0) == ts_ref[...] % stations).astype(jnp.float32)
    own_channel = iota((lanes, CB * rows_c), 0) // (2 * stations) == iota(
        (lanes, CB * rows_c), 1
    ) // rows_c

    station_rows_of = []
    for g in range(groups):
        swt = sw_ref[g * CB : (g + 1) * CB].astype(jnp.float32)
        right = []
        for c in range(CB):
            re = swt[c, 0:1] * member_table
            im = swt[c, 1:2] * member_table
            right.append(jnp.concatenate([re, -im], axis=1))
            right.append(jnp.concatenate([im, re], axis=1))
        station_rows_of.append(jnp.concatenate(right, axis=0).astype(jnp.bfloat16))

    def tile_beams(g):
        products = []
        weights = aw_ref[g * CB : (g + 1) * CB].astype(jnp.float32)
        for c in range(CB):
            w_re = jnp.broadcast_to(weights[c, 0:1], (samples, antennas)).astype(jnp.bfloat16)
            w_im = jnp.broadcast_to(weights[c, 1:2], (samples, antennas)).astype(jnp.bfloat16)
            v_re, v_im = volts[g * CB + c, 0], volts[g * CB + c, 1]
            products.append(w_re * v_re - w_im * v_im)
            products.append(w_re * v_im + w_im * v_re)
        return jnp.dot(
            jnp.concatenate(products, axis=0), sum_ref[...], preferred_element_type=jnp.float32
        ).astype(jnp.bfloat16)

    def tied_beams(g, beams_tile):
        left = []
        for c in range(CB):
            tile_re = beams_tile[c * rows_c : c * rows_c + samples]
            tile_im = beams_tile[c * rows_c + samples : (c + 1) * rows_c]
            left.append(jnp.concatenate([tile_re, tile_im], axis=1))
            left.append(jnp.concatenate([tile_im, -tile_re], axis=1))
        station = dot_nt(station_rows_of[g], jnp.concatenate(left, axis=0))
        station = jnp.where(own_channel, station, 0.0).astype(jnp.bfloat16)
        tied = jnp.dot(
            tied_ref[:, g * lanes : (g + 1) * lanes], station, preferred_element_type=jnp.float32
        )
        devices, rows, _ = out_ref.shape
        out_ref[:, :, g * CB * rows_c : (g + 1) * CB * rows_c] = tied.astype(jnp.bfloat16).reshape(
            devices, rows, CB * rows_c
        )

    last = None
    for g in range(groups):
        large[2 * g].wait()
        large[2 * g + 1].wait()
        now = tile_beams(g)
        if last is not None:
            tied_beams(g - 1, last)
        last = now
    tied_beams(groups - 1, last)


def last_kernel(parts_ref, out_ref):
    n_stn, n_chan = lax.axis_size("stn"), lax.axis_size("chan")
    own_beams, rows_c, total_chans = out_ref.shape
    channels = total_chans // n_chan
    width = channels * rows_c
    parts = parts_ref[...].astype(jnp.float32).reshape(n_stn, n_chan, own_beams, width)
    tied = jnp.sum(parts, axis=0)
    diagonal = iota((channels, width), 0) == iota((channels, width), 1) // rows_c
    spread = (iota((rows_c, width), 0) == iota((rows_c, width), 1) % rows_c).astype(jnp.bfloat16)
    for b in range(own_beams):
        rows = [jnp.where(diagonal, tied[chan, b : b + 1], 0.0) for chan in range(n_chan)]
        rows = jnp.concatenate(rows, axis=0).astype(jnp.bfloat16)
        out_ref[b] = dot_nt(spread, rows).astype(jnp.bfloat16)


def shards(
    volts,
    antenna_tile_weights,
    station_weights,
    tile_station,
    station_group,
    station_pos,
    beam_dir,
    beam_order,
):
    channels, _, samples, _ = volts.shape
    beams = beam_order.shape[0]
    n_stn, n_chan = lax.axis_size("stn"), lax.axis_size("chan")
    rows = beams // (n_stn * n_chan)
    width = channels * 2 * samples
    operands = (
        volts,
        antenna_tile_weights,
        station_weights,
        tile_station[None, :],
        station_group[None, :],
        station_pos.T,
        beam_dir.T,
        beam_order[None, :],
    )
    operands = [pltpu.with_memory_space_constraint(x, pltpu.HBM) for x in operands]
    groups = channels // CB
    partial = pl.pallas_call(
        kernel,
        out_shape=pltpu.VMEM((n_stn * n_chan, rows, width), jnp.bfloat16),
        in_specs=[pl.BlockSpec(memory_space=pltpu.HBM)] * len(operands),
        out_specs=pl.BlockSpec(memory_space=pltpu.VMEM),
        scratch_shapes=[pltpu.VMEM(x.shape, x.dtype) for x in operands]
        + [
            pltpu.VMEM((beams, channels * 2 * (station_weights.shape[2] // TPS)), jnp.bfloat16),
            pltpu.VMEM((volts.shape[3], station_weights.shape[2]), jnp.bfloat16),
            pltpu.SemaphoreType.DMA((len(operands) - 1 + 2 * groups,)),
        ],
        compiler_params=pltpu.CompilerParams(vmem_limit_bytes=24 * 2**20),
        name="partial_tied",
    )(*operands)
    parts = lax.all_to_all(partial, ("stn", "chan"), split_axis=0, concat_axis=0, tiled=True)
    vmem = pl.BlockSpec(memory_space=pltpu.VMEM)
    tied = pl.pallas_call(
        last_kernel,
        out_shape=jax.ShapeDtypeStruct((rows, 2 * samples, n_chan * channels), jnp.bfloat16),
        in_specs=[vmem],
        out_specs=vmem,
        compiler_params=pltpu.CompilerParams(vmem_limit_bytes=16 * 2**20),
        name="tied_beams",
    )(parts)
    return tied.transpose(0, 2, 1)


def solution(mesh):
    in_specs = (
        P("chan", None, None, "stn"),
        P("chan", None, "stn"),
        P("chan", None, "stn"),
        P("stn"),
        P(),
        P(),
        P(),
        P(),
    )
    out_specs = P(("stn", "chan"), None, None)
    return jax.shard_map(shards, mesh=mesh, in_specs=in_specs, out_specs=out_specs, check_vma=False)
```

```python
import functools
import math

import jax
import jax.numpy as jnp
from jax import lax
from jax.experimental import pallas as pl
from jax.experimental.pallas import tpu as pltpu
from jax.sharding import PartitionSpec as P

TILE_ANTENNAS = 16
TPS = 16
GROUPS = 4
CB = 8
NT = (((1,), (1,)), ((), ()))
SIN = [(-1) ** i * (2 * math.pi) ** (2 * i + 1) / math.factorial(2 * i + 1) for i in range(7)]


def dot_nt(a, b):
    return lax.dot_general(a, b, NT, preferred_element_type=jnp.float32)


def iota(shape, dim):
    return lax.broadcasted_iota(jnp.int32, shape, dim)


def beam_columns(order_ref, dir_ref, start, rows):
    beams = order_ref.shape[1]
    order = order_ref[...].astype(jnp.float32)
    lane = iota((rows, beams), 1)
    own = lane == iota((rows, beams), 0) + start
    ids = jnp.sum(jnp.where(own, order, 0.0), axis=1, keepdims=True)
    pick = lane.astype(jnp.float32) == ids
    east = jnp.sum(jnp.where(pick, dir_ref[0:1, :], 0.0), axis=1, keepdims=True)
    north = jnp.sum(jnp.where(pick, dir_ref[1:2, :], 0.0), axis=1, keepdims=True)
    group = ids - GROUPS * jnp.floor(ids * (1.0 / GROUPS))
    return east, north, group


def station_rows(pos_ref, group_ref, stations, lanes):
    total = group_ref.shape[1]
    first = lax.axis_index("stn") * stations
    own = iota((stations, total), 1) == iota((stations, total), 0) + first
    spread = iota((stations, lanes), 0) == iota((stations, lanes), 1) % stations

    def turn(row):
        column = jnp.sum(jnp.where(own, row, 0.0), axis=1, keepdims=True)
        return jnp.sum(jnp.where(spread, column, 0.0), axis=0, keepdims=True)

    return turn(pos_ref[0:1, :]), turn(pos_ref[1:2, :]), turn(group_ref[...].astype(jnp.float32))


def cos_turns(t):
    y = t - jnp.floor(t + 0.5)
    z = 0.25 - jnp.abs(y)
    z2 = z * z
    value = jnp.full_like(z, SIN[-1])
    for coefficient in SIN[-2::-1]:
        value = value * z2 + coefficient
    return value * z


def kernel(
    volt_hbm,
    aw_hbm,
    sw_hbm,
    ts_hbm,
    group_hbm,
    pos_hbm,
    dir_hbm,
    order_hbm,
    out_ref,
    volts,
    aw_ref,
    sw_ref,
    ts_ref,
    group_ref,
    pos_ref,
    dir_ref,
    order_ref,
    tied_ref,
    sum_ref,
    sems,
):
    channels, _, samples, antennas = volt_hbm.shape
    tiles = sw_ref.shape[2]
    stations = tiles // TPS
    groups = channels // CB
    rows_c = 2 * samples
    beams = order_ref.shape[1]
    lanes = CB * 2 * stations
    scale = 1.0 / math.sqrt(group_ref.shape[1])

    def start(source, target, k):
        copy = pltpu.make_async_copy(source, target, sems.at[k])
        copy.start()
        return copy

    small = [
        start(source, target, k)
        for k, (source, target) in enumerate(
            [
                (order_hbm, order_ref),
                (dir_hbm, dir_ref),
                (pos_hbm, pos_ref),
                (group_hbm, group_ref),
                (ts_hbm, ts_ref),
                (sw_hbm, sw_ref),
                (aw_hbm, aw_ref),
            ]
        )
    ]
    large = []
    for k in range(2 * groups):
        part = pl.ds(k * CB // 2, CB // 2)
        large.append(start(volt_hbm.at[part], volts.at[part], len(small) + k))
    antenna_tile = iota((antennas, tiles), 0) // TILE_ANTENNAS == iota((antennas, tiles), 1)
    sum_ref[...] = antenna_tile.astype(jnp.bfloat16)
    for copy in small + large[:2]:
        copy.wait()

    def tile_beams(g):
        products = []
        weights = aw_ref[g * CB : (g + 1) * CB].astype(jnp.float32)
        for c in range(CB):
            w_re = jnp.broadcast_to(weights[c, 0:1], (samples, antennas)).astype(jnp.bfloat16)
            w_im = jnp.broadcast_to(weights[c, 1:2], (samples, antennas)).astype(jnp.bfloat16)
            v_re, v_im = volts[g * CB + c, 0], volts[g * CB + c, 1]
            products.append(w_re * v_re - w_im * v_im)
            products.append(w_re * v_im + w_im * v_re)
        return jnp.dot(
            jnp.concatenate(products, axis=0), sum_ref[...], preferred_element_type=jnp.float32
        ).astype(jnp.bfloat16)

    last = tile_beams(0)

    east_s, north_s, group_s = station_rows(pos_ref, group_ref, stations, lanes)
    lane = iota((1, lanes), 1)
    channel_lane = lane // (2 * stations)
    quarter = 0.25 * ((lane // stations) % 2).astype(jnp.float32)
    first_chan = lax.axis_index("chan") * channels
    total_chans = channels * lax.axis_size("chan")
    block = min(64, beams)

    def tied_rows(first):
        east, north, group = beam_columns(order_ref, dir_ref, first, block)
        delay = east * east_s + north * north_s
        member = jnp.where(group == group_s, scale, 0.0)
        for g in range(groups):
            freq = 1.0 + (first_chan + g * CB + channel_lane).astype(jnp.float32) / total_chans
            wave = cos_turns(delay * freq - quarter)
            tied_ref[pl.ds(first, block), g * lanes : (g + 1) * lanes] = (wave * member).astype(
                jnp.bfloat16
            )

    if beams == block:
        tied_rows(0)
    else:

        def body(i, carry):
            tied_rows(pl.multiple_of(i * block, block))
            return carry

        lax.fori_loop(0, beams // block, body, 0)

    member_table = (iota((stations, tiles), 0) == ts_ref[...] % stations).astype(jnp.float32)
    own_channel = iota((lanes, CB * rows_c), 0) // (2 * stations) == iota(
        (lanes, CB * rows_c), 1
    ) // rows_c

    station_rows_of = []
    for g in range(groups):
        swt = sw_ref[g * CB : (g + 1) * CB].astype(jnp.float32)
        right = []
        for c in range(CB):
            re = swt[c, 0:1] * member_table
            im = swt[c, 1:2] * member_table
            right.append(jnp.concatenate([re, -im], axis=1))
            right.append(jnp.concatenate([im, re], axis=1))
        station_rows_of.append(jnp.concatenate(right, axis=0).astype(jnp.bfloat16))

    def tied_beams(g, beams_tile):
        left = []
        for c in range(CB):
            tile_re = beams_tile[c * rows_c : c * rows_c + samples]
            tile_im = beams_tile[c * rows_c + samples : (c + 1) * rows_c]
            left.append(jnp.concatenate([tile_re, tile_im], axis=1))
            left.append(jnp.concatenate([tile_im, -tile_re], axis=1))
        station = dot_nt(station_rows_of[g], jnp.concatenate(left, axis=0))
        station = jnp.where(own_channel, station, 0.0).astype(jnp.bfloat16)
        tied = jnp.dot(
            tied_ref[:, g * lanes : (g + 1) * lanes], station, preferred_element_type=jnp.float32
        )
        devices, rows, _ = out_ref.shape
        out_ref[:, :, g * CB * rows_c : (g + 1) * CB * rows_c] = tied.astype(jnp.bfloat16).reshape(
            devices, rows, CB * rows_c
        )

    for g in range(1, groups):
        large[2 * g].wait()
        large[2 * g + 1].wait()
        now = tile_beams(g)
        tied_beams(g - 1, last)
        last = now
    tied_beams(groups - 1, last)


def last_kernel(parts_ref, out_ref):
    n_stn, n_chan = lax.axis_size("stn"), lax.axis_size("chan")
    own_beams, rows_c, total_chans = out_ref.shape
    channels = total_chans // n_chan
    width = channels * rows_c
    parts = parts_ref[...].astype(jnp.float32).reshape(n_stn, n_chan, own_beams, width)
    tied = jnp.sum(parts, axis=0)
    diagonal = iota((channels, width), 0) == iota((channels, width), 1) // rows_c
    spread = (iota((rows_c, width), 0) == iota((rows_c, width), 1) % rows_c).astype(jnp.bfloat16)
    for b in range(own_beams):
        rows = [jnp.where(diagonal, tied[chan, b : b + 1], 0.0) for chan in range(n_chan)]
        rows = jnp.concatenate(rows, axis=0).astype(jnp.bfloat16)
        out_ref[b] = dot_nt(spread, rows).astype(jnp.bfloat16)


def shards(
    volts,
    antenna_tile_weights,
    station_weights,
    tile_station,
    station_group,
    station_pos,
    beam_dir,
    beam_order,
):
    channels, _, samples, _ = volts.shape
    beams = beam_order.shape[0]
    n_stn, n_chan = lax.axis_size("stn"), lax.axis_size("chan")
    rows = beams // (n_stn * n_chan)
    width = channels * 2 * samples
    operands = (
        volts,
        antenna_tile_weights,
        station_weights,
        tile_station[None, :],
        station_group[None, :],
        station_pos.T,
        beam_dir.T,
        beam_order[None, :],
    )
    operands = [pltpu.with_memory_space_constraint(x, pltpu.HBM) for x in operands]
    groups = channels // CB
    partial = pl.pallas_call(
        kernel,
        out_shape=pltpu.VMEM((n_stn * n_chan, rows, width), jnp.bfloat16),
        in_specs=[pl.BlockSpec(memory_space=pltpu.HBM)] * len(operands),
        out_specs=pl.BlockSpec(memory_space=pltpu.VMEM),
        scratch_shapes=[pltpu.VMEM(x.shape, x.dtype) for x in operands]
        + [
            pltpu.VMEM((beams, channels * 2 * (station_weights.shape[2] // TPS)), jnp.bfloat16),
            pltpu.VMEM((volts.shape[3], station_weights.shape[2]), jnp.bfloat16),
            pltpu.SemaphoreType.DMA((len(operands) - 1 + 2 * groups,)),
        ],
        compiler_params=pltpu.CompilerParams(vmem_limit_bytes=24 * 2**20),
        name="partial_tied",
    )(*operands)
    parts = lax.all_to_all(partial, ("stn", "chan"), split_axis=0, concat_axis=0, tiled=True)
    vmem = pl.BlockSpec(memory_space=pltpu.VMEM)
    tied = pl.pallas_call(
        last_kernel,
        out_shape=jax.ShapeDtypeStruct((rows, 2 * samples, n_chan * channels), jnp.bfloat16),
        in_specs=[vmem],
        out_specs=vmem,
        compiler_params=pltpu.CompilerParams(vmem_limit_bytes=16 * 2**20),
        name="tied_beams",
    )(parts)
    return tied.transpose(0, 2, 1)


def solution(mesh):
    in_specs = (
        P("chan", None, None, "stn"),
        P("chan", None, "stn"),
        P("chan", None, "stn"),
        P("stn"),
        P(),
        P(),
        P(),
        P(),
    )
    out_specs = P(("stn", "chan"), None, None)
    return jax.shard_map(shards, mesh=mesh, in_specs=in_specs, out_specs=out_specs, check_vma=False)
```

```python
import functools
import math

import jax
import jax.numpy as jnp
from jax import lax
from jax.experimental import pallas as pl
from jax.experimental.pallas import tpu as pltpu
from jax.sharding import PartitionSpec as P

TILE_ANTENNAS = 16
TPS = 16
GROUPS = 4
CB = 8
NT = (((1,), (1,)), ((), ()))
SIN = [(-1) ** i * (2 * math.pi) ** (2 * i + 1) / math.factorial(2 * i + 1) for i in range(7)]


def dot_nt(a, b):
    return lax.dot_general(a, b, NT, preferred_element_type=jnp.float32)


def iota(shape, dim):
    return lax.broadcasted_iota(jnp.int32, shape, dim)


def beam_columns(order_ref, dir_ref, start, rows):
    beams = order_ref.shape[1]
    each = beams // (lax.axis_size("stn") * lax.axis_size("chan"))
    order = order_ref[...].astype(jnp.float32)
    lane = iota((rows, beams), 1)
    slot = iota((rows, beams), 0) + start
    own = lane == beams - each - slot // each * each + slot % each
    ids = jnp.sum(jnp.where(own, order, 0.0), axis=1, keepdims=True)
    pick = lane.astype(jnp.float32) == ids
    east = jnp.sum(jnp.where(pick, dir_ref[0:1, :], 0.0), axis=1, keepdims=True)
    north = jnp.sum(jnp.where(pick, dir_ref[1:2, :], 0.0), axis=1, keepdims=True)
    group = ids - GROUPS * jnp.floor(ids * (1.0 / GROUPS))
    return east, north, group


def station_rows(pos_ref, group_ref, stations, lanes):
    total = group_ref.shape[1]
    first = lax.axis_index("stn") * stations
    own = iota((stations, total), 1) == iota((stations, total), 0) + first
    spread = iota((stations, lanes), 0) == iota((stations, lanes), 1) % stations

    def turn(row):
        column = jnp.sum(jnp.where(own, row, 0.0), axis=1, keepdims=True)
        return jnp.sum(jnp.where(spread, column, 0.0), axis=0, keepdims=True)

    return turn(pos_ref[0:1, :]), turn(pos_ref[1:2, :]), turn(group_ref[...].astype(jnp.float32))


def cos_turns(t):
    y = t - jnp.floor(t + 0.5)
    z = 0.25 - jnp.abs(y)
    z2 = z * z
    value = jnp.full_like(z, SIN[-1])
    for coefficient in SIN[-2::-1]:
        value = value * z2 + coefficient
    return value * z


def kernel(
    volt_hbm,
    aw_hbm,
    sw_hbm,
    ts_hbm,
    group_hbm,
    pos_hbm,
    dir_hbm,
    order_hbm,
    out_ref,
    volts,
    aw_ref,
    sw_ref,
    ts_ref,
    group_ref,
    pos_ref,
    dir_ref,
    order_ref,
    tied_ref,
    sum_ref,
    sems,
):
    channels, _, samples, antennas = volt_hbm.shape
    tiles = sw_ref.shape[2]
    stations = tiles // TPS
    groups = channels // CB
    rows_c = 2 * samples
    beams = order_ref.shape[1]
    lanes = CB * 2 * stations
    scale = 1.0 / math.sqrt(group_ref.shape[1])

    def start(source, target, k):
        copy = pltpu.make_async_copy(source, target, sems.at[k])
        copy.start()
        return copy

    small = [
        start(source, target, k)
        for k, (source, target) in enumerate(
            [
                (order_hbm, order_ref),
                (dir_hbm, dir_ref),
                (pos_hbm, pos_ref),
                (group_hbm, group_ref),
                (ts_hbm, ts_ref),
                (sw_hbm, sw_ref),
                (aw_hbm, aw_ref),
            ]
        )
    ]
    large = []
    for k in range(2 * groups):
        part = pl.ds(k * CB // 2, CB // 2)
        large.append(start(volt_hbm.at[part], volts.at[part], len(small) + k))
    antenna_tile = iota((antennas, tiles), 0) // TILE_ANTENNAS == iota((antennas, tiles), 1)
    sum_ref[...] = antenna_tile.astype(jnp.bfloat16)
    for copy in small[:4]:
        copy.wait()

    east_s, north_s, group_s = station_rows(pos_ref, group_ref, stations, lanes)
    lane = iota((1, lanes), 1)
    channel_lane = lane // (2 * stations)
    quarter = 0.25 * ((lane // stations) % 2).astype(jnp.float32)
    first_chan = lax.axis_index("chan") * channels
    total_chans = channels * lax.axis_size("chan")
    block = min(64, beams)

    def tied_rows(first):
        east, north, group = beam_columns(order_ref, dir_ref, first, block)
        delay = east * east_s + north * north_s
        member = jnp.where(group == group_s, scale, 0.0)
        for g in range(groups):
            freq = 1.0 + (first_chan + g * CB + channel_lane).astype(jnp.float32) / total_chans
            wave = cos_turns(delay * freq - quarter)
            tied_ref[pl.ds(first, block), g * lanes : (g + 1) * lanes] = (wave * member).astype(
                jnp.bfloat16
            )

    if beams == block:
        tied_rows(0)
    else:

        def body(i, carry):
            tied_rows(pl.multiple_of(i * block, block))
            return carry

        lax.fori_loop(0, beams // block, body, 0)

    for copy in small[4:]:
        copy.wait()
    member_table = (iota((stations, tiles), 0) == ts_ref[...] % stations).astype(jnp.float32)
    own_channel = iota((lanes, CB * rows_c), 0) // (2 * stations) == iota(
        (lanes, CB * rows_c), 1
    ) // rows_c

    station_rows_of = []
    for g in range(groups):
        swt = sw_ref[g * CB : (g + 1) * CB].astype(jnp.float32)
        right = []
        for c in range(CB):
            re = swt[c, 0:1] * member_table
            im = swt[c, 1:2] * member_table
            right.append(jnp.concatenate([re, -im], axis=1))
            right.append(jnp.concatenate([im, re], axis=1))
        station_rows_of.append(jnp.concatenate(right, axis=0).astype(jnp.bfloat16))

    def tile_beams(g):
        products = []
        weights = aw_ref[g * CB : (g + 1) * CB].astype(jnp.float32)
        for c in range(CB):
            w_re = jnp.broadcast_to(weights[c, 0:1], (samples, antennas)).astype(jnp.bfloat16)
            w_im = jnp.broadcast_to(weights[c, 1:2], (samples, antennas)).astype(jnp.bfloat16)
            v_re, v_im = volts[g * CB + c, 0], volts[g * CB + c, 1]
            products.append(w_re * v_re - w_im * v_im)
            products.append(w_re * v_im + w_im * v_re)
        return jnp.dot(
            jnp.concatenate(products, axis=0), sum_ref[...], preferred_element_type=jnp.float32
        ).astype(jnp.bfloat16)

    def tied_beams(g, beams_tile):
        left = []
        for c in range(CB):
            tile_re = beams_tile[c * rows_c : c * rows_c + samples]
            tile_im = beams_tile[c * rows_c + samples : (c + 1) * rows_c]
            left.append(jnp.concatenate([tile_re, tile_im], axis=1))
            left.append(jnp.concatenate([tile_im, -tile_re], axis=1))
        station = dot_nt(station_rows_of[g], jnp.concatenate(left, axis=0))
        station = jnp.where(own_channel, station, 0.0).astype(jnp.bfloat16)
        tied = jnp.dot(
            tied_ref[:, g * lanes : (g + 1) * lanes], station, preferred_element_type=jnp.float32
        )
        devices, rows, _ = out_ref.shape
        out_ref[:, :, g * CB * rows_c : (g + 1) * CB * rows_c] = tied.astype(jnp.bfloat16).reshape(
            devices, rows, CB * rows_c
        )

    last = None
    for g in range(groups):
        large[2 * g].wait()
        large[2 * g + 1].wait()
        now = tile_beams(g)
        if last is not None:
            tied_beams(g - 1, last)
        last = now
    tied_beams(groups - 1, last)


def last_kernel(parts_ref, out_ref):
    n_stn, n_chan = lax.axis_size("stn"), lax.axis_size("chan")
    own_beams, rows_c, total_chans = out_ref.shape
    channels = total_chans // n_chan
    width = channels * rows_c
    parts = parts_ref[...].astype(jnp.float32).reshape(n_stn, n_chan, own_beams, width)
    tied = jnp.sum(parts, axis=0)
    diagonal = iota((channels, width), 0) == iota((channels, width), 1) // rows_c
    spread = (iota((rows_c, width), 0) == iota((rows_c, width), 1) % rows_c).astype(jnp.bfloat16)
    for b in range(own_beams):
        rows = [jnp.where(diagonal, tied[chan, b : b + 1], 0.0) for chan in reversed(range(n_chan))]
        rows = jnp.concatenate(rows, axis=0).astype(jnp.bfloat16)
        out_ref[b] = dot_nt(spread, rows).astype(jnp.bfloat16)


def shards(
    volts,
    antenna_tile_weights,
    station_weights,
    tile_station,
    station_group,
    station_pos,
    beam_dir,
    beam_order,
):
    channels, _, samples, _ = volts.shape
    beams = beam_order.shape[0]
    n_stn, n_chan = lax.axis_size("stn"), lax.axis_size("chan")
    rows = beams // (n_stn * n_chan)
    width = channels * 2 * samples
    operands = (
        volts,
        antenna_tile_weights,
        station_weights,
        tile_station[None, :],
        station_group[None, :],
        station_pos.T,
        beam_dir.T,
        beam_order[None, :],
    )
    operands = [pltpu.with_memory_space_constraint(x, pltpu.HBM) for x in operands]
    groups = channels // CB
    partial = pl.pallas_call(
        kernel,
        out_shape=pltpu.VMEM((n_stn * n_chan, rows, width), jnp.bfloat16),
        in_specs=[pl.BlockSpec(memory_space=pltpu.HBM)] * len(operands),
        out_specs=pl.BlockSpec(memory_space=pltpu.VMEM),
        scratch_shapes=[pltpu.VMEM(x.shape, x.dtype) for x in operands]
        + [
            pltpu.VMEM((beams, channels * 2 * (station_weights.shape[2] // TPS)), jnp.bfloat16),
            pltpu.VMEM((volts.shape[3], station_weights.shape[2]), jnp.bfloat16),
            pltpu.SemaphoreType.DMA((len(operands) - 1 + 2 * groups,)),
        ],
        compiler_params=pltpu.CompilerParams(vmem_limit_bytes=24 * 2**20),
        name="partial_tied",
    )(*operands)
    parts = lax.all_to_all(
        partial,
        ("stn", "chan"),
        split_axis=0,
        concat_axis=0,
        axis_index_groups=[list(reversed(range(n_stn * n_chan)))],
        tiled=True,
    )
    vmem = pl.BlockSpec(memory_space=pltpu.VMEM)
    tied = pl.pallas_call(
        last_kernel,
        out_shape=jax.ShapeDtypeStruct((rows, 2 * samples, n_chan * channels), jnp.bfloat16),
        in_specs=[vmem],
        out_specs=vmem,
        compiler_params=pltpu.CompilerParams(vmem_limit_bytes=16 * 2**20),
        name="tied_beams",
    )(parts)
    return tied.transpose(0, 2, 1)


def solution(mesh):
    in_specs = (
        P("chan", None, None, "stn"),
        P("chan", None, "stn"),
        P("chan", None, "stn"),
        P("stn"),
        P(),
        P(),
        P(),
        P(),
    )
    out_specs = P(("stn", "chan"), None, None)
    return jax.shard_map(shards, mesh=mesh, in_specs=in_specs, out_specs=out_specs, check_vma=False)
```

```python
import functools
import math

import jax
import jax.numpy as jnp
from jax import lax
from jax.experimental import pallas as pl
from jax.experimental.pallas import tpu as pltpu
from jax.sharding import PartitionSpec as P

TILE_ANTENNAS = 16
TPS = 16
GROUPS = 4
CB = 8
TB = 4
COPY = 2
NT = (((1,), (1,)), ((), ()))
SIN = [(-1) ** i * (2 * math.pi) ** (2 * i + 1) / math.factorial(2 * i + 1) for i in range(7)]


def dot_nt(a, b):
    return lax.dot_general(a, b, NT, preferred_element_type=jnp.float32)


def iota(shape, dim):
    return lax.broadcasted_iota(jnp.int32, shape, dim)


def beam_columns(order_ref, dir_ref, start, rows):
    beams = order_ref.shape[1]
    each = beams // (lax.axis_size("stn") * lax.axis_size("chan"))
    order = order_ref[...].astype(jnp.float32)
    lane = iota((rows, beams), 1)
    slot = iota((rows, beams), 0) + start
    own = lane == beams - each - slot // each * each + slot % each
    ids = jnp.sum(jnp.where(own, order, 0.0), axis=1, keepdims=True)
    pick = lane.astype(jnp.float32) == ids
    east = jnp.sum(jnp.where(pick, dir_ref[0:1, :], 0.0), axis=1, keepdims=True)
    north = jnp.sum(jnp.where(pick, dir_ref[1:2, :], 0.0), axis=1, keepdims=True)
    group = ids - GROUPS * jnp.floor(ids * (1.0 / GROUPS))
    return east, north, group


def station_rows(pos_ref, group_ref, stations, lanes):
    total = group_ref.shape[1]
    first = lax.axis_index("stn") * stations
    own = iota((stations, total), 1) == iota((stations, total), 0) + first
    spread = iota((stations, lanes), 0) == iota((stations, lanes), 1) % stations

    def turn(row):
        column = jnp.sum(jnp.where(own, row, 0.0), axis=1, keepdims=True)
        return jnp.sum(jnp.where(spread, column, 0.0), axis=0, keepdims=True)

    return turn(pos_ref[0:1, :]), turn(pos_ref[1:2, :]), turn(group_ref[...].astype(jnp.float32))


def cos_turns(t):
    y = t - jnp.floor(t + 0.5)
    z = 0.25 - jnp.abs(y)
    z2 = z * z
    value = jnp.full_like(z, SIN[-1])
    for coefficient in SIN[-2::-1]:
        value = value * z2 + coefficient
    return value * z


def kernel(
    volt_hbm,
    aw_hbm,
    sw_hbm,
    ts_hbm,
    group_hbm,
    pos_hbm,
    dir_hbm,
    order_hbm,
    out_ref,
    volts,
    aw_ref,
    sw_ref,
    ts_ref,
    group_ref,
    pos_ref,
    dir_ref,
    order_ref,
    tied_ref,
    sum_ref,
    sems,
):
    channels, _, samples, antennas = volt_hbm.shape
    tiles = sw_ref.shape[2]
    stations = tiles // TPS
    groups = channels // CB
    rows_c = 2 * samples
    beams = order_ref.shape[1]
    lanes = CB * 2 * stations
    scale = 1.0 / math.sqrt(group_ref.shape[1])

    def start(source, target, k):
        copy = pltpu.make_async_copy(source, target, sems.at[k])
        copy.start()
        return copy

    small = [
        start(source, target, k)
        for k, (source, target) in enumerate(
            [
                (order_hbm, order_ref),
                (dir_hbm, dir_ref),
                (pos_hbm, pos_ref),
                (group_hbm, group_ref),
                (ts_hbm, ts_ref),
                (sw_hbm, sw_ref),
                (aw_hbm, aw_ref),
            ]
        )
    ]
    large = []
    for k in range(channels // COPY):
        part = pl.ds(k * COPY, COPY)
        large.append(start(volt_hbm.at[part], volts.at[part], len(small) + k))
    antenna_tile = iota((antennas, tiles), 0) // TILE_ANTENNAS == iota((antennas, tiles), 1)
    sum_ref[...] = antenna_tile.astype(jnp.bfloat16)
    for copy in small[:4]:
        copy.wait()

    east_s, north_s, group_s = station_rows(pos_ref, group_ref, stations, lanes)
    lane = iota((1, lanes), 1)
    channel_lane = lane // (2 * stations)
    quarter = 0.25 * ((lane // stations) % 2).astype(jnp.float32)
    first_chan = lax.axis_index("chan") * channels
    total_chans = channels * lax.axis_size("chan")
    block = min(64, beams)

    def tied_rows(first):
        east, north, group = beam_columns(order_ref, dir_ref, first, block)
        delay = east * east_s + north * north_s
        member = jnp.where(group == group_s, scale, 0.0)
        for g in range(groups):
            freq = 1.0 + (first_chan + g * CB + channel_lane).astype(jnp.float32) / total_chans
            wave = cos_turns(delay * freq - quarter)
            tied_ref[pl.ds(first, block), g * lanes : (g + 1) * lanes] = (wave * member).astype(
                jnp.bfloat16
            )

    if beams == block:
        tied_rows(0)
    else:

        def body(i, carry):
            tied_rows(pl.multiple_of(i * block, block))
            return carry

        lax.fori_loop(0, beams // block, body, 0)

    for copy in small[4:]:
        copy.wait()
    member_table = (iota((stations, tiles), 0) == ts_ref[...] % stations).astype(jnp.float32)
    own_channel = iota((CB * rows_c, lanes), 0) // rows_c == iota((CB * rows_c, lanes), 1) // (
        2 * stations
    )

    station_rows_of = []
    for g in range(groups):
        swt = sw_ref[g * CB : (g + 1) * CB].astype(jnp.float32)
        right = []
        for c in range(CB):
            re = swt[c, 0:1] * member_table
            im = swt[c, 1:2] * member_table
            right.append(jnp.concatenate([re, -im], axis=1))
            right.append(jnp.concatenate([im, re], axis=1))
        station_rows_of.append(jnp.concatenate(right, axis=0).T.astype(jnp.bfloat16))

    def tile_beams(k):
        products = []
        weights = aw_ref[k * TB : (k + 1) * TB].astype(jnp.float32)
        for c in range(TB):
            w_re = jnp.broadcast_to(weights[c, 0:1], (samples, antennas)).astype(jnp.bfloat16)
            w_im = jnp.broadcast_to(weights[c, 1:2], (samples, antennas)).astype(jnp.bfloat16)
            v_re, v_im = volts[k * TB + c, 0], volts[k * TB + c, 1]
            products.append(w_re * v_re - w_im * v_im)
            products.append(w_re * v_im + w_im * v_re)
        return jnp.dot(
            jnp.concatenate(products, axis=0), sum_ref[...], preferred_element_type=jnp.float32
        ).astype(jnp.bfloat16)

    def tied_beams(g, beams_tile):
        left = []
        for c in range(CB):
            tile_re = beams_tile[c * rows_c : c * rows_c + samples]
            tile_im = beams_tile[c * rows_c + samples : (c + 1) * rows_c]
            left.append(jnp.concatenate([tile_re, tile_im], axis=1))
            left.append(jnp.concatenate([tile_im, -tile_re], axis=1))
        station = jnp.dot(
            jnp.concatenate(left, axis=0),
            station_rows_of[g],
            preferred_element_type=jnp.float32,
        )
        station = jnp.where(own_channel, station, 0.0).astype(jnp.bfloat16)
        tied = dot_nt(tied_ref[:, g * lanes : (g + 1) * lanes], station)
        devices, rows, _ = out_ref.shape
        out_ref[:, :, g * CB * rows_c : (g + 1) * CB * rows_c] = tied.astype(jnp.bfloat16).reshape(
            devices, rows, CB * rows_c
        )

    found = []
    for k in range(channels // TB):
        for copy in large[k * TB // COPY : (k + 1) * TB // COPY]:
            copy.wait()
        found.append(tile_beams(k))
        g = k * TB // CB - 1
        if g >= 0 and k * TB % CB == 0:
            tied_beams(g, jnp.concatenate(found[g * CB // TB : (g + 1) * CB // TB], axis=0))
    tied_beams(groups - 1, jnp.concatenate(found[-CB // TB :], axis=0))


def last_kernel(parts_ref, out_ref):
    n_stn, n_chan = lax.axis_size("stn"), lax.axis_size("chan")
    own_beams, rows_c, total_chans = out_ref.shape
    channels = total_chans // n_chan
    width = channels * rows_c
    parts = parts_ref[...].astype(jnp.float32).reshape(n_stn, n_chan, own_beams, width)
    tied = jnp.sum(parts, axis=0)
    diagonal = iota((channels, width), 0) == iota((channels, width), 1) // rows_c
    spread = (iota((rows_c, width), 0) == iota((rows_c, width), 1) % rows_c).astype(jnp.bfloat16)
    for b in range(own_beams):
        rows = [jnp.where(diagonal, tied[chan, b : b + 1], 0.0) for chan in reversed(range(n_chan))]
        rows = jnp.concatenate(rows, axis=0).astype(jnp.bfloat16)
        out_ref[b] = dot_nt(spread, rows).astype(jnp.bfloat16)


def shards(
    volts,
    antenna_tile_weights,
    station_weights,
    tile_station,
    station_group,
    station_pos,
    beam_dir,
    beam_order,
):
    channels, _, samples, _ = volts.shape
    beams = beam_order.shape[0]
    n_stn, n_chan = lax.axis_size("stn"), lax.axis_size("chan")
    rows = beams // (n_stn * n_chan)
    width = channels * 2 * samples
    operands = (
        volts,
        antenna_tile_weights,
        station_weights,
        tile_station[None, :],
        station_group[None, :],
        station_pos.T,
        beam_dir.T,
        beam_order[None, :],
    )
    operands = [pltpu.with_memory_space_constraint(x, pltpu.HBM) for x in operands]
    partial = pl.pallas_call(
        kernel,
        out_shape=pltpu.VMEM((n_stn * n_chan, rows, width), jnp.bfloat16),
        in_specs=[pl.BlockSpec(memory_space=pltpu.HBM)] * len(operands),
        out_specs=pl.BlockSpec(memory_space=pltpu.VMEM),
        scratch_shapes=[pltpu.VMEM(x.shape, x.dtype) for x in operands]
        + [
            pltpu.VMEM((beams, channels * 2 * (station_weights.shape[2] // TPS)), jnp.bfloat16),
            pltpu.VMEM((volts.shape[3], station_weights.shape[2]), jnp.bfloat16),
            pltpu.SemaphoreType.DMA((len(operands) - 1 + channels // COPY,)),
        ],
        compiler_params=pltpu.CompilerParams(vmem_limit_bytes=24 * 2**20),
        name="partial_tied",
    )(*operands)
    parts = lax.all_to_all(
        partial,
        ("stn", "chan"),
        split_axis=0,
        concat_axis=0,
        axis_index_groups=[list(reversed(range(n_stn * n_chan)))],
        tiled=True,
    )
    vmem = pl.BlockSpec(memory_space=pltpu.VMEM)
    tied = pl.pallas_call(
        last_kernel,
        out_shape=jax.ShapeDtypeStruct((rows, 2 * samples, n_chan * channels), jnp.bfloat16),
        in_specs=[vmem],
        out_specs=vmem,
        compiler_params=pltpu.CompilerParams(vmem_limit_bytes=16 * 2**20),
        name="tied_beams",
    )(parts)
    return tied.transpose(0, 2, 1)


def solution(mesh):
    in_specs = (
        P("chan", None, None, "stn"),
        P("chan", None, "stn"),
        P("chan", None, "stn"),
        P("stn"),
        P(),
        P(),
        P(),
        P(),
    )
    out_specs = P(("stn", "chan"), None, None)
    return jax.shard_map(shards, mesh=mesh, in_specs=in_specs, out_specs=out_specs, check_vma=False)
```

```python
import functools
import math

import jax
import jax.numpy as jnp
from jax import lax
from jax.experimental import pallas as pl
from jax.experimental.pallas import tpu as pltpu
from jax.sharding import PartitionSpec as P

TILE_ANTENNAS = 16
TPS = 16
GROUPS = 4
CB = 8
STAGE = 512
NT = (((1,), (1,)), ((), ()))
SIN = [(-1) ** i * (2 * math.pi) ** (2 * i + 1) / math.factorial(2 * i + 1) for i in range(7)]


def dot_nt(a, b):
    return lax.dot_general(a, b, NT, preferred_element_type=jnp.float32)


def iota(shape, dim):
    return lax.broadcasted_iota(jnp.int32, shape, dim)


def beam_columns(order_ref, dir_ref, start, rows):
    beams = order_ref.shape[1]
    each = beams // (lax.axis_size("stn") * lax.axis_size("chan"))
    order = order_ref[...].astype(jnp.float32)
    lane = iota((rows, beams), 1)
    slot = iota((rows, beams), 0) + start
    own = lane == beams - each - slot // each * each + slot % each
    ids = jnp.sum(jnp.where(own, order, 0.0), axis=1, keepdims=True)
    pick = lane.astype(jnp.float32) == ids
    east = jnp.sum(jnp.where(pick, dir_ref[0:1, :], 0.0), axis=1, keepdims=True)
    north = jnp.sum(jnp.where(pick, dir_ref[1:2, :], 0.0), axis=1, keepdims=True)
    group = ids - GROUPS * jnp.floor(ids * (1.0 / GROUPS))
    return east, north, group


def station_rows(pos_ref, group_ref, stations, lanes):
    total = group_ref.shape[1]
    first = lax.axis_index("stn") * stations
    own = iota((stations, total), 1) == iota((stations, total), 0) + first
    spread = iota((stations, lanes), 0) == iota((stations, lanes), 1) % stations

    def turn(row):
        column = jnp.sum(jnp.where(own, row, 0.0), axis=1, keepdims=True)
        return jnp.sum(jnp.where(spread, column, 0.0), axis=0, keepdims=True)

    return turn(pos_ref[0:1, :]), turn(pos_ref[1:2, :]), turn(group_ref[...].astype(jnp.float32))


def cos_turns(t):
    y = t - jnp.floor(t + 0.5)
    z = 0.25 - jnp.abs(y)
    z2 = z * z
    value = jnp.full_like(z, SIN[-1])
    for coefficient in SIN[-2::-1]:
        value = value * z2 + coefficient
    return value * z


def kernel(
    volt_hbm,
    aw_hbm,
    sw_hbm,
    ts_hbm,
    group_hbm,
    pos_hbm,
    dir_hbm,
    order_hbm,
    out_ref,
    volts,
    aw_ref,
    sw_ref,
    ts_ref,
    group_ref,
    pos_ref,
    dir_ref,
    order_ref,
    tied_ref,
    sum_ref,
    tile_ref,
    sems,
):
    channels, _, samples, antennas = volt_hbm.shape
    tiles = sw_ref.shape[2]
    stations = tiles // TPS
    groups = channels // CB
    rows_c = 2 * samples
    beams = order_ref.shape[1]
    lanes = CB * 2 * stations
    scale = 1.0 / math.sqrt(group_ref.shape[1])

    def start(source, target, k):
        copy = pltpu.make_async_copy(source, target, sems.at[k])
        copy.start()
        return copy

    small = [
        start(source, target, k)
        for k, (source, target) in enumerate(
            [
                (order_hbm, order_ref),
                (dir_hbm, dir_ref),
                (pos_hbm, pos_ref),
                (group_hbm, group_ref),
                (ts_hbm, ts_ref),
                (sw_hbm, sw_ref),
                (aw_hbm, aw_ref),
            ]
        )
    ]
    large = []
    stage_slices = [slice(k, k + STAGE) for k in range(0, antennas, STAGE)]
    for k, part in enumerate(stage_slices):
        source, target = volt_hbm.at[:, :, :, part], volts.at[:, :, :, part]
        large.append(start(source, target, len(small) + k))
    antenna_tile = iota((antennas, tiles), 0) // TILE_ANTENNAS == iota((antennas, tiles), 1)
    sum_ref[...] = antenna_tile.astype(jnp.bfloat16)
    for copy in small[:4]:
        copy.wait()

    east_s, north_s, group_s = station_rows(pos_ref, group_ref, stations, lanes)
    lane = iota((1, lanes), 1)
    channel_lane = lane // (2 * stations)
    quarter = 0.25 * ((lane // stations) % 2).astype(jnp.float32)
    first_chan = lax.axis_index("chan") * channels
    total_chans = channels * lax.axis_size("chan")
    block = min(64, beams)

    def tied_rows(first):
        east, north, group = beam_columns(order_ref, dir_ref, first, block)
        delay = east * east_s + north * north_s
        member = jnp.where(group == group_s, scale, 0.0)
        for g in range(groups):
            freq = 1.0 + (first_chan + g * CB + channel_lane).astype(jnp.float32) / total_chans
            wave = cos_turns(delay * freq - quarter)
            tied_ref[pl.ds(first, block), g * lanes : (g + 1) * lanes] = (wave * member).astype(
                jnp.bfloat16
            )

    if beams == block:
        tied_rows(0)
    else:

        def body(i, carry):
            tied_rows(pl.multiple_of(i * block, block))
            return carry

        lax.fori_loop(0, beams // block, body, 0)

    for copy in small[4:]:
        copy.wait()
    member_table = (iota((stations, tiles), 0) == ts_ref[...] % stations).astype(jnp.float32)
    own_channel = iota((lanes, CB * rows_c), 0) // (2 * stations) == iota(
        (lanes, CB * rows_c), 1
    ) // rows_c

    station_rows_of = []
    for g in range(groups):
        swt = sw_ref[g * CB : (g + 1) * CB].astype(jnp.float32)
        right = []
        for c in range(CB):
            re = swt[c, 0:1] * member_table
            im = swt[c, 1:2] * member_table
            right.append(jnp.concatenate([re, -im], axis=1))
            right.append(jnp.concatenate([im, re], axis=1))
        station_rows_of.append(jnp.concatenate(right, axis=0).astype(jnp.bfloat16))

    def tile_sums(part):
        products = []
        for c in range(channels):
            weights = aw_ref[c, :, part].astype(jnp.float32)
            w_re = jnp.broadcast_to(weights[0:1], (samples, STAGE)).astype(jnp.bfloat16)
            w_im = jnp.broadcast_to(weights[1:2], (samples, STAGE)).astype(jnp.bfloat16)
            v_re, v_im = volts[c, 0, :, part], volts[c, 1, :, part]
            products.append(w_re * v_re - w_im * v_im)
            products.append(w_re * v_im + w_im * v_re)
        return jnp.dot(
            jnp.concatenate(products, axis=0),
            sum_ref[part, :],
            preferred_element_type=jnp.float32,
        )

    def tied_beams(g, beams_tile):
        left = []
        for c in range(CB):
            tile_re = beams_tile[c * rows_c : c * rows_c + samples]
            tile_im = beams_tile[c * rows_c + samples : (c + 1) * rows_c]
            left.append(jnp.concatenate([tile_re, tile_im], axis=1))
            left.append(jnp.concatenate([tile_im, -tile_re], axis=1))
        station = dot_nt(station_rows_of[g], jnp.concatenate(left, axis=0))
        station = jnp.where(own_channel, station, 0.0).astype(jnp.bfloat16)
        tied = jnp.dot(
            tied_ref[:, g * lanes : (g + 1) * lanes], station, preferred_element_type=jnp.float32
        )
        devices, rows, _ = out_ref.shape
        out_ref[:, :, g * CB * rows_c : (g + 1) * CB * rows_c] = tied.astype(jnp.bfloat16).reshape(
            devices, rows, CB * rows_c
        )

    for copy, part in zip(large, stage_slices):
        copy.wait()
        sums = tile_sums(part)
        if part.start == 0:
            tile_ref[...] = sums
        else:
            tile_ref[...] += sums
    for g in range(groups):
        rows_g = slice(g * CB * rows_c, (g + 1) * CB * rows_c)
        tied_beams(g, tile_ref[rows_g, :].astype(jnp.bfloat16))


def last_kernel(parts_ref, out_ref):
    n_stn, n_chan = lax.axis_size("stn"), lax.axis_size("chan")
    own_beams, rows_c, total_chans = out_ref.shape
    channels = total_chans // n_chan
    width = channels * rows_c
    parts = parts_ref[...].astype(jnp.float32).reshape(n_stn, n_chan, own_beams, width)
    tied = jnp.sum(parts, axis=0)
    diagonal = iota((channels, width), 0) == iota((channels, width), 1) // rows_c
    spread = (iota((rows_c, width), 0) == iota((rows_c, width), 1) % rows_c).astype(jnp.bfloat16)
    for b in range(own_beams):
        rows = [jnp.where(diagonal, tied[chan, b : b + 1], 0.0) for chan in reversed(range(n_chan))]
        rows = jnp.concatenate(rows, axis=0).astype(jnp.bfloat16)
        out_ref[b] = dot_nt(spread, rows).astype(jnp.bfloat16)


def shards(
    volts,
    antenna_tile_weights,
    station_weights,
    tile_station,
    station_group,
    station_pos,
    beam_dir,
    beam_order,
):
    channels, _, samples, _ = volts.shape
    beams = beam_order.shape[0]
    n_stn, n_chan = lax.axis_size("stn"), lax.axis_size("chan")
    rows = beams // (n_stn * n_chan)
    width = channels * 2 * samples
    operands = (
        volts,
        antenna_tile_weights,
        station_weights,
        tile_station[None, :],
        station_group[None, :],
        station_pos.T,
        beam_dir.T,
        beam_order[None, :],
    )
    operands = [pltpu.with_memory_space_constraint(x, pltpu.HBM) for x in operands]
    partial = pl.pallas_call(
        kernel,
        out_shape=pltpu.VMEM((n_stn * n_chan, rows, width), jnp.bfloat16),
        in_specs=[pl.BlockSpec(memory_space=pltpu.HBM)] * len(operands),
        out_specs=pl.BlockSpec(memory_space=pltpu.VMEM),
        scratch_shapes=[pltpu.VMEM(x.shape, x.dtype) for x in operands]
        + [
            pltpu.VMEM((beams, channels * 2 * (station_weights.shape[2] // TPS)), jnp.bfloat16),
            pltpu.VMEM((volts.shape[3], station_weights.shape[2]), jnp.bfloat16),
            pltpu.VMEM((width, station_weights.shape[2]), jnp.float32),
            pltpu.SemaphoreType.DMA((len(operands) - 1 + volts.shape[3] // STAGE,)),
        ],
        compiler_params=pltpu.CompilerParams(vmem_limit_bytes=24 * 2**20),
        name="partial_tied",
    )(*operands)
    parts = lax.all_to_all(
        partial,
        ("stn", "chan"),
        split_axis=0,
        concat_axis=0,
        axis_index_groups=[list(reversed(range(n_stn * n_chan)))],
        tiled=True,
    )
    vmem = pl.BlockSpec(memory_space=pltpu.VMEM)
    tied = pl.pallas_call(
        last_kernel,
        out_shape=jax.ShapeDtypeStruct((rows, 2 * samples, n_chan * channels), jnp.bfloat16),
        in_specs=[vmem],
        out_specs=vmem,
        compiler_params=pltpu.CompilerParams(vmem_limit_bytes=16 * 2**20),
        name="tied_beams",
    )(parts)
    return tied.transpose(0, 2, 1)


def solution(mesh):
    in_specs = (
        P("chan", None, None, "stn"),
        P("chan", None, "stn"),
        P("chan", None, "stn"),
        P("stn"),
        P(),
        P(),
        P(),
        P(),
    )
    out_specs = P(("stn", "chan"), None, None)
    return jax.shard_map(shards, mesh=mesh, in_specs=in_specs, out_specs=out_specs, check_vma=False)
```

```python
import functools
import math

import jax
import jax.numpy as jnp
from jax import lax
from jax.experimental import pallas as pl
from jax.experimental.pallas import tpu as pltpu
from jax.sharding import PartitionSpec as P

TILE_ANTENNAS = 16
TPS = 16
GROUPS = 4
CB = 8
NT = (((1,), (1,)), ((), ()))
SIN = [(-1) ** i * (2 * math.pi) ** (2 * i + 1) / math.factorial(2 * i + 1) for i in range(7)]


def dot_nt(a, b):
    return lax.dot_general(a, b, NT, preferred_element_type=jnp.float32)


def iota(shape, dim):
    return lax.broadcasted_iota(jnp.int32, shape, dim)


def beam_columns(order_ref, dir_ref, start, rows):
    beams = order_ref.shape[1]
    each = beams // (lax.axis_size("stn") * lax.axis_size("chan"))
    order = order_ref[...].astype(jnp.float32)
    lane = iota((rows, beams), 1)
    slot = iota((rows, beams), 0) + start
    own = lane == beams - each - slot // each * each + slot % each
    ids = jnp.sum(jnp.where(own, order, 0.0), axis=1, keepdims=True)
    pick = lane.astype(jnp.float32) == ids
    east = jnp.sum(jnp.where(pick, dir_ref[0:1, :], 0.0), axis=1, keepdims=True)
    north = jnp.sum(jnp.where(pick, dir_ref[1:2, :], 0.0), axis=1, keepdims=True)
    group = ids - GROUPS * jnp.floor(ids * (1.0 / GROUPS))
    return east, north, group


def station_rows(pos_ref, group_ref, stations, lanes):
    total = group_ref.shape[1]
    first = lax.axis_index("stn") * stations
    own = iota((stations, total), 1) == iota((stations, total), 0) + first
    spread = iota((stations, lanes), 0) == iota((stations, lanes), 1) % stations

    def turn(row):
        column = jnp.sum(jnp.where(own, row, 0.0), axis=1, keepdims=True)
        return jnp.sum(jnp.where(spread, column, 0.0), axis=0, keepdims=True)

    return turn(pos_ref[0:1, :]), turn(pos_ref[1:2, :]), turn(group_ref[...].astype(jnp.float32))


def cos_turns(t):
    y = t - jnp.floor(t + 0.5)
    z = 0.25 - jnp.abs(y)
    z2 = z * z
    value = jnp.full_like(z, SIN[-1])
    for coefficient in SIN[-2::-1]:
        value = value * z2 + coefficient
    return value * z


def kernel(
    volt_hbm,
    aw_hbm,
    sw_hbm,
    ts_hbm,
    group_hbm,
    pos_hbm,
    dir_hbm,
    order_hbm,
    out_ref,
    volts,
    aw_ref,
    sw_ref,
    ts_ref,
    group_ref,
    pos_ref,
    dir_ref,
    order_ref,
    tied_ref,
    sum_ref,
    sems,
):
    channels, _, samples, antennas = volt_hbm.shape
    tiles = sw_ref.shape[2]
    stations = tiles // TPS
    groups = channels // CB
    rows_c = 2 * samples
    beams = order_ref.shape[1]
    lanes = CB * 2 * stations
    scale = 1.0 / math.sqrt(group_ref.shape[1])

    def start(source, target, k):
        copy = pltpu.make_async_copy(source, target, sems.at[k])
        copy.start()
        return copy

    def voltages(g):
        part = pl.ds(g * CB, CB)
        return volt_hbm.at[part], volts.at[part]

    pairs = [
        (order_hbm, order_ref),
        (dir_hbm, dir_ref),
        (pos_hbm, pos_ref),
        (group_hbm, group_ref),
        voltages(0),
        (aw_hbm, aw_ref),
        (ts_hbm, ts_ref),
        (sw_hbm, sw_ref),
    ] + [voltages(g) for g in range(1, groups)]
    copies = [start(source, target, k) for k, (source, target) in enumerate(pairs)]
    small = copies[:4] + copies[5:8]
    large = copies[4:5] + copies[8:]
    antenna_tile = iota((antennas, tiles), 0) // TILE_ANTENNAS == iota((antennas, tiles), 1)
    sum_ref[...] = antenna_tile.astype(jnp.bfloat16)
    for copy in small[:4]:
        copy.wait()

    east_s, north_s, group_s = station_rows(pos_ref, group_ref, stations, lanes)
    lane = iota((1, lanes), 1)
    channel_lane = lane // (2 * stations)
    quarter = 0.25 * ((lane // stations) % 2).astype(jnp.float32)
    first_chan = lax.axis_index("chan") * channels
    total_chans = channels * lax.axis_size("chan")
    block = min(64, beams)

    def tied_rows(first):
        east, north, group = beam_columns(order_ref, dir_ref, first, block)
        delay = east * east_s + north * north_s
        member = jnp.where(group == group_s, scale, 0.0)
        for g in range(groups):
            freq = 1.0 + (first_chan + g * CB + channel_lane).astype(jnp.float32) / total_chans
            wave = cos_turns(delay * freq - quarter)
            tied_ref[pl.ds(first, block), g * lanes : (g + 1) * lanes] = (wave * member).astype(
                jnp.bfloat16
            )

    if beams == block:
        tied_rows(0)
    else:

        def body(i, carry):
            tied_rows(pl.multiple_of(i * block, block))
            return carry

        lax.fori_loop(0, beams // block, body, 0)

    for copy in small[4:]:
        copy.wait()
    member_table = (iota((stations, tiles), 0) == ts_ref[...] % stations).astype(jnp.float32)
    own_channel = iota((lanes, CB * rows_c), 0) // (2 * stations) == iota(
        (lanes, CB * rows_c), 1
    ) // rows_c

    station_rows_of = []
    for g in range(groups):
        swt = sw_ref[g * CB : (g + 1) * CB].astype(jnp.float32)
        right = []
        for c in range(CB):
            re = swt[c, 0:1] * member_table
            im = swt[c, 1:2] * member_table
            right.append(jnp.concatenate([re, -im], axis=1))
            right.append(jnp.concatenate([im, re], axis=1))
        station_rows_of.append(jnp.concatenate(right, axis=0).astype(jnp.bfloat16))

    def tile_beams(g):
        products = []
        weights = aw_ref[g * CB : (g + 1) * CB].astype(jnp.float32)
        for c in range(CB):
            w_re = jnp.broadcast_to(weights[c, 0:1], (samples, antennas)).astype(jnp.bfloat16)
            w_im = jnp.broadcast_to(weights[c, 1:2], (samples, antennas)).astype(jnp.bfloat16)
            v_re, v_im = volts[g * CB + c, 0], volts[g * CB + c, 1]
            products.append(w_re * v_re - w_im * v_im)
            products.append(w_re * v_im + w_im * v_re)
        return jnp.dot(
            jnp.concatenate(products, axis=0), sum_ref[...], preferred_element_type=jnp.float32
        ).astype(jnp.bfloat16)

    def tied_beams(g, beams_tile):
        left = []
        for c in range(CB):
            tile_re = beams_tile[c * rows_c : c * rows_c + samples]
            tile_im = beams_tile[c * rows_c + samples : (c + 1) * rows_c]
            left.append(jnp.concatenate([tile_re, tile_im], axis=1))
            left.append(jnp.concatenate([tile_im, -tile_re], axis=1))
        station = dot_nt(station_rows_of[g], jnp.concatenate(left, axis=0))
        station = jnp.where(own_channel, station, 0.0).astype(jnp.bfloat16)
        tied = jnp.dot(
            tied_ref[:, g * lanes : (g + 1) * lanes], station, preferred_element_type=jnp.float32
        )
        devices, rows, _ = out_ref.shape
        out_ref[:, :, g * CB * rows_c : (g + 1) * CB * rows_c] = tied.astype(jnp.bfloat16).reshape(
            devices, rows, CB * rows_c
        )

    last = None
    for g in range(groups):
        large[g].wait()
        now = tile_beams(g)
        if last is not None:
            tied_beams(g - 1, last)
        last = now
    tied_beams(groups - 1, last)


def last_kernel(parts_ref, out_ref):
    n_stn, n_chan = lax.axis_size("stn"), lax.axis_size("chan")
    own_beams, rows_c, total_chans = out_ref.shape
    channels = total_chans // n_chan
    width = channels * rows_c
    parts = parts_ref[...].astype(jnp.float32).reshape(n_stn, n_chan, own_beams, width)
    tied = jnp.sum(parts, axis=0)
    diagonal = iota((channels, width), 0) == iota((channels, width), 1) // rows_c
    spread = (iota((rows_c, width), 0) == iota((rows_c, width), 1) % rows_c).astype(jnp.bfloat16)
    for b in range(own_beams):
        rows = [jnp.where(diagonal, tied[chan, b : b + 1], 0.0) for chan in reversed(range(n_chan))]
        rows = jnp.concatenate(rows, axis=0).astype(jnp.bfloat16)
        out_ref[b] = dot_nt(spread, rows).astype(jnp.bfloat16)


def shards(
    volts,
    antenna_tile_weights,
    station_weights,
    tile_station,
    station_group,
    station_pos,
    beam_dir,
    beam_order,
):
    channels, _, samples, _ = volts.shape
    beams = beam_order.shape[0]
    n_stn, n_chan = lax.axis_size("stn"), lax.axis_size("chan")
    rows = beams // (n_stn * n_chan)
    width = channels * 2 * samples
    operands = (
        volts,
        antenna_tile_weights,
        station_weights,
        tile_station[None, :],
        station_group[None, :],
        station_pos.T,
        beam_dir.T,
        beam_order[None, :],
    )
    operands = [pltpu.with_memory_space_constraint(x, pltpu.HBM) for x in operands]
    partial = pl.pallas_call(
        kernel,
        out_shape=pltpu.VMEM((n_stn * n_chan, rows, width), jnp.bfloat16),
        in_specs=[pl.BlockSpec(memory_space=pltpu.HBM)] * len(operands),
        out_specs=pl.BlockSpec(memory_space=pltpu.VMEM),
        scratch_shapes=[pltpu.VMEM(x.shape, x.dtype) for x in operands]
        + [
            pltpu.VMEM((beams, channels * 2 * (station_weights.shape[2] // TPS)), jnp.bfloat16),
            pltpu.VMEM((volts.shape[3], station_weights.shape[2]), jnp.bfloat16),
            pltpu.SemaphoreType.DMA((len(operands) - 1 + channels // CB,)),
        ],
        compiler_params=pltpu.CompilerParams(vmem_limit_bytes=24 * 2**20),
        name="partial_tied",
    )(*operands)
    parts = lax.all_to_all(
        partial,
        ("stn", "chan"),
        split_axis=0,
        concat_axis=0,
        axis_index_groups=[list(reversed(range(n_stn * n_chan)))],
        tiled=True,
    )
    vmem = pl.BlockSpec(memory_space=pltpu.VMEM)
    tied = pl.pallas_call(
        last_kernel,
        out_shape=jax.ShapeDtypeStruct((rows, 2 * samples, n_chan * channels), jnp.bfloat16),
        in_specs=[vmem],
        out_specs=vmem,
        compiler_params=pltpu.CompilerParams(vmem_limit_bytes=16 * 2**20),
        name="tied_beams",
    )(parts)
    return tied.transpose(0, 2, 1)


def solution(mesh):
    in_specs = (
        P("chan", None, None, "stn"),
        P("chan", None, "stn"),
        P("chan", None, "stn"),
        P("stn"),
        P(),
        P(),
        P(),
        P(),
    )
    out_specs = P(("stn", "chan"), None, None)
    return jax.shard_map(shards, mesh=mesh, in_specs=in_specs, out_specs=out_specs, check_vma=False)
```

```python
import functools
import math

import jax
import jax.numpy as jnp
from jax import lax
from jax.experimental import pallas as pl
from jax.experimental.pallas import tpu as pltpu
from jax.sharding import PartitionSpec as P

TILE_ANTENNAS = 16
TPS = 16
GROUPS = 4
CB = 8
NT = (((1,), (1,)), ((), ()))
SIN = [(-1) ** i * (2 * math.pi) ** (2 * i + 1) / math.factorial(2 * i + 1) for i in range(7)]


def dot_nt(a, b):
    return lax.dot_general(a, b, NT, preferred_element_type=jnp.float32)


def iota(shape, dim):
    return lax.broadcasted_iota(jnp.int32, shape, dim)


def beam_columns(order_ref, dir_ref, start, rows):
    beams = order_ref.shape[1]
    each = beams // (lax.axis_size("stn") * lax.axis_size("chan"))
    order = order_ref[...].astype(jnp.float32)
    lane = iota((rows, beams), 1)
    slot = iota((rows, beams), 0) + start
    own = lane == beams - each - slot // each * each + slot % each
    ids = jnp.sum(jnp.where(own, order, 0.0), axis=1, keepdims=True)
    pick = lane.astype(jnp.float32) == ids
    east = jnp.sum(jnp.where(pick, dir_ref[0:1, :], 0.0), axis=1, keepdims=True)
    north = jnp.sum(jnp.where(pick, dir_ref[1:2, :], 0.0), axis=1, keepdims=True)
    group = ids - GROUPS * jnp.floor(ids * (1.0 / GROUPS))
    return east, north, group


def station_rows(pos_ref, group_ref, stations, lanes):
    total = group_ref.shape[1]
    first = lax.axis_index("stn") * stations
    own = iota((stations, total), 1) == iota((stations, total), 0) + first
    spread = iota((stations, lanes), 0) == iota((stations, lanes), 1) % stations

    def turn(row):
        column = jnp.sum(jnp.where(own, row, 0.0), axis=1, keepdims=True)
        return jnp.sum(jnp.where(spread, column, 0.0), axis=0, keepdims=True)

    return turn(pos_ref[0:1, :]), turn(pos_ref[1:2, :]), turn(group_ref[...].astype(jnp.float32))


def cos_turns(t):
    y = t - jnp.floor(t + 0.5)
    z = 0.25 - jnp.abs(y)
    z2 = z * z
    value = jnp.full_like(z, SIN[-1])
    for coefficient in SIN[-2::-1]:
        value = value * z2 + coefficient
    return value * z


def kernel(
    volt_hbm,
    aw_hbm,
    sw_hbm,
    ts_hbm,
    group_hbm,
    pos_hbm,
    dir_hbm,
    order_hbm,
    out_ref,
    volts,
    aw_ref,
    sw_ref,
    ts_ref,
    group_ref,
    pos_ref,
    dir_ref,
    order_ref,
    tied_ref,
    sum_ref,
    sems,
):
    channels, _, samples, antennas = volt_hbm.shape
    tiles = sw_ref.shape[2]
    stations = tiles // TPS
    groups = channels // CB
    rows_c = 2 * samples
    beams = order_ref.shape[1]
    lanes = CB * 2 * stations
    scale = 1.0 / math.sqrt(group_ref.shape[1])

    def start(source, target, k):
        copy = pltpu.make_async_copy(source, target, sems.at[k])
        copy.start()
        return copy

    def voltages(g):
        part = pl.ds(g * CB, CB)
        return volt_hbm.at[part], volts.at[part]

    pairs = [
        (order_hbm, order_ref),
        (dir_hbm, dir_ref),
        (pos_hbm, pos_ref),
        (group_hbm, group_ref),
        voltages(0),
        (aw_hbm, aw_ref),
        (ts_hbm, ts_ref),
        (sw_hbm, sw_ref),
    ] + [voltages(g) for g in range(1, groups)]
    copies = [start(source, target, k) for k, (source, target) in enumerate(pairs)]
    small = copies[:4] + copies[5:8]
    large = copies[4:5] + copies[8:]
    antenna_tile = iota((antennas, tiles), 0) // TILE_ANTENNAS == iota((antennas, tiles), 1)
    sum_ref[...] = antenna_tile.astype(jnp.bfloat16)
    for copy in small[:4]:
        copy.wait()

    east_s, north_s, group_s = station_rows(pos_ref, group_ref, stations, lanes)
    lane = iota((1, lanes), 1)
    channel_lane = lane // (2 * stations)
    quarter = 0.25 * ((lane // stations) % 2).astype(jnp.float32)
    first_chan = lax.axis_index("chan") * channels
    total_chans = channels * lax.axis_size("chan")
    block = min(64, beams)

    def tied_rows(first):
        east, north, group = beam_columns(order_ref, dir_ref, first, block)
        delay = east * east_s + north * north_s
        member = jnp.where(group == group_s, scale, 0.0)
        for g in range(groups):
            freq = 1.0 + (first_chan + g * CB + channel_lane).astype(jnp.float32) / total_chans
            wave = cos_turns(delay * freq - quarter)
            tied_ref[pl.ds(first, block), g * lanes : (g + 1) * lanes] = (wave * member).astype(
                jnp.bfloat16
            )

    if beams == block:
        tied_rows(0)
    else:

        def body(i, carry):
            tied_rows(pl.multiple_of(i * block, block))
            return carry

        lax.fori_loop(0, beams // block, body, 0)

    for copy in small[4:]:
        copy.wait()
    member_table = (iota((stations, tiles), 0) == ts_ref[...] % stations).astype(jnp.float32)
    own_channel = iota((lanes, CB * rows_c), 0) // (2 * stations) == iota(
        (lanes, CB * rows_c), 1
    ) // rows_c

    station_rows_of = []
    for g in range(groups):
        swt = sw_ref[g * CB : (g + 1) * CB].astype(jnp.float32)
        right = []
        for c in range(CB):
            re = swt[c, 0:1] * member_table
            im = swt[c, 1:2] * member_table
            right.append(jnp.concatenate([re, -im], axis=1))
            right.append(jnp.concatenate([im, re], axis=1))
        station_rows_of.append(jnp.concatenate(right, axis=0).astype(jnp.bfloat16))

    def tile_beams(g):
        products = []
        weights = aw_ref[g * CB : (g + 1) * CB].astype(jnp.float32)
        for c in range(CB):
            w_re = jnp.broadcast_to(weights[c, 0:1], (samples, antennas)).astype(jnp.bfloat16)
            w_im = jnp.broadcast_to(weights[c, 1:2], (samples, antennas)).astype(jnp.bfloat16)
            v_re, v_im = volts[g * CB + c, 0], volts[g * CB + c, 1]
            products.append(w_re * v_re - w_im * v_im)
            products.append(w_re * v_im + w_im * v_re)
        products = jnp.concatenate(products, axis=0)
        half = antennas // 2
        sums = [
            jnp.dot(
                products[:, part], sum_ref[part, :], preferred_element_type=jnp.float32
            )
            for part in (slice(0, half), slice(half, antennas))
        ]
        return (sums[0] + sums[1]).astype(jnp.bfloat16)

    def tied_beams(g, beams_tile):
        left = []
        for c in range(CB):
            tile_re = beams_tile[c * rows_c : c * rows_c + samples]
            tile_im = beams_tile[c * rows_c + samples : (c + 1) * rows_c]
            left.append(jnp.concatenate([tile_re, tile_im], axis=1))
            left.append(jnp.concatenate([tile_im, -tile_re], axis=1))
        station = dot_nt(station_rows_of[g], jnp.concatenate(left, axis=0))
        station = jnp.where(own_channel, station, 0.0).astype(jnp.bfloat16)
        tied = jnp.dot(
            tied_ref[:, g * lanes : (g + 1) * lanes], station, preferred_element_type=jnp.float32
        )
        devices, rows, _ = out_ref.shape
        out_ref[:, :, g * CB * rows_c : (g + 1) * CB * rows_c] = tied.astype(jnp.bfloat16).reshape(
            devices, rows, CB * rows_c
        )

    last = None
    for g in range(groups):
        large[g].wait()
        now = tile_beams(g)
        if last is not None:
            tied_beams(g - 1, last)
        last = now
    tied_beams(groups - 1, last)


def last_kernel(parts_ref, out_ref):
    n_stn, n_chan = lax.axis_size("stn"), lax.axis_size("chan")
    own_beams, rows_c, total_chans = out_ref.shape
    channels = total_chans // n_chan
    width = channels * rows_c
    parts = parts_ref[...].astype(jnp.float32).reshape(n_stn, n_chan, own_beams, width)
    tied = jnp.sum(parts, axis=0)
    diagonal = iota((channels, width), 0) == iota((channels, width), 1) // rows_c
    spread = (iota((rows_c, width), 0) == iota((rows_c, width), 1) % rows_c).astype(jnp.bfloat16)
    for b in range(own_beams):
        rows = [jnp.where(diagonal, tied[chan, b : b + 1], 0.0) for chan in reversed(range(n_chan))]
        rows = jnp.concatenate(rows, axis=0).astype(jnp.bfloat16)
        out_ref[b] = dot_nt(spread, rows).astype(jnp.bfloat16)


def shards(
    volts,
    antenna_tile_weights,
    station_weights,
    tile_station,
    station_group,
    station_pos,
    beam_dir,
    beam_order,
):
    channels, _, samples, _ = volts.shape
    beams = beam_order.shape[0]
    n_stn, n_chan = lax.axis_size("stn"), lax.axis_size("chan")
    rows = beams // (n_stn * n_chan)
    width = channels * 2 * samples
    operands = (
        volts,
        antenna_tile_weights,
        station_weights,
        tile_station[None, :],
        station_group[None, :],
        station_pos.T,
        beam_dir.T,
        beam_order[None, :],
    )
    operands = [pltpu.with_memory_space_constraint(x, pltpu.HBM) for x in operands]
    partial = pl.pallas_call(
        kernel,
        out_shape=pltpu.VMEM((n_stn * n_chan, rows, width), jnp.bfloat16),
        in_specs=[pl.BlockSpec(memory_space=pltpu.HBM)] * len(operands),
        out_specs=pl.BlockSpec(memory_space=pltpu.VMEM),
        scratch_shapes=[pltpu.VMEM(x.shape, x.dtype) for x in operands]
        + [
            pltpu.VMEM((beams, channels * 2 * (station_weights.shape[2] // TPS)), jnp.bfloat16),
            pltpu.VMEM((volts.shape[3], station_weights.shape[2]), jnp.bfloat16),
            pltpu.SemaphoreType.DMA((len(operands) - 1 + channels // CB,)),
        ],
        compiler_params=pltpu.CompilerParams(vmem_limit_bytes=24 * 2**20),
        name="partial_tied",
    )(*operands)
    parts = lax.all_to_all(
        partial,
        ("stn", "chan"),
        split_axis=0,
        concat_axis=0,
        axis_index_groups=[list(reversed(range(n_stn * n_chan)))],
        tiled=True,
    )
    vmem = pl.BlockSpec(memory_space=pltpu.VMEM)
    tied = pl.pallas_call(
        last_kernel,
        out_shape=jax.ShapeDtypeStruct((rows, 2 * samples, n_chan * channels), jnp.bfloat16),
        in_specs=[vmem],
        out_specs=vmem,
        compiler_params=pltpu.CompilerParams(vmem_limit_bytes=16 * 2**20),
        name="tied_beams",
    )(parts)
    return tied.transpose(0, 2, 1)


def solution(mesh):
    in_specs = (
        P("chan", None, None, "stn"),
        P("chan", None, "stn"),
        P("chan", None, "stn"),
        P("stn"),
        P(),
        P(),
        P(),
        P(),
    )
    out_specs = P(("stn", "chan"), None, None)
    return jax.shard_map(shards, mesh=mesh, in_specs=in_specs, out_specs=out_specs, check_vma=False)
```

```python
import functools
import math

import jax
import jax.numpy as jnp
from jax import lax
from jax.experimental import pallas as pl
from jax.experimental.pallas import tpu as pltpu
from jax.sharding import PartitionSpec as P

TILE_ANTENNAS = 16
TPS = 16
GROUPS = 4
CB = 8
NT = (((1,), (1,)), ((), ()))
SIN = [(-1) ** i * (2 * math.pi) ** (2 * i + 1) / math.factorial(2 * i + 1) for i in range(7)]


def dot_nt(a, b):
    return lax.dot_general(a, b, NT, preferred_element_type=jnp.float32)


def iota(shape, dim):
    return lax.broadcasted_iota(jnp.int32, shape, dim)


def beam_columns(order_ref, dir_ref, start, rows):
    beams = order_ref.shape[1]
    each = beams // (lax.axis_size("stn") * lax.axis_size("chan"))
    order = order_ref[...].astype(jnp.float32)
    lane = iota((rows, beams), 1)
    slot = iota((rows, beams), 0) + start
    own = lane == beams - each - slot // each * each + slot % each
    ids = jnp.sum(jnp.where(own, order, 0.0), axis=1, keepdims=True)
    pick = lane.astype(jnp.float32) == ids
    east = jnp.sum(jnp.where(pick, dir_ref[0:1, :], 0.0), axis=1, keepdims=True)
    north = jnp.sum(jnp.where(pick, dir_ref[1:2, :], 0.0), axis=1, keepdims=True)
    group = ids - GROUPS * jnp.floor(ids * (1.0 / GROUPS))
    return east, north, group


def station_rows(pos_ref, group_ref, stations, lanes):
    total = group_ref.shape[1]
    first = lax.axis_index("stn") * stations
    own = iota((stations, total), 1) == iota((stations, total), 0) + first
    spread = iota((stations, lanes), 0) == iota((stations, lanes), 1) % stations

    def turn(row):
        column = jnp.sum(jnp.where(own, row, 0.0), axis=1, keepdims=True)
        return jnp.sum(jnp.where(spread, column, 0.0), axis=0, keepdims=True)

    return turn(pos_ref[0:1, :]), turn(pos_ref[1:2, :]), turn(group_ref[...].astype(jnp.float32))


def cos_turns(t):
    y = t - jnp.floor(t + 0.5)
    z = 0.25 - jnp.abs(y)
    z2 = z * z
    value = jnp.full_like(z, SIN[-1])
    for coefficient in SIN[-2::-1]:
        value = value * z2 + coefficient
    return value * z


def kernel(
    volt_hbm,
    aw_hbm,
    sw_hbm,
    ts_hbm,
    group_hbm,
    pos_hbm,
    dir_hbm,
    order_hbm,
    out_ref,
    volts,
    aw_ref,
    sw_ref,
    ts_ref,
    group_ref,
    pos_ref,
    dir_ref,
    order_ref,
    tied_ref,
    sum_ref,
    sems,
):
    channels, _, samples, antennas = volt_hbm.shape
    tiles = sw_ref.shape[2]
    stations = tiles // TPS
    groups = channels // CB
    rows_c = 2 * samples
    beams = order_ref.shape[1]
    lanes = CB * 2 * stations
    scale = 1.0 / math.sqrt(group_ref.shape[1])

    def start(source, target, k):
        copy = pltpu.make_async_copy(source, target, sems.at[k])
        copy.start()
        return copy

    def voltages(g):
        part = pl.ds(g * CB, CB)
        return volt_hbm.at[part], volts.at[part]

    pairs = [
        voltages(0),
        (aw_hbm, aw_ref),
        (order_hbm, order_ref),
        (dir_hbm, dir_ref),
        (pos_hbm, pos_ref),
        (group_hbm, group_ref),
        (ts_hbm, ts_ref),
        (sw_hbm, sw_ref),
    ] + [voltages(g) for g in range(1, groups)]
    copies = [start(source, target, k) for k, (source, target) in enumerate(pairs)]
    large = copies[:1] + copies[8:]
    antenna_tile = iota((antennas, tiles), 0) // TILE_ANTENNAS == iota((antennas, tiles), 1)
    sum_ref[...] = antenna_tile.astype(jnp.bfloat16)
    for copy in copies[:2]:
        copy.wait()

    def tile_beams(g):
        products = []
        weights = aw_ref[g * CB : (g + 1) * CB].astype(jnp.float32)
        for c in range(CB):
            w_re = jnp.broadcast_to(weights[c, 0:1], (samples, antennas)).astype(jnp.bfloat16)
            w_im = jnp.broadcast_to(weights[c, 1:2], (samples, antennas)).astype(jnp.bfloat16)
            v_re, v_im = volts[g * CB + c, 0], volts[g * CB + c, 1]
            products.append(w_re * v_re - w_im * v_im)
            products.append(w_re * v_im + w_im * v_re)
        return jnp.dot(
            jnp.concatenate(products, axis=0), sum_ref[...], preferred_element_type=jnp.float32
        ).astype(jnp.bfloat16)

    last = tile_beams(0)
    for copy in copies[2:9]:
        copy.wait()

    east_s, north_s, group_s = station_rows(pos_ref, group_ref, stations, lanes)
    lane = iota((1, lanes), 1)
    channel_lane = lane // (2 * stations)
    quarter = 0.25 * ((lane // stations) % 2).astype(jnp.float32)
    first_chan = lax.axis_index("chan") * channels
    total_chans = channels * lax.axis_size("chan")
    block = min(64, beams)

    def tied_rows(first):
        east, north, group = beam_columns(order_ref, dir_ref, first, block)
        delay = east * east_s + north * north_s
        member = jnp.where(group == group_s, scale, 0.0)
        for g in range(groups):
            freq = 1.0 + (first_chan + g * CB + channel_lane).astype(jnp.float32) / total_chans
            wave = cos_turns(delay * freq - quarter)
            tied_ref[pl.ds(first, block), g * lanes : (g + 1) * lanes] = (wave * member).astype(
                jnp.bfloat16
            )

    if beams == block:
        tied_rows(0)
    else:

        def body(i, carry):
            tied_rows(pl.multiple_of(i * block, block))
            return carry

        lax.fori_loop(0, beams // block, body, 0)

    member_table = (iota((stations, tiles), 0) == ts_ref[...] % stations).astype(jnp.float32)
    own_channel = iota((lanes, CB * rows_c), 0) // (2 * stations) == iota(
        (lanes, CB * rows_c), 1
    ) // rows_c

    station_rows_of = []
    for g in range(groups):
        swt = sw_ref[g * CB : (g + 1) * CB].astype(jnp.float32)
        right = []
        for c in range(CB):
            re = swt[c, 0:1] * member_table
            im = swt[c, 1:2] * member_table
            right.append(jnp.concatenate([re, -im], axis=1))
            right.append(jnp.concatenate([im, re], axis=1))
        station_rows_of.append(jnp.concatenate(right, axis=0).astype(jnp.bfloat16))

    def tied_beams(g, beams_tile):
        left = []
        for c in range(CB):
            tile_re = beams_tile[c * rows_c : c * rows_c + samples]
            tile_im = beams_tile[c * rows_c + samples : (c + 1) * rows_c]
            left.append(jnp.concatenate([tile_re, tile_im], axis=1))
            left.append(jnp.concatenate([tile_im, -tile_re], axis=1))
        station = dot_nt(station_rows_of[g], jnp.concatenate(left, axis=0))
        station = jnp.where(own_channel, station, 0.0).astype(jnp.bfloat16)
        tied = jnp.dot(
            tied_ref[:, g * lanes : (g + 1) * lanes], station, preferred_element_type=jnp.float32
        )
        devices, rows, _ = out_ref.shape
        out_ref[:, :, g * CB * rows_c : (g + 1) * CB * rows_c] = tied.astype(jnp.bfloat16).reshape(
            devices, rows, CB * rows_c
        )

    for g in range(1, groups):
        if g > 1:
            large[g].wait()
        now = tile_beams(g)
        tied_beams(g - 1, last)
        last = now
    tied_beams(groups - 1, last)


def last_kernel(parts_ref, out_ref):
    n_stn, n_chan = lax.axis_size("stn"), lax.axis_size("chan")
    own_beams, rows_c, total_chans = out_ref.shape
    channels = total_chans // n_chan
    width = channels * rows_c
    parts = parts_ref[...].astype(jnp.float32).reshape(n_stn, n_chan, own_beams, width)
    tied = jnp.sum(parts, axis=0)
    diagonal = iota((channels, width), 0) == iota((channels, width), 1) // rows_c
    spread = (iota((rows_c, width), 0) == iota((rows_c, width), 1) % rows_c).astype(jnp.bfloat16)
    for b in range(own_beams):
        rows = [jnp.where(diagonal, tied[chan, b : b + 1], 0.0) for chan in reversed(range(n_chan))]
        rows = jnp.concatenate(rows, axis=0).astype(jnp.bfloat16)
        out_ref[b] = dot_nt(spread, rows).astype(jnp.bfloat16)


def shards(
    volts,
    antenna_tile_weights,
    station_weights,
    tile_station,
    station_group,
    station_pos,
    beam_dir,
    beam_order,
):
    channels, _, samples, _ = volts.shape
    beams = beam_order.shape[0]
    n_stn, n_chan = lax.axis_size("stn"), lax.axis_size("chan")
    rows = beams // (n_stn * n_chan)
    width = channels * 2 * samples
    operands = (
        volts,
        antenna_tile_weights,
        station_weights,
        tile_station[None, :],
        station_group[None, :],
        station_pos.T,
        beam_dir.T,
        beam_order[None, :],
    )
    operands = [pltpu.with_memory_space_constraint(x, pltpu.HBM) for x in operands]
    partial = pl.pallas_call(
        kernel,
        out_shape=pltpu.VMEM((n_stn * n_chan, rows, width), jnp.bfloat16),
        in_specs=[pl.BlockSpec(memory_space=pltpu.HBM)] * len(operands),
        out_specs=pl.BlockSpec(memory_space=pltpu.VMEM),
        scratch_shapes=[pltpu.VMEM(x.shape, x.dtype) for x in operands]
        + [
            pltpu.VMEM((beams, channels * 2 * (station_weights.shape[2] // TPS)), jnp.bfloat16),
            pltpu.VMEM((volts.shape[3], station_weights.shape[2]), jnp.bfloat16),
            pltpu.SemaphoreType.DMA((len(operands) - 1 + channels // CB,)),
        ],
        compiler_params=pltpu.CompilerParams(vmem_limit_bytes=24 * 2**20),
        name="partial_tied",
    )(*operands)
    parts = lax.all_to_all(
        partial,
        ("stn", "chan"),
        split_axis=0,
        concat_axis=0,
        axis_index_groups=[list(reversed(range(n_stn * n_chan)))],
        tiled=True,
    )
    vmem = pl.BlockSpec(memory_space=pltpu.VMEM)
    tied = pl.pallas_call(
        last_kernel,
        out_shape=jax.ShapeDtypeStruct((rows, 2 * samples, n_chan * channels), jnp.bfloat16),
        in_specs=[vmem],
        out_specs=vmem,
        compiler_params=pltpu.CompilerParams(vmem_limit_bytes=16 * 2**20),
        name="tied_beams",
    )(parts)
    return tied.transpose(0, 2, 1)


def solution(mesh):
    in_specs = (
        P("chan", None, None, "stn"),
        P("chan", None, "stn"),
        P("chan", None, "stn"),
        P("stn"),
        P(),
        P(),
        P(),
        P(),
    )
    out_specs = P(("stn", "chan"), None, None)
    return jax.shard_map(shards, mesh=mesh, in_specs=in_specs, out_specs=out_specs, check_vma=False)
```

```python
import functools
import math

import jax
import jax.numpy as jnp
from jax import lax
from jax.experimental import pallas as pl
from jax.experimental.pallas import tpu as pltpu
from jax.sharding import PartitionSpec as P

TILE_ANTENNAS = 16
TPS = 16
GROUPS = 4
CB = 8
NT = (((1,), (1,)), ((), ()))
SIN = [(-1) ** i * (2 * math.pi) ** (2 * i + 1) / math.factorial(2 * i + 1) for i in range(7)]


def dot_nt(a, b):
    return lax.dot_general(a, b, NT, preferred_element_type=jnp.float32)


def iota(shape, dim):
    return lax.broadcasted_iota(jnp.int32, shape, dim)


def beam_columns(order_ref, dir_ref, start, rows):
    beams = order_ref.shape[1]
    each = beams // (lax.axis_size("stn") * lax.axis_size("chan"))
    order = order_ref[...].astype(jnp.float32)
    lane = iota((rows, beams), 1)
    slot = iota((rows, beams), 0) + start
    own = lane == beams - each - slot // each * each + slot % each
    ids = jnp.sum(jnp.where(own, order, 0.0), axis=1, keepdims=True)
    pick = lane.astype(jnp.float32) == ids
    east = jnp.sum(jnp.where(pick, dir_ref[0:1, :], 0.0), axis=1, keepdims=True)
    north = jnp.sum(jnp.where(pick, dir_ref[1:2, :], 0.0), axis=1, keepdims=True)
    group = ids - GROUPS * jnp.floor(ids * (1.0 / GROUPS))
    return east, north, group


def station_rows(pos_ref, group_ref, stations, lanes):
    total = group_ref.shape[1]
    first = lax.axis_index("stn") * stations
    own = iota((stations, total), 1) == iota((stations, total), 0) + first
    spread = iota((stations, lanes), 0) == iota((stations, lanes), 1) % stations

    def turn(row):
        column = jnp.sum(jnp.where(own, row, 0.0), axis=1, keepdims=True)
        return jnp.sum(jnp.where(spread, column, 0.0), axis=0, keepdims=True)

    return turn(pos_ref[0:1, :]), turn(pos_ref[1:2, :]), turn(group_ref[...].astype(jnp.float32))


def cos_turns(t):
    y = t - jnp.floor(t + 0.5)
    z = 0.25 - jnp.abs(y)
    z2 = z * z
    value = jnp.full_like(z, SIN[-1])
    for coefficient in SIN[-2::-1]:
        value = value * z2 + coefficient
    return value * z


def kernel(
    volt_hbm,
    aw_hbm,
    sw_hbm,
    ts_hbm,
    group_hbm,
    pos_hbm,
    dir_hbm,
    order_hbm,
    out_ref,
    volts,
    aw_ref,
    sw_ref,
    ts_ref,
    group_ref,
    pos_ref,
    dir_ref,
    order_ref,
    tied_ref,
    sum_ref,
    sems,
):
    channels, _, samples, antennas = volt_hbm.shape
    tiles = sw_ref.shape[2]
    stations = tiles // TPS
    groups = channels // CB
    rows_c = 2 * samples
    beams = order_ref.shape[1]
    lanes = CB * 2 * stations
    scale = 1.0 / math.sqrt(group_ref.shape[1])

    def start(source, target, k):
        copy = pltpu.make_async_copy(source, target, sems.at[k])
        copy.start()
        return copy

    def voltages(g):
        part = pl.ds(g * CB, CB)
        return volt_hbm.at[part], volts.at[part]

    pairs = [voltages(0), (aw_hbm, aw_ref)]
    pairs += [voltages(g) for g in range(1, groups)]
    pairs += [
        (order_hbm, order_ref),
        (dir_hbm, dir_ref),
        (pos_hbm, pos_ref),
        (group_hbm, group_ref),
        (ts_hbm, ts_ref),
        (sw_hbm, sw_ref),
    ]
    copies = [start(source, target, k) for k, (source, target) in enumerate(pairs)]
    large = copies[:1] + copies[2 : groups + 1]
    small = copies[groups + 1 :]
    antenna_tile = iota((antennas, tiles), 0) // TILE_ANTENNAS == iota((antennas, tiles), 1)
    sum_ref[...] = antenna_tile.astype(jnp.bfloat16)
    for copy in copies[:2]:
        copy.wait()

    def tile_beams(g):
        products = []
        weights = aw_ref[g * CB : (g + 1) * CB].astype(jnp.float32)
        for c in range(CB):
            w_re = jnp.broadcast_to(weights[c, 0:1], (samples, antennas)).astype(jnp.bfloat16)
            w_im = jnp.broadcast_to(weights[c, 1:2], (samples, antennas)).astype(jnp.bfloat16)
            v_re, v_im = volts[g * CB + c, 0], volts[g * CB + c, 1]
            products.append(w_re * v_re - w_im * v_im)
            products.append(w_re * v_im + w_im * v_re)
        return jnp.dot(
            jnp.concatenate(products, axis=0), sum_ref[...], preferred_element_type=jnp.float32
        ).astype(jnp.bfloat16)

    last = tile_beams(0)
    for copy in small:
        copy.wait()
    large[1].wait()

    east_s, north_s, group_s = station_rows(pos_ref, group_ref, stations, lanes)
    lane = iota((1, lanes), 1)
    channel_lane = lane // (2 * stations)
    quarter = 0.25 * ((lane // stations) % 2).astype(jnp.float32)
    first_chan = lax.axis_index("chan") * channels
    total_chans = channels * lax.axis_size("chan")
    block = min(64, beams)

    def tied_rows(first):
        east, north, group = beam_columns(order_ref, dir_ref, first, block)
        delay = east * east_s + north * north_s
        member = jnp.where(group == group_s, scale, 0.0)
        for g in range(groups):
            freq = 1.0 + (first_chan + g * CB + channel_lane).astype(jnp.float32) / total_chans
            wave = cos_turns(delay * freq - quarter)
            tied_ref[pl.ds(first, block), g * lanes : (g + 1) * lanes] = (wave * member).astype(
                jnp.bfloat16
            )

    if beams == block:
        tied_rows(0)
    else:

        def body(i, carry):
            tied_rows(pl.multiple_of(i * block, block))
            return carry

        lax.fori_loop(0, beams // block, body, 0)

    member_table = (iota((stations, tiles), 0) == ts_ref[...] % stations).astype(jnp.float32)
    own_channel = iota((lanes, CB * rows_c), 0) // (2 * stations) == iota(
        (lanes, CB * rows_c), 1
    ) // rows_c

    station_rows_of = []
    for g in range(groups):
        swt = sw_ref[g * CB : (g + 1) * CB].astype(jnp.float32)
        right = []
        for c in range(CB):
            re = swt[c, 0:1] * member_table
            im = swt[c, 1:2] * member_table
            right.append(jnp.concatenate([re, -im], axis=1))
            right.append(jnp.concatenate([im, re], axis=1))
        station_rows_of.append(jnp.concatenate(right, axis=0).astype(jnp.bfloat16))

    def tied_beams(g, beams_tile):
        left = []
        for c in range(CB):
            tile_re = beams_tile[c * rows_c : c * rows_c + samples]
            tile_im = beams_tile[c * rows_c + samples : (c + 1) * rows_c]
            left.append(jnp.concatenate([tile_re, tile_im], axis=1))
            left.append(jnp.concatenate([tile_im, -tile_re], axis=1))
        station = dot_nt(station_rows_of[g], jnp.concatenate(left, axis=0))
        station = jnp.where(own_channel, station, 0.0).astype(jnp.bfloat16)
        tied = jnp.dot(
            tied_ref[:, g * lanes : (g + 1) * lanes], station, preferred_element_type=jnp.float32
        )
        devices, rows, _ = out_ref.shape
        out_ref[:, :, g * CB * rows_c : (g + 1) * CB * rows_c] = tied.astype(jnp.bfloat16).reshape(
            devices, rows, CB * rows_c
        )

    for g in range(1, groups):
        if g > 1:
            large[g].wait()
        now = tile_beams(g)
        tied_beams(g - 1, last)
        last = now
    tied_beams(groups - 1, last)


def last_kernel(parts_ref, out_ref):
    n_stn, n_chan = lax.axis_size("stn"), lax.axis_size("chan")
    own_beams, rows_c, total_chans = out_ref.shape
    channels = total_chans // n_chan
    width = channels * rows_c
    parts = parts_ref[...].astype(jnp.float32).reshape(n_stn, n_chan, own_beams, width)
    tied = jnp.sum(parts, axis=0)
    diagonal = iota((channels, width), 0) == iota((channels, width), 1) // rows_c
    spread = (iota((rows_c, width), 0) == iota((rows_c, width), 1) % rows_c).astype(jnp.bfloat16)
    for b in range(own_beams):
        rows = [jnp.where(diagonal, tied[chan, b : b + 1], 0.0) for chan in reversed(range(n_chan))]
        rows = jnp.concatenate(rows, axis=0).astype(jnp.bfloat16)
        out_ref[b] = dot_nt(spread, rows).astype(jnp.bfloat16)


def shards(
    volts,
    antenna_tile_weights,
    station_weights,
    tile_station,
    station_group,
    station_pos,
    beam_dir,
    beam_order,
):
    channels, _, samples, _ = volts.shape
    beams = beam_order.shape[0]
    n_stn, n_chan = lax.axis_size("stn"), lax.axis_size("chan")
    rows = beams // (n_stn * n_chan)
    width = channels * 2 * samples
    operands = (
        volts,
        antenna_tile_weights,
        station_weights,
        tile_station[None, :],
        station_group[None, :],
        station_pos.T,
        beam_dir.T,
        beam_order[None, :],
    )
    operands = [pltpu.with_memory_space_constraint(x, pltpu.HBM) for x in operands]
    partial = pl.pallas_call(
        kernel,
        out_shape=pltpu.VMEM((n_stn * n_chan, rows, width), jnp.bfloat16),
        in_specs=[pl.BlockSpec(memory_space=pltpu.HBM)] * len(operands),
        out_specs=pl.BlockSpec(memory_space=pltpu.VMEM),
        scratch_shapes=[pltpu.VMEM(x.shape, x.dtype) for x in operands]
        + [
            pltpu.VMEM((beams, channels * 2 * (station_weights.shape[2] // TPS)), jnp.bfloat16),
            pltpu.VMEM((volts.shape[3], station_weights.shape[2]), jnp.bfloat16),
            pltpu.SemaphoreType.DMA((len(operands) - 1 + channels // CB,)),
        ],
        compiler_params=pltpu.CompilerParams(vmem_limit_bytes=24 * 2**20),
        name="partial_tied",
    )(*operands)
    parts = lax.all_to_all(
        partial,
        ("stn", "chan"),
        split_axis=0,
        concat_axis=0,
        axis_index_groups=[list(reversed(range(n_stn * n_chan)))],
        tiled=True,
    )
    vmem = pl.BlockSpec(memory_space=pltpu.VMEM)
    tied = pl.pallas_call(
        last_kernel,
        out_shape=jax.ShapeDtypeStruct((rows, 2 * samples, n_chan * channels), jnp.bfloat16),
        in_specs=[vmem],
        out_specs=vmem,
        compiler_params=pltpu.CompilerParams(vmem_limit_bytes=16 * 2**20),
        name="tied_beams",
    )(parts)
    return tied.transpose(0, 2, 1)


def solution(mesh):
    in_specs = (
        P("chan", None, None, "stn"),
        P("chan", None, "stn"),
        P("chan", None, "stn"),
        P("stn"),
        P(),
        P(),
        P(),
        P(),
    )
    out_specs = P(("stn", "chan"), None, None)
    return jax.shard_map(shards, mesh=mesh, in_specs=in_specs, out_specs=out_specs, check_vma=False)
```

```python
import functools
import math

import jax
import jax.numpy as jnp
from jax import lax
from jax.experimental import pallas as pl
from jax.experimental.pallas import tpu as pltpu
from jax.sharding import PartitionSpec as P

TILE_ANTENNAS = 16
TPS = 16
GROUPS = 4
CB = 8
NT = (((1,), (1,)), ((), ()))
SIN = [(-1) ** i * (2 * math.pi) ** (2 * i + 1) / math.factorial(2 * i + 1) for i in range(7)]


def dot_nt(a, b):
    return lax.dot_general(a, b, NT, preferred_element_type=jnp.float32)


def iota(shape, dim):
    return lax.broadcasted_iota(jnp.int32, shape, dim)


def beam_columns(order_ref, dir_ref, start, rows):
    beams = order_ref.shape[1]
    each = beams // (lax.axis_size("stn") * lax.axis_size("chan"))
    order = order_ref[...].astype(jnp.float32)
    lane = iota((rows, beams), 1)
    slot = iota((rows, beams), 0) + start
    own = lane == beams - each - slot // each * each + slot % each
    ids = jnp.sum(jnp.where(own, order, 0.0), axis=1, keepdims=True)
    pick = lane.astype(jnp.float32) == ids
    east = jnp.sum(jnp.where(pick, dir_ref[0:1, :], 0.0), axis=1, keepdims=True)
    north = jnp.sum(jnp.where(pick, dir_ref[1:2, :], 0.0), axis=1, keepdims=True)
    group = ids - GROUPS * jnp.floor(ids * (1.0 / GROUPS))
    return east, north, group


def station_rows(pos_ref, group_ref, stations, lanes):
    total = group_ref.shape[1]
    first = lax.axis_index("stn") * stations
    own = iota((stations, total), 1) == iota((stations, total), 0) + first
    spread = iota((stations, lanes), 0) == iota((stations, lanes), 1) % stations

    def turn(row):
        column = jnp.sum(jnp.where(own, row, 0.0), axis=1, keepdims=True)
        return jnp.sum(jnp.where(spread, column, 0.0), axis=0, keepdims=True)

    return turn(pos_ref[0:1, :]), turn(pos_ref[1:2, :]), turn(group_ref[...].astype(jnp.float32))


def cos_turns(t):
    y = t - jnp.floor(t + 0.5)
    z = 0.25 - jnp.abs(y)
    z2 = z * z
    value = jnp.full_like(z, SIN[-1])
    for coefficient in SIN[-2::-1]:
        value = value * z2 + coefficient
    return value * z


def kernel(
    volt_hbm,
    aw_hbm,
    sw_hbm,
    ts_hbm,
    group_hbm,
    pos_hbm,
    dir_hbm,
    order_hbm,
    out_ref,
    volts,
    aw_ref,
    sw_ref,
    ts_ref,
    group_ref,
    pos_ref,
    dir_ref,
    order_ref,
    tied_ref,
    sum_ref,
    sems,
):
    channels, _, samples, antennas = volt_hbm.shape
    tiles = sw_ref.shape[2]
    stations = tiles // TPS
    groups = channels // CB
    rows_c = 2 * samples
    beams = order_ref.shape[1]
    lanes = CB * 2 * stations
    scale = 1.0 / math.sqrt(group_ref.shape[1])

    def start(source, target, k):
        copy = pltpu.make_async_copy(source, target, sems.at[k])
        copy.start()
        return copy

    def voltages(g):
        part = pl.ds(g * CB, CB)
        return volt_hbm.at[part], volts.at[part]

    pairs = [
        voltages(0),
        (aw_hbm, aw_ref),
        (order_hbm, order_ref),
        (dir_hbm, dir_ref),
        (pos_hbm, pos_ref),
        (group_hbm, group_ref),
        (ts_hbm, ts_ref),
        (sw_hbm, sw_ref),
    ] + [voltages(g) for g in range(1, groups)]
    copies = [start(source, target, k) for k, (source, target) in enumerate(pairs)]
    large = copies[:1] + copies[8:]
    antenna_tile = iota((antennas, tiles), 0) // TILE_ANTENNAS == iota((antennas, tiles), 1)
    sum_ref[...] = antenna_tile.astype(jnp.bfloat16)
    for copy in copies[:2]:
        copy.wait()

    def tile_beams(g):
        products = []
        weights = aw_ref[g * CB : (g + 1) * CB].astype(jnp.float32)
        for c in range(CB):
            w_re, w_im = weights[c, 0:1], weights[c, 1:2]
            v_re = volts[g * CB + c, 0].astype(jnp.float32)
            v_im = volts[g * CB + c, 1].astype(jnp.float32)
            products.append((w_re * v_re - w_im * v_im).astype(jnp.bfloat16))
            products.append((w_re * v_im + w_im * v_re).astype(jnp.bfloat16))
        return jnp.dot(
            jnp.concatenate(products, axis=0), sum_ref[...], preferred_element_type=jnp.float32
        ).astype(jnp.bfloat16)

    last = tile_beams(0)
    for copy in copies[2:9]:
        copy.wait()

    east_s, north_s, group_s = station_rows(pos_ref, group_ref, stations, lanes)
    lane = iota((1, lanes), 1)
    channel_lane = lane // (2 * stations)
    quarter = 0.25 * ((lane // stations) % 2).astype(jnp.float32)
    first_chan = lax.axis_index("chan") * channels
    total_chans = channels * lax.axis_size("chan")
    block = min(64, beams)

    def tied_rows(first):
        east, north, group = beam_columns(order_ref, dir_ref, first, block)
        delay = east * east_s + north * north_s
        member = jnp.where(group == group_s, scale, 0.0)
        for g in range(groups):
            freq = 1.0 + (first_chan + g * CB + channel_lane).astype(jnp.float32) / total_chans
            wave = cos_turns(delay * freq - quarter)
            tied_ref[pl.ds(first, block), g * lanes : (g + 1) * lanes] = (wave * member).astype(
                jnp.bfloat16
            )

    if beams == block:
        tied_rows(0)
    else:

        def body(i, carry):
            tied_rows(pl.multiple_of(i * block, block))
            return carry

        lax.fori_loop(0, beams // block, body, 0)

    member_table = (iota((stations, tiles), 0) == ts_ref[...] % stations).astype(jnp.float32)
    own_channel = iota((lanes, CB * rows_c), 0) // (2 * stations) == iota(
        (lanes, CB * rows_c), 1
    ) // rows_c

    station_rows_of = []
    for g in range(groups):
        swt = sw_ref[g * CB : (g + 1) * CB].astype(jnp.float32)
        right = []
        for c in range(CB):
            re = swt[c, 0:1] * member_table
            im = swt[c, 1:2] * member_table
            right.append(jnp.concatenate([re, -im], axis=1))
            right.append(jnp.concatenate([im, re], axis=1))
        station_rows_of.append(jnp.concatenate(right, axis=0).astype(jnp.bfloat16))

    def tied_beams(g, beams_tile):
        left = []
        for c in range(CB):
            tile_re = beams_tile[c * rows_c : c * rows_c + samples]
            tile_im = beams_tile[c * rows_c + samples : (c + 1) * rows_c]
            left.append(jnp.concatenate([tile_re, tile_im], axis=1))
            left.append(jnp.concatenate([tile_im, -tile_re], axis=1))
        station = dot_nt(station_rows_of[g], jnp.concatenate(left, axis=0))
        station = jnp.where(own_channel, station, 0.0).astype(jnp.bfloat16)
        tied = jnp.dot(
            tied_ref[:, g * lanes : (g + 1) * lanes], station, preferred_element_type=jnp.float32
        )
        devices, rows, _ = out_ref.shape
        out_ref[:, :, g * CB * rows_c : (g + 1) * CB * rows_c] = tied.astype(jnp.bfloat16).reshape(
            devices, rows, CB * rows_c
        )

    for g in range(1, groups):
        if g > 1:
            large[g].wait()
        now = tile_beams(g)
        tied_beams(g - 1, last)
        last = now
    tied_beams(groups - 1, last)


def last_kernel(parts_ref, out_ref):
    n_stn, n_chan = lax.axis_size("stn"), lax.axis_size("chan")
    own_beams, rows_c, total_chans = out_ref.shape
    channels = total_chans // n_chan
    width = channels * rows_c
    parts = parts_ref[...].astype(jnp.float32).reshape(n_stn, n_chan, own_beams, width)
    tied = jnp.sum(parts, axis=0)
    diagonal = iota((channels, width), 0) == iota((channels, width), 1) // rows_c
    spread = (iota((rows_c, width), 0) == iota((rows_c, width), 1) % rows_c).astype(jnp.bfloat16)
    for b in range(own_beams):
        rows = [jnp.where(diagonal, tied[chan, b : b + 1], 0.0) for chan in reversed(range(n_chan))]
        rows = jnp.concatenate(rows, axis=0).astype(jnp.bfloat16)
        out_ref[b] = dot_nt(spread, rows).astype(jnp.bfloat16)


def shards(
    volts,
    antenna_tile_weights,
    station_weights,
    tile_station,
    station_group,
    station_pos,
    beam_dir,
    beam_order,
):
    channels, _, samples, _ = volts.shape
    beams = beam_order.shape[0]
    n_stn, n_chan = lax.axis_size("stn"), lax.axis_size("chan")
    rows = beams // (n_stn * n_chan)
    width = channels * 2 * samples
    operands = (
        volts,
        antenna_tile_weights,
        station_weights,
        tile_station[None, :],
        station_group[None, :],
        station_pos.T,
        beam_dir.T,
        beam_order[None, :],
    )
    operands = [pltpu.with_memory_space_constraint(x, pltpu.HBM) for x in operands]
    partial = pl.pallas_call(
        kernel,
        out_shape=pltpu.VMEM((n_stn * n_chan, rows, width), jnp.bfloat16),
        in_specs=[pl.BlockSpec(memory_space=pltpu.HBM)] * len(operands),
        out_specs=pl.BlockSpec(memory_space=pltpu.VMEM),
        scratch_shapes=[pltpu.VMEM(x.shape, x.dtype) for x in operands]
        + [
            pltpu.VMEM((beams, channels * 2 * (station_weights.shape[2] // TPS)), jnp.bfloat16),
            pltpu.VMEM((volts.shape[3], station_weights.shape[2]), jnp.bfloat16),
            pltpu.SemaphoreType.DMA((len(operands) - 1 + channels // CB,)),
        ],
        compiler_params=pltpu.CompilerParams(vmem_limit_bytes=24 * 2**20),
        name="partial_tied",
    )(*operands)
    parts = lax.all_to_all(
        partial,
        ("stn", "chan"),
        split_axis=0,
        concat_axis=0,
        axis_index_groups=[list(reversed(range(n_stn * n_chan)))],
        tiled=True,
    )
    vmem = pl.BlockSpec(memory_space=pltpu.VMEM)
    tied = pl.pallas_call(
        last_kernel,
        out_shape=jax.ShapeDtypeStruct((rows, 2 * samples, n_chan * channels), jnp.bfloat16),
        in_specs=[vmem],
        out_specs=vmem,
        compiler_params=pltpu.CompilerParams(vmem_limit_bytes=16 * 2**20),
        name="tied_beams",
    )(parts)
    return tied.transpose(0, 2, 1)


def solution(mesh):
    in_specs = (
        P("chan", None, None, "stn"),
        P("chan", None, "stn"),
        P("chan", None, "stn"),
        P("stn"),
        P(),
        P(),
        P(),
        P(),
    )
    out_specs = P(("stn", "chan"), None, None)
    return jax.shard_map(shards, mesh=mesh, in_specs=in_specs, out_specs=out_specs, check_vma=False)
```

```python
import functools
import math

import jax
import jax.numpy as jnp
from jax import lax
from jax.experimental import pallas as pl
from jax.experimental.pallas import tpu as pltpu
from jax.sharding import PartitionSpec as P

TILE_ANTENNAS = 16
TPS = 16
GROUPS = 4
CB = 8
NT = (((1,), (1,)), ((), ()))
SIN = [(-1) ** i * (2 * math.pi) ** (2 * i + 1) / math.factorial(2 * i + 1) for i in range(7)]


def dot_nt(a, b):
    return lax.dot_general(a, b, NT, preferred_element_type=jnp.float32)


def iota(shape, dim):
    return lax.broadcasted_iota(jnp.int32, shape, dim)


def beam_columns(order_ref, dir_ref, start, rows):
    beams = order_ref.shape[1]
    each = beams // (lax.axis_size("stn") * lax.axis_size("chan"))
    order = order_ref[...].astype(jnp.float32)
    lane = iota((rows, beams), 1)
    slot = iota((rows, beams), 0) + start
    own = lane == beams - each - slot // each * each + slot % each
    ids = jnp.sum(jnp.where(own, order, 0.0), axis=1, keepdims=True)
    pick = lane.astype(jnp.float32) == ids
    east = jnp.sum(jnp.where(pick, dir_ref[0:1, :], 0.0), axis=1, keepdims=True)
    north = jnp.sum(jnp.where(pick, dir_ref[1:2, :], 0.0), axis=1, keepdims=True)
    group = ids - GROUPS * jnp.floor(ids * (1.0 / GROUPS))
    return east, north, group


def station_rows(pos_ref, group_ref, stations, lanes):
    total = group_ref.shape[1]
    first = lax.axis_index("stn") * stations
    own = iota((stations, total), 1) == iota((stations, total), 0) + first
    spread = iota((stations, lanes), 0) == iota((stations, lanes), 1) % stations

    def turn(row):
        column = jnp.sum(jnp.where(own, row, 0.0), axis=1, keepdims=True)
        return jnp.sum(jnp.where(spread, column, 0.0), axis=0, keepdims=True)

    return turn(pos_ref[0:1, :]), turn(pos_ref[1:2, :]), turn(group_ref[...].astype(jnp.float32))


def cos_turns(t):
    y = t - jnp.floor(t + 0.5)
    z = 0.25 - jnp.abs(y)
    z2 = z * z
    value = jnp.full_like(z, SIN[-1])
    for coefficient in SIN[-2::-1]:
        value = value * z2 + coefficient
    return value * z


def kernel(
    volt_hbm,
    aw_hbm,
    sw_hbm,
    ts_hbm,
    group_hbm,
    pos_hbm,
    dir_hbm,
    order_hbm,
    out_ref,
    volts,
    aw_ref,
    sw_ref,
    ts_ref,
    group_ref,
    pos_ref,
    dir_ref,
    order_ref,
    tied_ref,
    sum_ref,
    sems,
):
    channels, _, samples, antennas = volt_hbm.shape
    tiles = sw_ref.shape[2]
    stations = tiles // TPS
    groups = channels // CB
    rows_c = 2 * samples
    beams = order_ref.shape[1]
    lanes = CB * 2 * stations
    scale = 1.0 / math.sqrt(group_ref.shape[1])

    def start(source, target, k):
        copy = pltpu.make_async_copy(source, target, sems.at[k])
        copy.start()
        return copy

    def voltages(g):
        part = pl.ds(g * CB, CB)
        return volt_hbm.at[part], volts.at[part]

    pairs = [
        voltages(0),
        (aw_hbm, aw_ref),
        (order_hbm, order_ref),
        (dir_hbm, dir_ref),
        (pos_hbm, pos_ref),
        (group_hbm, group_ref),
        (ts_hbm, ts_ref),
        (sw_hbm, sw_ref),
    ] + [voltages(g) for g in range(1, groups)]
    copies = [start(source, target, k) for k, (source, target) in enumerate(pairs)]
    large = copies[:1] + copies[8:]
    antenna_tile = iota((antennas, tiles), 0) // TILE_ANTENNAS == iota((antennas, tiles), 1)
    sum_ref[...] = antenna_tile.astype(jnp.bfloat16)
    for copy in copies[:2]:
        copy.wait()

    def tile_beams(g):
        products = []
        for c in range(CB):
            w_re = jnp.broadcast_to(aw_ref[g * CB + c, 0:1], (samples, antennas))
            w_im = jnp.broadcast_to(aw_ref[g * CB + c, 1:2], (samples, antennas))
            v_re, v_im = volts[g * CB + c, 0], volts[g * CB + c, 1]
            products.append(w_re * v_re - w_im * v_im)
            products.append(w_re * v_im + w_im * v_re)
        return jnp.dot(
            jnp.concatenate(products, axis=0), sum_ref[...], preferred_element_type=jnp.float32
        ).astype(jnp.bfloat16)

    last = tile_beams(0)
    for copy in copies[2:9]:
        copy.wait()

    east_s, north_s, group_s = station_rows(pos_ref, group_ref, stations, lanes)
    lane = iota((1, lanes), 1)
    channel_lane = lane // (2 * stations)
    quarter = 0.25 * ((lane // stations) % 2).astype(jnp.float32)
    first_chan = lax.axis_index("chan") * channels
    total_chans = channels * lax.axis_size("chan")
    block = min(64, beams)

    def tied_rows(first):
        east, north, group = beam_columns(order_ref, dir_ref, first, block)
        delay = east * east_s + north * north_s
        member = jnp.where(group == group_s, scale, 0.0)
        for g in range(groups):
            freq = 1.0 + (first_chan + g * CB + channel_lane).astype(jnp.float32) / total_chans
            wave = cos_turns(delay * freq - quarter)
            tied_ref[pl.ds(first, block), g * lanes : (g + 1) * lanes] = (wave * member).astype(
                jnp.bfloat16
            )

    if beams == block:
        tied_rows(0)
    else:

        def body(i, carry):
            tied_rows(pl.multiple_of(i * block, block))
            return carry

        lax.fori_loop(0, beams // block, body, 0)

    member_table = (iota((stations, tiles), 0) == ts_ref[...] % stations).astype(jnp.float32)
    own_channel = iota((lanes, CB * rows_c), 0) // (2 * stations) == iota(
        (lanes, CB * rows_c), 1
    ) // rows_c

    station_rows_of = []
    for g in range(groups):
        swt = sw_ref[g * CB : (g + 1) * CB].astype(jnp.float32)
        right = []
        for c in range(CB):
            re = swt[c, 0:1] * member_table
            im = swt[c, 1:2] * member_table
            right.append(jnp.concatenate([re, -im], axis=1))
            right.append(jnp.concatenate([im, re], axis=1))
        station_rows_of.append(jnp.concatenate(right, axis=0).astype(jnp.bfloat16))

    def tied_beams(g, beams_tile):
        left = []
        for c in range(CB):
            tile_re = beams_tile[c * rows_c : c * rows_c + samples]
            tile_im = beams_tile[c * rows_c + samples : (c + 1) * rows_c]
            left.append(jnp.concatenate([tile_re, tile_im], axis=1))
            left.append(jnp.concatenate([tile_im, -tile_re], axis=1))
        station = dot_nt(station_rows_of[g], jnp.concatenate(left, axis=0))
        station = jnp.where(own_channel, station, 0.0).astype(jnp.bfloat16)
        tied = jnp.dot(
            tied_ref[:, g * lanes : (g + 1) * lanes], station, preferred_element_type=jnp.float32
        )
        devices, rows, _ = out_ref.shape
        out_ref[:, :, g * CB * rows_c : (g + 1) * CB * rows_c] = tied.astype(jnp.bfloat16).reshape(
            devices, rows, CB * rows_c
        )

    for g in range(1, groups):
        if g > 1:
            large[g].wait()
        now = tile_beams(g)
        tied_beams(g - 1, last)
        last = now
    tied_beams(groups - 1, last)


def last_kernel(parts_ref, out_ref):
    n_stn, n_chan = lax.axis_size("stn"), lax.axis_size("chan")
    own_beams, rows_c, total_chans = out_ref.shape
    channels = total_chans // n_chan
    width = channels * rows_c
    parts = parts_ref[...].astype(jnp.float32).reshape(n_stn, n_chan, own_beams, width)
    tied = jnp.sum(parts, axis=0)
    diagonal = iota((channels, width), 0) == iota((channels, width), 1) // rows_c
    spread = (iota((rows_c, width), 0) == iota((rows_c, width), 1) % rows_c).astype(jnp.bfloat16)
    for b in range(own_beams):
        rows = [jnp.where(diagonal, tied[chan, b : b + 1], 0.0) for chan in reversed(range(n_chan))]
        rows = jnp.concatenate(rows, axis=0).astype(jnp.bfloat16)
        out_ref[b] = dot_nt(spread, rows).astype(jnp.bfloat16)


def shards(
    volts,
    antenna_tile_weights,
    station_weights,
    tile_station,
    station_group,
    station_pos,
    beam_dir,
    beam_order,
):
    channels, _, samples, _ = volts.shape
    beams = beam_order.shape[0]
    n_stn, n_chan = lax.axis_size("stn"), lax.axis_size("chan")
    rows = beams // (n_stn * n_chan)
    width = channels * 2 * samples
    operands = (
        volts,
        antenna_tile_weights,
        station_weights,
        tile_station[None, :],
        station_group[None, :],
        station_pos.T,
        beam_dir.T,
        beam_order[None, :],
    )
    operands = [pltpu.with_memory_space_constraint(x, pltpu.HBM) for x in operands]
    partial = pl.pallas_call(
        kernel,
        out_shape=pltpu.VMEM((n_stn * n_chan, rows, width), jnp.bfloat16),
        in_specs=[pl.BlockSpec(memory_space=pltpu.HBM)] * len(operands),
        out_specs=pl.BlockSpec(memory_space=pltpu.VMEM),
        scratch_shapes=[pltpu.VMEM(x.shape, x.dtype) for x in operands]
        + [
            pltpu.VMEM((beams, channels * 2 * (station_weights.shape[2] // TPS)), jnp.bfloat16),
            pltpu.VMEM((volts.shape[3], station_weights.shape[2]), jnp.bfloat16),
            pltpu.SemaphoreType.DMA((len(operands) - 1 + channels // CB,)),
        ],
        compiler_params=pltpu.CompilerParams(vmem_limit_bytes=24 * 2**20),
        name="partial_tied",
    )(*operands)
    parts = lax.all_to_all(
        partial,
        ("stn", "chan"),
        split_axis=0,
        concat_axis=0,
        axis_index_groups=[list(reversed(range(n_stn * n_chan)))],
        tiled=True,
    )
    vmem = pl.BlockSpec(memory_space=pltpu.VMEM)
    tied = pl.pallas_call(
        last_kernel,
        out_shape=jax.ShapeDtypeStruct((rows, 2 * samples, n_chan * channels), jnp.bfloat16),
        in_specs=[vmem],
        out_specs=vmem,
        compiler_params=pltpu.CompilerParams(vmem_limit_bytes=16 * 2**20),
        name="tied_beams",
    )(parts)
    return tied.transpose(0, 2, 1)


def solution(mesh):
    in_specs = (
        P("chan", None, None, "stn"),
        P("chan", None, "stn"),
        P("chan", None, "stn"),
        P("stn"),
        P(),
        P(),
        P(),
        P(),
    )
    out_specs = P(("stn", "chan"), None, None)
    return jax.shard_map(shards, mesh=mesh, in_specs=in_specs, out_specs=out_specs, check_vma=False)
```

```python
import functools
import math

import jax
import jax.numpy as jnp
from jax import lax
from jax.experimental import pallas as pl
from jax.experimental.pallas import tpu as pltpu
from jax.sharding import PartitionSpec as P

TILE_ANTENNAS = 16
TPS = 16
GROUPS = 4
CB = 8
PIECE = 512
NT = (((1,), (1,)), ((), ()))
SIN = [(-1) ** i * (2 * math.pi) ** (2 * i + 1) / math.factorial(2 * i + 1) for i in range(7)]


def dot_nt(a, b):
    return lax.dot_general(a, b, NT, preferred_element_type=jnp.float32)


def iota(shape, dim):
    return lax.broadcasted_iota(jnp.int32, shape, dim)


def beam_columns(order_ref, dir_ref, start, rows):
    beams = order_ref.shape[1]
    each = beams // (lax.axis_size("stn") * lax.axis_size("chan"))
    order = order_ref[...].astype(jnp.float32)
    lane = iota((rows, beams), 1)
    slot = iota((rows, beams), 0) + start
    own = lane == beams - each - slot // each * each + slot % each
    ids = jnp.sum(jnp.where(own, order, 0.0), axis=1, keepdims=True)
    pick = lane.astype(jnp.float32) == ids
    east = jnp.sum(jnp.where(pick, dir_ref[0:1, :], 0.0), axis=1, keepdims=True)
    north = jnp.sum(jnp.where(pick, dir_ref[1:2, :], 0.0), axis=1, keepdims=True)
    group = ids - GROUPS * jnp.floor(ids * (1.0 / GROUPS))
    return east, north, group


def station_rows(pos_ref, group_ref, stations, lanes):
    total = group_ref.shape[1]
    first = lax.axis_index("stn") * stations
    own = iota((stations, total), 1) == iota((stations, total), 0) + first
    spread = iota((stations, lanes), 0) == iota((stations, lanes), 1) % stations

    def turn(row):
        column = jnp.sum(jnp.where(own, row, 0.0), axis=1, keepdims=True)
        return jnp.sum(jnp.where(spread, column, 0.0), axis=0, keepdims=True)

    return turn(pos_ref[0:1, :]), turn(pos_ref[1:2, :]), turn(group_ref[...].astype(jnp.float32))


def cos_turns(t):
    y = t - jnp.floor(t + 0.5)
    z = 0.25 - jnp.abs(y)
    z2 = z * z
    value = jnp.full_like(z, SIN[-1])
    for coefficient in SIN[-2::-1]:
        value = value * z2 + coefficient
    return value * z


def kernel(
    volt_hbm,
    aw_hbm,
    sw_hbm,
    ts_hbm,
    group_hbm,
    pos_hbm,
    dir_hbm,
    order_hbm,
    out_ref,
    volts,
    aw_ref,
    sw_ref,
    ts_ref,
    group_ref,
    pos_ref,
    dir_ref,
    order_ref,
    tied_ref,
    sum_ref,
    sems,
):
    channels, _, samples, antennas = volt_hbm.shape
    tiles = sw_ref.shape[2]
    stations = tiles // TPS
    groups = channels // CB
    rows_c = 2 * samples
    beams = order_ref.shape[1]
    lanes = CB * 2 * stations
    scale = 1.0 / math.sqrt(group_ref.shape[1])

    def start(source, target, k):
        copy = pltpu.make_async_copy(source, target, sems.at[k])
        copy.start()
        return copy

    def voltages(g):
        part = pl.ds(g * CB, CB)
        return volt_hbm.at[part], volts.at[part]

    pairs = [
        voltages(0),
        (aw_hbm, aw_ref),
        (order_hbm, order_ref),
        (dir_hbm, dir_ref),
        (pos_hbm, pos_ref),
        (group_hbm, group_ref),
        (ts_hbm, ts_ref),
        (sw_hbm, sw_ref),
    ] + [voltages(g) for g in range(1, groups)]
    copies = [start(source, target, k) for k, (source, target) in enumerate(pairs)]
    large = copies[:1] + copies[8:]
    antenna_tile = iota((antennas, tiles), 0) // TILE_ANTENNAS == iota((antennas, tiles), 1)
    sum_ref[...] = antenna_tile.astype(jnp.bfloat16)
    for copy in copies[:2]:
        copy.wait()

    def tile_beams(g):
        weights = aw_ref[g * CB : (g + 1) * CB].astype(jnp.float32)
        sums = None
        for first in range(0, antennas, PIECE):
            part = slice(first, first + PIECE)
            products = []
            for c in range(CB):
                w_re = jnp.broadcast_to(weights[c, 0:1, part], (samples, PIECE))
                w_im = jnp.broadcast_to(weights[c, 1:2, part], (samples, PIECE))
                w_re, w_im = w_re.astype(jnp.bfloat16), w_im.astype(jnp.bfloat16)
                v_re, v_im = volts[g * CB + c, 0, :, part], volts[g * CB + c, 1, :, part]
                products.append(w_re * v_re - w_im * v_im)
                products.append(w_re * v_im + w_im * v_re)
            piece = jnp.dot(
                jnp.concatenate(products, axis=0),
                sum_ref[part, :],
                preferred_element_type=jnp.float32,
            )
            sums = piece if sums is None else sums + piece
        return sums.astype(jnp.bfloat16)

    last = tile_beams(0)
    for copy in copies[2:9]:
        copy.wait()

    east_s, north_s, group_s = station_rows(pos_ref, group_ref, stations, lanes)
    lane = iota((1, lanes), 1)
    channel_lane = lane // (2 * stations)
    quarter = 0.25 * ((lane // stations) % 2).astype(jnp.float32)
    first_chan = lax.axis_index("chan") * channels
    total_chans = channels * lax.axis_size("chan")
    block = min(64, beams)

    def tied_rows(first):
        east, north, group = beam_columns(order_ref, dir_ref, first, block)
        delay = east * east_s + north * north_s
        member = jnp.where(group == group_s, scale, 0.0)
        for g in range(groups):
            freq = 1.0 + (first_chan + g * CB + channel_lane).astype(jnp.float32) / total_chans
            wave = cos_turns(delay * freq - quarter)
            tied_ref[pl.ds(first, block), g * lanes : (g + 1) * lanes] = (wave * member).astype(
                jnp.bfloat16
            )

    if beams == block:
        tied_rows(0)
    else:

        def body(i, carry):
            tied_rows(pl.multiple_of(i * block, block))
            return carry

        lax.fori_loop(0, beams // block, body, 0)

    member_table = (iota((stations, tiles), 0) == ts_ref[...] % stations).astype(jnp.float32)
    own_channel = iota((lanes, CB * rows_c), 0) // (2 * stations) == iota(
        (lanes, CB * rows_c), 1
    ) // rows_c

    station_rows_of = []
    for g in range(groups):
        swt = sw_ref[g * CB : (g + 1) * CB].astype(jnp.float32)
        right = []
        for c in range(CB):
            re = swt[c, 0:1] * member_table
            im = swt[c, 1:2] * member_table
            right.append(jnp.concatenate([re, -im], axis=1))
            right.append(jnp.concatenate([im, re], axis=1))
        station_rows_of.append(jnp.concatenate(right, axis=0).astype(jnp.bfloat16))

    def tied_beams(g, beams_tile):
        left = []
        for c in range(CB):
            tile_re = beams_tile[c * rows_c : c * rows_c + samples]
            tile_im = beams_tile[c * rows_c + samples : (c + 1) * rows_c]
            left.append(jnp.concatenate([tile_re, tile_im], axis=1))
            left.append(jnp.concatenate([tile_im, -tile_re], axis=1))
        station = dot_nt(station_rows_of[g], jnp.concatenate(left, axis=0))
        station = jnp.where(own_channel, station, 0.0).astype(jnp.bfloat16)
        tied = jnp.dot(
            tied_ref[:, g * lanes : (g + 1) * lanes], station, preferred_element_type=jnp.float32
        )
        devices, rows, _ = out_ref.shape
        out_ref[:, :, g * CB * rows_c : (g + 1) * CB * rows_c] = tied.astype(jnp.bfloat16).reshape(
            devices, rows, CB * rows_c
        )

    for g in range(1, groups):
        if g > 1:
            large[g].wait()
        now = tile_beams(g)
        tied_beams(g - 1, last)
        last = now
    tied_beams(groups - 1, last)


def last_kernel(parts_ref, out_ref):
    n_stn, n_chan = lax.axis_size("stn"), lax.axis_size("chan")
    own_beams, rows_c, total_chans = out_ref.shape
    channels = total_chans // n_chan
    width = channels * rows_c
    parts = parts_ref[...].astype(jnp.float32).reshape(n_stn, n_chan, own_beams, width)
    tied = jnp.sum(parts, axis=0)
    diagonal = iota((channels, width), 0) == iota((channels, width), 1) // rows_c
    spread = (iota((rows_c, width), 0) == iota((rows_c, width), 1) % rows_c).astype(jnp.bfloat16)
    for b in range(own_beams):
        rows = [jnp.where(diagonal, tied[chan, b : b + 1], 0.0) for chan in reversed(range(n_chan))]
        rows = jnp.concatenate(rows, axis=0).astype(jnp.bfloat16)
        out_ref[b] = dot_nt(spread, rows).astype(jnp.bfloat16)


def shards(
    volts,
    antenna_tile_weights,
    station_weights,
    tile_station,
    station_group,
    station_pos,
    beam_dir,
    beam_order,
):
    channels, _, samples, _ = volts.shape
    beams = beam_order.shape[0]
    n_stn, n_chan = lax.axis_size("stn"), lax.axis_size("chan")
    rows = beams // (n_stn * n_chan)
    width = channels * 2 * samples
    operands = (
        volts,
        antenna_tile_weights,
        station_weights,
        tile_station[None, :],
        station_group[None, :],
        station_pos.T,
        beam_dir.T,
        beam_order[None, :],
    )
    operands = [pltpu.with_memory_space_constraint(x, pltpu.HBM) for x in operands]
    partial = pl.pallas_call(
        kernel,
        out_shape=pltpu.VMEM((n_stn * n_chan, rows, width), jnp.bfloat16),
        in_specs=[pl.BlockSpec(memory_space=pltpu.HBM)] * len(operands),
        out_specs=pl.BlockSpec(memory_space=pltpu.VMEM),
        scratch_shapes=[pltpu.VMEM(x.shape, x.dtype) for x in operands]
        + [
            pltpu.VMEM((beams, channels * 2 * (station_weights.shape[2] // TPS)), jnp.bfloat16),
            pltpu.VMEM((volts.shape[3], station_weights.shape[2]), jnp.bfloat16),
            pltpu.SemaphoreType.DMA((len(operands) - 1 + channels // CB,)),
        ],
        compiler_params=pltpu.CompilerParams(vmem_limit_bytes=24 * 2**20),
        name="partial_tied",
    )(*operands)
    parts = lax.all_to_all(
        partial,
        ("stn", "chan"),
        split_axis=0,
        concat_axis=0,
        axis_index_groups=[list(reversed(range(n_stn * n_chan)))],
        tiled=True,
    )
    vmem = pl.BlockSpec(memory_space=pltpu.VMEM)
    tied = pl.pallas_call(
        last_kernel,
        out_shape=jax.ShapeDtypeStruct((rows, 2 * samples, n_chan * channels), jnp.bfloat16),
        in_specs=[vmem],
        out_specs=vmem,
        compiler_params=pltpu.CompilerParams(vmem_limit_bytes=16 * 2**20),
        name="tied_beams",
    )(parts)
    return tied.transpose(0, 2, 1)


def solution(mesh):
    in_specs = (
        P("chan", None, None, "stn"),
        P("chan", None, "stn"),
        P("chan", None, "stn"),
        P("stn"),
        P(),
        P(),
        P(),
        P(),
    )
    out_specs = P(("stn", "chan"), None, None)
    return jax.shard_map(shards, mesh=mesh, in_specs=in_specs, out_specs=out_specs, check_vma=False)
```

```python
import functools
import math

import jax
import jax.numpy as jnp
from jax import lax
from jax.experimental import pallas as pl
from jax.experimental.pallas import tpu as pltpu
from jax.sharding import PartitionSpec as P

TILE_ANTENNAS = 16
TPS = 16
GROUPS = 4
CB = 8
QUEUES = (0, 1, 1, 1, 1, 1, 1, 1, 1, 0)
NT = (((1,), (1,)), ((), ()))
SIN = [(-1) ** i * (2 * math.pi) ** (2 * i + 1) / math.factorial(2 * i + 1) for i in range(7)]


def dot_nt(a, b):
    return lax.dot_general(a, b, NT, preferred_element_type=jnp.float32)


def iota(shape, dim):
    return lax.broadcasted_iota(jnp.int32, shape, dim)


def beam_columns(order_ref, dir_ref, start, rows):
    beams = order_ref.shape[1]
    each = beams // (lax.axis_size("stn") * lax.axis_size("chan"))
    order = order_ref[...].astype(jnp.float32)
    lane = iota((rows, beams), 1)
    slot = iota((rows, beams), 0) + start
    own = lane == beams - each - slot // each * each + slot % each
    ids = jnp.sum(jnp.where(own, order, 0.0), axis=1, keepdims=True)
    pick = lane.astype(jnp.float32) == ids
    east = jnp.sum(jnp.where(pick, dir_ref[0:1, :], 0.0), axis=1, keepdims=True)
    north = jnp.sum(jnp.where(pick, dir_ref[1:2, :], 0.0), axis=1, keepdims=True)
    group = ids - GROUPS * jnp.floor(ids * (1.0 / GROUPS))
    return east, north, group


def station_rows(pos_ref, group_ref, stations, lanes):
    total = group_ref.shape[1]
    first = lax.axis_index("stn") * stations
    own = iota((stations, total), 1) == iota((stations, total), 0) + first
    spread = iota((stations, lanes), 0) == iota((stations, lanes), 1) % stations

    def turn(row):
        column = jnp.sum(jnp.where(own, row, 0.0), axis=1, keepdims=True)
        return jnp.sum(jnp.where(spread, column, 0.0), axis=0, keepdims=True)

    return turn(pos_ref[0:1, :]), turn(pos_ref[1:2, :]), turn(group_ref[...].astype(jnp.float32))


def cos_turns(t):
    y = t - jnp.floor(t + 0.5)
    z = 0.25 - jnp.abs(y)
    z2 = z * z
    value = jnp.full_like(z, SIN[-1])
    for coefficient in SIN[-2::-1]:
        value = value * z2 + coefficient
    return value * z


def kernel(
    volt_hbm,
    aw_hbm,
    sw_hbm,
    ts_hbm,
    group_hbm,
    pos_hbm,
    dir_hbm,
    order_hbm,
    out_ref,
    volts,
    aw_ref,
    sw_ref,
    ts_ref,
    group_ref,
    pos_ref,
    dir_ref,
    order_ref,
    tied_ref,
    sum_ref,
    sems,
):
    channels, _, samples, antennas = volt_hbm.shape
    tiles = sw_ref.shape[2]
    stations = tiles // TPS
    groups = channels // CB
    rows_c = 2 * samples
    beams = order_ref.shape[1]
    lanes = CB * 2 * stations
    scale = 1.0 / math.sqrt(group_ref.shape[1])

    def start(source, target, k):
        copy = pltpu.make_async_copy(source, target, sems.at[k])
        copy.start(priority=QUEUES[k])
        return copy

    def voltages(g):
        part = pl.ds(g * CB, CB)
        return volt_hbm.at[part], volts.at[part]

    pairs = [
        voltages(0),
        (aw_hbm, aw_ref),
        (order_hbm, order_ref),
        (dir_hbm, dir_ref),
        (pos_hbm, pos_ref),
        (group_hbm, group_ref),
        (ts_hbm, ts_ref),
        (sw_hbm, sw_ref),
    ] + [voltages(g) for g in range(1, groups)]
    copies = [start(source, target, k) for k, (source, target) in enumerate(pairs)]
    large = copies[:1] + copies[8:]
    antenna_tile = iota((antennas, tiles), 0) // TILE_ANTENNAS == iota((antennas, tiles), 1)
    sum_ref[...] = antenna_tile.astype(jnp.bfloat16)
    for copy in copies[:2]:
        copy.wait()

    def tile_beams(g):
        products = []
        weights = aw_ref[g * CB : (g + 1) * CB].astype(jnp.float32)
        for c in range(CB):
            w_re = jnp.broadcast_to(weights[c, 0:1], (samples, antennas)).astype(jnp.bfloat16)
            w_im = jnp.broadcast_to(weights[c, 1:2], (samples, antennas)).astype(jnp.bfloat16)
            v_re, v_im = volts[g * CB + c, 0], volts[g * CB + c, 1]
            products.append(w_re * v_re - w_im * v_im)
            products.append(w_re * v_im + w_im * v_re)
        return jnp.dot(
            jnp.concatenate(products, axis=0), sum_ref[...], preferred_element_type=jnp.float32
        ).astype(jnp.bfloat16)

    last = tile_beams(0)
    for copy in copies[2:9]:
        copy.wait()

    east_s, north_s, group_s = station_rows(pos_ref, group_ref, stations, lanes)
    lane = iota((1, lanes), 1)
    channel_lane = lane // (2 * stations)
    quarter = 0.25 * ((lane // stations) % 2).astype(jnp.float32)
    first_chan = lax.axis_index("chan") * channels
    total_chans = channels * lax.axis_size("chan")
    block = min(64, beams)

    def tied_rows(first):
        east, north, group = beam_columns(order_ref, dir_ref, first, block)
        delay = east * east_s + north * north_s
        member = jnp.where(group == group_s, scale, 0.0)
        for g in range(groups):
            freq = 1.0 + (first_chan + g * CB + channel_lane).astype(jnp.float32) / total_chans
            wave = cos_turns(delay * freq - quarter)
            tied_ref[pl.ds(first, block), g * lanes : (g + 1) * lanes] = (wave * member).astype(
                jnp.bfloat16
            )

    if beams == block:
        tied_rows(0)
    else:

        def body(i, carry):
            tied_rows(pl.multiple_of(i * block, block))
            return carry

        lax.fori_loop(0, beams // block, body, 0)

    member_table = (iota((stations, tiles), 0) == ts_ref[...] % stations).astype(jnp.float32)
    own_channel = iota((lanes, CB * rows_c), 0) // (2 * stations) == iota(
        (lanes, CB * rows_c), 1
    ) // rows_c

    station_rows_of = []
    for g in range(groups):
        swt = sw_ref[g * CB : (g + 1) * CB].astype(jnp.float32)
        right = []
        for c in range(CB):
            re = swt[c, 0:1] * member_table
            im = swt[c, 1:2] * member_table
            right.append(jnp.concatenate([re, -im], axis=1))
            right.append(jnp.concatenate([im, re], axis=1))
        station_rows_of.append(jnp.concatenate(right, axis=0).astype(jnp.bfloat16))

    def tied_beams(g, beams_tile):
        left = []
        for c in range(CB):
            tile_re = beams_tile[c * rows_c : c * rows_c + samples]
            tile_im = beams_tile[c * rows_c + samples : (c + 1) * rows_c]
            left.append(jnp.concatenate([tile_re, tile_im], axis=1))
            left.append(jnp.concatenate([tile_im, -tile_re], axis=1))
        station = dot_nt(station_rows_of[g], jnp.concatenate(left, axis=0))
        station = jnp.where(own_channel, station, 0.0).astype(jnp.bfloat16)
        tied = jnp.dot(
            tied_ref[:, g * lanes : (g + 1) * lanes], station, preferred_element_type=jnp.float32
        )
        devices, rows, _ = out_ref.shape
        out_ref[:, :, g * CB * rows_c : (g + 1) * CB * rows_c] = tied.astype(jnp.bfloat16).reshape(
            devices, rows, CB * rows_c
        )

    for g in range(1, groups):
        if g > 1:
            large[g].wait()
        now = tile_beams(g)
        tied_beams(g - 1, last)
        last = now
    tied_beams(groups - 1, last)


def last_kernel(parts_ref, out_ref):
    n_stn, n_chan = lax.axis_size("stn"), lax.axis_size("chan")
    own_beams, rows_c, total_chans = out_ref.shape
    channels = total_chans // n_chan
    width = channels * rows_c
    parts = parts_ref[...].astype(jnp.float32).reshape(n_stn, n_chan, own_beams, width)
    tied = jnp.sum(parts, axis=0)
    diagonal = iota((channels, width), 0) == iota((channels, width), 1) // rows_c
    spread = (iota((rows_c, width), 0) == iota((rows_c, width), 1) % rows_c).astype(jnp.bfloat16)
    for b in range(own_beams):
        rows = [jnp.where(diagonal, tied[chan, b : b + 1], 0.0) for chan in reversed(range(n_chan))]
        rows = jnp.concatenate(rows, axis=0).astype(jnp.bfloat16)
        out_ref[b] = dot_nt(spread, rows).astype(jnp.bfloat16)


def shards(
    volts,
    antenna_tile_weights,
    station_weights,
    tile_station,
    station_group,
    station_pos,
    beam_dir,
    beam_order,
):
    channels, _, samples, _ = volts.shape
    beams = beam_order.shape[0]
    n_stn, n_chan = lax.axis_size("stn"), lax.axis_size("chan")
    rows = beams // (n_stn * n_chan)
    width = channels * 2 * samples
    operands = (
        volts,
        antenna_tile_weights,
        station_weights,
        tile_station[None, :],
        station_group[None, :],
        station_pos.T,
        beam_dir.T,
        beam_order[None, :],
    )
    operands = [pltpu.with_memory_space_constraint(x, pltpu.HBM) for x in operands]
    partial = pl.pallas_call(
        kernel,
        out_shape=pltpu.VMEM((n_stn * n_chan, rows, width), jnp.bfloat16),
        in_specs=[pl.BlockSpec(memory_space=pltpu.HBM)] * len(operands),
        out_specs=pl.BlockSpec(memory_space=pltpu.VMEM),
        scratch_shapes=[pltpu.VMEM(x.shape, x.dtype) for x in operands]
        + [
            pltpu.VMEM((beams, channels * 2 * (station_weights.shape[2] // TPS)), jnp.bfloat16),
            pltpu.VMEM((volts.shape[3], station_weights.shape[2]), jnp.bfloat16),
            pltpu.SemaphoreType.DMA((len(operands) - 1 + channels // CB,)),
        ],
        compiler_params=pltpu.CompilerParams(vmem_limit_bytes=24 * 2**20),
        name="partial_tied",
    )(*operands)
    parts = lax.all_to_all(
        partial,
        ("stn", "chan"),
        split_axis=0,
        concat_axis=0,
        axis_index_groups=[list(reversed(range(n_stn * n_chan)))],
        tiled=True,
    )
    vmem = pl.BlockSpec(memory_space=pltpu.VMEM)
    tied = pl.pallas_call(
        last_kernel,
        out_shape=jax.ShapeDtypeStruct((rows, 2 * samples, n_chan * channels), jnp.bfloat16),
        in_specs=[vmem],
        out_specs=vmem,
        compiler_params=pltpu.CompilerParams(vmem_limit_bytes=16 * 2**20),
        name="tied_beams",
    )(parts)
    return tied.transpose(0, 2, 1)


def solution(mesh):
    in_specs = (
        P("chan", None, None, "stn"),
        P("chan", None, "stn"),
        P("chan", None, "stn"),
        P("stn"),
        P(),
        P(),
        P(),
        P(),
    )
    out_specs = P(("stn", "chan"), None, None)
    return jax.shard_map(shards, mesh=mesh, in_specs=in_specs, out_specs=out_specs, check_vma=False)
```

```python
import functools
import math

import jax
import jax.numpy as jnp
from jax import lax
from jax.experimental import pallas as pl
from jax.experimental.pallas import tpu as pltpu
from jax.sharding import PartitionSpec as P

TILE_ANTENNAS = 16
TPS = 16
GROUPS = 4
CB = 8
NT = (((1,), (1,)), ((), ()))
SIN = [(-1) ** i * (2 * math.pi) ** (2 * i + 1) / math.factorial(2 * i + 1) for i in range(7)]


def dot_nt(a, b):
    return lax.dot_general(a, b, NT, preferred_element_type=jnp.float32)


def iota(shape, dim):
    return lax.broadcasted_iota(jnp.int32, shape, dim)


def beam_columns(order_ref, dir_ref, start, rows):
    beams = order_ref.shape[1]
    each = beams // (lax.axis_size("stn") * lax.axis_size("chan"))
    order = order_ref[...].astype(jnp.float32)
    lane = iota((rows, beams), 1)
    slot = iota((rows, beams), 0) + start
    own = lane == beams - each - slot // each * each + slot % each
    ids = jnp.sum(jnp.where(own, order, 0.0), axis=1, keepdims=True)
    pick = lane.astype(jnp.float32) == ids
    east = jnp.sum(jnp.where(pick, dir_ref[0:1, :], 0.0), axis=1, keepdims=True)
    north = jnp.sum(jnp.where(pick, dir_ref[1:2, :], 0.0), axis=1, keepdims=True)
    group = ids - GROUPS * jnp.floor(ids * (1.0 / GROUPS))
    return east, north, group


def station_rows(pos_ref, group_ref, stations, lanes):
    total = group_ref.shape[1]
    first = lax.axis_index("stn") * stations
    own = iota((stations, total), 1) == iota((stations, total), 0) + first
    spread = iota((stations, lanes), 0) == iota((stations, lanes), 1) % stations

    def turn(row):
        column = jnp.sum(jnp.where(own, row, 0.0), axis=1, keepdims=True)
        return jnp.sum(jnp.where(spread, column, 0.0), axis=0, keepdims=True)

    return turn(pos_ref[0:1, :]), turn(pos_ref[1:2, :]), turn(group_ref[...].astype(jnp.float32))


def cos_turns(t):
    y = t - jnp.floor(t + 0.5)
    z = 0.25 - jnp.abs(y)
    z2 = z * z
    value = jnp.full_like(z, SIN[-1])
    for coefficient in SIN[-2::-1]:
        value = value * z2 + coefficient
    return value * z


def kernel(
    volt_hbm,
    aw_hbm,
    sw_hbm,
    ts_hbm,
    group_hbm,
    pos_hbm,
    dir_hbm,
    order_hbm,
    out_ref,
    volts,
    aw_ref,
    sw_ref,
    ts_ref,
    group_ref,
    pos_ref,
    dir_ref,
    order_ref,
    tied_ref,
    sum_ref,
    sems,
):
    channels, _, samples, antennas = volt_hbm.shape
    tiles = sw_ref.shape[2]
    stations = tiles // TPS
    groups = channels // CB
    rows_c = 2 * samples
    beams = order_ref.shape[1]
    lanes = CB * 2 * stations
    scale = 1.0 / math.sqrt(group_ref.shape[1])

    def start(source, target, k):
        copy = pltpu.make_async_copy(source, target, sems.at[k])
        copy.start(priority=int(k > groups))
        return copy

    def voltages(g):
        part = pl.ds(g * CB, CB)
        return volt_hbm.at[part], volts.at[part]

    pairs = [voltages(0), (aw_hbm, aw_ref)]
    pairs += [voltages(g) for g in range(1, groups)]
    pairs += [
        (order_hbm, order_ref),
        (dir_hbm, dir_ref),
        (pos_hbm, pos_ref),
        (group_hbm, group_ref),
        (ts_hbm, ts_ref),
        (sw_hbm, sw_ref),
    ]
    copies = [start(source, target, k) for k, (source, target) in enumerate(pairs)]
    large = copies[:1] + copies[2 : groups + 1]
    small = copies[groups + 1 :]
    antenna_tile = iota((antennas, tiles), 0) // TILE_ANTENNAS == iota((antennas, tiles), 1)
    sum_ref[...] = antenna_tile.astype(jnp.bfloat16)
    for copy in copies[:2]:
        copy.wait()

    def tile_beams(g):
        products = []
        weights = aw_ref[g * CB : (g + 1) * CB].astype(jnp.float32)
        for c in range(CB):
            w_re = jnp.broadcast_to(weights[c, 0:1], (samples, antennas)).astype(jnp.bfloat16)
            w_im = jnp.broadcast_to(weights[c, 1:2], (samples, antennas)).astype(jnp.bfloat16)
            v_re, v_im = volts[g * CB + c, 0], volts[g * CB + c, 1]
            products.append(w_re * v_re - w_im * v_im)
            products.append(w_re * v_im + w_im * v_re)
        return jnp.dot(
            jnp.concatenate(products, axis=0), sum_ref[...], preferred_element_type=jnp.float32
        ).astype(jnp.bfloat16)

    last = tile_beams(0)
    for copy in small:
        copy.wait()
    large[1].wait()

    east_s, north_s, group_s = station_rows(pos_ref, group_ref, stations, lanes)
    lane = iota((1, lanes), 1)
    channel_lane = lane // (2 * stations)
    quarter = 0.25 * ((lane // stations) % 2).astype(jnp.float32)
    first_chan = lax.axis_index("chan") * channels
    total_chans = channels * lax.axis_size("chan")
    block = min(64, beams)

    def tied_rows(first):
        east, north, group = beam_columns(order_ref, dir_ref, first, block)
        delay = east * east_s + north * north_s
        member = jnp.where(group == group_s, scale, 0.0)
        for g in range(groups):
            freq = 1.0 + (first_chan + g * CB + channel_lane).astype(jnp.float32) / total_chans
            wave = cos_turns(delay * freq - quarter)
            tied_ref[pl.ds(first, block), g * lanes : (g + 1) * lanes] = (wave * member).astype(
                jnp.bfloat16
            )

    if beams == block:
        tied_rows(0)
    else:

        def body(i, carry):
            tied_rows(pl.multiple_of(i * block, block))
            return carry

        lax.fori_loop(0, beams // block, body, 0)

    member_table = (iota((stations, tiles), 0) == ts_ref[...] % stations).astype(jnp.float32)
    own_channel = iota((lanes, CB * rows_c), 0) // (2 * stations) == iota(
        (lanes, CB * rows_c), 1
    ) // rows_c

    station_rows_of = []
    for g in range(groups):
        swt = sw_ref[g * CB : (g + 1) * CB].astype(jnp.float32)
        right = []
        for c in range(CB):
            re = swt[c, 0:1] * member_table
            im = swt[c, 1:2] * member_table
            right.append(jnp.concatenate([re, -im], axis=1))
            right.append(jnp.concatenate([im, re], axis=1))
        station_rows_of.append(jnp.concatenate(right, axis=0).astype(jnp.bfloat16))

    def tied_beams(g, beams_tile):
        left = []
        for c in range(CB):
            tile_re = beams_tile[c * rows_c : c * rows_c + samples]
            tile_im = beams_tile[c * rows_c + samples : (c + 1) * rows_c]
            left.append(jnp.concatenate([tile_re, tile_im], axis=1))
            left.append(jnp.concatenate([tile_im, -tile_re], axis=1))
        station = dot_nt(station_rows_of[g], jnp.concatenate(left, axis=0))
        station = jnp.where(own_channel, station, 0.0).astype(jnp.bfloat16)
        tied = jnp.dot(
            tied_ref[:, g * lanes : (g + 1) * lanes], station, preferred_element_type=jnp.float32
        )
        devices, rows, _ = out_ref.shape
        out_ref[:, :, g * CB * rows_c : (g + 1) * CB * rows_c] = tied.astype(jnp.bfloat16).reshape(
            devices, rows, CB * rows_c
        )

    for g in range(1, groups):
        if g > 1:
            large[g].wait()
        now = tile_beams(g)
        tied_beams(g - 1, last)
        last = now
    tied_beams(groups - 1, last)


def last_kernel(parts_ref, out_ref):
    n_stn, n_chan = lax.axis_size("stn"), lax.axis_size("chan")
    own_beams, rows_c, total_chans = out_ref.shape
    channels = total_chans // n_chan
    width = channels * rows_c
    parts = parts_ref[...].astype(jnp.float32).reshape(n_stn, n_chan, own_beams, width)
    tied = jnp.sum(parts, axis=0)
    diagonal = iota((channels, width), 0) == iota((channels, width), 1) // rows_c
    spread = (iota((rows_c, width), 0) == iota((rows_c, width), 1) % rows_c).astype(jnp.bfloat16)
    for b in range(own_beams):
        rows = [jnp.where(diagonal, tied[chan, b : b + 1], 0.0) for chan in reversed(range(n_chan))]
        rows = jnp.concatenate(rows, axis=0).astype(jnp.bfloat16)
        out_ref[b] = dot_nt(spread, rows).astype(jnp.bfloat16)


def shards(
    volts,
    antenna_tile_weights,
    station_weights,
    tile_station,
    station_group,
    station_pos,
    beam_dir,
    beam_order,
):
    channels, _, samples, _ = volts.shape
    beams = beam_order.shape[0]
    n_stn, n_chan = lax.axis_size("stn"), lax.axis_size("chan")
    rows = beams // (n_stn * n_chan)
    width = channels * 2 * samples
    operands = (
        volts,
        antenna_tile_weights,
        station_weights,
        tile_station[None, :],
        station_group[None, :],
        station_pos.T,
        beam_dir.T,
        beam_order[None, :],
    )
    operands = [pltpu.with_memory_space_constraint(x, pltpu.HBM) for x in operands]
    partial = pl.pallas_call(
        kernel,
        out_shape=pltpu.VMEM((n_stn * n_chan, rows, width), jnp.bfloat16),
        in_specs=[pl.BlockSpec(memory_space=pltpu.HBM)] * len(operands),
        out_specs=pl.BlockSpec(memory_space=pltpu.VMEM),
        scratch_shapes=[pltpu.VMEM(x.shape, x.dtype) for x in operands]
        + [
            pltpu.VMEM((beams, channels * 2 * (station_weights.shape[2] // TPS)), jnp.bfloat16),
            pltpu.VMEM((volts.shape[3], station_weights.shape[2]), jnp.bfloat16),
            pltpu.SemaphoreType.DMA((len(operands) - 1 + channels // CB,)),
        ],
        compiler_params=pltpu.CompilerParams(vmem_limit_bytes=24 * 2**20),
        name="partial_tied",
    )(*operands)
    parts = lax.all_to_all(
        partial,
        ("stn", "chan"),
        split_axis=0,
        concat_axis=0,
        axis_index_groups=[list(reversed(range(n_stn * n_chan)))],
        tiled=True,
    )
    vmem = pl.BlockSpec(memory_space=pltpu.VMEM)
    tied = pl.pallas_call(
        last_kernel,
        out_shape=jax.ShapeDtypeStruct((rows, 2 * samples, n_chan * channels), jnp.bfloat16),
        in_specs=[vmem],
        out_specs=vmem,
        compiler_params=pltpu.CompilerParams(vmem_limit_bytes=16 * 2**20),
        name="tied_beams",
    )(parts)
    return tied.transpose(0, 2, 1)


def solution(mesh):
    in_specs = (
        P("chan", None, None, "stn"),
        P("chan", None, "stn"),
        P("chan", None, "stn"),
        P("stn"),
        P(),
        P(),
        P(),
        P(),
    )
    out_specs = P(("stn", "chan"), None, None)
    return jax.shard_map(shards, mesh=mesh, in_specs=in_specs, out_specs=out_specs, check_vma=False)
```

```python
import functools
import math

import jax
import jax.numpy as jnp
from jax import lax
from jax.experimental import pallas as pl
from jax.experimental.pallas import tpu as pltpu
from jax.sharding import PartitionSpec as P

TILE_ANTENNAS = 16
TPS = 16
GROUPS = 4
CB = 8
NT = (((1,), (1,)), ((), ()))
SIN = [(-1) ** i * (2 * math.pi) ** (2 * i + 1) / math.factorial(2 * i + 1) for i in range(7)]


def dot_nt(a, b):
    return lax.dot_general(a, b, NT, preferred_element_type=jnp.float32)


def iota(shape, dim):
    return lax.broadcasted_iota(jnp.int32, shape, dim)


def exchange_order(devices):
    bits = devices.bit_length() - 1
    return [reversed_bits(devices - 1 - place, bits) for place in range(devices)]


def reversed_bits(index, bits):
    return sum((index >> bit & 1) << (bits - 1 - bit) for bit in range(bits))


def beam_columns(order_ref, dir_ref, start, rows):
    beams = order_ref.shape[1]
    devices = lax.axis_size("stn") * lax.axis_size("chan")
    each = beams // devices
    order = order_ref[...].astype(jnp.float32)
    lane = iota((rows, beams), 1)
    slot = iota((rows, beams), 0) + start
    device = reversed_bits(devices - 1 - slot // each, devices.bit_length() - 1)
    own = lane == device * each + slot % each
    ids = jnp.sum(jnp.where(own, order, 0.0), axis=1, keepdims=True)
    pick = lane.astype(jnp.float32) == ids
    east = jnp.sum(jnp.where(pick, dir_ref[0:1, :], 0.0), axis=1, keepdims=True)
    north = jnp.sum(jnp.where(pick, dir_ref[1:2, :], 0.0), axis=1, keepdims=True)
    group = ids - GROUPS * jnp.floor(ids * (1.0 / GROUPS))
    return east, north, group


def station_rows(pos_ref, group_ref, stations, lanes):
    total = group_ref.shape[1]
    first = lax.axis_index("stn") * stations
    own = iota((stations, total), 1) == iota((stations, total), 0) + first
    spread = iota((stations, lanes), 0) == iota((stations, lanes), 1) % stations

    def turn(row):
        column = jnp.sum(jnp.where(own, row, 0.0), axis=1, keepdims=True)
        return jnp.sum(jnp.where(spread, column, 0.0), axis=0, keepdims=True)

    return turn(pos_ref[0:1, :]), turn(pos_ref[1:2, :]), turn(group_ref[...].astype(jnp.float32))


def cos_turns(t):
    y = t - jnp.floor(t + 0.5)
    z = 0.25 - jnp.abs(y)
    z2 = z * z
    value = jnp.full_like(z, SIN[-1])
    for coefficient in SIN[-2::-1]:
        value = value * z2 + coefficient
    return value * z


def kernel(
    volt_hbm,
    aw_hbm,
    sw_hbm,
    ts_hbm,
    group_hbm,
    pos_hbm,
    dir_hbm,
    order_hbm,
    out_ref,
    volts,
    aw_ref,
    sw_ref,
    ts_ref,
    group_ref,
    pos_ref,
    dir_ref,
    order_ref,
    tied_ref,
    sum_ref,
    sems,
):
    channels, _, samples, antennas = volt_hbm.shape
    tiles = sw_ref.shape[2]
    stations = tiles // TPS
    groups = channels // CB
    rows_c = 2 * samples
    beams = order_ref.shape[1]
    lanes = CB * 2 * stations
    scale = 1.0 / math.sqrt(group_ref.shape[1])

    def start(source, target, k):
        copy = pltpu.make_async_copy(source, target, sems.at[k])
        copy.start()
        return copy

    def voltages(g):
        part = pl.ds(g * CB, CB)
        return volt_hbm.at[part], volts.at[part]

    pairs = [
        voltages(0),
        (aw_hbm, aw_ref),
        (order_hbm, order_ref),
        (dir_hbm, dir_ref),
        (pos_hbm, pos_ref),
        (group_hbm, group_ref),
        (ts_hbm, ts_ref),
        (sw_hbm, sw_ref),
    ] + [voltages(g) for g in range(1, groups)]
    copies = [start(source, target, k) for k, (source, target) in enumerate(pairs)]
    large = copies[:1] + copies[8:]
    antenna_tile = iota((antennas, tiles), 0) // TILE_ANTENNAS == iota((antennas, tiles), 1)
    sum_ref[...] = antenna_tile.astype(jnp.bfloat16)
    for copy in copies[:2]:
        copy.wait()

    def tile_beams(g):
        products = []
        weights = aw_ref[g * CB : (g + 1) * CB].astype(jnp.float32)
        for c in range(CB):
            w_re = jnp.broadcast_to(weights[c, 0:1], (samples, antennas)).astype(jnp.bfloat16)
            w_im = jnp.broadcast_to(weights[c, 1:2], (samples, antennas)).astype(jnp.bfloat16)
            v_re, v_im = volts[g * CB + c, 0], volts[g * CB + c, 1]
            products.append(w_re * v_re - w_im * v_im)
            products.append(w_re * v_im + w_im * v_re)
        return jnp.dot(
            jnp.concatenate(products, axis=0), sum_ref[...], preferred_element_type=jnp.float32
        ).astype(jnp.bfloat16)

    last = tile_beams(0)
    for copy in copies[2:9]:
        copy.wait()

    east_s, north_s, group_s = station_rows(pos_ref, group_ref, stations, lanes)
    lane = iota((1, lanes), 1)
    channel_lane = lane // (2 * stations)
    quarter = 0.25 * ((lane // stations) % 2).astype(jnp.float32)
    first_chan = lax.axis_index("chan") * channels
    total_chans = channels * lax.axis_size("chan")
    block = min(64, beams)

    def tied_rows(first):
        east, north, group = beam_columns(order_ref, dir_ref, first, block)
        delay = east * east_s + north * north_s
        member = jnp.where(group == group_s, scale, 0.0)
        for g in range(groups):
            freq = 1.0 + (first_chan + g * CB + channel_lane).astype(jnp.float32) / total_chans
            wave = cos_turns(delay * freq - quarter)
            tied_ref[pl.ds(first, block), g * lanes : (g + 1) * lanes] = (wave * member).astype(
                jnp.bfloat16
            )

    if beams == block:
        tied_rows(0)
    else:

        def body(i, carry):
            tied_rows(pl.multiple_of(i * block, block))
            return carry

        lax.fori_loop(0, beams // block, body, 0)

    member_table = (iota((stations, tiles), 0) == ts_ref[...] % stations).astype(jnp.float32)
    own_channel = iota((lanes, CB * rows_c), 0) // (2 * stations) == iota(
        (lanes, CB * rows_c), 1
    ) // rows_c

    station_rows_of = []
    for g in range(groups):
        swt = sw_ref[g * CB : (g + 1) * CB].astype(jnp.float32)
        right = []
        for c in range(CB):
            re = swt[c, 0:1] * member_table
            im = swt[c, 1:2] * member_table
            right.append(jnp.concatenate([re, -im], axis=1))
            right.append(jnp.concatenate([im, re], axis=1))
        station_rows_of.append(jnp.concatenate(right, axis=0).astype(jnp.bfloat16))

    def tied_beams(g, beams_tile):
        left = []
        for c in range(CB):
            tile_re = beams_tile[c * rows_c : c * rows_c + samples]
            tile_im = beams_tile[c * rows_c + samples : (c + 1) * rows_c]
            left.append(jnp.concatenate([tile_re, tile_im], axis=1))
            left.append(jnp.concatenate([tile_im, -tile_re], axis=1))
        station = dot_nt(station_rows_of[g], jnp.concatenate(left, axis=0))
        station = jnp.where(own_channel, station, 0.0).astype(jnp.bfloat16)
        tied = jnp.dot(
            tied_ref[:, g * lanes : (g + 1) * lanes], station, preferred_element_type=jnp.float32
        )
        devices, rows, _ = out_ref.shape
        out_ref[:, :, g * CB * rows_c : (g + 1) * CB * rows_c] = tied.astype(jnp.bfloat16).reshape(
            devices, rows, CB * rows_c
        )

    for g in range(1, groups):
        if g > 1:
            large[g].wait()
        now = tile_beams(g)
        tied_beams(g - 1, last)
        last = now
    tied_beams(groups - 1, last)


def last_kernel(parts_ref, out_ref):
    n_chan = lax.axis_size("chan")
    own_beams, rows_c, total_chans = out_ref.shape
    channels = total_chans // n_chan
    width = channels * rows_c
    parts = parts_ref[...].astype(jnp.float32)
    order = exchange_order(parts_ref.shape[0])
    tied = [
        sum(parts[place] for place, device in enumerate(order) if device % n_chan == chan)
        for chan in range(n_chan)
    ]
    diagonal = iota((channels, width), 0) == iota((channels, width), 1) // rows_c
    spread = (iota((rows_c, width), 0) == iota((rows_c, width), 1) % rows_c).astype(jnp.bfloat16)
    for b in range(own_beams):
        rows = [jnp.where(diagonal, tied[chan][b : b + 1], 0.0) for chan in range(n_chan)]
        rows = jnp.concatenate(rows, axis=0).astype(jnp.bfloat16)
        out_ref[b] = dot_nt(spread, rows).astype(jnp.bfloat16)


def shards(
    volts,
    antenna_tile_weights,
    station_weights,
    tile_station,
    station_group,
    station_pos,
    beam_dir,
    beam_order,
):
    channels, _, samples, _ = volts.shape
    beams = beam_order.shape[0]
    n_stn, n_chan = lax.axis_size("stn"), lax.axis_size("chan")
    rows = beams // (n_stn * n_chan)
    width = channels * 2 * samples
    operands = (
        volts,
        antenna_tile_weights,
        station_weights,
        tile_station[None, :],
        station_group[None, :],
        station_pos.T,
        beam_dir.T,
        beam_order[None, :],
    )
    operands = [pltpu.with_memory_space_constraint(x, pltpu.HBM) for x in operands]
    partial = pl.pallas_call(
        kernel,
        out_shape=pltpu.VMEM((n_stn * n_chan, rows, width), jnp.bfloat16),
        in_specs=[pl.BlockSpec(memory_space=pltpu.HBM)] * len(operands),
        out_specs=pl.BlockSpec(memory_space=pltpu.VMEM),
        scratch_shapes=[pltpu.VMEM(x.shape, x.dtype) for x in operands]
        + [
            pltpu.VMEM((beams, channels * 2 * (station_weights.shape[2] // TPS)), jnp.bfloat16),
            pltpu.VMEM((volts.shape[3], station_weights.shape[2]), jnp.bfloat16),
            pltpu.SemaphoreType.DMA((len(operands) - 1 + channels // CB,)),
        ],
        compiler_params=pltpu.CompilerParams(vmem_limit_bytes=24 * 2**20),
        name="partial_tied",
    )(*operands)
    parts = lax.all_to_all(
        partial,
        ("stn", "chan"),
        split_axis=0,
        concat_axis=0,
        axis_index_groups=[exchange_order(n_stn * n_chan)],
        tiled=True,
    )
    vmem = pl.BlockSpec(memory_space=pltpu.VMEM)
    tied = pl.pallas_call(
        last_kernel,
        out_shape=jax.ShapeDtypeStruct((rows, 2 * samples, n_chan * channels), jnp.bfloat16),
        in_specs=[vmem],
        out_specs=vmem,
        compiler_params=pltpu.CompilerParams(vmem_limit_bytes=16 * 2**20),
        name="tied_beams",
    )(parts)
    return tied.transpose(0, 2, 1)


def solution(mesh):
    in_specs = (
        P("chan", None, None, "stn"),
        P("chan", None, "stn"),
        P("chan", None, "stn"),
        P("stn"),
        P(),
        P(),
        P(),
        P(),
    )
    out_specs = P(("stn", "chan"), None, None)
    return jax.shard_map(shards, mesh=mesh, in_specs=in_specs, out_specs=out_specs, check_vma=False)
```

```python
import functools
import math

import jax
import jax.numpy as jnp
from jax import lax
from jax.experimental import pallas as pl
from jax.experimental.pallas import tpu as pltpu
from jax.sharding import PartitionSpec as P

TILE_ANTENNAS = 16
TPS = 16
GROUPS = 4
CB = 8
NT = (((1,), (1,)), ((), ()))
SIN = [(-1) ** i * (2 * math.pi) ** (2 * i + 1) / math.factorial(2 * i + 1) for i in range(7)]


def dot_nt(a, b):
    return lax.dot_general(a, b, NT, preferred_element_type=jnp.float32)


def iota(shape, dim):
    return lax.broadcasted_iota(jnp.int32, shape, dim)


def exchange_order(n_stn, n_chan):
    def key(device):
        stn = device // n_chan
        return device == n_chan, 2 * (stn // 4) + 3 * (stn % 2) if device else -1, device

    return sorted(range(n_stn * n_chan), key=key, reverse=True)


def beam_columns(order_ref, dir_ref, start, rows):
    beams = order_ref.shape[1]
    n_stn, n_chan = lax.axis_size("stn"), lax.axis_size("chan")
    each = beams // (n_stn * n_chan)
    order = order_ref[...].astype(jnp.float32)
    lane = iota((rows, beams), 1)
    slot = iota((rows, 1), 0) + start
    own_row = jnp.zeros((rows, 1), jnp.int32)
    for place, device in enumerate(exchange_order(n_stn, n_chan)):
        own_row = jnp.where(slot // each == place, device * each + slot % each, own_row)
    own = lane == own_row
    ids = jnp.sum(jnp.where(own, order, 0.0), axis=1, keepdims=True)
    pick = lane.astype(jnp.float32) == ids
    east = jnp.sum(jnp.where(pick, dir_ref[0:1, :], 0.0), axis=1, keepdims=True)
    north = jnp.sum(jnp.where(pick, dir_ref[1:2, :], 0.0), axis=1, keepdims=True)
    group = ids - GROUPS * jnp.floor(ids * (1.0 / GROUPS))
    return east, north, group


def station_rows(pos_ref, group_ref, stations, lanes):
    total = group_ref.shape[1]
    first = lax.axis_index("stn") * stations
    own = iota((stations, total), 1) == iota((stations, total), 0) + first
    spread = iota((stations, lanes), 0) == iota((stations, lanes), 1) % stations

    def turn(row):
        column = jnp.sum(jnp.where(own, row, 0.0), axis=1, keepdims=True)
        return jnp.sum(jnp.where(spread, column, 0.0), axis=0, keepdims=True)

    return turn(pos_ref[0:1, :]), turn(pos_ref[1:2, :]), turn(group_ref[...].astype(jnp.float32))


def cos_turns(t):
    y = t - jnp.floor(t + 0.5)
    z = 0.25 - jnp.abs(y)
    z2 = z * z
    value = jnp.full_like(z, SIN[-1])
    for coefficient in SIN[-2::-1]:
        value = value * z2 + coefficient
    return value * z


def kernel(
    volt_hbm,
    aw_hbm,
    sw_hbm,
    ts_hbm,
    group_hbm,
    pos_hbm,
    dir_hbm,
    order_hbm,
    out_ref,
    volts,
    aw_ref,
    sw_ref,
    ts_ref,
    group_ref,
    pos_ref,
    dir_ref,
    order_ref,
    tied_ref,
    sum_ref,
    sems,
):
    channels, _, samples, antennas = volt_hbm.shape
    tiles = sw_ref.shape[2]
    stations = tiles // TPS
    groups = channels // CB
    rows_c = 2 * samples
    beams = order_ref.shape[1]
    lanes = CB * 2 * stations
    scale = 1.0 / math.sqrt(group_ref.shape[1])

    def start(source, target, k):
        copy = pltpu.make_async_copy(source, target, sems.at[k])
        copy.start()
        return copy

    def voltages(g):
        part = pl.ds(g * CB, CB)
        return volt_hbm.at[part], volts.at[part]

    pairs = [
        voltages(0),
        (aw_hbm, aw_ref),
        (order_hbm, order_ref),
        (dir_hbm, dir_ref),
        (pos_hbm, pos_ref),
        (group_hbm, group_ref),
        (ts_hbm, ts_ref),
        (sw_hbm, sw_ref),
    ] + [voltages(g) for g in range(1, groups)]
    copies = [start(source, target, k) for k, (source, target) in enumerate(pairs)]
    large = copies[:1] + copies[8:]
    antenna_tile = iota((antennas, tiles), 0) // TILE_ANTENNAS == iota((antennas, tiles), 1)
    sum_ref[...] = antenna_tile.astype(jnp.bfloat16)
    for copy in copies[:2]:
        copy.wait()

    def tile_beams(g):
        products = []
        weights = aw_ref[g * CB : (g + 1) * CB].astype(jnp.float32)
        for c in range(CB):
            w_re = jnp.broadcast_to(weights[c, 0:1], (samples, antennas)).astype(jnp.bfloat16)
            w_im = jnp.broadcast_to(weights[c, 1:2], (samples, antennas)).astype(jnp.bfloat16)
            v_re, v_im = volts[g * CB + c, 0], volts[g * CB + c, 1]
            products.append(w_re * v_re - w_im * v_im)
            products.append(w_re * v_im + w_im * v_re)
        return jnp.dot(
            jnp.concatenate(products, axis=0), sum_ref[...], preferred_element_type=jnp.float32
        ).astype(jnp.bfloat16)

    last = tile_beams(0)
    for copy in copies[2:9]:
        copy.wait()

    east_s, north_s, group_s = station_rows(pos_ref, group_ref, stations, lanes)
    lane = iota((1, lanes), 1)
    channel_lane = lane // (2 * stations)
    quarter = 0.25 * ((lane // stations) % 2).astype(jnp.float32)
    first_chan = lax.axis_index("chan") * channels
    total_chans = channels * lax.axis_size("chan")
    block = min(64, beams)

    def tied_rows(first):
        east, north, group = beam_columns(order_ref, dir_ref, first, block)
        delay = east * east_s + north * north_s
        member = jnp.where(group == group_s, scale, 0.0)
        for g in range(groups):
            freq = 1.0 + (first_chan + g * CB + channel_lane).astype(jnp.float32) / total_chans
            wave = cos_turns(delay * freq - quarter)
            tied_ref[pl.ds(first, block), g * lanes : (g + 1) * lanes] = (wave * member).astype(
                jnp.bfloat16
            )

    if beams == block:
        tied_rows(0)
    else:

        def body(i, carry):
            tied_rows(pl.multiple_of(i * block, block))
            return carry

        lax.fori_loop(0, beams // block, body, 0)

    member_table = (iota((stations, tiles), 0) == ts_ref[...] % stations).astype(jnp.float32)
    own_channel = iota((lanes, CB * rows_c), 0) // (2 * stations) == iota(
        (lanes, CB * rows_c), 1
    ) // rows_c

    station_rows_of = []
    for g in range(groups):
        swt = sw_ref[g * CB : (g + 1) * CB].astype(jnp.float32)
        right = []
        for c in range(CB):
            re = swt[c, 0:1] * member_table
            im = swt[c, 1:2] * member_table
            right.append(jnp.concatenate([re, -im], axis=1))
            right.append(jnp.concatenate([im, re], axis=1))
        station_rows_of.append(jnp.concatenate(right, axis=0).astype(jnp.bfloat16))

    def tied_beams(g, beams_tile):
        left = []
        for c in range(CB):
            tile_re = beams_tile[c * rows_c : c * rows_c + samples]
            tile_im = beams_tile[c * rows_c + samples : (c + 1) * rows_c]
            left.append(jnp.concatenate([tile_re, tile_im], axis=1))
            left.append(jnp.concatenate([tile_im, -tile_re], axis=1))
        station = dot_nt(station_rows_of[g], jnp.concatenate(left, axis=0))
        station = jnp.where(own_channel, station, 0.0).astype(jnp.bfloat16)
        tied = jnp.dot(
            tied_ref[:, g * lanes : (g + 1) * lanes], station, preferred_element_type=jnp.float32
        )
        devices, rows, _ = out_ref.shape
        out_ref[:, :, g * CB * rows_c : (g + 1) * CB * rows_c] = tied.astype(jnp.bfloat16).reshape(
            devices, rows, CB * rows_c
        )

    for g in range(1, groups):
        if g > 1:
            large[g].wait()
        now = tile_beams(g)
        tied_beams(g - 1, last)
        last = now
    tied_beams(groups - 1, last)


def last_kernel(parts_ref, out_ref):
    n_chan = lax.axis_size("chan")
    own_beams, rows_c, total_chans = out_ref.shape
    channels = total_chans // n_chan
    width = channels * rows_c
    parts = parts_ref[...].astype(jnp.float32)
    order = exchange_order(lax.axis_size("stn"), n_chan)
    tied = [
        sum(parts[place] for place, device in enumerate(order) if device % n_chan == chan)
        for chan in range(n_chan)
    ]
    diagonal = iota((channels, width), 0) == iota((channels, width), 1) // rows_c
    spread = (iota((rows_c, width), 0) == iota((rows_c, width), 1) % rows_c).astype(jnp.bfloat16)
    for b in range(own_beams):
        rows = [jnp.where(diagonal, tied[chan][b : b + 1], 0.0) for chan in range(n_chan)]
        rows = jnp.concatenate(rows, axis=0).astype(jnp.bfloat16)
        out_ref[b] = dot_nt(spread, rows).astype(jnp.bfloat16)


def shards(
    volts,
    antenna_tile_weights,
    station_weights,
    tile_station,
    station_group,
    station_pos,
    beam_dir,
    beam_order,
):
    channels, _, samples, _ = volts.shape
    beams = beam_order.shape[0]
    n_stn, n_chan = lax.axis_size("stn"), lax.axis_size("chan")
    rows = beams // (n_stn * n_chan)
    width = channels * 2 * samples
    operands = (
        volts,
        antenna_tile_weights,
        station_weights,
        tile_station[None, :],
        station_group[None, :],
        station_pos.T,
        beam_dir.T,
        beam_order[None, :],
    )
    operands = [pltpu.with_memory_space_constraint(x, pltpu.HBM) for x in operands]
    partial = pl.pallas_call(
        kernel,
        out_shape=pltpu.VMEM((n_stn * n_chan, rows, width), jnp.bfloat16),
        in_specs=[pl.BlockSpec(memory_space=pltpu.HBM)] * len(operands),
        out_specs=pl.BlockSpec(memory_space=pltpu.VMEM),
        scratch_shapes=[pltpu.VMEM(x.shape, x.dtype) for x in operands]
        + [
            pltpu.VMEM((beams, channels * 2 * (station_weights.shape[2] // TPS)), jnp.bfloat16),
            pltpu.VMEM((volts.shape[3], station_weights.shape[2]), jnp.bfloat16),
            pltpu.SemaphoreType.DMA((len(operands) - 1 + channels // CB,)),
        ],
        compiler_params=pltpu.CompilerParams(vmem_limit_bytes=24 * 2**20),
        name="partial_tied",
    )(*operands)
    parts = lax.all_to_all(
        partial,
        ("stn", "chan"),
        split_axis=0,
        concat_axis=0,
        axis_index_groups=[exchange_order(n_stn, n_chan)],
        tiled=True,
    )
    vmem = pl.BlockSpec(memory_space=pltpu.VMEM)
    tied = pl.pallas_call(
        last_kernel,
        out_shape=jax.ShapeDtypeStruct((rows, 2 * samples, n_chan * channels), jnp.bfloat16),
        in_specs=[vmem],
        out_specs=vmem,
        compiler_params=pltpu.CompilerParams(vmem_limit_bytes=16 * 2**20),
        name="tied_beams",
    )(parts)
    return tied.transpose(0, 2, 1)


def solution(mesh):
    in_specs = (
        P("chan", None, None, "stn"),
        P("chan", None, "stn"),
        P("chan", None, "stn"),
        P("stn"),
        P(),
        P(),
        P(),
        P(),
    )
    out_specs = P(("stn", "chan"), None, None)
    return jax.shard_map(shards, mesh=mesh, in_specs=in_specs, out_specs=out_specs, check_vma=False)
```

```python
import functools
import math

import jax
import jax.numpy as jnp
from jax import lax
from jax.experimental import pallas as pl
from jax.experimental.pallas import tpu as pltpu
from jax.sharding import PartitionSpec as P

TILE_ANTENNAS = 16
TPS = 16
GROUPS = 4
CB = 8
NT = (((1,), (1,)), ((), ()))
SIN = [(-1) ** i * (2 * math.pi) ** (2 * i + 1) / math.factorial(2 * i + 1) for i in range(7)]


def dot_nt(a, b):
    return lax.dot_general(a, b, NT, preferred_element_type=jnp.float32)


def iota(shape, dim):
    return lax.broadcasted_iota(jnp.int32, shape, dim)


def beam_columns(order_ref, dir_ref, start, rows):
    beams = order_ref.shape[1]
    each = beams // (lax.axis_size("stn") * lax.axis_size("chan"))
    order = order_ref[...].astype(jnp.float32)
    lane = iota((rows, beams), 1)
    slot = iota((rows, beams), 0) + start
    own = lane == beams - each - slot // each * each + slot % each
    ids = jnp.sum(jnp.where(own, order, 0.0), axis=1, keepdims=True)
    pick = lane.astype(jnp.float32) == ids
    east = jnp.sum(jnp.where(pick, dir_ref[0:1, :], 0.0), axis=1, keepdims=True)
    north = jnp.sum(jnp.where(pick, dir_ref[1:2, :], 0.0), axis=1, keepdims=True)
    group = ids - GROUPS * jnp.floor(ids * (1.0 / GROUPS))
    return east, north, group


def station_rows(pos_ref, group_ref, stations, lanes):
    total = group_ref.shape[1]
    first = lax.axis_index("stn") * stations
    own = iota((stations, total), 1) == iota((stations, total), 0) + first
    spread = iota((stations, lanes), 0) == iota((stations, lanes), 1) % stations

    def turn(row):
        column = jnp.sum(jnp.where(own, row, 0.0), axis=1, keepdims=True)
        return jnp.sum(jnp.where(spread, column, 0.0), axis=0, keepdims=True)

    return turn(pos_ref[0:1, :]), turn(pos_ref[1:2, :]), turn(group_ref[...].astype(jnp.float32))


def cos_turns(t):
    y = t - jnp.floor(t + 0.5)
    z = 0.25 - jnp.abs(y)
    z2 = z * z
    value = jnp.full_like(z, SIN[-1])
    for coefficient in SIN[-2::-1]:
        value = value * z2 + coefficient
    return value * z


def kernel(
    volt_hbm,
    aw_hbm,
    sw_hbm,
    ts_hbm,
    group_hbm,
    pos_hbm,
    dir_hbm,
    order_hbm,
    out_ref,
    volts,
    aw_ref,
    sw_ref,
    ts_ref,
    group_ref,
    pos_ref,
    dir_ref,
    order_ref,
    tied_ref,
    spread_ref,
    weights_ref,
    sems,
):
    channels, _, samples, antennas = volt_hbm.shape
    tiles = sw_ref.shape[2]
    stations = tiles // TPS
    groups = channels // CB
    rows_c = 2 * samples
    beams = order_ref.shape[1]
    lanes = CB * 2 * stations
    scale = 1.0 / math.sqrt(group_ref.shape[1])

    def start(source, target, k):
        copy = pltpu.make_async_copy(source, target, sems.at[k])
        copy.start()
        return copy

    def voltages(g):
        part = pl.ds(g * CB, CB)
        return volt_hbm.at[part], volts.at[part]

    pairs = [
        (aw_hbm, aw_ref),
        (sw_hbm, sw_ref),
        (ts_hbm, ts_ref),
        voltages(0),
        (order_hbm, order_ref),
        (dir_hbm, dir_ref),
        (pos_hbm, pos_ref),
        (group_hbm, group_ref),
    ] + [voltages(g) for g in range(1, groups)]
    copies = [start(source, target, k) for k, (source, target) in enumerate(pairs)]
    large = copies[3:4] + copies[8:]
    tile_of = iota((tiles, antennas), 1) // TILE_ANTENNAS == iota((tiles, antennas), 0)
    spread_ref[...] = tile_of.astype(jnp.bfloat16)
    own_channel = iota((CB * rows_c, lanes), 0) // rows_c == iota((CB * rows_c, lanes), 1) // (
        2 * stations
    )
    imag_row = iota((CB * rows_c, lanes), 0) // samples % 2
    imag_lane = iota((CB * rows_c, lanes), 1) // stations % 2
    sign = jnp.where(imag_row == imag_lane, -1.0, 1.0)
    for copy in copies[:3]:
        copy.wait()

    member_table = (iota((stations, tiles), 0) == ts_ref[...] % stations).astype(jnp.float32)
    swt = sw_ref[...].astype(jnp.float32)
    rows = jnp.concatenate([swt[c] for c in range(channels)] + [member_table], axis=0)
    spread = jnp.dot(
        rows.astype(jnp.bfloat16), spread_ref[...], preferred_element_type=jnp.float32
    )
    member = spread[2 * channels :]

    def station_weights(g):
        out = []
        for c in range(g * CB, (g + 1) * CB):
            antenna = aw_ref[c].astype(jnp.float32)
            a_re, a_im = antenna[0:1], antenna[1:2]
            s_re = spread[2 * c : 2 * c + 1] * member
            s_im = spread[2 * c + 1 : 2 * c + 2] * member
            out += [s_re * a_re - s_im * a_im, s_re * a_im + s_im * a_re]
        weights_ref[g] = jnp.concatenate(out, axis=0).astype(jnp.bfloat16)

    def products(g):
        left = volts[g * CB : (g + 1) * CB].reshape(CB * rows_c, antennas)
        return dot_nt(left, weights_ref[g])

    def tied_beams(g, product):
        other = product.reshape(CB, 2, samples, lanes)
        other = jnp.concatenate([other[:, 1:], other[:, :1]], axis=1).reshape(CB * rows_c, lanes)
        other = jnp.where(
            imag_lane == 0,
            pltpu.roll(other, lanes - stations, 1),
            pltpu.roll(other, stations, 1),
        )
        station = jnp.where(own_channel, product + sign * other, 0.0).astype(jnp.bfloat16)
        tied = dot_nt(tied_ref[:, g * lanes : (g + 1) * lanes], station)
        devices, rows, _ = out_ref.shape
        out_ref[:, :, g * CB * rows_c : (g + 1) * CB * rows_c] = tied.astype(jnp.bfloat16).reshape(
            devices, rows, CB * rows_c
        )

    station_weights(0)
    found = []
    for g in range(groups - 1):
        large[g].wait()
        if g == groups - 2:
            for copy in copies[4:8]:
                copy.wait()
        found.append(products(g))
        station_weights(g + 1)

    east_s, north_s, group_s = station_rows(pos_ref, group_ref, stations, lanes)
    lane = iota((1, lanes), 1)
    channel_lane = lane // (2 * stations)
    quarter = 0.25 * ((lane // stations) % 2).astype(jnp.float32)
    first_chan = lax.axis_index("chan") * channels
    total_chans = channels * lax.axis_size("chan")
    block = min(64, beams)

    def tied_rows(first):
        east, north, group = beam_columns(order_ref, dir_ref, first, block)
        delay = east * east_s + north * north_s
        member = jnp.where(group == group_s, scale, 0.0)
        for g in range(groups):
            freq = 1.0 + (first_chan + g * CB + channel_lane).astype(jnp.float32) / total_chans
            wave = cos_turns(delay * freq - quarter)
            tied_ref[pl.ds(first, block), g * lanes : (g + 1) * lanes] = (wave * member).astype(
                jnp.bfloat16
            )

    if beams == block:
        tied_rows(0)
    else:

        def body(i, carry):
            tied_rows(pl.multiple_of(i * block, block))
            return carry

        lax.fori_loop(0, beams // block, body, 0)

    large[-1].wait()
    found.append(products(groups - 1))
    for g in range(groups):
        tied_beams(g, found[g])


def last_kernel(parts_ref, out_ref):
    n_stn, n_chan = lax.axis_size("stn"), lax.axis_size("chan")
    own_beams, rows_c, total_chans = out_ref.shape
    channels = total_chans // n_chan
    width = channels * rows_c
    parts = parts_ref[...].astype(jnp.float32)
    tied = [sum(parts[n_chan - 1 - chan + k * n_chan] for k in range(n_stn)) for chan in range(n_chan)]
    diagonal = iota((channels, width), 0) == iota((channels, width), 1) // rows_c
    spread = (iota((rows_c, width), 0) == iota((rows_c, width), 1) % rows_c).astype(jnp.bfloat16)
    for b in range(own_beams):
        rows = [jnp.where(diagonal, tied[chan][b : b + 1], 0.0) for chan in range(n_chan)]
        rows = jnp.concatenate(rows, axis=0).astype(jnp.bfloat16)
        out_ref[b] = dot_nt(spread, rows).astype(jnp.bfloat16)


def shards(
    volts,
    antenna_tile_weights,
    station_weights,
    tile_station,
    station_group,
    station_pos,
    beam_dir,
    beam_order,
):
    channels, _, samples, _ = volts.shape
    beams = beam_order.shape[0]
    n_stn, n_chan = lax.axis_size("stn"), lax.axis_size("chan")
    rows = beams // (n_stn * n_chan)
    width = channels * 2 * samples
    operands = (
        volts,
        antenna_tile_weights,
        station_weights,
        tile_station[None, :],
        station_group[None, :],
        station_pos.T,
        beam_dir.T,
        beam_order[None, :],
    )
    operands = [pltpu.with_memory_space_constraint(x, pltpu.HBM) for x in operands]
    partial = pl.pallas_call(
        kernel,
        out_shape=pltpu.VMEM((n_stn * n_chan, rows, width), jnp.bfloat16),
        in_specs=[pl.BlockSpec(memory_space=pltpu.HBM)] * len(operands),
        out_specs=pl.BlockSpec(memory_space=pltpu.VMEM),
        scratch_shapes=[pltpu.VMEM(x.shape, x.dtype) for x in operands]
        + [
            pltpu.VMEM((beams, channels * 2 * (station_weights.shape[2] // TPS)), jnp.bfloat16),
            pltpu.VMEM((station_weights.shape[2], volts.shape[3]), jnp.bfloat16),
            pltpu.VMEM(
                (channels // CB, CB * 2 * (station_weights.shape[2] // TPS), volts.shape[3]),
                jnp.bfloat16,
            ),
            pltpu.SemaphoreType.DMA((len(operands) - 1 + channels // CB,)),
        ],
        compiler_params=pltpu.CompilerParams(vmem_limit_bytes=24 * 2**20),
        name="partial_tied",
    )(*operands)
    parts = lax.all_to_all(
        partial,
        ("stn", "chan"),
        split_axis=0,
        concat_axis=0,
        axis_index_groups=[list(reversed(range(n_stn * n_chan)))],
        tiled=True,
    )
    vmem = pl.BlockSpec(memory_space=pltpu.VMEM)
    tied = pl.pallas_call(
        last_kernel,
        out_shape=jax.ShapeDtypeStruct((rows, 2 * samples, n_chan * channels), jnp.bfloat16),
        in_specs=[vmem],
        out_specs=vmem,
        compiler_params=pltpu.CompilerParams(vmem_limit_bytes=16 * 2**20),
        name="tied_beams",
    )(parts)
    return tied.transpose(0, 2, 1)


def solution(mesh):
    in_specs = (
        P("chan", None, None, "stn"),
        P("chan", None, "stn"),
        P("chan", None, "stn"),
        P("stn"),
        P(),
        P(),
        P(),
        P(),
    )
    out_specs = P(("stn", "chan"), None, None)
    return jax.shard_map(shards, mesh=mesh, in_specs=in_specs, out_specs=out_specs, check_vma=False)
```

```python
import functools
import math

import jax
import jax.numpy as jnp
from jax import lax
from jax.experimental import pallas as pl
from jax.experimental.pallas import tpu as pltpu
from jax.sharding import PartitionSpec as P

TILE_ANTENNAS = 16
TPS = 16
GROUPS = 4
CB = 8
CHUNK = 256
NT = (((1,), (1,)), ((), ()))
SIN = [(-1) ** i * (2 * math.pi) ** (2 * i + 1) / math.factorial(2 * i + 1) for i in range(7)]


def dot_nt(a, b):
    return lax.dot_general(a, b, NT, preferred_element_type=jnp.float32)


def iota(shape, dim):
    return lax.broadcasted_iota(jnp.int32, shape, dim)


def beam_columns(order_ref, dir_ref, start, rows):
    beams = order_ref.shape[1]
    each = beams // (lax.axis_size("stn") * lax.axis_size("chan"))
    order = order_ref[...].astype(jnp.float32)
    lane = iota((rows, beams), 1)
    slot = iota((rows, beams), 0) + start
    own = lane == beams - each - slot // each * each + slot % each
    ids = jnp.sum(jnp.where(own, order, 0.0), axis=1, keepdims=True)
    pick = lane.astype(jnp.float32) == ids
    east = jnp.sum(jnp.where(pick, dir_ref[0:1, :], 0.0), axis=1, keepdims=True)
    north = jnp.sum(jnp.where(pick, dir_ref[1:2, :], 0.0), axis=1, keepdims=True)
    group = ids - GROUPS * jnp.floor(ids * (1.0 / GROUPS))
    return east, north, group


def station_rows(pos_ref, group_ref, stations, lanes):
    total = group_ref.shape[1]
    first = lax.axis_index("stn") * stations
    own = iota((stations, total), 1) == iota((stations, total), 0) + first
    spread = iota((stations, lanes), 0) == iota((stations, lanes), 1) % stations

    def turn(row):
        column = jnp.sum(jnp.where(own, row, 0.0), axis=1, keepdims=True)
        return jnp.sum(jnp.where(spread, column, 0.0), axis=0, keepdims=True)

    return turn(pos_ref[0:1, :]), turn(pos_ref[1:2, :]), turn(group_ref[...].astype(jnp.float32))


def cos_turns(t):
    y = t - jnp.floor(t + 0.5)
    z = 0.25 - jnp.abs(y)
    z2 = z * z
    value = jnp.full_like(z, SIN[-1])
    for coefficient in SIN[-2::-1]:
        value = value * z2 + coefficient
    return value * z


def kernel(
    volt_hbm,
    aw_hbm,
    sw_hbm,
    ts_hbm,
    group_hbm,
    pos_hbm,
    dir_hbm,
    order_hbm,
    out_ref,
    volts,
    aw_ref,
    sw_ref,
    ts_ref,
    group_ref,
    pos_ref,
    dir_ref,
    order_ref,
    tied_ref,
    sems,
):
    channels, _, samples, antennas = volt_hbm.shape
    tiles = sw_ref.shape[2]
    stations = tiles // TPS
    groups = channels // CB
    rows_c = 2 * samples
    beams = order_ref.shape[1]
    lanes = CB * 2 * stations
    scale = 1.0 / math.sqrt(group_ref.shape[1])

    def start(source, target, k):
        copy = pltpu.make_async_copy(source, target, sems.at[k])
        copy.start()
        return copy

    def voltages(g):
        part = pl.ds(g * CB, CB)
        return volt_hbm.at[part], volts.at[part]

    pairs = [
        voltages(0),
        (aw_hbm, aw_ref),
        (order_hbm, order_ref),
        (dir_hbm, dir_ref),
        (pos_hbm, pos_ref),
        (group_hbm, group_ref),
        (ts_hbm, ts_ref),
        (sw_hbm, sw_ref),
    ] + [voltages(g) for g in range(1, groups)]
    copies = [start(source, target, k) for k, (source, target) in enumerate(pairs)]
    large = copies[:1] + copies[8:]
    antenna_tile = iota((CHUNK // TILE_ANTENNAS, CHUNK), 1) // TILE_ANTENNAS
    sum_tile = (antenna_tile == iota(antenna_tile.shape, 0)).astype(jnp.bfloat16)
    for copy in copies[:2]:
        copy.wait()

    def tile_beams(g):
        products = []
        weights = aw_ref[g * CB : (g + 1) * CB].astype(jnp.float32)
        for c in range(CB):
            w_re = jnp.broadcast_to(weights[c, 0:1], (samples, antennas)).astype(jnp.bfloat16)
            w_im = jnp.broadcast_to(weights[c, 1:2], (samples, antennas)).astype(jnp.bfloat16)
            v_re, v_im = volts[g * CB + c, 0], volts[g * CB + c, 1]
            products.append(w_re * v_re - w_im * v_im)
            products.append(w_re * v_im + w_im * v_re)
        products = jnp.concatenate(products, axis=0)
        sums = [
            dot_nt(sum_tile, products[:, first : first + CHUNK])
            for first in range(0, antennas, CHUNK)
        ]
        return jnp.concatenate(sums, axis=0)

    last = tile_beams(0)
    for copy in copies[2:9]:
        copy.wait()

    east_s, north_s, group_s = station_rows(pos_ref, group_ref, stations, lanes)
    lane = iota((1, lanes), 1)
    channel_lane = lane // (2 * stations)
    quarter = 0.25 * ((lane // stations) % 2).astype(jnp.float32)
    first_chan = lax.axis_index("chan") * channels
    total_chans = channels * lax.axis_size("chan")
    block = min(64, beams)

    def tied_rows(first):
        east, north, group = beam_columns(order_ref, dir_ref, first, block)
        delay = east * east_s + north * north_s
        member = jnp.where(group == group_s, scale, 0.0)
        for g in range(groups):
            freq = 1.0 + (first_chan + g * CB + channel_lane).astype(jnp.float32) / total_chans
            wave = cos_turns(delay * freq - quarter)
            tied_ref[pl.ds(first, block), g * lanes : (g + 1) * lanes] = (wave * member).astype(
                jnp.bfloat16
            )

    if beams == block:
        tied_rows(0)
    else:

        def body(i, carry):
            tied_rows(pl.multiple_of(i * block, block))
            return carry

        lax.fori_loop(0, beams // block, body, 0)

    member_table = (iota((stations, tiles), 0) == ts_ref[...] % stations).astype(jnp.float32)
    own_channel = iota((lanes, CB * rows_c), 0) // (2 * stations) == iota(
        (lanes, CB * rows_c), 1
    ) // rows_c

    imag_column = iota((tiles, CB * rows_c), 1) // samples % 2 == 1
    station_rows_of = []
    for g in range(groups):
        swt = sw_ref[g * CB : (g + 1) * CB].astype(jnp.float32)
        right = []
        for c in range(CB):
            re = swt[c, 0:1] * member_table
            im = swt[c, 1:2] * member_table
            right.append(jnp.concatenate([re, -im], axis=1))
            right.append(jnp.concatenate([im, re], axis=1))
        station_rows_of.append(jnp.concatenate(right, axis=0).astype(jnp.bfloat16))

    def tied_beams(g, beams_tile):
        width = CB * rows_c
        other = jnp.where(
            imag_column,
            -pltpu.roll(beams_tile, samples, 1),
            pltpu.roll(beams_tile, width - samples, 1),
        )
        left = jnp.concatenate([beams_tile, other], axis=0).astype(jnp.bfloat16)
        station = jnp.dot(station_rows_of[g], left, preferred_element_type=jnp.float32)
        station = jnp.where(own_channel, station, 0.0).astype(jnp.bfloat16)
        tied = jnp.dot(
            tied_ref[:, g * lanes : (g + 1) * lanes], station, preferred_element_type=jnp.float32
        )
        devices, rows, _ = out_ref.shape
        out_ref[:, :, g * CB * rows_c : (g + 1) * CB * rows_c] = tied.astype(jnp.bfloat16).reshape(
            devices, rows, CB * rows_c
        )

    for g in range(1, groups):
        if g > 1:
            large[g].wait()
        now = tile_beams(g)
        tied_beams(g - 1, last)
        last = now
    tied_beams(groups - 1, last)


def last_kernel(parts_ref, out_ref):
    n_stn, n_chan = lax.axis_size("stn"), lax.axis_size("chan")
    own_beams, rows_c, total_chans = out_ref.shape
    channels = total_chans // n_chan
    width = channels * rows_c
    parts = parts_ref[...].astype(jnp.float32)
    tied = [sum(parts[n_chan - 1 - chan + k * n_chan] for k in range(n_stn)) for chan in range(n_chan)]
    diagonal = iota((channels, width), 0) == iota((channels, width), 1) // rows_c
    spread = (iota((rows_c, width), 0) == iota((rows_c, width), 1) % rows_c).astype(jnp.bfloat16)
    for b in range(own_beams):
        rows = [jnp.where(diagonal, tied[chan][b : b + 1], 0.0) for chan in range(n_chan)]
        rows = jnp.concatenate(rows, axis=0).astype(jnp.bfloat16)
        out_ref[b] = dot_nt(spread, rows).astype(jnp.bfloat16)


def shards(
    volts,
    antenna_tile_weights,
    station_weights,
    tile_station,
    station_group,
    station_pos,
    beam_dir,
    beam_order,
):
    channels, _, samples, _ = volts.shape
    beams = beam_order.shape[0]
    n_stn, n_chan = lax.axis_size("stn"), lax.axis_size("chan")
    rows = beams // (n_stn * n_chan)
    width = channels * 2 * samples
    operands = (
        volts,
        antenna_tile_weights,
        station_weights,
        tile_station[None, :],
        station_group[None, :],
        station_pos.T,
        beam_dir.T,
        beam_order[None, :],
    )
    operands = [pltpu.with_memory_space_constraint(x, pltpu.HBM) for x in operands]
    partial = pl.pallas_call(
        kernel,
        out_shape=pltpu.VMEM((n_stn * n_chan, rows, width), jnp.bfloat16),
        in_specs=[pl.BlockSpec(memory_space=pltpu.HBM)] * len(operands),
        out_specs=pl.BlockSpec(memory_space=pltpu.VMEM),
        scratch_shapes=[pltpu.VMEM(x.shape, x.dtype) for x in operands]
        + [
            pltpu.VMEM((beams, channels * 2 * (station_weights.shape[2] // TPS)), jnp.bfloat16),
            pltpu.SemaphoreType.DMA((len(operands) - 1 + channels // CB,)),
        ],
        compiler_params=pltpu.CompilerParams(vmem_limit_bytes=24 * 2**20),
        name="partial_tied",
    )(*operands)
    parts = lax.all_to_all(
        partial,
        ("stn", "chan"),
        split_axis=0,
        concat_axis=0,
        axis_index_groups=[list(reversed(range(n_stn * n_chan)))],
        tiled=True,
    )
    vmem = pl.BlockSpec(memory_space=pltpu.VMEM)
    tied = pl.pallas_call(
        last_kernel,
        out_shape=jax.ShapeDtypeStruct((rows, 2 * samples, n_chan * channels), jnp.bfloat16),
        in_specs=[vmem],
        out_specs=vmem,
        compiler_params=pltpu.CompilerParams(vmem_limit_bytes=16 * 2**20),
        name="tied_beams",
    )(parts)
    return tied.transpose(0, 2, 1)


def solution(mesh):
    in_specs = (
        P("chan", None, None, "stn"),
        P("chan", None, "stn"),
        P("chan", None, "stn"),
        P("stn"),
        P(),
        P(),
        P(),
        P(),
    )
    out_specs = P(("stn", "chan"), None, None)
    return jax.shard_map(shards, mesh=mesh, in_specs=in_specs, out_specs=out_specs, check_vma=False)
```

```python
import functools
import math

import jax
import jax.numpy as jnp
from jax import lax
from jax.experimental import pallas as pl
from jax.experimental.pallas import tpu as pltpu
from jax.sharding import PartitionSpec as P

TILE_ANTENNAS = 16
TPS = 16
GROUPS = 4
CB = 8
CHUNK = 256
NT = (((1,), (1,)), ((), ()))
SIN = [(-1) ** i * (2 * math.pi) ** (2 * i + 1) / math.factorial(2 * i + 1) for i in range(7)]


def dot_nt(a, b):
    return lax.dot_general(a, b, NT, preferred_element_type=jnp.float32)


def iota(shape, dim):
    return lax.broadcasted_iota(jnp.int32, shape, dim)


def beam_columns(order_ref, dir_ref, start, rows):
    beams = order_ref.shape[1]
    each = beams // (lax.axis_size("stn") * lax.axis_size("chan"))
    order = order_ref[...].astype(jnp.float32)
    lane = iota((rows, beams), 1)
    slot = iota((rows, beams), 0) + start
    own = lane == beams - each - slot // each * each + slot % each
    ids = jnp.sum(jnp.where(own, order, 0.0), axis=1, keepdims=True)
    pick = lane.astype(jnp.float32) == ids
    east = jnp.sum(jnp.where(pick, dir_ref[0:1, :], 0.0), axis=1, keepdims=True)
    north = jnp.sum(jnp.where(pick, dir_ref[1:2, :], 0.0), axis=1, keepdims=True)
    group = ids - GROUPS * jnp.floor(ids * (1.0 / GROUPS))
    return east, north, group


def station_rows(pos_ref, group_ref, stations, lanes):
    total = group_ref.shape[1]
    first = lax.axis_index("stn") * stations
    own = iota((stations, total), 1) == iota((stations, total), 0) + first
    spread = iota((stations, lanes), 0) == iota((stations, lanes), 1) % stations

    def turn(row):
        column = jnp.sum(jnp.where(own, row, 0.0), axis=1, keepdims=True)
        return jnp.sum(jnp.where(spread, column, 0.0), axis=0, keepdims=True)

    return turn(pos_ref[0:1, :]), turn(pos_ref[1:2, :]), turn(group_ref[...].astype(jnp.float32))


def cos_turns(t):
    y = t - jnp.floor(t + 0.5)
    z = 0.25 - jnp.abs(y)
    z2 = z * z
    value = jnp.full_like(z, SIN[-1])
    for coefficient in SIN[-2::-1]:
        value = value * z2 + coefficient
    return value * z


def kernel(
    volt_hbm,
    aw_hbm,
    sw_hbm,
    ts_hbm,
    group_hbm,
    pos_hbm,
    dir_hbm,
    order_hbm,
    out_ref,
    volts,
    aw_ref,
    sw_ref,
    ts_ref,
    group_ref,
    pos_ref,
    dir_ref,
    order_ref,
    tied_ref,
    sems,
):
    channels, _, tiles = sw_ref.shape
    antennas = volt_hbm.shape[1]
    samples = volt_hbm.shape[0] // (2 * channels)
    stations = tiles // TPS
    groups = channels // CB
    rows_c = 2 * samples
    beams = order_ref.shape[1]
    lanes = CB * 2 * stations
    scale = 1.0 / math.sqrt(group_ref.shape[1])

    def start(source, target, k):
        copy = pltpu.make_async_copy(source, target, sems.at[k])
        copy.start()
        return copy

    def voltages(g):
        part = pl.ds(g * CB * rows_c, CB * rows_c)
        return volt_hbm.at[part], volts.at[part]

    pairs = [
        voltages(0),
        (aw_hbm, aw_ref),
        (order_hbm, order_ref),
        (dir_hbm, dir_ref),
        (pos_hbm, pos_ref),
        (group_hbm, group_ref),
        (ts_hbm, ts_ref),
        (sw_hbm, sw_ref),
    ] + [voltages(g) for g in range(1, groups)]
    copies = [start(source, target, k) for k, (source, target) in enumerate(pairs)]
    large = copies[:1] + copies[8:]
    antenna_tile = iota((CHUNK // TILE_ANTENNAS, CHUNK), 1) // TILE_ANTENNAS
    sum_tile = (antenna_tile == iota(antenna_tile.shape, 0)).astype(jnp.bfloat16)
    for copy in copies[:2]:
        copy.wait()

    def tile_beams(g):
        products = []
        weights = aw_ref[g * CB : (g + 1) * CB].astype(jnp.float32)
        for c in range(CB):
            w_re = jnp.broadcast_to(weights[c, 0:1], (samples, antennas)).astype(jnp.bfloat16)
            w_im = jnp.broadcast_to(weights[c, 1:2], (samples, antennas)).astype(jnp.bfloat16)
            first = (g * CB + c) * rows_c
            v_re, v_im = volts[first : first + samples], volts[first + samples : first + rows_c]
            products.append(w_re * v_re - w_im * v_im)
            products.append(w_re * v_im + w_im * v_re)
        products = jnp.concatenate(products, axis=0)
        sums = [
            dot_nt(sum_tile, products[:, first : first + CHUNK])
            for first in range(0, antennas, CHUNK)
        ]
        return jnp.concatenate(sums, axis=0)

    last = tile_beams(0)
    for copy in copies[2:9]:
        copy.wait()

    east_s, north_s, group_s = station_rows(pos_ref, group_ref, stations, lanes)
    lane = iota((1, lanes), 1)
    channel_lane = lane // (2 * stations)
    quarter = 0.25 * ((lane // stations) % 2).astype(jnp.float32)
    first_chan = lax.axis_index("chan") * channels
    total_chans = channels * lax.axis_size("chan")
    block = min(64, beams)

    def tied_rows(first):
        east, north, group = beam_columns(order_ref, dir_ref, first, block)
        delay = east * east_s + north * north_s
        member = jnp.where(group == group_s, scale, 0.0)
        for g in range(groups):
            freq = 1.0 + (first_chan + g * CB + channel_lane).astype(jnp.float32) / total_chans
            wave = cos_turns(delay * freq - quarter)
            tied_ref[pl.ds(first, block), g * lanes : (g + 1) * lanes] = (wave * member).astype(
                jnp.bfloat16
            )

    if beams == block:
        tied_rows(0)
    else:

        def body(i, carry):
            tied_rows(pl.multiple_of(i * block, block))
            return carry

        lax.fori_loop(0, beams // block, body, 0)

    member_table = (iota((stations, tiles), 0) == ts_ref[...] % stations).astype(jnp.float32)
    own_channel = iota((lanes, CB * rows_c), 0) // (2 * stations) == iota(
        (lanes, CB * rows_c), 1
    ) // rows_c

    imag_column = iota((tiles, CB * rows_c), 1) // samples % 2 == 1
    station_rows_of = []
    for g in range(groups):
        swt = sw_ref[g * CB : (g + 1) * CB].astype(jnp.float32)
        right = []
        for c in range(CB):
            re = swt[c, 0:1] * member_table
            im = swt[c, 1:2] * member_table
            right.append(jnp.concatenate([re, -im], axis=1))
            right.append(jnp.concatenate([im, re], axis=1))
        station_rows_of.append(jnp.concatenate(right, axis=0).astype(jnp.bfloat16))

    def tied_beams(g, beams_tile):
        width = CB * rows_c
        other = jnp.where(
            imag_column,
            -pltpu.roll(beams_tile, samples, 1),
            pltpu.roll(beams_tile, width - samples, 1),
        )
        left = jnp.concatenate([beams_tile, other], axis=0).astype(jnp.bfloat16)
        station = jnp.dot(station_rows_of[g], left, preferred_element_type=jnp.float32)
        station = jnp.where(own_channel, station, 0.0).astype(jnp.bfloat16)
        tied = jnp.dot(
            tied_ref[:, g * lanes : (g + 1) * lanes], station, preferred_element_type=jnp.float32
        )
        devices, rows, _ = out_ref.shape
        out_ref[:, :, g * CB * rows_c : (g + 1) * CB * rows_c] = tied.astype(jnp.bfloat16).reshape(
            devices, rows, CB * rows_c
        )

    for g in range(1, groups):
        if g > 1:
            large[g].wait()
        now = tile_beams(g)
        tied_beams(g - 1, last)
        last = now
    tied_beams(groups - 1, last)


def last_kernel(parts_ref, out_ref):
    n_stn, n_chan = lax.axis_size("stn"), lax.axis_size("chan")
    own_beams, rows_c, total_chans = out_ref.shape
    channels = total_chans // n_chan
    width = channels * rows_c
    parts = parts_ref[...].astype(jnp.float32)
    tied = [sum(parts[n_chan - 1 - chan + k * n_chan] for k in range(n_stn)) for chan in range(n_chan)]
    diagonal = iota((channels, width), 0) == iota((channels, width), 1) // rows_c
    spread = (iota((rows_c, width), 0) == iota((rows_c, width), 1) % rows_c).astype(jnp.bfloat16)
    for b in range(own_beams):
        rows = [jnp.where(diagonal, tied[chan][b : b + 1], 0.0) for chan in range(n_chan)]
        rows = jnp.concatenate(rows, axis=0).astype(jnp.bfloat16)
        out_ref[b] = dot_nt(spread, rows).astype(jnp.bfloat16)


def shards(
    volts,
    antenna_tile_weights,
    station_weights,
    tile_station,
    station_group,
    station_pos,
    beam_dir,
    beam_order,
):
    channels, _, samples, _ = volts.shape
    beams = beam_order.shape[0]
    n_stn, n_chan = lax.axis_size("stn"), lax.axis_size("chan")
    rows = beams // (n_stn * n_chan)
    width = channels * 2 * samples
    operands = (
        volts.reshape(-1, volts.shape[3]),
        antenna_tile_weights,
        station_weights,
        tile_station[None, :],
        station_group[None, :],
        station_pos.T,
        beam_dir.T,
        beam_order[None, :],
    )
    operands = [pltpu.with_memory_space_constraint(x, pltpu.HBM) for x in operands]
    partial = pl.pallas_call(
        kernel,
        out_shape=pltpu.VMEM((n_stn * n_chan, rows, width), jnp.bfloat16),
        in_specs=[pl.BlockSpec(memory_space=pltpu.HBM)] * len(operands),
        out_specs=pl.BlockSpec(memory_space=pltpu.VMEM),
        scratch_shapes=[pltpu.VMEM(x.shape, x.dtype) for x in operands]
        + [
            pltpu.VMEM((beams, channels * 2 * (station_weights.shape[2] // TPS)), jnp.bfloat16),
            pltpu.SemaphoreType.DMA((len(operands) - 1 + channels // CB,)),
        ],
        compiler_params=pltpu.CompilerParams(vmem_limit_bytes=24 * 2**20),
        name="partial_tied",
    )(*operands)
    parts = lax.all_to_all(
        partial,
        ("stn", "chan"),
        split_axis=0,
        concat_axis=0,
        axis_index_groups=[list(reversed(range(n_stn * n_chan)))],
        tiled=True,
    )
    vmem = pl.BlockSpec(memory_space=pltpu.VMEM)
    tied = pl.pallas_call(
        last_kernel,
        out_shape=jax.ShapeDtypeStruct((rows, 2 * samples, n_chan * channels), jnp.bfloat16),
        in_specs=[vmem],
        out_specs=vmem,
        compiler_params=pltpu.CompilerParams(vmem_limit_bytes=16 * 2**20),
        name="tied_beams",
    )(parts)
    return tied.transpose(0, 2, 1)


def solution(mesh):
    in_specs = (
        P("chan", None, None, "stn"),
        P("chan", None, "stn"),
        P("chan", None, "stn"),
        P("stn"),
        P(),
        P(),
        P(),
        P(),
    )
    out_specs = P(("stn", "chan"), None, None)
    return jax.shard_map(shards, mesh=mesh, in_specs=in_specs, out_specs=out_specs, check_vma=False)
```

```python
import functools
import math

import jax
import jax.numpy as jnp
from jax import lax
from jax.experimental import pallas as pl
from jax.experimental.pallas import tpu as pltpu
from jax.sharding import PartitionSpec as P

TILE_ANTENNAS = 16
TPS = 16
GROUPS = 4
CB = 8
CHUNK = 256
NT = (((1,), (1,)), ((), ()))
SIN = [(-1) ** i * (2 * math.pi) ** (2 * i + 1) / math.factorial(2 * i + 1) for i in range(7)]


def dot_nt(a, b):
    return lax.dot_general(a, b, NT, preferred_element_type=jnp.float32)


def iota(shape, dim):
    return lax.broadcasted_iota(jnp.int32, shape, dim)


def beam_columns(order_ref, dir_ref, start, rows):
    beams = order_ref.shape[1]
    each = beams // (lax.axis_size("stn") * lax.axis_size("chan"))
    order = order_ref[...].astype(jnp.float32)
    lane = iota((rows, beams), 1)
    slot = iota((rows, beams), 0) + start
    own = lane == beams - each - slot // each * each + slot % each
    ids = jnp.sum(jnp.where(own, order, 0.0), axis=1, keepdims=True)
    pick = lane.astype(jnp.float32) == ids
    east = jnp.sum(jnp.where(pick, dir_ref[0:1, :], 0.0), axis=1, keepdims=True)
    north = jnp.sum(jnp.where(pick, dir_ref[1:2, :], 0.0), axis=1, keepdims=True)
    group = ids - GROUPS * jnp.floor(ids * (1.0 / GROUPS))
    return east, north, group


def station_rows(pos_ref, group_ref, stations, lanes):
    total = group_ref.shape[1]
    first = lax.axis_index("stn") * stations
    own = iota((stations, total), 1) == iota((stations, total), 0) + first
    spread = iota((stations, lanes), 0) == iota((stations, lanes), 1) % stations

    def turn(row):
        column = jnp.sum(jnp.where(own, row, 0.0), axis=1, keepdims=True)
        return jnp.sum(jnp.where(spread, column, 0.0), axis=0, keepdims=True)

    return turn(pos_ref[0:1, :]), turn(pos_ref[1:2, :]), turn(group_ref[...].astype(jnp.float32))


def cos_turns(t):
    y = t - jnp.floor(t + 0.5)
    z = 0.25 - jnp.abs(y)
    z2 = z * z
    value = jnp.full_like(z, SIN[-1])
    for coefficient in SIN[-2::-1]:
        value = value * z2 + coefficient
    return value * z


def kernel(
    volt_hbm,
    aw_hbm,
    sw_hbm,
    ts_hbm,
    group_hbm,
    pos_hbm,
    dir_hbm,
    order_hbm,
    out_ref,
    volts,
    aw_ref,
    sw_ref,
    ts_ref,
    group_ref,
    pos_ref,
    dir_ref,
    order_ref,
    tied_ref,
    station_ref,
    tile_ref,
    sems,
):
    channels, _, tiles = sw_ref.shape
    groups, rows_g, antennas = volt_hbm.shape
    stations = tiles // TPS
    rows_c = rows_g // CB
    samples = rows_c // 2
    beams = order_ref.shape[1]
    lanes = CB * 2 * stations
    scale = 1.0 / math.sqrt(group_ref.shape[1])

    small = [
        (order_hbm, order_ref),
        (dir_hbm, dir_ref),
        (pos_hbm, pos_ref),
        (group_hbm, group_ref),
        (ts_hbm, ts_ref),
        (sw_hbm, sw_ref),
        (aw_hbm, aw_ref),
    ]
    small = [pltpu.make_async_copy(*pair, sems.at[k]) for k, pair in enumerate(small)]

    def voltages(g):
        return pltpu.make_async_copy(volt_hbm.at[g], volts.at[g], sems.at[len(small) + g])

    for copy in small[:4] + [voltages(0)] + small[4:] + [voltages(g) for g in range(1, groups)]:
        copy.start()
    antenna_tile = iota((CHUNK // TILE_ANTENNAS, CHUNK), 1) // TILE_ANTENNAS
    sum_tile = (antenna_tile == iota(antenna_tile.shape, 0)).astype(jnp.bfloat16)
    own_channel = iota((lanes, rows_g), 0) // (2 * stations) == iota((lanes, rows_g), 1) // rows_c
    imag_column = iota((tiles, rows_g), 1) // samples % 2 == 1
    tile_ref[...] = jnp.zeros_like(tile_ref)
    for copy in small:
        copy.wait()

    east_s, north_s, group_s = station_rows(pos_ref, group_ref, stations, lanes)
    lane = iota((1, lanes), 1)
    channel_lane = lane // (2 * stations)
    quarter = 0.25 * ((lane // stations) % 2).astype(jnp.float32)
    first_chan = lax.axis_index("chan") * channels
    total_chans = channels * lax.axis_size("chan")
    block = min(64, beams)

    def tied_rows(i, carry):
        first = pl.multiple_of(i * block, block)
        east, north, group = beam_columns(order_ref, dir_ref, first, block)
        delay = east * east_s + north * north_s
        member = jnp.where(group == group_s, scale, 0.0)

        def tied_group(g, carry):
            freq = 1.0 + (first_chan + g * CB + channel_lane).astype(jnp.float32) / total_chans
            wave = cos_turns(delay * freq - quarter)
            tied_ref[g, pl.ds(first, block), :] = (wave * member).astype(jnp.bfloat16)
            return carry

        return lax.fori_loop(0, groups, tied_group, carry)

    lax.fori_loop(0, beams // block, tied_rows, 0)
    member_table = (iota((stations, tiles), 0) == ts_ref[...] % stations).astype(jnp.float32)

    def station_group(g, carry):
        swt = sw_ref[pl.ds(g * CB, CB)].astype(jnp.float32)
        right = []
        for c in range(CB):
            re = swt[c, 0:1] * member_table
            im = swt[c, 1:2] * member_table
            right.append(jnp.concatenate([re, -im], axis=1))
            right.append(jnp.concatenate([im, re], axis=1))
        station_ref[g] = jnp.concatenate(right, axis=0).astype(jnp.bfloat16)
        return carry

    lax.fori_loop(0, groups, station_group, 0)

    def tile_beams(g):
        products = []
        weights = aw_ref[pl.ds(g * CB, CB)].astype(jnp.float32)
        for c in range(CB):
            w_re = jnp.broadcast_to(weights[c, 0:1], (samples, antennas)).astype(jnp.bfloat16)
            w_im = jnp.broadcast_to(weights[c, 1:2], (samples, antennas)).astype(jnp.bfloat16)
            first = c * rows_c
            v_re = volts[g, first : first + samples]
            v_im = volts[g, first + samples : first + rows_c]
            products.append(w_re * v_re - w_im * v_im)
            products.append(w_re * v_im + w_im * v_re)
        products = jnp.concatenate(products, axis=0)
        sums = [
            dot_nt(sum_tile, products[:, first : first + CHUNK])
            for first in range(0, antennas, CHUNK)
        ]
        return jnp.concatenate(sums, axis=0)

    def tied_beams(g, beams_tile):
        other = jnp.where(
            imag_column,
            -pltpu.roll(beams_tile, samples, 1),
            pltpu.roll(beams_tile, rows_g - samples, 1),
        )
        left = jnp.concatenate([beams_tile, other], axis=0).astype(jnp.bfloat16)
        station = jnp.dot(station_ref[g], left, preferred_element_type=jnp.float32)
        station = jnp.where(own_channel, station, 0.0).astype(jnp.bfloat16)
        tied = jnp.dot(tied_ref[g], station, preferred_element_type=jnp.float32)
        devices, rows, _ = out_ref.shape
        columns = pl.ds(pl.multiple_of(g * rows_g, rows_g), rows_g)
        out_ref[:, :, columns] = tied.astype(jnp.bfloat16).reshape(devices, rows, rows_g)

    def step(g, carry):
        voltages(g).wait()
        now = tile_beams(g)
        tied_beams(jnp.maximum(g - 1, 0), tile_ref[...])
        tile_ref[...] = now
        return carry

    lax.fori_loop(0, groups, step, 0)
    tied_beams(groups - 1, tile_ref[...])


def last_kernel(parts_ref, out_ref):
    n_stn, n_chan = lax.axis_size("stn"), lax.axis_size("chan")
    own_beams, rows_c, total_chans = out_ref.shape
    channels = total_chans // n_chan
    width = channels * rows_c
    parts = parts_ref[...].astype(jnp.float32)
    tied = [sum(parts[n_chan - 1 - chan + k * n_chan] for k in range(n_stn)) for chan in range(n_chan)]
    diagonal = iota((channels, width), 0) == iota((channels, width), 1) // rows_c
    spread = (iota((rows_c, width), 0) == iota((rows_c, width), 1) % rows_c).astype(jnp.bfloat16)
    for b in range(own_beams):
        rows = [jnp.where(diagonal, tied[chan][b : b + 1], 0.0) for chan in range(n_chan)]
        rows = jnp.concatenate(rows, axis=0).astype(jnp.bfloat16)
        out_ref[b] = dot_nt(spread, rows).astype(jnp.bfloat16)


def shards(
    volts,
    antenna_tile_weights,
    station_weights,
    tile_station,
    station_group,
    station_pos,
    beam_dir,
    beam_order,
):
    channels, _, samples, _ = volts.shape
    beams = beam_order.shape[0]
    n_stn, n_chan = lax.axis_size("stn"), lax.axis_size("chan")
    rows = beams // (n_stn * n_chan)
    width = channels * 2 * samples
    tiles = station_weights.shape[2]
    lanes = CB * 2 * (tiles // TPS)
    operands = (
        volts.reshape(channels // CB, CB * 2 * samples, volts.shape[3]),
        antenna_tile_weights,
        station_weights,
        tile_station[None, :],
        station_group[None, :],
        station_pos.T,
        beam_dir.T,
        beam_order[None, :],
    )
    operands = [pltpu.with_memory_space_constraint(x, pltpu.HBM) for x in operands]
    partial = pl.pallas_call(
        kernel,
        out_shape=pltpu.VMEM((n_stn * n_chan, rows, width), jnp.bfloat16),
        in_specs=[pl.BlockSpec(memory_space=pltpu.HBM)] * len(operands),
        out_specs=pl.BlockSpec(memory_space=pltpu.VMEM),
        scratch_shapes=[pltpu.VMEM(x.shape, x.dtype) for x in operands]
        + [
            pltpu.VMEM((channels // CB, beams, lanes), jnp.bfloat16),
            pltpu.VMEM((channels // CB, lanes, 2 * tiles), jnp.bfloat16),
            pltpu.VMEM((tiles, CB * 2 * samples), jnp.float32),
            pltpu.SemaphoreType.DMA((len(operands) - 1 + channels // CB,)),
        ],
        compiler_params=pltpu.CompilerParams(vmem_limit_bytes=24 * 2**20),
        name="partial_tied",
    )(*operands)
    parts = lax.all_to_all(
        partial,
        ("stn", "chan"),
        split_axis=0,
        concat_axis=0,
        axis_index_groups=[list(reversed(range(n_stn * n_chan)))],
        tiled=True,
    )
    vmem = pl.BlockSpec(memory_space=pltpu.VMEM)
    tied = pl.pallas_call(
        last_kernel,
        out_shape=jax.ShapeDtypeStruct((rows, 2 * samples, n_chan * channels), jnp.bfloat16),
        in_specs=[vmem],
        out_specs=vmem,
        compiler_params=pltpu.CompilerParams(vmem_limit_bytes=16 * 2**20),
        name="tied_beams",
    )(parts)
    return tied.transpose(0, 2, 1)


def solution(mesh):
    in_specs = (
        P("chan", None, None, "stn"),
        P("chan", None, "stn"),
        P("chan", None, "stn"),
        P("stn"),
        P(),
        P(),
        P(),
        P(),
    )
    out_specs = P(("stn", "chan"), None, None)
    return jax.shard_map(shards, mesh=mesh, in_specs=in_specs, out_specs=out_specs, check_vma=False)
```

```python
import functools
import math

import jax
import jax.numpy as jnp
from jax import lax
from jax.experimental import pallas as pl
from jax.experimental.pallas import tpu as pltpu
from jax.sharding import PartitionSpec as P

TILE_ANTENNAS = 16
TPS = 16
GROUPS = 4
CB = 8
CHUNK = 256
NT = (((1,), (1,)), ((), ()))
SIN = [(-1) ** i * (2 * math.pi) ** (2 * i + 1) / math.factorial(2 * i + 1) for i in range(7)]


def dot_nt(a, b):
    return lax.dot_general(a, b, NT, preferred_element_type=jnp.float32)


def iota(shape, dim):
    return lax.broadcasted_iota(jnp.int32, shape, dim)


def beam_columns(order_ref, dir_ref, start, rows):
    beams = order_ref.shape[1]
    each = beams // (lax.axis_size("stn") * lax.axis_size("chan"))
    order = order_ref[...].astype(jnp.float32)
    lane = iota((rows, beams), 1)
    slot = iota((rows, beams), 0) + start
    own = lane == beams - each - slot // each * each + slot % each
    ids = jnp.sum(jnp.where(own, order, 0.0), axis=1, keepdims=True)
    pick = lane.astype(jnp.float32) == ids
    east = jnp.sum(jnp.where(pick, dir_ref[0:1, :], 0.0), axis=1, keepdims=True)
    north = jnp.sum(jnp.where(pick, dir_ref[1:2, :], 0.0), axis=1, keepdims=True)
    group = ids - GROUPS * jnp.floor(ids * (1.0 / GROUPS))
    return east, north, group


def station_rows(pos_ref, group_ref, stations, lanes):
    total = group_ref.shape[1]
    first = lax.axis_index("stn") * stations
    own = iota((stations, total), 1) == iota((stations, total), 0) + first
    spread = iota((stations, lanes), 0) == iota((stations, lanes), 1) % stations

    def turn(row):
        column = jnp.sum(jnp.where(own, row, 0.0), axis=1, keepdims=True)
        return jnp.sum(jnp.where(spread, column, 0.0), axis=0, keepdims=True)

    return turn(pos_ref[0:1, :]), turn(pos_ref[1:2, :]), turn(group_ref[...].astype(jnp.float32))


def cos_turns(t):
    y = t - jnp.floor(t + 0.5)
    z = 0.25 - jnp.abs(y)
    z2 = z * z
    value = jnp.full_like(z, SIN[-1])
    for coefficient in SIN[-2::-1]:
        value = value * z2 + coefficient
    return value * z


def kernel(
    volt_hbm,
    aw_hbm,
    sw_hbm,
    ts_hbm,
    group_hbm,
    pos_hbm,
    dir_hbm,
    order_hbm,
    out_ref,
    volts,
    aw_ref,
    sw_ref,
    ts_ref,
    group_ref,
    pos_ref,
    dir_ref,
    order_ref,
    tied_ref,
    sems,
):
    channels, _, tiles = sw_ref.shape
    antennas = volt_hbm.shape[1]
    samples = volt_hbm.shape[0] // (2 * channels)
    stations = tiles // TPS
    groups = channels // CB
    rows_c = 2 * samples
    beams = order_ref.shape[1]
    lanes = CB * 2 * stations
    scale = 1.0 / math.sqrt(group_ref.shape[1])

    def start(source, target, k):
        copy = pltpu.make_async_copy(source, target, sems.at[k])
        copy.start()
        return copy

    def voltages(g):
        part = pl.ds(g * CB * rows_c, CB * rows_c)
        return volt_hbm.at[part], volts.at[part]

    pairs = [
        voltages(0),
        (aw_hbm, aw_ref),
        (order_hbm, order_ref),
        (dir_hbm, dir_ref),
        (pos_hbm, pos_ref),
        (group_hbm, group_ref),
        (ts_hbm, ts_ref),
        (sw_hbm, sw_ref),
    ] + [voltages(g) for g in range(1, groups)]
    copies = [start(source, target, k) for k, (source, target) in enumerate(pairs)]
    large = copies[:1] + copies[8:]
    antenna_tile = iota((CHUNK // TILE_ANTENNAS, CHUNK), 1) // TILE_ANTENNAS
    sum_tile = (antenna_tile == iota(antenna_tile.shape, 0)).astype(jnp.bfloat16)
    for copy in copies[:2]:
        copy.wait()

    def tile_beams(g):
        products = []
        weights = aw_ref[g * CB : (g + 1) * CB].astype(jnp.float32)
        for c in range(CB):
            w_re = jnp.broadcast_to(weights[c, 0:1], (samples, antennas)).astype(jnp.bfloat16)
            w_im = jnp.broadcast_to(weights[c, 1:2], (samples, antennas)).astype(jnp.bfloat16)
            first = (g * CB + c) * rows_c
            v_re, v_im = volts[first : first + samples], volts[first + samples : first + rows_c]
            products.append(w_re * v_re - w_im * v_im)
            products.append(w_re * v_im + w_im * v_re)
        products = jnp.concatenate(products, axis=0)
        sums = [
            dot_nt(sum_tile, products[:, first : first + CHUNK])
            for first in range(0, antennas, CHUNK)
        ]
        return jnp.concatenate(sums, axis=0)

    last = tile_beams(0)
    for copy in copies[2:9]:
        copy.wait()

    east_s, north_s, group_s = station_rows(pos_ref, group_ref, stations, lanes)
    lane = iota((1, lanes), 1)
    channel_lane = lane // (2 * stations)
    quarter = 0.25 * ((lane // stations) % 2).astype(jnp.float32)
    first_chan = lax.axis_index("chan") * channels
    total_chans = channels * lax.axis_size("chan")
    block = min(64, beams)

    def tied_rows(first):
        east, north, group = beam_columns(order_ref, dir_ref, first, block)
        delay = east * east_s + north * north_s
        member = jnp.where(group == group_s, scale, 0.0)
        for g in range(groups):
            freq = 1.0 + (first_chan + g * CB + channel_lane).astype(jnp.float32) / total_chans
            wave = cos_turns(delay * freq - quarter)
            tied_ref[pl.ds(first, block), g * lanes : (g + 1) * lanes] = (wave * member).astype(
                jnp.bfloat16
            )

    if beams == block:
        tied_rows(0)
    else:

        def body(i, carry):
            tied_rows(pl.multiple_of(i * block, block))
            return carry

        lax.fori_loop(0, beams // block, body, 0)

    member_table = (iota((stations, tiles), 0) == ts_ref[...] % stations).astype(jnp.float32)
    own_channel = iota((lanes, CB * rows_c), 0) // (2 * stations) == iota(
        (lanes, CB * rows_c), 1
    ) // rows_c

    imag_column = iota((tiles, CB * rows_c), 1) // samples % 2 == 1
    station_rows_of = []
    for g in range(groups):
        swt = sw_ref[g * CB : (g + 1) * CB].astype(jnp.float32)
        right = []
        for c in range(CB):
            re = swt[c, 0:1] * member_table
            im = swt[c, 1:2] * member_table
            right.append(jnp.concatenate([re, -im], axis=1))
            right.append(jnp.concatenate([im, re], axis=1))
        station_rows_of.append(jnp.concatenate(right, axis=0).astype(jnp.bfloat16))

    def tied_beams(g, beams_tile):
        width = CB * rows_c
        other = jnp.where(
            imag_column,
            -pltpu.roll(beams_tile, samples, 1),
            pltpu.roll(beams_tile, width - samples, 1),
        )
        left = jnp.concatenate([beams_tile, other], axis=0).astype(jnp.bfloat16)
        station = jnp.dot(station_rows_of[g], left, preferred_element_type=jnp.float32)
        station = jnp.where(own_channel, station, 0.0).astype(jnp.bfloat16)
        tied = jnp.dot(
            tied_ref[:, g * lanes : (g + 1) * lanes], station, preferred_element_type=jnp.float32
        )
        out_ref[:, g * CB * rows_c : (g + 1) * CB * rows_c] = tied.astype(jnp.bfloat16)

    for g in range(1, groups):
        if g > 1:
            large[g].wait()
        now = tile_beams(g)
        tied_beams(g - 1, last)
        last = now
    tied_beams(groups - 1, last)


def last_kernel(parts_ref, out_ref):
    n_stn, n_chan = lax.axis_size("stn"), lax.axis_size("chan")
    own_beams, rows_c, total_chans = out_ref.shape
    channels = total_chans // n_chan
    width = channels * rows_c
    parts = parts_ref[...].astype(jnp.float32)
    tied = [sum(parts[n_chan - 1 - chan + k * n_chan] for k in range(n_stn)) for chan in range(n_chan)]
    diagonal = iota((channels, width), 0) == iota((channels, width), 1) // rows_c
    spread = (iota((rows_c, width), 0) == iota((rows_c, width), 1) % rows_c).astype(jnp.bfloat16)
    for b in range(own_beams):
        rows = [jnp.where(diagonal, tied[chan][b : b + 1], 0.0) for chan in range(n_chan)]
        rows = jnp.concatenate(rows, axis=0).astype(jnp.bfloat16)
        out_ref[b] = dot_nt(spread, rows).astype(jnp.bfloat16)


def shards(
    volts,
    antenna_tile_weights,
    station_weights,
    tile_station,
    station_group,
    station_pos,
    beam_dir,
    beam_order,
):
    channels, _, samples, _ = volts.shape
    beams = beam_order.shape[0]
    n_stn, n_chan = lax.axis_size("stn"), lax.axis_size("chan")
    rows = beams // (n_stn * n_chan)
    width = channels * 2 * samples
    operands = (
        volts.reshape(-1, volts.shape[3]),
        antenna_tile_weights,
        station_weights,
        tile_station[None, :],
        station_group[None, :],
        station_pos.T,
        beam_dir.T,
        beam_order[None, :],
    )
    operands = [pltpu.with_memory_space_constraint(x, pltpu.HBM) for x in operands]
    partial = pl.pallas_call(
        kernel,
        out_shape=pltpu.VMEM((beams, width), jnp.bfloat16),
        in_specs=[pl.BlockSpec(memory_space=pltpu.HBM)] * len(operands),
        out_specs=pl.BlockSpec(memory_space=pltpu.VMEM),
        scratch_shapes=[pltpu.VMEM(x.shape, x.dtype) for x in operands]
        + [
            pltpu.VMEM((beams, channels * 2 * (station_weights.shape[2] // TPS)), jnp.bfloat16),
            pltpu.SemaphoreType.DMA((len(operands) - 1 + channels // CB,)),
        ],
        compiler_params=pltpu.CompilerParams(vmem_limit_bytes=24 * 2**20),
        name="partial_tied",
    )(*operands)
    parts = lax.all_to_all(
        partial.reshape(n_stn * n_chan, rows, width),
        ("stn", "chan"),
        split_axis=0,
        concat_axis=0,
        axis_index_groups=[list(reversed(range(n_stn * n_chan)))],
        tiled=True,
    )
    vmem = pl.BlockSpec(memory_space=pltpu.VMEM)
    tied = pl.pallas_call(
        last_kernel,
        out_shape=jax.ShapeDtypeStruct((rows, 2 * samples, n_chan * channels), jnp.bfloat16),
        in_specs=[vmem],
        out_specs=vmem,
        compiler_params=pltpu.CompilerParams(vmem_limit_bytes=16 * 2**20),
        name="tied_beams",
    )(parts)
    return tied.transpose(0, 2, 1)


def solution(mesh):
    in_specs = (
        P("chan", None, None, "stn"),
        P("chan", None, "stn"),
        P("chan", None, "stn"),
        P("stn"),
        P(),
        P(),
        P(),
        P(),
    )
    out_specs = P(("stn", "chan"), None, None)
    return jax.shard_map(shards, mesh=mesh, in_specs=in_specs, out_specs=out_specs, check_vma=False)
```

```python
import functools
import math

import jax
import jax.numpy as jnp
from jax import lax
from jax.experimental import pallas as pl
from jax.experimental.pallas import tpu as pltpu
from jax.sharding import PartitionSpec as P

TILE_ANTENNAS = 16
TPS = 16
GROUPS = 4
CB = 8
CHUNK = 256
NT = (((1,), (1,)), ((), ()))
SIN = [(-1) ** i * (2 * math.pi) ** (2 * i + 1) / math.factorial(2 * i + 1) for i in range(7)]


def dot_nt(a, b):
    return lax.dot_general(a, b, NT, preferred_element_type=jnp.float32)


def iota(shape, dim):
    return lax.broadcasted_iota(jnp.int32, shape, dim)


def beam_columns(order_ref, dir_ref, start, rows):
    beams = order_ref.shape[1]
    each = beams // (lax.axis_size("stn") * lax.axis_size("chan"))
    order = order_ref[...].astype(jnp.float32)
    lane = iota((rows, beams), 1)
    slot = iota((rows, beams), 0) + start
    own = lane == beams - each - slot // each * each + slot % each
    ids = jnp.sum(jnp.where(own, order, 0.0), axis=1, keepdims=True)
    pick = lane.astype(jnp.float32) == ids
    east = jnp.sum(jnp.where(pick, dir_ref[0:1, :], 0.0), axis=1, keepdims=True)
    north = jnp.sum(jnp.where(pick, dir_ref[1:2, :], 0.0), axis=1, keepdims=True)
    group = ids - GROUPS * jnp.floor(ids * (1.0 / GROUPS))
    return east, north, group


def station_rows(pos_ref, group_ref, stations, lanes):
    total = group_ref.shape[1]
    first = lax.axis_index("stn") * stations
    own = iota((stations, total), 1) == iota((stations, total), 0) + first
    spread = iota((stations, lanes), 0) == iota((stations, lanes), 1) % stations

    def turn(row):
        column = jnp.sum(jnp.where(own, row, 0.0), axis=1, keepdims=True)
        return jnp.sum(jnp.where(spread, column, 0.0), axis=0, keepdims=True)

    return turn(pos_ref[0:1, :]), turn(pos_ref[1:2, :]), turn(group_ref[...].astype(jnp.float32))


def cos_turns(t):
    y = t - jnp.floor(t + 0.5)
    z = 0.25 - jnp.abs(y)
    z2 = z * z
    value = jnp.full_like(z, SIN[-1])
    for coefficient in SIN[-2::-1]:
        value = value * z2 + coefficient
    return value * z


def kernel(
    volt_hbm,
    aw_hbm,
    sw_hbm,
    ts_hbm,
    group_hbm,
    pos_hbm,
    dir_hbm,
    order_hbm,
    out_ref,
    volts,
    aw_ref,
    sw_ref,
    ts_ref,
    group_ref,
    pos_ref,
    dir_ref,
    order_ref,
    tied_ref,
    sems,
):
    channels, _, tiles = sw_ref.shape
    antennas = volt_hbm.shape[1]
    samples = volt_hbm.shape[0] // (2 * channels)
    stations = tiles // TPS
    groups = channels // CB
    rows_c = 2 * samples
    beams = order_ref.shape[1]
    lanes = CB * 2 * stations
    scale = 1.0 / math.sqrt(group_ref.shape[1])

    def start(source, target, k):
        copy = pltpu.make_async_copy(source, target, sems.at[k])
        copy.start()
        return copy

    pairs = [
        (aw_hbm, aw_ref),
        (volt_hbm, volts),
        (order_hbm, order_ref),
        (dir_hbm, dir_ref),
        (pos_hbm, pos_ref),
        (group_hbm, group_ref),
        (ts_hbm, ts_ref),
        (sw_hbm, sw_ref),
    ]
    copies = [start(source, target, k) for k, (source, target) in enumerate(pairs)]
    antenna_tile = iota((CHUNK // TILE_ANTENNAS, CHUNK), 1) // TILE_ANTENNAS
    sum_tile = (antenna_tile == iota(antenna_tile.shape, 0)).astype(jnp.bfloat16)
    for copy in copies[2:]:
        copy.wait()

    def tile_beams(g):
        products = []
        weights = aw_ref[g * CB : (g + 1) * CB].astype(jnp.float32)
        for c in range(CB):
            w_re = jnp.broadcast_to(weights[c, 0:1], (samples, antennas)).astype(jnp.bfloat16)
            w_im = jnp.broadcast_to(weights[c, 1:2], (samples, antennas)).astype(jnp.bfloat16)
            first = (g * CB + c) * rows_c
            v_re, v_im = volts[first : first + samples], volts[first + samples : first + rows_c]
            products.append(w_re * v_re - w_im * v_im)
            products.append(w_re * v_im + w_im * v_re)
        products = jnp.concatenate(products, axis=0)
        sums = [
            dot_nt(sum_tile, products[:, first : first + CHUNK])
            for first in range(0, antennas, CHUNK)
        ]
        return jnp.concatenate(sums, axis=0)

    east_s, north_s, group_s = station_rows(pos_ref, group_ref, stations, lanes)
    lane = iota((1, lanes), 1)
    channel_lane = lane // (2 * stations)
    quarter = 0.25 * ((lane // stations) % 2).astype(jnp.float32)
    first_chan = lax.axis_index("chan") * channels
    total_chans = channels * lax.axis_size("chan")
    block = min(64, beams)

    def tied_rows(first):
        east, north, group = beam_columns(order_ref, dir_ref, first, block)
        delay = east * east_s + north * north_s
        member = jnp.where(group == group_s, scale, 0.0)
        for g in range(groups):
            freq = 1.0 + (first_chan + g * CB + channel_lane).astype(jnp.float32) / total_chans
            wave = cos_turns(delay * freq - quarter)
            tied_ref[pl.ds(first, block), g * lanes : (g + 1) * lanes] = (wave * member).astype(
                jnp.bfloat16
            )

    if beams == block:
        tied_rows(0)
    else:

        def body(i, carry):
            tied_rows(pl.multiple_of(i * block, block))
            return carry

        lax.fori_loop(0, beams // block, body, 0)

    member_table = (iota((stations, tiles), 0) == ts_ref[...] % stations).astype(jnp.float32)
    own_channel = iota((lanes, CB * rows_c), 0) // (2 * stations) == iota(
        (lanes, CB * rows_c), 1
    ) // rows_c

    imag_column = iota((tiles, CB * rows_c), 1) // samples % 2 == 1
    station_rows_of = []
    for g in range(groups):
        swt = sw_ref[g * CB : (g + 1) * CB].astype(jnp.float32)
        right = []
        for c in range(CB):
            re = swt[c, 0:1] * member_table
            im = swt[c, 1:2] * member_table
            right.append(jnp.concatenate([re, -im], axis=1))
            right.append(jnp.concatenate([im, re], axis=1))
        station_rows_of.append(jnp.concatenate(right, axis=0).astype(jnp.bfloat16))

    def tied_beams(g, beams_tile):
        width = CB * rows_c
        other = jnp.where(
            imag_column,
            -pltpu.roll(beams_tile, samples, 1),
            pltpu.roll(beams_tile, width - samples, 1),
        )
        left = jnp.concatenate([beams_tile, other], axis=0).astype(jnp.bfloat16)
        station = jnp.dot(station_rows_of[g], left, preferred_element_type=jnp.float32)
        station = jnp.where(own_channel, station, 0.0).astype(jnp.bfloat16)
        tied = jnp.dot(
            tied_ref[:, g * lanes : (g + 1) * lanes], station, preferred_element_type=jnp.float32
        )
        devices, rows, _ = out_ref.shape
        out_ref[:, :, g * CB * rows_c : (g + 1) * CB * rows_c] = tied.astype(jnp.bfloat16).reshape(
            devices, rows, CB * rows_c
        )

    for copy in copies[:2]:
        copy.wait()
    last = tile_beams(0)
    for g in range(1, groups):
        now = tile_beams(g)
        tied_beams(g - 1, last)
        last = now
    tied_beams(groups - 1, last)


def last_kernel(parts_ref, out_ref):
    n_stn, n_chan = lax.axis_size("stn"), lax.axis_size("chan")
    own_beams, rows_c, total_chans = out_ref.shape
    channels = total_chans // n_chan
    width = channels * rows_c
    parts = parts_ref[...].astype(jnp.float32)
    tied = [sum(parts[n_chan - 1 - chan + k * n_chan] for k in range(n_stn)) for chan in range(n_chan)]
    diagonal = iota((channels, width), 0) == iota((channels, width), 1) // rows_c
    spread = (iota((rows_c, width), 0) == iota((rows_c, width), 1) % rows_c).astype(jnp.bfloat16)
    for b in range(own_beams):
        rows = [jnp.where(diagonal, tied[chan][b : b + 1], 0.0) for chan in range(n_chan)]
        rows = jnp.concatenate(rows, axis=0).astype(jnp.bfloat16)
        out_ref[b] = dot_nt(spread, rows).astype(jnp.bfloat16)


def shards(
    volts,
    antenna_tile_weights,
    station_weights,
    tile_station,
    station_group,
    station_pos,
    beam_dir,
    beam_order,
):
    channels, _, samples, _ = volts.shape
    beams = beam_order.shape[0]
    n_stn, n_chan = lax.axis_size("stn"), lax.axis_size("chan")
    rows = beams // (n_stn * n_chan)
    width = channels * 2 * samples
    operands = (
        volts.reshape(-1, volts.shape[3]),
        antenna_tile_weights,
        station_weights,
        tile_station[None, :],
        station_group[None, :],
        station_pos.T,
        beam_dir.T,
        beam_order[None, :],
    )
    operands = [pltpu.with_memory_space_constraint(x, pltpu.HBM) for x in operands]
    partial = pl.pallas_call(
        kernel,
        out_shape=pltpu.VMEM((n_stn * n_chan, rows, width), jnp.bfloat16),
        in_specs=[pl.BlockSpec(memory_space=pltpu.HBM)] * len(operands),
        out_specs=pl.BlockSpec(memory_space=pltpu.VMEM),
        scratch_shapes=[pltpu.VMEM(x.shape, x.dtype) for x in operands]
        + [
            pltpu.VMEM((beams, channels * 2 * (station_weights.shape[2] // TPS)), jnp.bfloat16),
            pltpu.SemaphoreType.DMA((len(operands),)),
        ],
        compiler_params=pltpu.CompilerParams(vmem_limit_bytes=24 * 2**20),
        name="partial_tied",
    )(*operands)
    parts = lax.all_to_all(
        partial,
        ("stn", "chan"),
        split_axis=0,
        concat_axis=0,
        axis_index_groups=[list(reversed(range(n_stn * n_chan)))],
        tiled=True,
    )
    vmem = pl.BlockSpec(memory_space=pltpu.VMEM)
    tied = pl.pallas_call(
        last_kernel,
        out_shape=jax.ShapeDtypeStruct((rows, 2 * samples, n_chan * channels), jnp.bfloat16),
        in_specs=[vmem],
        out_specs=vmem,
        compiler_params=pltpu.CompilerParams(vmem_limit_bytes=16 * 2**20),
        name="tied_beams",
    )(parts)
    return tied.transpose(0, 2, 1)


def solution(mesh):
    in_specs = (
        P("chan", None, None, "stn"),
        P("chan", None, "stn"),
        P("chan", None, "stn"),
        P("stn"),
        P(),
        P(),
        P(),
        P(),
    )
    out_specs = P(("stn", "chan"), None, None)
    return jax.shard_map(shards, mesh=mesh, in_specs=in_specs, out_specs=out_specs, check_vma=False)
```

```python
import functools
import math

import jax
import jax.numpy as jnp
from jax import lax
from jax.experimental import pallas as pl
from jax.experimental.pallas import tpu as pltpu
from jax.sharding import PartitionSpec as P

TILE_ANTENNAS = 16
TPS = 16
GROUPS = 4
CB = 8
CHUNK = 256
NT = (((1,), (1,)), ((), ()))
SIN = [(-1) ** i * (2 * math.pi) ** (2 * i + 1) / math.factorial(2 * i + 1) for i in range(7)]


def dot_nt(a, b):
    return lax.dot_general(a, b, NT, preferred_element_type=jnp.float32)


def iota(shape, dim):
    return lax.broadcasted_iota(jnp.int32, shape, dim)


def beam_columns(order_ref, dir_ref, start, rows):
    beams = order_ref.shape[1]
    each = beams // (lax.axis_size("stn") * lax.axis_size("chan"))
    order = order_ref[...].astype(jnp.float32)
    lane = iota((rows, beams), 1)
    slot = iota((rows, beams), 0) + start
    own = lane == beams - each - slot // each * each + slot % each
    ids = jnp.sum(jnp.where(own, order, 0.0), axis=1, keepdims=True)
    pick = lane.astype(jnp.float32) == ids
    east = jnp.sum(jnp.where(pick, dir_ref[0:1, :], 0.0), axis=1, keepdims=True)
    north = jnp.sum(jnp.where(pick, dir_ref[1:2, :], 0.0), axis=1, keepdims=True)
    group = ids - GROUPS * jnp.floor(ids * (1.0 / GROUPS))
    return east, north, group


def station_rows(pos_ref, group_ref, stations, lanes):
    total = group_ref.shape[1]
    first = lax.axis_index("stn") * stations
    own = iota((stations, total), 1) == iota((stations, total), 0) + first
    spread = iota((stations, lanes), 0) == iota((stations, lanes), 1) % stations

    def turn(row):
        column = jnp.sum(jnp.where(own, row, 0.0), axis=1, keepdims=True)
        return jnp.sum(jnp.where(spread, column, 0.0), axis=0, keepdims=True)

    return turn(pos_ref[0:1, :]), turn(pos_ref[1:2, :]), turn(group_ref[...].astype(jnp.float32))


def cos_turns(t):
    y = t - jnp.floor(t + 0.5)
    z = 0.25 - jnp.abs(y)
    z2 = z * z
    value = jnp.full_like(z, SIN[-1])
    for coefficient in SIN[-2::-1]:
        value = value * z2 + coefficient
    return value * z


def kernel(
    volt_hbm,
    aw_hbm,
    sw_hbm,
    ts_hbm,
    group_hbm,
    pos_hbm,
    dir_hbm,
    order_hbm,
    out_ref,
    volts,
    aw_ref,
    sw_ref,
    ts_ref,
    group_ref,
    pos_ref,
    dir_ref,
    order_ref,
    tied_ref,
    rows_ref,
    sems,
):
    channels, _, tiles = sw_ref.shape
    antennas = volt_hbm.shape[1]
    samples = volt_hbm.shape[0] // (2 * channels)
    stations = tiles // TPS
    groups = channels // CB
    rows_c = 2 * samples
    beams = order_ref.shape[1]
    lanes = CB * 2 * stations
    scale = 1.0 / math.sqrt(group_ref.shape[1])

    def start(source, target, k):
        copy = pltpu.make_async_copy(source, target, sems.at[k])
        copy.start()
        return copy

    def voltages(g):
        part = pl.ds(g * CB * rows_c, CB * rows_c)
        return volt_hbm.at[part], volts.at[part]

    pairs = [
        (aw_hbm, aw_ref),
        voltages(0),
        (order_hbm, order_ref),
        (dir_hbm, dir_ref),
        (pos_hbm, pos_ref),
        (group_hbm, group_ref),
        (ts_hbm, ts_ref),
        (sw_hbm, sw_ref),
    ] + [voltages(g) for g in range(1, groups)]
    copies = [start(source, target, k) for k, (source, target) in enumerate(pairs)]
    large = copies[1:2] + copies[8:]
    antenna_tile = iota((CHUNK // TILE_ANTENNAS, CHUNK), 1) // TILE_ANTENNAS
    sum_tile = (antenna_tile == iota(antenna_tile.shape, 0)).astype(jnp.bfloat16)
    copies[0].wait()
    for c in range(channels):
        weights = aw_ref[c].astype(jnp.float32)
        for part in range(2):
            row = jnp.broadcast_to(weights[part : part + 1], (samples, antennas))
            rows_ref[c, part] = row.astype(jnp.bfloat16)
    large[0].wait()

    def tile_beams(g):
        products = []
        for c in range(CB):
            w_re, w_im = rows_ref[g * CB + c, 0], rows_ref[g * CB + c, 1]
            first = (g * CB + c) * rows_c
            v_re, v_im = volts[first : first + samples], volts[first + samples : first + rows_c]
            products.append(w_re * v_re - w_im * v_im)
            products.append(w_re * v_im + w_im * v_re)
        products = jnp.concatenate(products, axis=0)
        sums = [
            dot_nt(sum_tile, products[:, first : first + CHUNK])
            for first in range(0, antennas, CHUNK)
        ]
        return jnp.concatenate(sums, axis=0)

    last = tile_beams(0)
    for copy in copies[2:9]:
        copy.wait()

    east_s, north_s, group_s = station_rows(pos_ref, group_ref, stations, lanes)
    lane = iota((1, lanes), 1)
    channel_lane = lane // (2 * stations)
    quarter = 0.25 * ((lane // stations) % 2).astype(jnp.float32)
    first_chan = lax.axis_index("chan") * channels
    total_chans = channels * lax.axis_size("chan")
    block = min(64, beams)

    def tied_rows(first):
        east, north, group = beam_columns(order_ref, dir_ref, first, block)
        delay = east * east_s + north * north_s
        member = jnp.where(group == group_s, scale, 0.0)
        for g in range(groups):
            freq = 1.0 + (first_chan + g * CB + channel_lane).astype(jnp.float32) / total_chans
            wave = cos_turns(delay * freq - quarter)
            tied_ref[pl.ds(first, block), g * lanes : (g + 1) * lanes] = (wave * member).astype(
                jnp.bfloat16
            )

    if beams == block:
        tied_rows(0)
    else:

        def body(i, carry):
            tied_rows(pl.multiple_of(i * block, block))
            return carry

        lax.fori_loop(0, beams // block, body, 0)

    member_table = (iota((stations, tiles), 0) == ts_ref[...] % stations).astype(jnp.float32)
    own_channel = iota((lanes, CB * rows_c), 0) // (2 * stations) == iota(
        (lanes, CB * rows_c), 1
    ) // rows_c

    imag_column = iota((tiles, CB * rows_c), 1) // samples % 2 == 1
    station_rows_of = []
    for g in range(groups):
        swt = sw_ref[g * CB : (g + 1) * CB].astype(jnp.float32)
        right = []
        for c in range(CB):
            re = swt[c, 0:1] * member_table
            im = swt[c, 1:2] * member_table
            right.append(jnp.concatenate([re, -im], axis=1))
            right.append(jnp.concatenate([im, re], axis=1))
        station_rows_of.append(jnp.concatenate(right, axis=0).astype(jnp.bfloat16))

    def tied_beams(g, beams_tile):
        width = CB * rows_c
        other = jnp.where(
            imag_column,
            -pltpu.roll(beams_tile, samples, 1),
            pltpu.roll(beams_tile, width - samples, 1),
        )
        left = jnp.concatenate([beams_tile, other], axis=0).astype(jnp.bfloat16)
        station = jnp.dot(station_rows_of[g], left, preferred_element_type=jnp.float32)
        station = jnp.where(own_channel, station, 0.0).astype(jnp.bfloat16)
        tied = jnp.dot(
            tied_ref[:, g * lanes : (g + 1) * lanes], station, preferred_element_type=jnp.float32
        )
        devices, rows, _ = out_ref.shape
        out_ref[:, :, g * CB * rows_c : (g + 1) * CB * rows_c] = tied.astype(jnp.bfloat16).reshape(
            devices, rows, CB * rows_c
        )

    for g in range(1, groups):
        if g > 1:
            large[g].wait()
        now = tile_beams(g)
        tied_beams(g - 1, last)
        last = now
    tied_beams(groups - 1, last)


def last_kernel(parts_ref, out_ref):
    n_stn, n_chan = lax.axis_size("stn"), lax.axis_size("chan")
    own_beams, rows_c, total_chans = out_ref.shape
    channels = total_chans // n_chan
    width = channels * rows_c
    parts = parts_ref[...].astype(jnp.float32)
    tied = [sum(parts[n_chan - 1 - chan + k * n_chan] for k in range(n_stn)) for chan in range(n_chan)]
    diagonal = iota((channels, width), 0) == iota((channels, width), 1) // rows_c
    spread = (iota((rows_c, width), 0) == iota((rows_c, width), 1) % rows_c).astype(jnp.bfloat16)
    for b in range(own_beams):
        rows = [jnp.where(diagonal, tied[chan][b : b + 1], 0.0) for chan in range(n_chan)]
        rows = jnp.concatenate(rows, axis=0).astype(jnp.bfloat16)
        out_ref[b] = dot_nt(spread, rows).astype(jnp.bfloat16)


def shards(
    volts,
    antenna_tile_weights,
    station_weights,
    tile_station,
    station_group,
    station_pos,
    beam_dir,
    beam_order,
):
    channels, _, samples, _ = volts.shape
    beams = beam_order.shape[0]
    n_stn, n_chan = lax.axis_size("stn"), lax.axis_size("chan")
    rows = beams // (n_stn * n_chan)
    width = channels * 2 * samples
    operands = (
        volts.reshape(-1, volts.shape[3]),
        antenna_tile_weights,
        station_weights,
        tile_station[None, :],
        station_group[None, :],
        station_pos.T,
        beam_dir.T,
        beam_order[None, :],
    )
    operands = [pltpu.with_memory_space_constraint(x, pltpu.HBM) for x in operands]
    partial = pl.pallas_call(
        kernel,
        out_shape=pltpu.VMEM((n_stn * n_chan, rows, width), jnp.bfloat16),
        in_specs=[pl.BlockSpec(memory_space=pltpu.HBM)] * len(operands),
        out_specs=pl.BlockSpec(memory_space=pltpu.VMEM),
        scratch_shapes=[pltpu.VMEM(x.shape, x.dtype) for x in operands]
        + [
            pltpu.VMEM((beams, channels * 2 * (station_weights.shape[2] // TPS)), jnp.bfloat16),
            pltpu.VMEM(volts.shape, jnp.bfloat16),
            pltpu.SemaphoreType.DMA((len(operands) - 1 + channels // CB,)),
        ],
        compiler_params=pltpu.CompilerParams(vmem_limit_bytes=24 * 2**20),
        name="partial_tied",
    )(*operands)
    parts = lax.all_to_all(
        partial,
        ("stn", "chan"),
        split_axis=0,
        concat_axis=0,
        axis_index_groups=[list(reversed(range(n_stn * n_chan)))],
        tiled=True,
    )
    vmem = pl.BlockSpec(memory_space=pltpu.VMEM)
    tied = pl.pallas_call(
        last_kernel,
        out_shape=jax.ShapeDtypeStruct((rows, 2 * samples, n_chan * channels), jnp.bfloat16),
        in_specs=[vmem],
        out_specs=vmem,
        compiler_params=pltpu.CompilerParams(vmem_limit_bytes=16 * 2**20),
        name="tied_beams",
    )(parts)
    return tied.transpose(0, 2, 1)


def solution(mesh):
    in_specs = (
        P("chan", None, None, "stn"),
        P("chan", None, "stn"),
        P("chan", None, "stn"),
        P("stn"),
        P(),
        P(),
        P(),
        P(),
    )
    out_specs = P(("stn", "chan"), None, None)
    return jax.shard_map(shards, mesh=mesh, in_specs=in_specs, out_specs=out_specs, check_vma=False)
```

```python
import functools
import math

import jax
import jax.numpy as jnp
from jax import lax
from jax.experimental import pallas as pl
from jax.experimental.pallas import tpu as pltpu
from jax.sharding import PartitionSpec as P

TILE_ANTENNAS = 16
TPS = 16
GROUPS = 4
CB = 8
SPLIT = (4, 2, 1)
CHUNK = 256
NT = (((1,), (1,)), ((), ()))
SIN = [(-1) ** i * (2 * math.pi) ** (2 * i + 1) / math.factorial(2 * i + 1) for i in range(7)]


def dot_nt(a, b):
    return lax.dot_general(a, b, NT, preferred_element_type=jnp.float32)


def iota(shape, dim):
    return lax.broadcasted_iota(jnp.int32, shape, dim)


def beam_columns(order_ref, dir_ref, start, rows):
    beams = order_ref.shape[1]
    each = beams // (lax.axis_size("stn") * lax.axis_size("chan"))
    order = order_ref[...].astype(jnp.float32)
    lane = iota((rows, beams), 1)
    slot = iota((rows, beams), 0) + start
    own = lane == beams - each - slot // each * each + slot % each
    ids = jnp.sum(jnp.where(own, order, 0.0), axis=1, keepdims=True)
    pick = lane.astype(jnp.float32) == ids
    east = jnp.sum(jnp.where(pick, dir_ref[0:1, :], 0.0), axis=1, keepdims=True)
    north = jnp.sum(jnp.where(pick, dir_ref[1:2, :], 0.0), axis=1, keepdims=True)
    group = ids - GROUPS * jnp.floor(ids * (1.0 / GROUPS))
    return east, north, group


def station_rows(pos_ref, group_ref, stations, lanes):
    total = group_ref.shape[1]
    first = lax.axis_index("stn") * stations
    own = iota((stations, total), 1) == iota((stations, total), 0) + first
    spread = iota((stations, lanes), 0) == iota((stations, lanes), 1) % stations

    def turn(row):
        column = jnp.sum(jnp.where(own, row, 0.0), axis=1, keepdims=True)
        return jnp.sum(jnp.where(spread, column, 0.0), axis=0, keepdims=True)

    return turn(pos_ref[0:1, :]), turn(pos_ref[1:2, :]), turn(group_ref[...].astype(jnp.float32))


def cos_turns(t):
    y = t - jnp.floor(t + 0.5)
    z = 0.25 - jnp.abs(y)
    z2 = z * z
    value = jnp.full_like(z, SIN[-1])
    for coefficient in SIN[-2::-1]:
        value = value * z2 + coefficient
    return value * z


def kernel(
    volt_hbm,
    aw_hbm,
    sw_hbm,
    ts_hbm,
    group_hbm,
    pos_hbm,
    dir_hbm,
    order_hbm,
    out_ref,
    volts,
    aw_ref,
    sw_ref,
    ts_ref,
    group_ref,
    pos_ref,
    dir_ref,
    order_ref,
    tied_ref,
    sems,
):
    channels, _, tiles = sw_ref.shape
    antennas = volt_hbm.shape[1]
    samples = volt_hbm.shape[0] // (2 * channels)
    stations = tiles // TPS
    groups = channels // CB
    assert groups == len(SPLIT)
    rows_c = 2 * samples
    beams = order_ref.shape[1]
    lanes = CB * 2 * stations
    scale = 1.0 / math.sqrt(group_ref.shape[1])

    def start(source, target, k):
        copy = pltpu.make_async_copy(source, target, sems.at[k])
        copy.start()
        return copy

    def voltages(g):
        rows = CB * rows_c // SPLIT[g]
        parts = [pl.ds(g * CB * rows_c + k * rows, rows) for k in range(SPLIT[g])]
        return [(volt_hbm.at[part], volts.at[part]) for part in parts]

    pairs = voltages(0) + [
        (aw_hbm, aw_ref),
        (order_hbm, order_ref),
        (dir_hbm, dir_ref),
        (pos_hbm, pos_ref),
        (group_hbm, group_ref),
        (ts_hbm, ts_ref),
        (sw_hbm, sw_ref),
    ]
    ends = [len(pairs)]
    for g in range(1, groups):
        pairs += voltages(g)
        ends.append(len(pairs))
    copies = [start(source, target, k) for k, (source, target) in enumerate(pairs)]
    antenna_tile = iota((CHUNK // TILE_ANTENNAS, CHUNK), 1) // TILE_ANTENNAS
    sum_tile = (antenna_tile == iota(antenna_tile.shape, 0)).astype(jnp.bfloat16)
    for copy in copies[: SPLIT[0] + 1]:
        copy.wait()

    def tile_beams(g):
        products = []
        weights = aw_ref[g * CB : (g + 1) * CB].astype(jnp.float32)
        for c in range(CB):
            w_re = jnp.broadcast_to(weights[c, 0:1], (samples, antennas)).astype(jnp.bfloat16)
            w_im = jnp.broadcast_to(weights[c, 1:2], (samples, antennas)).astype(jnp.bfloat16)
            first = (g * CB + c) * rows_c
            v_re, v_im = volts[first : first + samples], volts[first + samples : first + rows_c]
            products.append(w_re * v_re - w_im * v_im)
            products.append(w_re * v_im + w_im * v_re)
        products = jnp.concatenate(products, axis=0)
        sums = [
            dot_nt(sum_tile, products[:, first : first + CHUNK])
            for first in range(0, antennas, CHUNK)
        ]
        return jnp.concatenate(sums, axis=0)

    last = tile_beams(0)
    for copy in copies[SPLIT[0] + 1 : ends[1]]:
        copy.wait()

    east_s, north_s, group_s = station_rows(pos_ref, group_ref, stations, lanes)
    lane = iota((1, lanes), 1)
    channel_lane = lane // (2 * stations)
    quarter = 0.25 * ((lane // stations) % 2).astype(jnp.float32)
    first_chan = lax.axis_index("chan") * channels
    total_chans = channels * lax.axis_size("chan")
    block = min(64, beams)

    def tied_rows(first):
        east, north, group = beam_columns(order_ref, dir_ref, first, block)
        delay = east * east_s + north * north_s
        member = jnp.where(group == group_s, scale, 0.0)
        for g in range(groups):
            freq = 1.0 + (first_chan + g * CB + channel_lane).astype(jnp.float32) / total_chans
            wave = cos_turns(delay * freq - quarter)
            tied_ref[pl.ds(first, block), g * lanes : (g + 1) * lanes] = (wave * member).astype(
                jnp.bfloat16
            )

    if beams == block:
        tied_rows(0)
    else:

        def body(i, carry):
            tied_rows(pl.multiple_of(i * block, block))
            return carry

        lax.fori_loop(0, beams // block, body, 0)

    member_table = (iota((stations, tiles), 0) == ts_ref[...] % stations).astype(jnp.float32)
    own_channel = iota((lanes, CB * rows_c), 0) // (2 * stations) == iota(
        (lanes, CB * rows_c), 1
    ) // rows_c

    imag_column = iota((tiles, CB * rows_c), 1) // samples % 2 == 1
    station_rows_of = []
    for g in range(groups):
        swt = sw_ref[g * CB : (g + 1) * CB].astype(jnp.float32)
        right = []
        for c in range(CB):
            re = swt[c, 0:1] * member_table
            im = swt[c, 1:2] * member_table
            right.append(jnp.concatenate([re, -im], axis=1))
            right.append(jnp.concatenate([im, re], axis=1))
        station_rows_of.append(jnp.concatenate(right, axis=0).astype(jnp.bfloat16))

    def tied_beams(g, beams_tile):
        width = CB * rows_c
        other = jnp.where(
            imag_column,
            -pltpu.roll(beams_tile, samples, 1),
            pltpu.roll(beams_tile, width - samples, 1),
        )
        left = jnp.concatenate([beams_tile, other], axis=0).astype(jnp.bfloat16)
        station = jnp.dot(station_rows_of[g], left, preferred_element_type=jnp.float32)
        station = jnp.where(own_channel, station, 0.0).astype(jnp.bfloat16)
        tied = jnp.dot(
            tied_ref[:, g * lanes : (g + 1) * lanes], station, preferred_element_type=jnp.float32
        )
        devices, rows, _ = out_ref.shape
        out_ref[:, :, g * CB * rows_c : (g + 1) * CB * rows_c] = tied.astype(jnp.bfloat16).reshape(
            devices, rows, CB * rows_c
        )

    for g in range(1, groups):
        if g > 1:
            for copy in copies[ends[g - 1] : ends[g]]:
                copy.wait()
        now = tile_beams(g)
        tied_beams(g - 1, last)
        last = now
    tied_beams(groups - 1, last)


def last_kernel(parts_ref, out_ref):
    n_stn, n_chan = lax.axis_size("stn"), lax.axis_size("chan")
    own_beams, rows_c, total_chans = out_ref.shape
    channels = total_chans // n_chan
    width = channels * rows_c
    parts = parts_ref[...].astype(jnp.float32)
    tied = [sum(parts[n_chan - 1 - chan + k * n_chan] for k in range(n_stn)) for chan in range(n_chan)]
    diagonal = iota((channels, width), 0) == iota((channels, width), 1) // rows_c
    spread = (iota((rows_c, width), 0) == iota((rows_c, width), 1) % rows_c).astype(jnp.bfloat16)
    for b in range(own_beams):
        rows = [jnp.where(diagonal, tied[chan][b : b + 1], 0.0) for chan in range(n_chan)]
        rows = jnp.concatenate(rows, axis=0).astype(jnp.bfloat16)
        out_ref[b] = dot_nt(spread, rows).astype(jnp.bfloat16)


def shards(
    volts,
    antenna_tile_weights,
    station_weights,
    tile_station,
    station_group,
    station_pos,
    beam_dir,
    beam_order,
):
    channels, _, samples, _ = volts.shape
    beams = beam_order.shape[0]
    n_stn, n_chan = lax.axis_size("stn"), lax.axis_size("chan")
    rows = beams // (n_stn * n_chan)
    width = channels * 2 * samples
    operands = (
        volts.reshape(-1, volts.shape[3]),
        antenna_tile_weights,
        station_weights,
        tile_station[None, :],
        station_group[None, :],
        station_pos.T,
        beam_dir.T,
        beam_order[None, :],
    )
    operands = [pltpu.with_memory_space_constraint(x, pltpu.HBM) for x in operands]
    partial = pl.pallas_call(
        kernel,
        out_shape=pltpu.VMEM((n_stn * n_chan, rows, width), jnp.bfloat16),
        in_specs=[pl.BlockSpec(memory_space=pltpu.HBM)] * len(operands),
        out_specs=pl.BlockSpec(memory_space=pltpu.VMEM),
        scratch_shapes=[pltpu.VMEM(x.shape, x.dtype) for x in operands]
        + [
            pltpu.VMEM((beams, channels * 2 * (station_weights.shape[2] // TPS)), jnp.bfloat16),
            pltpu.SemaphoreType.DMA((len(operands) - 1 + sum(SPLIT),)),
        ],
        compiler_params=pltpu.CompilerParams(vmem_limit_bytes=24 * 2**20),
        name="partial_tied",
    )(*operands)
    parts = lax.all_to_all(
        partial,
        ("stn", "chan"),
        split_axis=0,
        concat_axis=0,
        axis_index_groups=[list(reversed(range(n_stn * n_chan)))],
        tiled=True,
    )
    vmem = pl.BlockSpec(memory_space=pltpu.VMEM)
    tied = pl.pallas_call(
        last_kernel,
        out_shape=jax.ShapeDtypeStruct((rows, 2 * samples, n_chan * channels), jnp.bfloat16),
        in_specs=[vmem],
        out_specs=vmem,
        compiler_params=pltpu.CompilerParams(vmem_limit_bytes=16 * 2**20),
        name="tied_beams",
    )(parts)
    return tied.transpose(0, 2, 1)


def solution(mesh):
    in_specs = (
        P("chan", None, None, "stn"),
        P("chan", None, "stn"),
        P("chan", None, "stn"),
        P("stn"),
        P(),
        P(),
        P(),
        P(),
    )
    out_specs = P(("stn", "chan"), None, None)
    return jax.shard_map(shards, mesh=mesh, in_specs=in_specs, out_specs=out_specs, check_vma=False)
```

```python
import functools
import math

import jax
import jax.numpy as jnp
from jax import lax
from jax.experimental import pallas as pl
from jax.experimental.pallas import tpu as pltpu
from jax.sharding import PartitionSpec as P

TILE_ANTENNAS = 16
TPS = 16
GROUPS = 4
CB = 8
CHUNK = 256
NT = (((1,), (1,)), ((), ()))
SIN = [(-1) ** i * (2 * math.pi) ** (2 * i + 1) / math.factorial(2 * i + 1) for i in range(7)]


def dot_nt(a, b):
    return lax.dot_general(a, b, NT, preferred_element_type=jnp.float32)


def iota(shape, dim):
    return lax.broadcasted_iota(jnp.int32, shape, dim)


def beam_columns(order_ref, dir_ref, start, rows):
    beams = order_ref.shape[1]
    n_stn, n_chan = lax.axis_size("stn"), lax.axis_size("chan")
    each = beams // (n_stn * n_chan)
    order = order_ref[...].astype(jnp.float32)
    lane = iota((rows, beams), 1)
    slot = iota((rows, 1), 0) + start
    place = n_stn * n_chan - 1 - slot // each
    own = lane == (place % n_stn * n_chan + place // n_stn) * each + slot % each
    ids = jnp.sum(jnp.where(own, order, 0.0), axis=1, keepdims=True)
    pick = lane.astype(jnp.float32) == ids
    east = jnp.sum(jnp.where(pick, dir_ref[0:1, :], 0.0), axis=1, keepdims=True)
    north = jnp.sum(jnp.where(pick, dir_ref[1:2, :], 0.0), axis=1, keepdims=True)
    group = ids - GROUPS * jnp.floor(ids * (1.0 / GROUPS))
    return east, north, group


def station_rows(pos_ref, group_ref, stations, lanes):
    total = group_ref.shape[1]
    first = lax.axis_index("stn") * stations
    own = iota((stations, total), 1) == iota((stations, total), 0) + first
    spread = iota((stations, lanes), 0) == iota((stations, lanes), 1) % stations

    def turn(row):
        column = jnp.sum(jnp.where(own, row, 0.0), axis=1, keepdims=True)
        return jnp.sum(jnp.where(spread, column, 0.0), axis=0, keepdims=True)

    return turn(pos_ref[0:1, :]), turn(pos_ref[1:2, :]), turn(group_ref[...].astype(jnp.float32))


def cos_turns(t):
    y = t - jnp.floor(t + 0.5)
    z = 0.25 - jnp.abs(y)
    z2 = z * z
    value = jnp.full_like(z, SIN[-1])
    for coefficient in SIN[-2::-1]:
        value = value * z2 + coefficient
    return value * z


def kernel(
    volt_hbm,
    aw_hbm,
    sw_hbm,
    ts_hbm,
    group_hbm,
    pos_hbm,
    dir_hbm,
    order_hbm,
    out_ref,
    volts,
    aw_ref,
    sw_ref,
    ts_ref,
    group_ref,
    pos_ref,
    dir_ref,
    order_ref,
    tied_ref,
    sems,
):
    channels, _, tiles = sw_ref.shape
    antennas = volt_hbm.shape[1]
    samples = volt_hbm.shape[0] // (2 * channels)
    stations = tiles // TPS
    groups = channels // CB
    rows_c = 2 * samples
    beams = order_ref.shape[1]
    lanes = CB * 2 * stations
    scale = 1.0 / math.sqrt(group_ref.shape[1])

    def start(source, target, k):
        copy = pltpu.make_async_copy(source, target, sems.at[k])
        copy.start()
        return copy

    def voltages(g):
        part = pl.ds(g * CB * rows_c, CB * rows_c)
        return volt_hbm.at[part], volts.at[part]

    pairs = [
        voltages(0),
        (aw_hbm, aw_ref),
        (order_hbm, order_ref),
        (dir_hbm, dir_ref),
        (pos_hbm, pos_ref),
        (group_hbm, group_ref),
        (ts_hbm, ts_ref),
        (sw_hbm, sw_ref),
    ] + [voltages(g) for g in range(1, groups)]
    copies = [start(source, target, k) for k, (source, target) in enumerate(pairs)]
    large = copies[:1] + copies[8:]
    antenna_tile = iota((CHUNK // TILE_ANTENNAS, CHUNK), 1) // TILE_ANTENNAS
    sum_tile = (antenna_tile == iota(antenna_tile.shape, 0)).astype(jnp.bfloat16)
    for copy in copies[:2]:
        copy.wait()

    def tile_beams(g):
        products = []
        weights = aw_ref[g * CB : (g + 1) * CB].astype(jnp.float32)
        for c in range(CB):
            w_re = jnp.broadcast_to(weights[c, 0:1], (samples, antennas)).astype(jnp.bfloat16)
            w_im = jnp.broadcast_to(weights[c, 1:2], (samples, antennas)).astype(jnp.bfloat16)
            first = (g * CB + c) * rows_c
            v_re, v_im = volts[first : first + samples], volts[first + samples : first + rows_c]
            products.append(w_re * v_re - w_im * v_im)
            products.append(w_re * v_im + w_im * v_re)
        products = jnp.concatenate(products, axis=0)
        sums = [
            dot_nt(sum_tile, products[:, first : first + CHUNK])
            for first in range(0, antennas, CHUNK)
        ]
        return jnp.concatenate(sums, axis=0)

    last = tile_beams(0)
    for copy in copies[2:9]:
        copy.wait()

    east_s, north_s, group_s = station_rows(pos_ref, group_ref, stations, lanes)
    lane = iota((1, lanes), 1)
    channel_lane = lane // (2 * stations)
    quarter = 0.25 * ((lane // stations) % 2).astype(jnp.float32)
    first_chan = lax.axis_index("chan") * channels
    total_chans = channels * lax.axis_size("chan")
    block = min(64, beams)

    def tied_rows(first):
        east, north, group = beam_columns(order_ref, dir_ref, first, block)
        delay = east * east_s + north * north_s
        member = jnp.where(group == group_s, scale, 0.0)
        for g in range(groups):
            freq = 1.0 + (first_chan + g * CB + channel_lane).astype(jnp.float32) / total_chans
            wave = cos_turns(delay * freq - quarter)
            tied_ref[pl.ds(first, block), g * lanes : (g + 1) * lanes] = (wave * member).astype(
                jnp.bfloat16
            )

    if beams == block:
        tied_rows(0)
    else:

        def body(i, carry):
            tied_rows(pl.multiple_of(i * block, block))
            return carry

        lax.fori_loop(0, beams // block, body, 0)

    member_table = (iota((stations, tiles), 0) == ts_ref[...] % stations).astype(jnp.float32)
    own_channel = iota((lanes, CB * rows_c), 0) // (2 * stations) == iota(
        (lanes, CB * rows_c), 1
    ) // rows_c

    imag_column = iota((tiles, CB * rows_c), 1) // samples % 2 == 1
    station_rows_of = []
    for g in range(groups):
        swt = sw_ref[g * CB : (g + 1) * CB].astype(jnp.float32)
        right = []
        for c in range(CB):
            re = swt[c, 0:1] * member_table
            im = swt[c, 1:2] * member_table
            right.append(jnp.concatenate([re, -im], axis=1))
            right.append(jnp.concatenate([im, re], axis=1))
        station_rows_of.append(jnp.concatenate(right, axis=0).astype(jnp.bfloat16))

    def tied_beams(g, beams_tile):
        width = CB * rows_c
        other = jnp.where(
            imag_column,
            -pltpu.roll(beams_tile, samples, 1),
            pltpu.roll(beams_tile, width - samples, 1),
        )
        left = jnp.concatenate([beams_tile, other], axis=0).astype(jnp.bfloat16)
        station = jnp.dot(station_rows_of[g], left, preferred_element_type=jnp.float32)
        station = jnp.where(own_channel, station, 0.0).astype(jnp.bfloat16)
        tied = jnp.dot(
            tied_ref[:, g * lanes : (g + 1) * lanes], station, preferred_element_type=jnp.float32
        )
        devices, rows, _ = out_ref.shape
        out_ref[:, :, g * CB * rows_c : (g + 1) * CB * rows_c] = tied.astype(jnp.bfloat16).reshape(
            devices, rows, CB * rows_c
        )

    for g in range(1, groups):
        if g > 1:
            large[g].wait()
        now = tile_beams(g)
        tied_beams(g - 1, last)
        last = now
    tied_beams(groups - 1, last)


def last_kernel(parts_ref, out_ref):
    n_stn, n_chan = lax.axis_size("stn"), lax.axis_size("chan")
    own_beams, rows_c, total_chans = out_ref.shape
    channels = total_chans // n_chan
    width = channels * rows_c
    parts = parts_ref[...].astype(jnp.float32)
    tied = [sum(parts[(n_chan - 1 - chan) * n_stn + k] for k in range(n_stn)) for chan in range(n_chan)]
    diagonal = iota((channels, width), 0) == iota((channels, width), 1) // rows_c
    spread = (iota((rows_c, width), 0) == iota((rows_c, width), 1) % rows_c).astype(jnp.bfloat16)
    for b in range(own_beams):
        rows = [jnp.where(diagonal, tied[chan][b : b + 1], 0.0) for chan in range(n_chan)]
        rows = jnp.concatenate(rows, axis=0).astype(jnp.bfloat16)
        out_ref[b] = dot_nt(spread, rows).astype(jnp.bfloat16)


def shards(
    volts,
    antenna_tile_weights,
    station_weights,
    tile_station,
    station_group,
    station_pos,
    beam_dir,
    beam_order,
):
    channels, _, samples, _ = volts.shape
    beams = beam_order.shape[0]
    n_stn, n_chan = lax.axis_size("stn"), lax.axis_size("chan")
    rows = beams // (n_stn * n_chan)
    width = channels * 2 * samples
    operands = (
        volts.reshape(-1, volts.shape[3]),
        antenna_tile_weights,
        station_weights,
        tile_station[None, :],
        station_group[None, :],
        station_pos.T,
        beam_dir.T,
        beam_order[None, :],
    )
    operands = [pltpu.with_memory_space_constraint(x, pltpu.HBM) for x in operands]
    partial = pl.pallas_call(
        kernel,
        out_shape=pltpu.VMEM((n_stn * n_chan, rows, width), jnp.bfloat16),
        in_specs=[pl.BlockSpec(memory_space=pltpu.HBM)] * len(operands),
        out_specs=pl.BlockSpec(memory_space=pltpu.VMEM),
        scratch_shapes=[pltpu.VMEM(x.shape, x.dtype) for x in operands]
        + [
            pltpu.VMEM((beams, channels * 2 * (station_weights.shape[2] // TPS)), jnp.bfloat16),
            pltpu.SemaphoreType.DMA((len(operands) - 1 + channels // CB,)),
        ],
        compiler_params=pltpu.CompilerParams(vmem_limit_bytes=24 * 2**20),
        name="partial_tied",
    )(*operands)
    order = [stn * n_chan + chan for chan in range(n_chan) for stn in range(n_stn)][::-1]
    parts = lax.all_to_all(
        partial,
        ("stn", "chan"),
        split_axis=0,
        concat_axis=0,
        axis_index_groups=[order],
        tiled=True,
    )
    vmem = pl.BlockSpec(memory_space=pltpu.VMEM)
    tied = pl.pallas_call(
        last_kernel,
        out_shape=jax.ShapeDtypeStruct((rows, 2 * samples, n_chan * channels), jnp.bfloat16),
        in_specs=[vmem],
        out_specs=vmem,
        compiler_params=pltpu.CompilerParams(vmem_limit_bytes=16 * 2**20),
        name="tied_beams",
    )(parts)
    return tied.transpose(0, 2, 1)


def solution(mesh):
    in_specs = (
        P("chan", None, None, "stn"),
        P("chan", None, "stn"),
        P("chan", None, "stn"),
        P("stn"),
        P(),
        P(),
        P(),
        P(),
    )
    out_specs = P(("stn", "chan"), None, None)
    return jax.shard_map(shards, mesh=mesh, in_specs=in_specs, out_specs=out_specs, check_vma=False)
```

```python
import functools
import math

import jax
import jax.numpy as jnp
from jax import lax
from jax.experimental import pallas as pl
from jax.experimental.pallas import tpu as pltpu
from jax.sharding import PartitionSpec as P

TILE_ANTENNAS = 16
TPS = 16
GROUPS = 4
CB = 8
CHUNK = 256
NT = (((1,), (1,)), ((), ()))
SIN = [(-1) ** i * (2 * math.pi) ** (2 * i + 1) / math.factorial(2 * i + 1) for i in range(7)]


def dot_nt(a, b):
    return lax.dot_general(a, b, NT, preferred_element_type=jnp.float32)


def iota(shape, dim):
    return lax.broadcasted_iota(jnp.int32, shape, dim)


def beam_columns(order_ref, dir_ref, start, rows):
    beams = order_ref.shape[1]
    each = beams // (lax.axis_size("stn") * lax.axis_size("chan"))
    order = order_ref[...].astype(jnp.float32)
    lane = iota((rows, beams), 1)
    slot = iota((rows, beams), 0) + start
    own = lane == beams - each - slot // each * each + slot % each
    ids = jnp.sum(jnp.where(own, order, 0.0), axis=1, keepdims=True)
    pick = lane.astype(jnp.float32) == ids
    east = jnp.sum(jnp.where(pick, dir_ref[0:1, :], 0.0), axis=1, keepdims=True)
    north = jnp.sum(jnp.where(pick, dir_ref[1:2, :], 0.0), axis=1, keepdims=True)
    group = ids - GROUPS * jnp.floor(ids * (1.0 / GROUPS))
    return east, north, group


def station_rows(pos_ref, group_ref, stations, lanes):
    total = group_ref.shape[1]
    first = lax.axis_index("stn") * stations
    own = iota((stations, total), 1) == iota((stations, total), 0) + first
    spread = iota((stations, lanes), 0) == iota((stations, lanes), 1) % stations

    def turn(row):
        column = jnp.sum(jnp.where(own, row, 0.0), axis=1, keepdims=True)
        return jnp.sum(jnp.where(spread, column, 0.0), axis=0, keepdims=True)

    return turn(pos_ref[0:1, :]), turn(pos_ref[1:2, :]), turn(group_ref[...].astype(jnp.float32))


def cos_turns(t):
    y = t - jnp.floor(t + 0.5)
    z = 0.25 - jnp.abs(y)
    z2 = z * z
    value = jnp.full_like(z, SIN[-1])
    for coefficient in SIN[-2::-1]:
        value = value * z2 + coefficient
    return value * z


def kernel(
    volt_hbm,
    aw_hbm,
    sw_hbm,
    ts_hbm,
    group_hbm,
    pos_hbm,
    dir_hbm,
    order_hbm,
    out_ref,
    volts,
    aw_ref,
    sw_ref,
    ts_ref,
    group_ref,
    pos_ref,
    dir_ref,
    order_ref,
    tied_ref,
    sems,
):
    channels, _, tiles = sw_ref.shape
    antennas = volt_hbm.shape[1]
    samples = volt_hbm.shape[0] // (2 * channels)
    stations = tiles // TPS
    groups = channels // CB
    rows_c = 2 * samples
    beams = order_ref.shape[1]
    lanes = CB * 2 * stations
    scale = 1.0 / math.sqrt(group_ref.shape[1])

    def start(source, target, k):
        copy = pltpu.make_async_copy(source, target, sems.at[k])
        copy.start()
        return copy

    def voltages(g):
        part = pl.ds(g * CB * rows_c, CB * rows_c)
        return volt_hbm.at[part], volts.at[part]

    pairs = [
        voltages(0),
        (aw_hbm, aw_ref),
        (order_hbm, order_ref),
        (dir_hbm, dir_ref),
        (pos_hbm, pos_ref),
        (group_hbm, group_ref),
        (ts_hbm, ts_ref),
        (sw_hbm, sw_ref),
    ] + [voltages(g) for g in range(1, groups)]
    copies = [start(source, target, k) for k, (source, target) in enumerate(pairs)]
    antenna_tile = iota((CHUNK // TILE_ANTENNAS, CHUNK), 1) // TILE_ANTENNAS
    sum_tile = (antenna_tile == iota(antenna_tile.shape, 0)).astype(jnp.bfloat16)
    for copy in copies[:2]:
        copy.wait()

    def tile_beams(g):
        products = []
        weights = aw_ref[g * CB : (g + 1) * CB].astype(jnp.float32)
        for c in range(CB):
            w_re = jnp.broadcast_to(weights[c, 0:1], (samples, antennas)).astype(jnp.bfloat16)
            w_im = jnp.broadcast_to(weights[c, 1:2], (samples, antennas)).astype(jnp.bfloat16)
            first = (g * CB + c) * rows_c
            v_re, v_im = volts[first : first + samples], volts[first + samples : first + rows_c]
            products.append(w_re * v_re - w_im * v_im)
            products.append(w_re * v_im + w_im * v_re)
        products = jnp.concatenate(products, axis=0)
        sums = [
            dot_nt(sum_tile, products[:, first : first + CHUNK])
            for first in range(0, antennas, CHUNK)
        ]
        return jnp.concatenate(sums, axis=0)

    last = tile_beams(0)
    for copy in copies[2:]:
        copy.wait()

    east_s, north_s, group_s = station_rows(pos_ref, group_ref, stations, lanes)
    lane = iota((1, lanes), 1)
    channel_lane = lane // (2 * stations)
    quarter = 0.25 * ((lane // stations) % 2).astype(jnp.float32)
    first_chan = lax.axis_index("chan") * channels
    total_chans = channels * lax.axis_size("chan")
    block = min(64, beams)

    def tied_rows(first):
        east, north, group = beam_columns(order_ref, dir_ref, first, block)
        delay = east * east_s + north * north_s
        member = jnp.where(group == group_s, scale, 0.0)
        for g in range(groups):
            freq = 1.0 + (first_chan + g * CB + channel_lane).astype(jnp.float32) / total_chans
            wave = cos_turns(delay * freq - quarter)
            tied_ref[pl.ds(first, block), g * lanes : (g + 1) * lanes] = (wave * member).astype(
                jnp.bfloat16
            )

    if beams == block:
        tied_rows(0)
    else:

        def body(i, carry):
            tied_rows(pl.multiple_of(i * block, block))
            return carry

        lax.fori_loop(0, beams // block, body, 0)

    member_table = (iota((stations, tiles), 0) == ts_ref[...] % stations).astype(jnp.float32)
    own_channel = iota((lanes, CB * rows_c), 0) // (2 * stations) == iota(
        (lanes, CB * rows_c), 1
    ) // rows_c

    imag_column = iota((tiles, CB * rows_c), 1) // samples % 2 == 1
    station_rows_of = []
    for g in range(groups):
        swt = sw_ref[g * CB : (g + 1) * CB].astype(jnp.float32)
        right = []
        for c in range(CB):
            re = swt[c, 0:1] * member_table
            im = swt[c, 1:2] * member_table
            right.append(jnp.concatenate([re, -im], axis=1))
            right.append(jnp.concatenate([im, re], axis=1))
        station_rows_of.append(jnp.concatenate(right, axis=0).astype(jnp.bfloat16))

    def tied_beams(g, beams_tile):
        width = CB * rows_c
        other = jnp.where(
            imag_column,
            -pltpu.roll(beams_tile, samples, 1),
            pltpu.roll(beams_tile, width - samples, 1),
        )
        left = jnp.concatenate([beams_tile, other], axis=0).astype(jnp.bfloat16)
        station = jnp.dot(station_rows_of[g], left, preferred_element_type=jnp.float32)
        station = jnp.where(own_channel, station, 0.0).astype(jnp.bfloat16)
        tied = jnp.dot(
            tied_ref[:, g * lanes : (g + 1) * lanes], station, preferred_element_type=jnp.float32
        )
        devices, rows, _ = out_ref.shape
        out_ref[:, :, g * CB * rows_c : (g + 1) * CB * rows_c] = tied.astype(jnp.bfloat16).reshape(
            devices, rows, CB * rows_c
        )

    found = [last] + [tile_beams(g) for g in range(1, groups)]
    for g in range(groups):
        tied_beams(g, found[g])


def last_kernel(parts_ref, out_ref):
    n_stn, n_chan = lax.axis_size("stn"), lax.axis_size("chan")
    own_beams, rows_c, total_chans = out_ref.shape
    channels = total_chans // n_chan
    width = channels * rows_c
    parts = parts_ref[...].astype(jnp.float32)
    tied = [sum(parts[n_chan - 1 - chan + k * n_chan] for k in range(n_stn)) for chan in range(n_chan)]
    diagonal = iota((channels, width), 0) == iota((channels, width), 1) // rows_c
    spread = (iota((rows_c, width), 0) == iota((rows_c, width), 1) % rows_c).astype(jnp.bfloat16)
    for b in range(own_beams):
        rows = [jnp.where(diagonal, tied[chan][b : b + 1], 0.0) for chan in range(n_chan)]
        rows = jnp.concatenate(rows, axis=0).astype(jnp.bfloat16)
        out_ref[b] = dot_nt(spread, rows).astype(jnp.bfloat16)


def shards(
    volts,
    antenna_tile_weights,
    station_weights,
    tile_station,
    station_group,
    station_pos,
    beam_dir,
    beam_order,
):
    channels, _, samples, _ = volts.shape
    beams = beam_order.shape[0]
    n_stn, n_chan = lax.axis_size("stn"), lax.axis_size("chan")
    rows = beams // (n_stn * n_chan)
    width = channels * 2 * samples
    operands = (
        volts.reshape(-1, volts.shape[3]),
        antenna_tile_weights,
        station_weights,
        tile_station[None, :],
        station_group[None, :],
        station_pos.T,
        beam_dir.T,
        beam_order[None, :],
    )
    operands = [pltpu.with_memory_space_constraint(x, pltpu.HBM) for x in operands]
    partial = pl.pallas_call(
        kernel,
        out_shape=pltpu.VMEM((n_stn * n_chan, rows, width), jnp.bfloat16),
        in_specs=[pl.BlockSpec(memory_space=pltpu.HBM)] * len(operands),
        out_specs=pl.BlockSpec(memory_space=pltpu.VMEM),
        scratch_shapes=[pltpu.VMEM(x.shape, x.dtype) for x in operands]
        + [
            pltpu.VMEM((beams, channels * 2 * (station_weights.shape[2] // TPS)), jnp.bfloat16),
            pltpu.SemaphoreType.DMA((len(operands) - 1 + channels // CB,)),
        ],
        compiler_params=pltpu.CompilerParams(vmem_limit_bytes=24 * 2**20),
        name="partial_tied",
    )(*operands)
    parts = lax.all_to_all(
        partial,
        ("stn", "chan"),
        split_axis=0,
        concat_axis=0,
        axis_index_groups=[list(reversed(range(n_stn * n_chan)))],
        tiled=True,
    )
    vmem = pl.BlockSpec(memory_space=pltpu.VMEM)
    tied = pl.pallas_call(
        last_kernel,
        out_shape=jax.ShapeDtypeStruct((rows, 2 * samples, n_chan * channels), jnp.bfloat16),
        in_specs=[vmem],
        out_specs=vmem,
        compiler_params=pltpu.CompilerParams(vmem_limit_bytes=16 * 2**20),
        name="tied_beams",
    )(parts)
    return tied.transpose(0, 2, 1)


def solution(mesh):
    in_specs = (
        P("chan", None, None, "stn"),
        P("chan", None, "stn"),
        P("chan", None, "stn"),
        P("stn"),
        P(),
        P(),
        P(),
        P(),
    )
    out_specs = P(("stn", "chan"), None, None)
    return jax.shard_map(shards, mesh=mesh, in_specs=in_specs, out_specs=out_specs, check_vma=False)
```

```python
import functools
import math

import jax
import jax.numpy as jnp
from jax import lax
from jax.experimental import pallas as pl
from jax.experimental.pallas import tpu as pltpu
from jax.sharding import PartitionSpec as P

TILE_ANTENNAS = 16
TPS = 16
GROUPS = 4
CB = 12
CHUNK = 256
NT = (((1,), (1,)), ((), ()))
SIN = [(-1) ** i * (2 * math.pi) ** (2 * i + 1) / math.factorial(2 * i + 1) for i in range(7)]


def dot_nt(a, b):
    return lax.dot_general(a, b, NT, preferred_element_type=jnp.float32)


def iota(shape, dim):
    return lax.broadcasted_iota(jnp.int32, shape, dim)


def beam_columns(order_ref, dir_ref, start, rows):
    beams = order_ref.shape[1]
    each = beams // (lax.axis_size("stn") * lax.axis_size("chan"))
    order = order_ref[...].astype(jnp.float32)
    lane = iota((rows, beams), 1)
    slot = iota((rows, beams), 0) + start
    own = lane == beams - each - slot // each * each + slot % each
    ids = jnp.sum(jnp.where(own, order, 0.0), axis=1, keepdims=True)
    pick = lane.astype(jnp.float32) == ids
    east = jnp.sum(jnp.where(pick, dir_ref[0:1, :], 0.0), axis=1, keepdims=True)
    north = jnp.sum(jnp.where(pick, dir_ref[1:2, :], 0.0), axis=1, keepdims=True)
    group = ids - GROUPS * jnp.floor(ids * (1.0 / GROUPS))
    return east, north, group


def station_rows(pos_ref, group_ref, stations, lanes):
    total = group_ref.shape[1]
    first = lax.axis_index("stn") * stations
    own = iota((stations, total), 1) == iota((stations, total), 0) + first
    spread = iota((stations, lanes), 0) == iota((stations, lanes), 1) % stations

    def turn(row):
        column = jnp.sum(jnp.where(own, row, 0.0), axis=1, keepdims=True)
        return jnp.sum(jnp.where(spread, column, 0.0), axis=0, keepdims=True)

    return turn(pos_ref[0:1, :]), turn(pos_ref[1:2, :]), turn(group_ref[...].astype(jnp.float32))


def cos_turns(t):
    y = t - jnp.floor(t + 0.5)
    z = 0.25 - jnp.abs(y)
    z2 = z * z
    value = jnp.full_like(z, SIN[-1])
    for coefficient in SIN[-2::-1]:
        value = value * z2 + coefficient
    return value * z


def kernel(
    volt_hbm,
    aw_hbm,
    sw_hbm,
    ts_hbm,
    group_hbm,
    pos_hbm,
    dir_hbm,
    order_hbm,
    out_ref,
    volts,
    aw_ref,
    sw_ref,
    ts_ref,
    group_ref,
    pos_ref,
    dir_ref,
    order_ref,
    tied_ref,
    sems,
):
    channels, _, tiles = sw_ref.shape
    antennas = volt_hbm.shape[1]
    samples = volt_hbm.shape[0] // (2 * channels)
    stations = tiles // TPS
    groups = channels // CB
    rows_c = 2 * samples
    beams = order_ref.shape[1]
    lanes = CB * 2 * stations
    scale = 1.0 / math.sqrt(group_ref.shape[1])

    def start(source, target, k):
        copy = pltpu.make_async_copy(source, target, sems.at[k])
        copy.start()
        return copy

    def voltages(g):
        part = pl.ds(g * CB * rows_c, CB * rows_c)
        return volt_hbm.at[part], volts.at[part]

    pairs = [
        voltages(0),
        (aw_hbm, aw_ref),
        (order_hbm, order_ref),
        (dir_hbm, dir_ref),
        (pos_hbm, pos_ref),
        (group_hbm, group_ref),
        (ts_hbm, ts_ref),
        (sw_hbm, sw_ref),
    ] + [voltages(g) for g in range(1, groups)]
    copies = [start(source, target, k) for k, (source, target) in enumerate(pairs)]
    large = copies[:1] + copies[8:]
    antenna_tile = iota((CHUNK // TILE_ANTENNAS, CHUNK), 1) // TILE_ANTENNAS
    sum_tile = (antenna_tile == iota(antenna_tile.shape, 0)).astype(jnp.bfloat16)
    for copy in copies[:2]:
        copy.wait()

    def tile_beams(g):
        products = []
        weights = aw_ref[g * CB : (g + 1) * CB].astype(jnp.float32)
        for c in range(CB):
            w_re = jnp.broadcast_to(weights[c, 0:1], (samples, antennas)).astype(jnp.bfloat16)
            w_im = jnp.broadcast_to(weights[c, 1:2], (samples, antennas)).astype(jnp.bfloat16)
            first = (g * CB + c) * rows_c
            v_re, v_im = volts[first : first + samples], volts[first + samples : first + rows_c]
            products.append(w_re * v_re - w_im * v_im)
            products.append(w_re * v_im + w_im * v_re)
        products = jnp.concatenate(products, axis=0)
        sums = [
            dot_nt(sum_tile, products[:, first : first + CHUNK])
            for first in range(0, antennas, CHUNK)
        ]
        return jnp.concatenate(sums, axis=0)

    last = tile_beams(0)
    for copy in copies[2:9]:
        copy.wait()

    east_s, north_s, group_s = station_rows(pos_ref, group_ref, stations, lanes)
    lane = iota((1, lanes), 1)
    channel_lane = lane // (2 * stations)
    quarter = 0.25 * ((lane // stations) % 2).astype(jnp.float32)
    first_chan = lax.axis_index("chan") * channels
    total_chans = channels * lax.axis_size("chan")
    block = min(64, beams)

    def tied_rows(first):
        east, north, group = beam_columns(order_ref, dir_ref, first, block)
        delay = east * east_s + north * north_s
        member = jnp.where(group == group_s, scale, 0.0)
        for g in range(groups):
            freq = 1.0 + (first_chan + g * CB + channel_lane).astype(jnp.float32) / total_chans
            wave = cos_turns(delay * freq - quarter)
            tied_ref[pl.ds(first, block), g * lanes : (g + 1) * lanes] = (wave * member).astype(
                jnp.bfloat16
            )

    if beams == block:
        tied_rows(0)
    else:

        def body(i, carry):
            tied_rows(pl.multiple_of(i * block, block))
            return carry

        lax.fori_loop(0, beams // block, body, 0)

    member_table = (iota((stations, tiles), 0) == ts_ref[...] % stations).astype(jnp.float32)
    own_channel = iota((lanes, CB * rows_c), 0) // (2 * stations) == iota(
        (lanes, CB * rows_c), 1
    ) // rows_c

    imag_column = iota((tiles, CB * rows_c), 1) // samples % 2 == 1
    station_rows_of = []
    for g in range(groups):
        swt = sw_ref[g * CB : (g + 1) * CB].astype(jnp.float32)
        right = []
        for c in range(CB):
            re = swt[c, 0:1] * member_table
            im = swt[c, 1:2] * member_table
            right.append(jnp.concatenate([re, -im], axis=1))
            right.append(jnp.concatenate([im, re], axis=1))
        station_rows_of.append(jnp.concatenate(right, axis=0).astype(jnp.bfloat16))

    def tied_beams(g, beams_tile):
        width = CB * rows_c
        other = jnp.where(
            imag_column,
            -pltpu.roll(beams_tile, samples, 1),
            pltpu.roll(beams_tile, width - samples, 1),
        )
        left = jnp.concatenate([beams_tile, other], axis=0).astype(jnp.bfloat16)
        station = jnp.dot(station_rows_of[g], left, preferred_element_type=jnp.float32)
        station = jnp.where(own_channel, station, 0.0).astype(jnp.bfloat16)
        tied = jnp.dot(
            tied_ref[:, g * lanes : (g + 1) * lanes], station, preferred_element_type=jnp.float32
        )
        devices, rows, _ = out_ref.shape
        out_ref[:, :, g * CB * rows_c : (g + 1) * CB * rows_c] = tied.astype(jnp.bfloat16).reshape(
            devices, rows, CB * rows_c
        )

    for g in range(1, groups):
        if g > 1:
            large[g].wait()
        now = tile_beams(g)
        tied_beams(g - 1, last)
        last = now
    tied_beams(groups - 1, last)


def last_kernel(parts_ref, out_ref):
    n_stn, n_chan = lax.axis_size("stn"), lax.axis_size("chan")
    own_beams, rows_c, total_chans = out_ref.shape
    channels = total_chans // n_chan
    width = channels * rows_c
    parts = parts_ref[...].astype(jnp.float32)
    tied = [sum(parts[n_chan - 1 - chan + k * n_chan] for k in range(n_stn)) for chan in range(n_chan)]
    diagonal = iota((channels, width), 0) == iota((channels, width), 1) // rows_c
    spread = (iota((rows_c, width), 0) == iota((rows_c, width), 1) % rows_c).astype(jnp.bfloat16)
    for b in range(own_beams):
        rows = [jnp.where(diagonal, tied[chan][b : b + 1], 0.0) for chan in range(n_chan)]
        rows = jnp.concatenate(rows, axis=0).astype(jnp.bfloat16)
        out_ref[b] = dot_nt(spread, rows).astype(jnp.bfloat16)


def shards(
    volts,
    antenna_tile_weights,
    station_weights,
    tile_station,
    station_group,
    station_pos,
    beam_dir,
    beam_order,
):
    channels, _, samples, _ = volts.shape
    beams = beam_order.shape[0]
    n_stn, n_chan = lax.axis_size("stn"), lax.axis_size("chan")
    rows = beams // (n_stn * n_chan)
    width = channels * 2 * samples
    operands = (
        volts.reshape(-1, volts.shape[3]),
        antenna_tile_weights,
        station_weights,
        tile_station[None, :],
        station_group[None, :],
        station_pos.T,
        beam_dir.T,
        beam_order[None, :],
    )
    operands = [pltpu.with_memory_space_constraint(x, pltpu.HBM) for x in operands]
    partial = pl.pallas_call(
        kernel,
        out_shape=pltpu.VMEM((n_stn * n_chan, rows, width), jnp.bfloat16),
        in_specs=[pl.BlockSpec(memory_space=pltpu.HBM)] * len(operands),
        out_specs=pl.BlockSpec(memory_space=pltpu.VMEM),
        scratch_shapes=[pltpu.VMEM(x.shape, x.dtype) for x in operands]
        + [
            pltpu.VMEM((beams, channels * 2 * (station_weights.shape[2] // TPS)), jnp.bfloat16),
            pltpu.SemaphoreType.DMA((len(operands) - 1 + channels // CB,)),
        ],
        compiler_params=pltpu.CompilerParams(vmem_limit_bytes=24 * 2**20),
        name="partial_tied",
    )(*operands)
    parts = lax.all_to_all(
        partial,
        ("stn", "chan"),
        split_axis=0,
        concat_axis=0,
        axis_index_groups=[list(reversed(range(n_stn * n_chan)))],
        tiled=True,
    )
    vmem = pl.BlockSpec(memory_space=pltpu.VMEM)
    tied = pl.pallas_call(
        last_kernel,
        out_shape=jax.ShapeDtypeStruct((rows, 2 * samples, n_chan * channels), jnp.bfloat16),
        in_specs=[vmem],
        out_specs=vmem,
        compiler_params=pltpu.CompilerParams(vmem_limit_bytes=16 * 2**20),
        name="tied_beams",
    )(parts)
    return tied.transpose(0, 2, 1)


def solution(mesh):
    in_specs = (
        P("chan", None, None, "stn"),
        P("chan", None, "stn"),
        P("chan", None, "stn"),
        P("stn"),
        P(),
        P(),
        P(),
        P(),
    )
    out_specs = P(("stn", "chan"), None, None)
    return jax.shard_map(shards, mesh=mesh, in_specs=in_specs, out_specs=out_specs, check_vma=False)
```

```python
import functools
import math

import jax
import jax.numpy as jnp
from jax import lax
from jax.experimental import pallas as pl
from jax.experimental.pallas import tpu as pltpu
from jax.sharding import PartitionSpec as P

TILE_ANTENNAS = 16
TPS = 16
GROUPS = 4
CB = 8
SPLIT = (4, 2, 1)
CHUNK = 256
NT = (((1,), (1,)), ((), ()))
SIN = [(-1) ** i * (2 * math.pi) ** (2 * i + 1) / math.factorial(2 * i + 1) for i in range(7)]


def dot_nt(a, b):
    return lax.dot_general(a, b, NT, preferred_element_type=jnp.float32)


def iota(shape, dim):
    return lax.broadcasted_iota(jnp.int32, shape, dim)


def beam_columns(order_ref, dir_ref, start, rows):
    beams = order_ref.shape[1]
    each = beams // (lax.axis_size("stn") * lax.axis_size("chan"))
    order = order_ref[...].astype(jnp.float32)
    lane = iota((rows, beams), 1)
    slot = iota((rows, beams), 0) + start
    own = lane == (beams - slot // each * each) % beams + slot % each
    ids = jnp.sum(jnp.where(own, order, 0.0), axis=1, keepdims=True)
    pick = lane.astype(jnp.float32) == ids
    east = jnp.sum(jnp.where(pick, dir_ref[0:1, :], 0.0), axis=1, keepdims=True)
    north = jnp.sum(jnp.where(pick, dir_ref[1:2, :], 0.0), axis=1, keepdims=True)
    group = ids - GROUPS * jnp.floor(ids * (1.0 / GROUPS))
    return east, north, group


def station_rows(pos_ref, group_ref, stations, lanes):
    total = group_ref.shape[1]
    first = lax.axis_index("stn") * stations
    own = iota((stations, total), 1) == iota((stations, total), 0) + first
    spread = iota((stations, lanes), 0) == iota((stations, lanes), 1) % stations

    def turn(row):
        column = jnp.sum(jnp.where(own, row, 0.0), axis=1, keepdims=True)
        return jnp.sum(jnp.where(spread, column, 0.0), axis=0, keepdims=True)

    return turn(pos_ref[0:1, :]), turn(pos_ref[1:2, :]), turn(group_ref[...].astype(jnp.float32))


def cos_turns(t):
    y = t - jnp.floor(t + 0.5)
    z = 0.25 - jnp.abs(y)
    z2 = z * z
    value = jnp.full_like(z, SIN[-1])
    for coefficient in SIN[-2::-1]:
        value = value * z2 + coefficient
    return value * z


def kernel(
    volt_hbm,
    aw_hbm,
    sw_hbm,
    ts_hbm,
    group_hbm,
    pos_hbm,
    dir_hbm,
    order_hbm,
    out_ref,
    volts,
    aw_ref,
    sw_ref,
    ts_ref,
    group_ref,
    pos_ref,
    dir_ref,
    order_ref,
    tied_ref,
    sems,
):
    channels, _, tiles = sw_ref.shape
    antennas = volt_hbm.shape[1]
    samples = volt_hbm.shape[0] // (2 * channels)
    stations = tiles // TPS
    groups = channels // CB
    assert groups == len(SPLIT)
    rows_c = 2 * samples
    beams = order_ref.shape[1]
    lanes = CB * 2 * stations
    scale = 1.0 / math.sqrt(group_ref.shape[1])

    def start(source, target, k):
        copy = pltpu.make_async_copy(source, target, sems.at[k])
        copy.start()
        return copy

    def voltages(g):
        rows = CB * rows_c // SPLIT[g]
        parts = [pl.ds(g * CB * rows_c + k * rows, rows) for k in range(SPLIT[g])]
        return [(volt_hbm.at[part], volts.at[part]) for part in parts]

    pairs = voltages(0) + [
        (aw_hbm, aw_ref),
        (order_hbm, order_ref),
        (dir_hbm, dir_ref),
        (pos_hbm, pos_ref),
        (group_hbm, group_ref),
        (ts_hbm, ts_ref),
        (sw_hbm, sw_ref),
    ]
    ends = [len(pairs)]
    for g in range(1, groups):
        pairs += voltages(g)
        ends.append(len(pairs))
    copies = [start(source, target, k) for k, (source, target) in enumerate(pairs)]
    antenna_tile = iota((CHUNK // TILE_ANTENNAS, CHUNK), 1) // TILE_ANTENNAS
    sum_tile = (antenna_tile == iota(antenna_tile.shape, 0)).astype(jnp.bfloat16)
    for copy in copies[: SPLIT[0] + 1]:
        copy.wait()

    def tile_beams(g):
        products = []
        weights = aw_ref[g * CB : (g + 1) * CB].astype(jnp.float32)
        for c in range(CB):
            w_re = jnp.broadcast_to(weights[c, 0:1], (samples, antennas)).astype(jnp.bfloat16)
            w_im = jnp.broadcast_to(weights[c, 1:2], (samples, antennas)).astype(jnp.bfloat16)
            first = (g * CB + c) * rows_c
            v_re, v_im = volts[first : first + samples], volts[first + samples : first + rows_c]
            products.append(w_re * v_re - w_im * v_im)
            products.append(w_re * v_im + w_im * v_re)
        products = jnp.concatenate(products, axis=0)
        sums = [
            dot_nt(sum_tile, products[:, first : first + CHUNK])
            for first in range(0, antennas, CHUNK)
        ]
        return jnp.concatenate(sums, axis=0)

    last = tile_beams(0)
    for copy in copies[SPLIT[0] + 1 : ends[1]]:
        copy.wait()

    east_s, north_s, group_s = station_rows(pos_ref, group_ref, stations, lanes)
    lane = iota((1, lanes), 1)
    channel_lane = lane // (2 * stations)
    quarter = 0.25 * ((lane // stations) % 2).astype(jnp.float32)
    first_chan = lax.axis_index("chan") * channels
    total_chans = channels * lax.axis_size("chan")
    block = min(64, beams)

    def tied_rows(first):
        east, north, group = beam_columns(order_ref, dir_ref, first, block)
        delay = east * east_s + north * north_s
        member = jnp.where(group == group_s, scale, 0.0)
        for g in range(groups):
            freq = 1.0 + (first_chan + g * CB + channel_lane).astype(jnp.float32) / total_chans
            wave = cos_turns(delay * freq - quarter)
            tied_ref[pl.ds(first, block), g * lanes : (g + 1) * lanes] = (wave * member).astype(
                jnp.bfloat16
            )

    if beams == block:
        tied_rows(0)
    else:

        def body(i, carry):
            tied_rows(pl.multiple_of(i * block, block))
            return carry

        lax.fori_loop(0, beams // block, body, 0)

    member_table = (iota((stations, tiles), 0) == ts_ref[...] % stations).astype(jnp.float32)
    own_channel = iota((lanes, CB * rows_c), 0) // (2 * stations) == iota(
        (lanes, CB * rows_c), 1
    ) // rows_c

    imag_column = iota((tiles, CB * rows_c), 1) // samples % 2 == 1
    station_rows_of = []
    for g in range(groups):
        swt = sw_ref[g * CB : (g + 1) * CB].astype(jnp.float32)
        right = []
        for c in range(CB):
            re = swt[c, 0:1] * member_table
            im = swt[c, 1:2] * member_table
            right.append(jnp.concatenate([re, -im], axis=1))
            right.append(jnp.concatenate([im, re], axis=1))
        station_rows_of.append(jnp.concatenate(right, axis=0).astype(jnp.bfloat16))

    def tied_beams(g, beams_tile):
        width = CB * rows_c
        other = jnp.where(
            imag_column,
            -pltpu.roll(beams_tile, samples, 1),
            pltpu.roll(beams_tile, width - samples, 1),
        )
        left = jnp.concatenate([beams_tile, other], axis=0).astype(jnp.bfloat16)
        station = jnp.dot(station_rows_of[g], left, preferred_element_type=jnp.float32)
        station = jnp.where(own_channel, station, 0.0).astype(jnp.bfloat16)
        tied = jnp.dot(
            tied_ref[:, g * lanes : (g + 1) * lanes], station, preferred_element_type=jnp.float32
        )
        devices, rows, _ = out_ref.shape
        out_ref[:, :, g * CB * rows_c : (g + 1) * CB * rows_c] = tied.astype(jnp.bfloat16).reshape(
            devices, rows, CB * rows_c
        )

    for g in range(1, groups):
        if g > 1:
            for copy in copies[ends[g - 1] : ends[g]]:
                copy.wait()
        now = tile_beams(g)
        tied_beams(g - 1, last)
        last = now
    tied_beams(groups - 1, last)


def last_kernel(parts_ref, out_ref):
    n_stn, n_chan = lax.axis_size("stn"), lax.axis_size("chan")
    own_beams, rows_c, total_chans = out_ref.shape
    channels = total_chans // n_chan
    width = channels * rows_c
    parts = parts_ref[...].astype(jnp.float32)
    devices = n_stn * n_chan
    tied = [sum(parts[(devices - k * n_chan - chan) % devices] for k in range(n_stn)) for chan in range(n_chan)]
    diagonal = iota((channels, width), 0) == iota((channels, width), 1) // rows_c
    spread = (iota((rows_c, width), 0) == iota((rows_c, width), 1) % rows_c).astype(jnp.bfloat16)
    for b in range(own_beams):
        rows = [jnp.where(diagonal, tied[chan][b : b + 1], 0.0) for chan in range(n_chan)]
        rows = jnp.concatenate(rows, axis=0).astype(jnp.bfloat16)
        out_ref[b] = dot_nt(spread, rows).astype(jnp.bfloat16)


def shards(
    volts,
    antenna_tile_weights,
    station_weights,
    tile_station,
    station_group,
    station_pos,
    beam_dir,
    beam_order,
):
    channels, _, samples, _ = volts.shape
    beams = beam_order.shape[0]
    n_stn, n_chan = lax.axis_size("stn"), lax.axis_size("chan")
    rows = beams // (n_stn * n_chan)
    width = channels * 2 * samples
    operands = (
        volts.reshape(-1, volts.shape[3]),
        antenna_tile_weights,
        station_weights,
        tile_station[None, :],
        station_group[None, :],
        station_pos.T,
        beam_dir.T,
        beam_order[None, :],
    )
    operands = [pltpu.with_memory_space_constraint(x, pltpu.HBM) for x in operands]
    partial = pl.pallas_call(
        kernel,
        out_shape=pltpu.VMEM((n_stn * n_chan, rows, width), jnp.bfloat16),
        in_specs=[pl.BlockSpec(memory_space=pltpu.HBM)] * len(operands),
        out_specs=pl.BlockSpec(memory_space=pltpu.VMEM),
        scratch_shapes=[pltpu.VMEM(x.shape, x.dtype) for x in operands]
        + [
            pltpu.VMEM((beams, channels * 2 * (station_weights.shape[2] // TPS)), jnp.bfloat16),
            pltpu.SemaphoreType.DMA((len(operands) - 1 + sum(SPLIT),)),
        ],
        compiler_params=pltpu.CompilerParams(vmem_limit_bytes=24 * 2**20),
        name="partial_tied",
    )(*operands)
    parts = lax.all_to_all(
        partial,
        ("stn", "chan"),
        split_axis=0,
        concat_axis=0,
        axis_index_groups=[[0, *reversed(range(1, n_stn * n_chan))]],
        tiled=True,
    )
    vmem = pl.BlockSpec(memory_space=pltpu.VMEM)
    tied = pl.pallas_call(
        last_kernel,
        out_shape=jax.ShapeDtypeStruct((rows, 2 * samples, n_chan * channels), jnp.bfloat16),
        in_specs=[vmem],
        out_specs=vmem,
        compiler_params=pltpu.CompilerParams(vmem_limit_bytes=16 * 2**20),
        name="tied_beams",
    )(parts)
    return tied.transpose(0, 2, 1)


def solution(mesh):
    in_specs = (
        P("chan", None, None, "stn"),
        P("chan", None, "stn"),
        P("chan", None, "stn"),
        P("stn"),
        P(),
        P(),
        P(),
        P(),
    )
    out_specs = P(("stn", "chan"), None, None)
    return jax.shard_map(shards, mesh=mesh, in_specs=in_specs, out_specs=out_specs, check_vma=False)
```

```python
import functools
import math

import jax
import jax.numpy as jnp
from jax import lax
from jax.experimental import pallas as pl
from jax.experimental.pallas import tpu as pltpu
from jax.sharding import PartitionSpec as P

TILE_ANTENNAS = 16
TPS = 16
GROUPS = 4
LANES = 128
CB = 8
SPLIT = (4, 2, 1)
CHUNK = 256
NT = (((1,), (1,)), ((), ()))
SIN = [(-1) ** i * (2 * math.pi) ** (2 * i + 1) / math.factorial(2 * i + 1) for i in range(7)]


def dot_nt(a, b):
    return lax.dot_general(a, b, NT, preferred_element_type=jnp.float32)


def iota(shape, dim):
    return lax.broadcasted_iota(jnp.int32, shape, dim)


def beam_columns(order_ref, dir_ref, start, rows):
    beams = order_ref.shape[1]
    each = beams // (lax.axis_size("stn") * lax.axis_size("chan"))
    order = order_ref[...].astype(jnp.float32)
    lane = iota((rows, beams), 1)
    slot = iota((rows, beams), 0) + start
    own = lane == beams - each - slot // each * each + slot % each
    ids = jnp.sum(jnp.where(own, order, 0.0), axis=1, keepdims=True)
    pick = lane.astype(jnp.float32) == ids
    east = jnp.sum(jnp.where(pick, dir_ref[0:1, :], 0.0), axis=1, keepdims=True)
    north = jnp.sum(jnp.where(pick, dir_ref[1:2, :], 0.0), axis=1, keepdims=True)
    group = ids - GROUPS * jnp.floor(ids * (1.0 / GROUPS))
    return east, north, group


def station_rows(pos_ref, group_ref, stations, lanes):
    total = group_ref.shape[1]
    first = lax.axis_index("stn") * stations
    own = iota((stations, total), 1) == iota((stations, total), 0) + first
    spread = iota((stations, lanes), 0) == iota((stations, lanes), 1) % stations

    def turn(row):
        column = jnp.sum(jnp.where(own, row, 0.0), axis=1, keepdims=True)
        return jnp.sum(jnp.where(spread, column, 0.0), axis=0, keepdims=True)

    return turn(pos_ref[0:1, :]), turn(pos_ref[1:2, :]), turn(group_ref[...].astype(jnp.float32))


def cos_turns(t):
    y = t - jnp.floor(t + 0.5)
    z = 0.25 - jnp.abs(y)
    z2 = z * z
    value = jnp.full_like(z, SIN[-1])
    for coefficient in SIN[-2::-1]:
        value = value * z2 + coefficient
    return value * z


def kernel(
    volt_hbm,
    aw_hbm,
    sw_hbm,
    ts_hbm,
    group_hbm,
    pos_hbm,
    dir_hbm,
    order_hbm,
    out_ref,
    volts,
    aw_ref,
    sw_ref,
    ts_ref,
    group_ref,
    pos_ref,
    dir_ref,
    order_ref,
    tied_ref,
    sems,
):
    channels, _, tiles = sw_ref.shape
    antennas = volt_hbm.shape[1]
    samples = volt_hbm.shape[0] // (2 * channels)
    stations = tiles // TPS
    groups = channels // CB
    assert groups == len(SPLIT)
    rows_c = 2 * samples
    beams = order_ref.shape[1]
    lanes = CB * 2 * stations
    scale = 1.0 / math.sqrt(group_ref.shape[1])

    def start(source, target, k):
        copy = pltpu.make_async_copy(source, target, sems.at[k])
        copy.start()
        return copy

    def voltages(g):
        rows = CB * rows_c // SPLIT[g]
        parts = [pl.ds(g * CB * rows_c + k * rows, rows) for k in range(SPLIT[g])]
        return [(volt_hbm.at[part], volts.at[part]) for part in parts]

    pairs = voltages(0) + [
        (aw_hbm, aw_ref),
        (order_hbm, order_ref),
        (dir_hbm, dir_ref),
        (pos_hbm, pos_ref),
        (group_hbm, group_ref),
        (ts_hbm, ts_ref),
        (sw_hbm, sw_ref),
    ]
    ends = [len(pairs)]
    for g in range(1, groups):
        pairs += voltages(g)
        ends.append(len(pairs))
    copies = [start(source, target, k) for k, (source, target) in enumerate(pairs)]
    antenna_tile = iota((CHUNK // TILE_ANTENNAS, CHUNK), 1) // TILE_ANTENNAS
    sum_tile = (antenna_tile == iota(antenna_tile.shape, 0)).astype(jnp.bfloat16)
    for copy in copies[: SPLIT[0] + 1]:
        copy.wait()

    def tile_beams(g):
        products = []
        weights = aw_ref[g * CB : (g + 1) * CB].astype(jnp.float32)
        for c in range(CB):
            w_re = jnp.broadcast_to(weights[c, 0:1], (samples, antennas)).astype(jnp.bfloat16)
            w_im = jnp.broadcast_to(weights[c, 1:2], (samples, antennas)).astype(jnp.bfloat16)
            first = (g * CB + c) * rows_c
            v_re, v_im = volts[first : first + samples], volts[first + samples : first + rows_c]
            products.append(w_re * v_re - w_im * v_im)
            products.append(w_re * v_im + w_im * v_re)
        products = jnp.concatenate(products, axis=0)
        sums = [
            dot_nt(sum_tile, products[:, first : first + CHUNK])
            for first in range(0, antennas, CHUNK)
        ]
        return jnp.concatenate(sums, axis=0)

    last = tile_beams(0)
    for copy in copies[SPLIT[0] + 1 : ends[1]]:
        copy.wait()

    east_s, north_s, group_s = station_rows(pos_ref, group_ref, stations, lanes)
    lane = iota((1, lanes), 1)
    channel_lane = lane // (2 * stations)
    quarter = 0.25 * ((lane // stations) % 2).astype(jnp.float32)
    first_chan = lax.axis_index("chan") * channels
    total_chans = channels * lax.axis_size("chan")
    block = min(64, beams)

    def tied_rows(first):
        east, north, group = beam_columns(order_ref, dir_ref, first, block)
        delay = east * east_s + north * north_s
        member = jnp.where(group == group_s, scale, 0.0)
        for g in range(groups):
            freq = 1.0 + (first_chan + g * CB + channel_lane).astype(jnp.float32) / total_chans
            wave = cos_turns(delay * freq - quarter)
            tied_ref[pl.ds(first, block), g * lanes : (g + 1) * lanes] = (wave * member).astype(
                jnp.bfloat16
            )

    if beams == block:
        tied_rows(0)
    else:

        def body(i, carry):
            tied_rows(pl.multiple_of(i * block, block))
            return carry

        lax.fori_loop(0, beams // block, body, 0)

    member_table = (iota((stations, tiles), 0) == ts_ref[...] % stations).astype(jnp.float32)
    own_channel = iota((lanes, CB * rows_c), 0) // (2 * stations) == iota(
        (lanes, CB * rows_c), 1
    ) // rows_c

    imag_column = iota((tiles, CB * rows_c), 1) // samples % 2 == 1
    station_rows_of = []
    for g in range(groups):
        swt = sw_ref[g * CB : (g + 1) * CB].astype(jnp.float32)
        right = []
        for c in range(CB):
            re = swt[c, 0:1] * member_table
            im = swt[c, 1:2] * member_table
            right.append(jnp.concatenate([re, -im], axis=1))
            right.append(jnp.concatenate([im, re], axis=1))
        station_rows_of.append(jnp.concatenate(right, axis=0).astype(jnp.bfloat16))

    def tied_beams(g, beams_tile):
        width = CB * rows_c
        other = jnp.where(
            imag_column,
            -pltpu.roll(beams_tile, samples, 1),
            pltpu.roll(beams_tile, width - samples, 1),
        )
        left = jnp.concatenate([beams_tile, other], axis=0).astype(jnp.bfloat16)
        station = jnp.dot(station_rows_of[g], left, preferred_element_type=jnp.float32)
        station = jnp.where(own_channel, station, 0.0).astype(jnp.bfloat16)
        tied = jnp.dot(
            tied_ref[:, g * lanes : (g + 1) * lanes], station, preferred_element_type=jnp.float32
        )
        devices, rows, _ = out_ref.shape
        out_ref[:, :, g * CB * rows_c : (g + 1) * CB * rows_c] = tied.astype(jnp.bfloat16).reshape(
            devices, rows, CB * rows_c
        )

    for g in range(1, groups):
        if g > 1:
            for copy in copies[ends[g - 1] : ends[g]]:
                copy.wait()
        now = tile_beams(g)
        tied_beams(g - 1, last)
        last = now
    tied_beams(groups - 1, last)


def last_kernel(parts_ref, out_ref):
    n_stn, n_chan = lax.axis_size("stn"), lax.axis_size("chan")
    own_beams, rows_c, total_chans = out_ref.shape
    channels = total_chans // n_chan
    width = channels * rows_c
    parts = parts_ref[...].astype(jnp.float32)
    tied = [sum(parts[n_chan - 1 - chan + k * n_chan] for k in range(n_stn)) for chan in range(n_chan)]
    per_tile = LANES // rows_c
    row, lane = iota((2 * per_tile, LANES), 0), iota((2 * per_tile, LANES), 1)
    own_lane = row % per_tile == lane // rows_c
    spread = (iota((rows_c, LANES), 0) == iota((rows_c, LANES), 1) % rows_c).astype(jnp.bfloat16)
    rows = []
    for b in range(own_beams):
        for chan in range(n_chan):
            for first in range(0, width, 2 * LANES):
                low = tied[chan][b : b + 1, first : first + LANES]
                high = tied[chan][b : b + 1, first + LANES : first + 2 * LANES]
                rows.append(jnp.where(own_lane, jnp.where(row < per_tile, low, high), 0.0))
    rows = jnp.concatenate(rows, axis=0).astype(jnp.bfloat16)
    columns = dot_nt(spread, rows).astype(jnp.bfloat16)
    for b in range(own_beams):
        out_ref[b] = columns[:, b * total_chans : (b + 1) * total_chans]


def shards(
    volts,
    antenna_tile_weights,
    station_weights,
    tile_station,
    station_group,
    station_pos,
    beam_dir,
    beam_order,
):
    channels, _, samples, _ = volts.shape
    beams = beam_order.shape[0]
    n_stn, n_chan = lax.axis_size("stn"), lax.axis_size("chan")
    rows = beams // (n_stn * n_chan)
    width = channels * 2 * samples
    operands = (
        volts.reshape(-1, volts.shape[3]),
        antenna_tile_weights,
        station_weights,
        tile_station[None, :],
        station_group[None, :],
        station_pos.T,
        beam_dir.T,
        beam_order[None, :],
    )
    operands = [pltpu.with_memory_space_constraint(x, pltpu.HBM) for x in operands]
    partial = pl.pallas_call(
        kernel,
        out_shape=pltpu.VMEM((n_stn * n_chan, rows, width), jnp.bfloat16),
        in_specs=[pl.BlockSpec(memory_space=pltpu.HBM)] * len(operands),
        out_specs=pl.BlockSpec(memory_space=pltpu.VMEM),
        scratch_shapes=[pltpu.VMEM(x.shape, x.dtype) for x in operands]
        + [
            pltpu.VMEM((beams, channels * 2 * (station_weights.shape[2] // TPS)), jnp.bfloat16),
            pltpu.SemaphoreType.DMA((len(operands) - 1 + sum(SPLIT),)),
        ],
        compiler_params=pltpu.CompilerParams(vmem_limit_bytes=24 * 2**20),
        name="partial_tied",
    )(*operands)
    parts = lax.all_to_all(
        partial,
        ("stn", "chan"),
        split_axis=0,
        concat_axis=0,
        axis_index_groups=[list(reversed(range(n_stn * n_chan)))],
        tiled=True,
    )
    vmem = pl.BlockSpec(memory_space=pltpu.VMEM)
    tied = pl.pallas_call(
        last_kernel,
        out_shape=jax.ShapeDtypeStruct((rows, 2 * samples, n_chan * channels), jnp.bfloat16),
        in_specs=[vmem],
        out_specs=vmem,
        compiler_params=pltpu.CompilerParams(vmem_limit_bytes=16 * 2**20),
        name="tied_beams",
    )(parts)
    return tied.transpose(0, 2, 1)


def solution(mesh):
    in_specs = (
        P("chan", None, None, "stn"),
        P("chan", None, "stn"),
        P("chan", None, "stn"),
        P("stn"),
        P(),
        P(),
        P(),
        P(),
    )
    out_specs = P(("stn", "chan"), None, None)
    return jax.shard_map(shards, mesh=mesh, in_specs=in_specs, out_specs=out_specs, check_vma=False)
```

```python
import functools
import math

import jax
import jax.numpy as jnp
from jax import lax
from jax.experimental import pallas as pl
from jax.experimental.pallas import tpu as pltpu
from jax.sharding import PartitionSpec as P

TILE_ANTENNAS = 16
TPS = 16
GROUPS = 4
CB = 8
SPLIT = (4, 2, 1)
CHUNK = 256
NT = (((1,), (1,)), ((), ()))
SIN = [(-1) ** i * (2 * math.pi) ** (2 * i + 1) / math.factorial(2 * i + 1) for i in range(7)]


def dot_nt(a, b):
    return lax.dot_general(a, b, NT, preferred_element_type=jnp.float32)


def iota(shape, dim):
    return lax.broadcasted_iota(jnp.int32, shape, dim)


def device_at(place, n_chan):
    stn = place // n_chan
    stn = stn // 4 * 4 + stn % 2 * 2 + stn // 2 % 2
    return stn * n_chan + place % n_chan


def beam_columns(order_ref, dir_ref, start, rows):
    beams = order_ref.shape[1]
    n_chan = lax.axis_size("chan")
    devices = lax.axis_size("stn") * n_chan
    each = beams // devices
    order = order_ref[...].astype(jnp.float32)
    lane = iota((rows, beams), 1)
    slot = iota((rows, beams), 0) + start
    place = devices - 1 - slot // each
    own = lane == device_at(place, n_chan) * each + slot % each
    ids = jnp.sum(jnp.where(own, order, 0.0), axis=1, keepdims=True)
    pick = lane.astype(jnp.float32) == ids
    east = jnp.sum(jnp.where(pick, dir_ref[0:1, :], 0.0), axis=1, keepdims=True)
    north = jnp.sum(jnp.where(pick, dir_ref[1:2, :], 0.0), axis=1, keepdims=True)
    group = ids - GROUPS * jnp.floor(ids * (1.0 / GROUPS))
    return east, north, group


def station_rows(pos_ref, group_ref, stations, lanes):
    total = group_ref.shape[1]
    first = lax.axis_index("stn") * stations
    own = iota((stations, total), 1) == iota((stations, total), 0) + first
    spread = iota((stations, lanes), 0) == iota((stations, lanes), 1) % stations

    def turn(row):
        column = jnp.sum(jnp.where(own, row, 0.0), axis=1, keepdims=True)
        return jnp.sum(jnp.where(spread, column, 0.0), axis=0, keepdims=True)

    return turn(pos_ref[0:1, :]), turn(pos_ref[1:2, :]), turn(group_ref[...].astype(jnp.float32))


def cos_turns(t):
    y = t - jnp.floor(t + 0.5)
    z = 0.25 - jnp.abs(y)
    z2 = z * z
    value = jnp.full_like(z, SIN[-1])
    for coefficient in SIN[-2::-1]:
        value = value * z2 + coefficient
    return value * z


def kernel(
    volt_hbm,
    aw_hbm,
    sw_hbm,
    ts_hbm,
    group_hbm,
    pos_hbm,
    dir_hbm,
    order_hbm,
    out_ref,
    volts,
    aw_ref,
    sw_ref,
    ts_ref,
    group_ref,
    pos_ref,
    dir_ref,
    order_ref,
    tied_ref,
    sems,
):
    channels, _, tiles = sw_ref.shape
    antennas = volt_hbm.shape[1]
    samples = volt_hbm.shape[0] // (2 * channels)
    stations = tiles // TPS
    groups = channels // CB
    assert groups == len(SPLIT)
    rows_c = 2 * samples
    beams = order_ref.shape[1]
    lanes = CB * 2 * stations
    scale = 1.0 / math.sqrt(group_ref.shape[1])

    def start(source, target, k):
        copy = pltpu.make_async_copy(source, target, sems.at[k])
        copy.start()
        return copy

    def voltages(g):
        rows = CB * rows_c // SPLIT[g]
        parts = [pl.ds(g * CB * rows_c + k * rows, rows) for k in range(SPLIT[g])]
        return [(volt_hbm.at[part], volts.at[part]) for part in parts]

    pairs = voltages(0) + [
        (aw_hbm, aw_ref),
        (order_hbm, order_ref),
        (dir_hbm, dir_ref),
        (pos_hbm, pos_ref),
        (group_hbm, group_ref),
        (ts_hbm, ts_ref),
        (sw_hbm, sw_ref),
    ]
    ends = [len(pairs)]
    for g in range(1, groups):
        pairs += voltages(g)
        ends.append(len(pairs))
    copies = [start(source, target, k) for k, (source, target) in enumerate(pairs)]
    antenna_tile = iota((CHUNK // TILE_ANTENNAS, CHUNK), 1) // TILE_ANTENNAS
    sum_tile = (antenna_tile == iota(antenna_tile.shape, 0)).astype(jnp.bfloat16)
    for copy in copies[: SPLIT[0] + 1]:
        copy.wait()

    def tile_beams(g):
        products = []
        weights = aw_ref[g * CB : (g + 1) * CB].astype(jnp.float32)
        for c in range(CB):
            w_re = jnp.broadcast_to(weights[c, 0:1], (samples, antennas)).astype(jnp.bfloat16)
            w_im = jnp.broadcast_to(weights[c, 1:2], (samples, antennas)).astype(jnp.bfloat16)
            first = (g * CB + c) * rows_c
            v_re, v_im = volts[first : first + samples], volts[first + samples : first + rows_c]
            products.append(w_re * v_re - w_im * v_im)
            products.append(w_re * v_im + w_im * v_re)
        products = jnp.concatenate(products, axis=0)
        sums = [
            dot_nt(sum_tile, products[:, first : first + CHUNK])
            for first in range(0, antennas, CHUNK)
        ]
        return jnp.concatenate(sums, axis=0)

    last = tile_beams(0)
    for copy in copies[SPLIT[0] + 1 : ends[1]]:
        copy.wait()

    east_s, north_s, group_s = station_rows(pos_ref, group_ref, stations, lanes)
    lane = iota((1, lanes), 1)
    channel_lane = lane // (2 * stations)
    quarter = 0.25 * ((lane // stations) % 2).astype(jnp.float32)
    first_chan = lax.axis_index("chan") * channels
    total_chans = channels * lax.axis_size("chan")
    block = min(64, beams)

    def tied_rows(first):
        east, north, group = beam_columns(order_ref, dir_ref, first, block)
        delay = east * east_s + north * north_s
        member = jnp.where(group == group_s, scale, 0.0)
        for g in range(groups):
            freq = 1.0 + (first_chan + g * CB + channel_lane).astype(jnp.float32) / total_chans
            wave = cos_turns(delay * freq - quarter)
            tied_ref[pl.ds(first, block), g * lanes : (g + 1) * lanes] = (wave * member).astype(
                jnp.bfloat16
            )

    if beams == block:
        tied_rows(0)
    else:

        def body(i, carry):
            tied_rows(pl.multiple_of(i * block, block))
            return carry

        lax.fori_loop(0, beams // block, body, 0)

    member_table = (iota((stations, tiles), 0) == ts_ref[...] % stations).astype(jnp.float32)
    own_channel = iota((lanes, CB * rows_c), 0) // (2 * stations) == iota(
        (lanes, CB * rows_c), 1
    ) // rows_c

    imag_column = iota((tiles, CB * rows_c), 1) // samples % 2 == 1
    station_rows_of = []
    for g in range(groups):
        swt = sw_ref[g * CB : (g + 1) * CB].astype(jnp.float32)
        right = []
        for c in range(CB):
            re = swt[c, 0:1] * member_table
            im = swt[c, 1:2] * member_table
            right.append(jnp.concatenate([re, -im], axis=1))
            right.append(jnp.concatenate([im, re], axis=1))
        station_rows_of.append(jnp.concatenate(right, axis=0).astype(jnp.bfloat16))

    def tied_beams(g, beams_tile):
        width = CB * rows_c
        other = jnp.where(
            imag_column,
            -pltpu.roll(beams_tile, samples, 1),
            pltpu.roll(beams_tile, width - samples, 1),
        )
        left = jnp.concatenate([beams_tile, other], axis=0).astype(jnp.bfloat16)
        station = jnp.dot(station_rows_of[g], left, preferred_element_type=jnp.float32)
        station = jnp.where(own_channel, station, 0.0).astype(jnp.bfloat16)
        tied = jnp.dot(
            tied_ref[:, g * lanes : (g + 1) * lanes], station, preferred_element_type=jnp.float32
        )
        devices, rows, _ = out_ref.shape
        out_ref[:, :, g * CB * rows_c : (g + 1) * CB * rows_c] = tied.astype(jnp.bfloat16).reshape(
            devices, rows, CB * rows_c
        )

    for g in range(1, groups):
        if g > 1:
            for copy in copies[ends[g - 1] : ends[g]]:
                copy.wait()
        now = tile_beams(g)
        tied_beams(g - 1, last)
        last = now
    tied_beams(groups - 1, last)


def last_kernel(parts_ref, out_ref):
    n_stn, n_chan = lax.axis_size("stn"), lax.axis_size("chan")
    own_beams, rows_c, total_chans = out_ref.shape
    channels = total_chans // n_chan
    width = channels * rows_c
    parts = parts_ref[...].astype(jnp.float32)
    tied = [sum(parts[n_chan - 1 - chan + k * n_chan] for k in range(n_stn)) for chan in range(n_chan)]
    diagonal = iota((channels, width), 0) == iota((channels, width), 1) // rows_c
    spread = (iota((rows_c, width), 0) == iota((rows_c, width), 1) % rows_c).astype(jnp.bfloat16)
    for b in range(own_beams):
        rows = [jnp.where(diagonal, tied[chan][b : b + 1], 0.0) for chan in range(n_chan)]
        rows = jnp.concatenate(rows, axis=0).astype(jnp.bfloat16)
        out_ref[b] = dot_nt(spread, rows).astype(jnp.bfloat16)


def shards(
    volts,
    antenna_tile_weights,
    station_weights,
    tile_station,
    station_group,
    station_pos,
    beam_dir,
    beam_order,
):
    channels, _, samples, _ = volts.shape
    beams = beam_order.shape[0]
    n_stn, n_chan = lax.axis_size("stn"), lax.axis_size("chan")
    rows = beams // (n_stn * n_chan)
    width = channels * 2 * samples
    operands = (
        volts.reshape(-1, volts.shape[3]),
        antenna_tile_weights,
        station_weights,
        tile_station[None, :],
        station_group[None, :],
        station_pos.T,
        beam_dir.T,
        beam_order[None, :],
    )
    operands = [pltpu.with_memory_space_constraint(x, pltpu.HBM) for x in operands]
    partial = pl.pallas_call(
        kernel,
        out_shape=pltpu.VMEM((n_stn * n_chan, rows, width), jnp.bfloat16),
        in_specs=[pl.BlockSpec(memory_space=pltpu.HBM)] * len(operands),
        out_specs=pl.BlockSpec(memory_space=pltpu.VMEM),
        scratch_shapes=[pltpu.VMEM(x.shape, x.dtype) for x in operands]
        + [
            pltpu.VMEM((beams, channels * 2 * (station_weights.shape[2] // TPS)), jnp.bfloat16),
            pltpu.SemaphoreType.DMA((len(operands) - 1 + sum(SPLIT),)),
        ],
        compiler_params=pltpu.CompilerParams(vmem_limit_bytes=24 * 2**20),
        name="partial_tied",
    )(*operands)
    parts = lax.all_to_all(
        partial,
        ("stn", "chan"),
        split_axis=0,
        concat_axis=0,
        axis_index_groups=[[device_at(k, n_chan) for k in reversed(range(n_stn * n_chan))]],
        tiled=True,
    )
    vmem = pl.BlockSpec(memory_space=pltpu.VMEM)
    tied = pl.pallas_call(
        last_kernel,
        out_shape=jax.ShapeDtypeStruct((rows, 2 * samples, n_chan * channels), jnp.bfloat16),
        in_specs=[vmem],
        out_specs=vmem,
        compiler_params=pltpu.CompilerParams(vmem_limit_bytes=16 * 2**20),
        name="tied_beams",
    )(parts)
    return tied.transpose(0, 2, 1)


def solution(mesh):
    in_specs = (
        P("chan", None, None, "stn"),
        P("chan", None, "stn"),
        P("chan", None, "stn"),
        P("stn"),
        P(),
        P(),
        P(),
        P(),
    )
    out_specs = P(("stn", "chan"), None, None)
    return jax.shard_map(shards, mesh=mesh, in_specs=in_specs, out_specs=out_specs, check_vma=False)
```

```python
import functools
import math

import jax
import jax.numpy as jnp
from jax import lax
from jax.experimental import pallas as pl
from jax.experimental.pallas import tpu as pltpu
from jax.sharding import PartitionSpec as P

TILE_ANTENNAS = 16
TPS = 16
GROUPS = 4
CB = 8
SPLIT = (4, 2, 1)
CHUNK = 256
NT = (((1,), (1,)), ((), ()))
SIN = [(-1) ** i * (2 * math.pi) ** (2 * i + 1) / math.factorial(2 * i + 1) for i in range(7)]


def dot_nt(a, b):
    return lax.dot_general(a, b, NT, preferred_element_type=jnp.float32)


def iota(shape, dim):
    return lax.broadcasted_iota(jnp.int32, shape, dim)


def device_at(place, n_chan):
    pair, rest = place // (2 * n_chan), place % (2 * n_chan)
    return (pair * 2 + rest % 2) * n_chan + rest // 2


def beam_columns(order_ref, dir_ref, start, rows):
    beams = order_ref.shape[1]
    n_chan = lax.axis_size("chan")
    devices = lax.axis_size("stn") * n_chan
    each = beams // devices
    order = order_ref[...].astype(jnp.float32)
    lane = iota((rows, beams), 1)
    slot = iota((rows, beams), 0) + start
    place = devices - 1 - slot // each
    own = lane == device_at(place, n_chan) * each + slot % each
    ids = jnp.sum(jnp.where(own, order, 0.0), axis=1, keepdims=True)
    pick = lane.astype(jnp.float32) == ids
    east = jnp.sum(jnp.where(pick, dir_ref[0:1, :], 0.0), axis=1, keepdims=True)
    north = jnp.sum(jnp.where(pick, dir_ref[1:2, :], 0.0), axis=1, keepdims=True)
    group = ids - GROUPS * jnp.floor(ids * (1.0 / GROUPS))
    return east, north, group


def station_rows(pos_ref, group_ref, stations, lanes):
    total = group_ref.shape[1]
    first = lax.axis_index("stn") * stations
    own = iota((stations, total), 1) == iota((stations, total), 0) + first
    spread = iota((stations, lanes), 0) == iota((stations, lanes), 1) % stations

    def turn(row):
        column = jnp.sum(jnp.where(own, row, 0.0), axis=1, keepdims=True)
        return jnp.sum(jnp.where(spread, column, 0.0), axis=0, keepdims=True)

    return turn(pos_ref[0:1, :]), turn(pos_ref[1:2, :]), turn(group_ref[...].astype(jnp.float32))


def cos_turns(t):
    y = t - jnp.floor(t + 0.5)
    z = 0.25 - jnp.abs(y)
    z2 = z * z
    value = jnp.full_like(z, SIN[-1])
    for coefficient in SIN[-2::-1]:
        value = value * z2 + coefficient
    return value * z


def kernel(
    volt_hbm,
    aw_hbm,
    sw_hbm,
    ts_hbm,
    group_hbm,
    pos_hbm,
    dir_hbm,
    order_hbm,
    out_ref,
    volts,
    aw_ref,
    sw_ref,
    ts_ref,
    group_ref,
    pos_ref,
    dir_ref,
    order_ref,
    tied_ref,
    sems,
):
    channels, _, tiles = sw_ref.shape
    antennas = volt_hbm.shape[1]
    samples = volt_hbm.shape[0] // (2 * channels)
    stations = tiles // TPS
    groups = channels // CB
    assert groups == len(SPLIT)
    rows_c = 2 * samples
    beams = order_ref.shape[1]
    lanes = CB * 2 * stations
    scale = 1.0 / math.sqrt(group_ref.shape[1])

    def start(source, target, k):
        copy = pltpu.make_async_copy(source, target, sems.at[k])
        copy.start()
        return copy

    def voltages(g):
        rows = CB * rows_c // SPLIT[g]
        parts = [pl.ds(g * CB * rows_c + k * rows, rows) for k in range(SPLIT[g])]
        return [(volt_hbm.at[part], volts.at[part]) for part in parts]

    pairs = voltages(0) + [
        (aw_hbm, aw_ref),
        (order_hbm, order_ref),
        (dir_hbm, dir_ref),
        (pos_hbm, pos_ref),
        (group_hbm, group_ref),
        (ts_hbm, ts_ref),
        (sw_hbm, sw_ref),
    ]
    ends = [len(pairs)]
    for g in range(1, groups):
        pairs += voltages(g)
        ends.append(len(pairs))
    copies = [start(source, target, k) for k, (source, target) in enumerate(pairs)]
    antenna_tile = iota((CHUNK // TILE_ANTENNAS, CHUNK), 1) // TILE_ANTENNAS
    sum_tile = (antenna_tile == iota(antenna_tile.shape, 0)).astype(jnp.bfloat16)
    for copy in copies[: SPLIT[0] + 1]:
        copy.wait()

    def tile_beams(g):
        products = []
        weights = aw_ref[g * CB : (g + 1) * CB].astype(jnp.float32)
        for c in range(CB):
            w_re = jnp.broadcast_to(weights[c, 0:1], (samples, antennas)).astype(jnp.bfloat16)
            w_im = jnp.broadcast_to(weights[c, 1:2], (samples, antennas)).astype(jnp.bfloat16)
            first = (g * CB + c) * rows_c
            v_re, v_im = volts[first : first + samples], volts[first + samples : first + rows_c]
            products.append(w_re * v_re - w_im * v_im)
            products.append(w_re * v_im + w_im * v_re)
        products = jnp.concatenate(products, axis=0)
        sums = [
            dot_nt(sum_tile, products[:, first : first + CHUNK])
            for first in range(0, antennas, CHUNK)
        ]
        return jnp.concatenate(sums, axis=0)

    last = tile_beams(0)
    for copy in copies[SPLIT[0] + 1 : ends[1]]:
        copy.wait()

    east_s, north_s, group_s = station_rows(pos_ref, group_ref, stations, lanes)
    lane = iota((1, lanes), 1)
    channel_lane = lane // (2 * stations)
    quarter = 0.25 * ((lane // stations) % 2).astype(jnp.float32)
    first_chan = lax.axis_index("chan") * channels
    total_chans = channels * lax.axis_size("chan")
    block = min(64, beams)

    def tied_rows(first):
        east, north, group = beam_columns(order_ref, dir_ref, first, block)
        delay = east * east_s + north * north_s
        member = jnp.where(group == group_s, scale, 0.0)
        for g in range(groups):
            freq = 1.0 + (first_chan + g * CB + channel_lane).astype(jnp.float32) / total_chans
            wave = cos_turns(delay * freq - quarter)
            tied_ref[pl.ds(first, block), g * lanes : (g + 1) * lanes] = (wave * member).astype(
                jnp.bfloat16
            )

    if beams == block:
        tied_rows(0)
    else:

        def body(i, carry):
            tied_rows(pl.multiple_of(i * block, block))
            return carry

        lax.fori_loop(0, beams // block, body, 0)

    member_table = (iota((stations, tiles), 0) == ts_ref[...] % stations).astype(jnp.float32)
    own_channel = iota((lanes, CB * rows_c), 0) // (2 * stations) == iota(
        (lanes, CB * rows_c), 1
    ) // rows_c

    imag_column = iota((tiles, CB * rows_c), 1) // samples % 2 == 1
    station_rows_of = []
    for g in range(groups):
        swt = sw_ref[g * CB : (g + 1) * CB].astype(jnp.float32)
        right = []
        for c in range(CB):
            re = swt[c, 0:1] * member_table
            im = swt[c, 1:2] * member_table
            right.append(jnp.concatenate([re, -im], axis=1))
            right.append(jnp.concatenate([im, re], axis=1))
        station_rows_of.append(jnp.concatenate(right, axis=0).astype(jnp.bfloat16))

    def tied_beams(g, beams_tile):
        width = CB * rows_c
        other = jnp.where(
            imag_column,
            -pltpu.roll(beams_tile, samples, 1),
            pltpu.roll(beams_tile, width - samples, 1),
        )
        left = jnp.concatenate([beams_tile, other], axis=0).astype(jnp.bfloat16)
        station = jnp.dot(station_rows_of[g], left, preferred_element_type=jnp.float32)
        station = jnp.where(own_channel, station, 0.0).astype(jnp.bfloat16)
        tied = jnp.dot(
            tied_ref[:, g * lanes : (g + 1) * lanes], station, preferred_element_type=jnp.float32
        )
        devices, rows, _ = out_ref.shape
        out_ref[:, :, g * CB * rows_c : (g + 1) * CB * rows_c] = tied.astype(jnp.bfloat16).reshape(
            devices, rows, CB * rows_c
        )

    for g in range(1, groups):
        if g > 1:
            for copy in copies[ends[g - 1] : ends[g]]:
                copy.wait()
        now = tile_beams(g)
        tied_beams(g - 1, last)
        last = now
    tied_beams(groups - 1, last)


def last_kernel(parts_ref, out_ref):
    n_stn, n_chan = lax.axis_size("stn"), lax.axis_size("chan")
    own_beams, rows_c, total_chans = out_ref.shape
    channels = total_chans // n_chan
    width = channels * rows_c
    parts = parts_ref[...].astype(jnp.float32)
    devices = n_stn * n_chan
    chan_of = [device_at(devices - 1 - k, n_chan) % n_chan for k in range(devices)]
    tied = [sum(parts[k] for k in range(devices) if chan_of[k] == chan) for chan in range(n_chan)]
    diagonal = iota((channels, width), 0) == iota((channels, width), 1) // rows_c
    spread = (iota((rows_c, width), 0) == iota((rows_c, width), 1) % rows_c).astype(jnp.bfloat16)
    for b in range(own_beams):
        rows = [jnp.where(diagonal, tied[chan][b : b + 1], 0.0) for chan in range(n_chan)]
        rows = jnp.concatenate(rows, axis=0).astype(jnp.bfloat16)
        out_ref[b] = dot_nt(spread, rows).astype(jnp.bfloat16)


def shards(
    volts,
    antenna_tile_weights,
    station_weights,
    tile_station,
    station_group,
    station_pos,
    beam_dir,
    beam_order,
):
    channels, _, samples, _ = volts.shape
    beams = beam_order.shape[0]
    n_stn, n_chan = lax.axis_size("stn"), lax.axis_size("chan")
    rows = beams // (n_stn * n_chan)
    width = channels * 2 * samples
    operands = (
        volts.reshape(-1, volts.shape[3]),
        antenna_tile_weights,
        station_weights,
        tile_station[None, :],
        station_group[None, :],
        station_pos.T,
        beam_dir.T,
        beam_order[None, :],
    )
    operands = [pltpu.with_memory_space_constraint(x, pltpu.HBM) for x in operands]
    partial = pl.pallas_call(
        kernel,
        out_shape=pltpu.VMEM((n_stn * n_chan, rows, width), jnp.bfloat16),
        in_specs=[pl.BlockSpec(memory_space=pltpu.HBM)] * len(operands),
        out_specs=pl.BlockSpec(memory_space=pltpu.VMEM),
        scratch_shapes=[pltpu.VMEM(x.shape, x.dtype) for x in operands]
        + [
            pltpu.VMEM((beams, channels * 2 * (station_weights.shape[2] // TPS)), jnp.bfloat16),
            pltpu.SemaphoreType.DMA((len(operands) - 1 + sum(SPLIT),)),
        ],
        compiler_params=pltpu.CompilerParams(vmem_limit_bytes=24 * 2**20),
        name="partial_tied",
    )(*operands)
    parts = lax.all_to_all(
        partial,
        ("stn", "chan"),
        split_axis=0,
        concat_axis=0,
        axis_index_groups=[[device_at(k, n_chan) for k in reversed(range(n_stn * n_chan))]],
        tiled=True,
    )
    vmem = pl.BlockSpec(memory_space=pltpu.VMEM)
    tied = pl.pallas_call(
        last_kernel,
        out_shape=jax.ShapeDtypeStruct((rows, 2 * samples, n_chan * channels), jnp.bfloat16),
        in_specs=[vmem],
        out_specs=vmem,
        compiler_params=pltpu.CompilerParams(vmem_limit_bytes=16 * 2**20),
        name="tied_beams",
    )(parts)
    return tied.transpose(0, 2, 1)


def solution(mesh):
    in_specs = (
        P("chan", None, None, "stn"),
        P("chan", None, "stn"),
        P("chan", None, "stn"),
        P("stn"),
        P(),
        P(),
        P(),
        P(),
    )
    out_specs = P(("stn", "chan"), None, None)
    return jax.shard_map(shards, mesh=mesh, in_specs=in_specs, out_specs=out_specs, check_vma=False)
```

```python
import functools
import math

import jax
import jax.numpy as jnp
from jax import lax
from jax.experimental import pallas as pl
from jax.experimental.pallas import tpu as pltpu
from jax.sharding import PartitionSpec as P

TILE_ANTENNAS = 16
TPS = 16
GROUPS = 4
CB = 8
SPLIT = (4, 2, 1)
CHUNK = 256
NT = (((1,), (1,)), ((), ()))
SIN = [(-1) ** i * (2 * math.pi) ** (2 * i + 1) / math.factorial(2 * i + 1) for i in range(7)]


def dot_nt(a, b):
    return lax.dot_general(a, b, NT, preferred_element_type=jnp.float32)


def iota(shape, dim):
    return lax.broadcasted_iota(jnp.int32, shape, dim)


def device_at(place, n_chan):
    pair, rest = place // (2 * n_chan), place % (2 * n_chan)
    return (pair * 2 + 1 - rest % 2) * n_chan + rest // 2


def beam_columns(order_ref, dir_ref, start, rows):
    beams = order_ref.shape[1]
    n_chan = lax.axis_size("chan")
    devices = lax.axis_size("stn") * n_chan
    each = beams // devices
    order = order_ref[...].astype(jnp.float32)
    lane = iota((rows, beams), 1)
    slot = iota((rows, beams), 0) + start
    place = devices - 1 - slot // each
    own = lane == device_at(place, n_chan) * each + slot % each
    ids = jnp.sum(jnp.where(own, order, 0.0), axis=1, keepdims=True)
    pick = lane.astype(jnp.float32) == ids
    east = jnp.sum(jnp.where(pick, dir_ref[0:1, :], 0.0), axis=1, keepdims=True)
    north = jnp.sum(jnp.where(pick, dir_ref[1:2, :], 0.0), axis=1, keepdims=True)
    group = ids - GROUPS * jnp.floor(ids * (1.0 / GROUPS))
    return east, north, group


def station_rows(pos_ref, group_ref, stations, lanes):
    total = group_ref.shape[1]
    first = lax.axis_index("stn") * stations
    own = iota((stations, total), 1) == iota((stations, total), 0) + first
    spread = iota((stations, lanes), 0) == iota((stations, lanes), 1) % stations

    def turn(row):
        column = jnp.sum(jnp.where(own, row, 0.0), axis=1, keepdims=True)
        return jnp.sum(jnp.where(spread, column, 0.0), axis=0, keepdims=True)

    return turn(pos_ref[0:1, :]), turn(pos_ref[1:2, :]), turn(group_ref[...].astype(jnp.float32))


def cos_turns(t):
    y = t - jnp.floor(t + 0.5)
    z = 0.25 - jnp.abs(y)
    z2 = z * z
    value = jnp.full_like(z, SIN[-1])
    for coefficient in SIN[-2::-1]:
        value = value * z2 + coefficient
    return value * z


def kernel(
    volt_hbm,
    aw_hbm,
    sw_hbm,
    ts_hbm,
    group_hbm,
    pos_hbm,
    dir_hbm,
    order_hbm,
    out_ref,
    volts,
    aw_ref,
    sw_ref,
    ts_ref,
    group_ref,
    pos_ref,
    dir_ref,
    order_ref,
    tied_ref,
    sems,
):
    channels, _, tiles = sw_ref.shape
    antennas = volt_hbm.shape[1]
    samples = volt_hbm.shape[0] // (2 * channels)
    stations = tiles // TPS
    groups = channels // CB
    assert groups == len(SPLIT)
    rows_c = 2 * samples
    beams = order_ref.shape[1]
    lanes = CB * 2 * stations
    scale = 1.0 / math.sqrt(group_ref.shape[1])

    def start(source, target, k):
        copy = pltpu.make_async_copy(source, target, sems.at[k])
        copy.start()
        return copy

    def voltages(g):
        rows = CB * rows_c // SPLIT[g]
        parts = [pl.ds(g * CB * rows_c + k * rows, rows) for k in range(SPLIT[g])]
        return [(volt_hbm.at[part], volts.at[part]) for part in parts]

    pairs = voltages(0) + [
        (aw_hbm, aw_ref),
        (order_hbm, order_ref),
        (dir_hbm, dir_ref),
        (pos_hbm, pos_ref),
        (group_hbm, group_ref),
        (ts_hbm, ts_ref),
        (sw_hbm, sw_ref),
    ]
    ends = [len(pairs)]
    for g in range(1, groups):
        pairs += voltages(g)
        ends.append(len(pairs))
    copies = [start(source, target, k) for k, (source, target) in enumerate(pairs)]
    antenna_tile = iota((CHUNK // TILE_ANTENNAS, CHUNK), 1) // TILE_ANTENNAS
    sum_tile = (antenna_tile == iota(antenna_tile.shape, 0)).astype(jnp.bfloat16)
    for copy in copies[: SPLIT[0] + 1]:
        copy.wait()

    def tile_beams(g):
        products = []
        weights = aw_ref[g * CB : (g + 1) * CB].astype(jnp.float32)
        for c in range(CB):
            w_re = jnp.broadcast_to(weights[c, 0:1], (samples, antennas)).astype(jnp.bfloat16)
            w_im = jnp.broadcast_to(weights[c, 1:2], (samples, antennas)).astype(jnp.bfloat16)
            first = (g * CB + c) * rows_c
            v_re, v_im = volts[first : first + samples], volts[first + samples : first + rows_c]
            products.append(w_re * v_re - w_im * v_im)
            products.append(w_re * v_im + w_im * v_re)
        products = jnp.concatenate(products, axis=0)
        sums = [
            dot_nt(sum_tile, products[:, first : first + CHUNK])
            for first in range(0, antennas, CHUNK)
        ]
        return jnp.concatenate(sums, axis=0)

    last = tile_beams(0)
    for copy in copies[SPLIT[0] + 1 : ends[1]]:
        copy.wait()

    east_s, north_s, group_s = station_rows(pos_ref, group_ref, stations, lanes)
    lane = iota((1, lanes), 1)
    channel_lane = lane // (2 * stations)
    quarter = 0.25 * ((lane // stations) % 2).astype(jnp.float32)
    first_chan = lax.axis_index("chan") * channels
    total_chans = channels * lax.axis_size("chan")
    block = min(64, beams)

    def tied_rows(first):
        east, north, group = beam_columns(order_ref, dir_ref, first, block)
        delay = east * east_s + north * north_s
        member = jnp.where(group == group_s, scale, 0.0)
        for g in range(groups):
            freq = 1.0 + (first_chan + g * CB + channel_lane).astype(jnp.float32) / total_chans
            wave = cos_turns(delay * freq - quarter)
            tied_ref[pl.ds(first, block), g * lanes : (g + 1) * lanes] = (wave * member).astype(
                jnp.bfloat16
            )

    if beams == block:
        tied_rows(0)
    else:

        def body(i, carry):
            tied_rows(pl.multiple_of(i * block, block))
            return carry

        lax.fori_loop(0, beams // block, body, 0)

    member_table = (iota((stations, tiles), 0) == ts_ref[...] % stations).astype(jnp.float32)
    own_channel = iota((lanes, CB * rows_c), 0) // (2 * stations) == iota(
        (lanes, CB * rows_c), 1
    ) // rows_c

    imag_column = iota((tiles, CB * rows_c), 1) // samples % 2 == 1
    station_rows_of = []
    for g in range(groups):
        swt = sw_ref[g * CB : (g + 1) * CB].astype(jnp.float32)
        right = []
        for c in range(CB):
            re = swt[c, 0:1] * member_table
            im = swt[c, 1:2] * member_table
            right.append(jnp.concatenate([re, -im], axis=1))
            right.append(jnp.concatenate([im, re], axis=1))
        station_rows_of.append(jnp.concatenate(right, axis=0).astype(jnp.bfloat16))

    def tied_beams(g, beams_tile):
        width = CB * rows_c
        other = jnp.where(
            imag_column,
            -pltpu.roll(beams_tile, samples, 1),
            pltpu.roll(beams_tile, width - samples, 1),
        )
        left = jnp.concatenate([beams_tile, other], axis=0).astype(jnp.bfloat16)
        station = jnp.dot(station_rows_of[g], left, preferred_element_type=jnp.float32)
        station = jnp.where(own_channel, station, 0.0).astype(jnp.bfloat16)
        tied = jnp.dot(
            tied_ref[:, g * lanes : (g + 1) * lanes], station, preferred_element_type=jnp.float32
        )
        devices, rows, _ = out_ref.shape
        out_ref[:, :, g * CB * rows_c : (g + 1) * CB * rows_c] = tied.astype(jnp.bfloat16).reshape(
            devices, rows, CB * rows_c
        )

    for g in range(1, groups):
        if g > 1:
            for copy in copies[ends[g - 1] : ends[g]]:
                copy.wait()
        now = tile_beams(g)
        tied_beams(g - 1, last)
        last = now
    tied_beams(groups - 1, last)


def last_kernel(parts_ref, out_ref):
    n_stn, n_chan = lax.axis_size("stn"), lax.axis_size("chan")
    own_beams, rows_c, total_chans = out_ref.shape
    channels = total_chans // n_chan
    width = channels * rows_c
    parts = parts_ref[...].astype(jnp.float32)
    devices = n_stn * n_chan
    chan_of = [device_at(devices - 1 - k, n_chan) % n_chan for k in range(devices)]
    tied = [sum(parts[k] for k in range(devices) if chan_of[k] == chan) for chan in range(n_chan)]
    diagonal = iota((channels, width), 0) == iota((channels, width), 1) // rows_c
    spread = (iota((rows_c, width), 0) == iota((rows_c, width), 1) % rows_c).astype(jnp.bfloat16)
    for b in range(own_beams):
        rows = [jnp.where(diagonal, tied[chan][b : b + 1], 0.0) for chan in range(n_chan)]
        rows = jnp.concatenate(rows, axis=0).astype(jnp.bfloat16)
        out_ref[b] = dot_nt(spread, rows).astype(jnp.bfloat16)


def shards(
    volts,
    antenna_tile_weights,
    station_weights,
    tile_station,
    station_group,
    station_pos,
    beam_dir,
    beam_order,
):
    channels, _, samples, _ = volts.shape
    beams = beam_order.shape[0]
    n_stn, n_chan = lax.axis_size("stn"), lax.axis_size("chan")
    rows = beams // (n_stn * n_chan)
    width = channels * 2 * samples
    operands = (
        volts.reshape(-1, volts.shape[3]),
        antenna_tile_weights,
        station_weights,
        tile_station[None, :],
        station_group[None, :],
        station_pos.T,
        beam_dir.T,
        beam_order[None, :],
    )
    operands = [pltpu.with_memory_space_constraint(x, pltpu.HBM) for x in operands]
    partial = pl.pallas_call(
        kernel,
        out_shape=pltpu.VMEM((n_stn * n_chan, rows, width), jnp.bfloat16),
        in_specs=[pl.BlockSpec(memory_space=pltpu.HBM)] * len(operands),
        out_specs=pl.BlockSpec(memory_space=pltpu.VMEM),
        scratch_shapes=[pltpu.VMEM(x.shape, x.dtype) for x in operands]
        + [
            pltpu.VMEM((beams, channels * 2 * (station_weights.shape[2] // TPS)), jnp.bfloat16),
            pltpu.SemaphoreType.DMA((len(operands) - 1 + sum(SPLIT),)),
        ],
        compiler_params=pltpu.CompilerParams(vmem_limit_bytes=24 * 2**20),
        name="partial_tied",
    )(*operands)
    parts = lax.all_to_all(
        partial,
        ("stn", "chan"),
        split_axis=0,
        concat_axis=0,
        axis_index_groups=[[device_at(k, n_chan) for k in reversed(range(n_stn * n_chan))]],
        tiled=True,
    )
    vmem = pl.BlockSpec(memory_space=pltpu.VMEM)
    tied = pl.pallas_call(
        last_kernel,
        out_shape=jax.ShapeDtypeStruct((rows, 2 * samples, n_chan * channels), jnp.bfloat16),
        in_specs=[vmem],
        out_specs=vmem,
        compiler_params=pltpu.CompilerParams(vmem_limit_bytes=16 * 2**20),
        name="tied_beams",
    )(parts)
    return tied.transpose(0, 2, 1)


def solution(mesh):
    in_specs = (
        P("chan", None, None, "stn"),
        P("chan", None, "stn"),
        P("chan", None, "stn"),
        P("stn"),
        P(),
        P(),
        P(),
        P(),
    )
    out_specs = P(("stn", "chan"), None, None)
    return jax.shard_map(shards, mesh=mesh, in_specs=in_specs, out_specs=out_specs, check_vma=False)
```
